128 devices in a mesh: dp: 8 (over z, x_lo), fsdp: 16 (over y, x_hi, core).
Axes of the slice: x: 4 (x_hi: 2, x_lo: 2; x = x_hi * 2 + x_lo), y: 4, z: 4, core: 2. Of those that a mesh axis runs over, the one named last changes fastest.
Arguments:
- incoming_activations: bfloat16 [16384, 768], P(('dp', 'fsdp')), may hold values from -24 to 24
- sequence_opening_memory: float32 [128, 12, 64, 64], P(('dp', 'fsdp')), may hold values from -10 to 10
- prior_standardize_factor: bfloat16 [768], P(('dp', 'fsdp')), may hold values from 0.099609375 to 1.8984375
- prior_standardize_offset: bfloat16 [768], P(('dp', 'fsdp')), may hold values from -3 to 3
- acceptor_lerp_factor: bfloat16 [768], P(('dp', 'fsdp')), may hold values from 0 to 1
- address_lerp_factor: bfloat16 [768], P(('dp', 'fsdp')), may hold values from 0 to 1
- content_lerp_factor: bfloat16 [768], P(('dp', 'fsdp')), may hold values from 0 to 1
- sigmoid_lerp_factor: bfloat16 [768], P(('dp', 'fsdp')), may hold values from 0 to 1
- acceptor_matrix: bfloat16 [768, 768], P(('dp', 'fsdp')), may hold values from -0.21875 to 0.21875
- address_matrix: bfloat16 [768, 768], P(('dp', 'fsdp')), may hold values from -0.21875 to 0.21875
- content_matrix: bfloat16 [768, 768], P(('dp', 'fsdp')), may hold values from -0.21875 to 0.21875
- sigmoid_matrix: bfloat16 [768, 768], P(('dp', 'fsdp')), may hold values from -0.21875 to 0.21875
- lane_fading_exponent: bfloat16 [768], P(('dp', 'fsdp')), may hold values from -6.5 to -1
- present_reward_vector: bfloat16 [768], P(('dp', 'fsdp')), may hold values from -3 to 3
- cluster_standardize_factor: bfloat16 [768], P(('dp', 'fsdp')), may hold values from 0.099609375 to 1.8984375
- cluster_standardize_offset: bfloat16 [768], P(('dp', 'fsdp')), may hold values from -3 to 3
- mixer_result_matrix: bfloat16 [768, 768], P(('dp', 'fsdp')), may hold values from -0.21875 to 0.21875
- latter_standardize_factor: bfloat16 [768], P(('dp', 'fsdp')), may hold values from 0.099609375 to 1.8984375
- latter_standardize_offset: bfloat16 [768], P(('dp', 'fsdp')), may hold values from -3 to 3
- feedforward_address_lerp: bfloat16 [768], P(('dp', 'fsdp')), may hold values from 0 to 1
- feedforward_sigmoid_lerp: bfloat16 [768], P(('dp', 'fsdp')), may hold values from 0 to 1
- feedforward_address_matrix: bfloat16 [768, 2688], P(('dp', 'fsdp')), may hold values from -0.21875 to 0.21875
- feedforward_content_matrix: bfloat16 [2688, 768], P(('dp', 'fsdp')), may hold values from -0.125 to 0.125
- feedforward_acceptor_matrix: bfloat16 [768, 768], P(('dp', 'fsdp')), may hold values from -0.21875 to 0.21875
- upstream_derivative: bfloat16 [16384, 768], P(('dp', 'fsdp')), may hold values from -6 to 6
Outputs:
- layer_output: float32 [16384, 768], P(('dp', 'fsdp'))
- input_grad: float32 [16384, 768], P(('dp', 'fsdp'))
- grad_first_gain: float32 [768], P(('dp', 'fsdp'))
- grad_first_bias: float32 [768], P(('dp', 'fsdp'))
- grad_lerp_recept: float32 [768], P(('dp', 'fsdp'))
- grad_lerp_key: float32 [768], P(('dp', 'fsdp'))
- grad_lerp_value: float32 [768], P(('dp', 'fsdp'))
- grad_lerp_gate: float32 [768], P(('dp', 'fsdp'))
- grad_proj_recept: float32 [768, 768], P(('dp', 'fsdp'))
- grad_proj_key: float32 [768, 768], P(('dp', 'fsdp'))
- grad_proj_value: float32 [768, 768], P(('dp', 'fsdp'))
- grad_proj_gate: float32 [768, 768], P(('dp', 'fsdp'))
- grad_time_decay: float32 [768], P(('dp', 'fsdp'))
- grad_time_bonus: float32 [768], P(('dp', 'fsdp'))
- grad_group_gain: float32 [768], P(('dp', 'fsdp'))
- grad_group_bias: float32 [768], P(('dp', 'fsdp'))
- grad_proj_output: float32 [768, 768], P(('dp', 'fsdp'))
- grad_second_gain: float32 [768], P(('dp', 'fsdp'))
- grad_second_bias: float32 [768], P(('dp', 'fsdp'))
- grad_lerp_channel: float32 [768], P(('dp', 'fsdp'))
- grad_lerp_gating: float32 [768], P(('dp', 'fsdp'))
- grad_channel_key: float32 [768, 2688], P(('dp', 'fsdp'))
- grad_channel_value: float32 [2688, 768], P(('dp', 'fsdp'))
- grad_channel_gate: float32 [768, 768], P(('dp', 'fsdp'))
The draws below stay inside these ranges and needn't reach their ends.
All inputs are finite; a program needn't handle non-finite values.
Results may differ from the reference program's by a relative error of at most 0.02.
Values may be sent and summed in bfloat16 or wider, within the bound.
A program may use at most 128 MiB of HBM per device.

```python
import math
import jax
import jax.numpy as jnp
from jax import lax

EMBED_SIZE = 768
MIXER_LANES = 12
LANE_SIZE = 64
FF = 2688
SPAN = 64
TOK_DEV = 128
SEQS = 128
TOKENS = 16384


def with_spikes(result, key, source, target, parts, factor):
    owner, partner = [(jnp.arange(result.shape[axis_at]) // (result.shape[axis_at] // parts)).reshape([-1 if axis == axis_at else 1 for axis in range(result.ndim)]) for axis_at in (source, target)]
    chosen = jax.random.permutation(key, parts)[partner]
    strong = (owner == chosen) | (owner == (partner + parts // 2) % parts)
    return jnp.where(strong, factor * result, result)


def levels(rng, extent, pieces, least, top_value):
    def one(axis_at, shards_of):
        heights = jax.random.uniform(jax.random.fold_in(jax.random.fold_in(rng, 6), axis_at), (shards_of,), jnp.float32, least / len(pieces), top_value / len(pieces))
        return jnp.repeat(jnp.exp(heights), extent[axis_at] // shards_of).reshape((-1,) + (1,) * (len(extent) - axis_at - 1))

    gain = one(*pieces[0])
    for cut in pieces[1:]:
        gain = gain * one(*cut)
    return gain


def gaussian(key, dims, deviation, most, split=(), kind=jnp.bfloat16):
    result = jax.random.normal(key, dims, jnp.float32) * deviation
    if len(split) > 0:
        result = levels(key, dims, split, -0.22, 0.18) * result
    return jnp.clip(result, min=-most, max=most).astype(kind)


def bell_draw_with(own_key, shape, width, limit, pieces, heavy, held_as=jnp.bfloat16):
    array = width * jax.random.normal(own_key, shape, jnp.float32)
    if pieces:
        array = array * levels(own_key, shape, pieces, -0.22, 0.18)
    return jnp.clip(with_spikes(array, jax.random.fold_in(own_key, 3), *heavy), -limit, limit).astype(held_as)


def setup_inputs(seed: int = 0) -> dict:
    key_of = jax.random.split(jax.random.key(seed), 26)
    return {
        "incoming_activations": bell_draw_with(key_of[0], (TOKENS, EMBED_SIZE), 1.0, 24.0, ((0, 128),), (0, 1, 128, 5.5)),
        "sequence_opening_memory": gaussian(key_of[1], (SEQS, MIXER_LANES, LANE_SIZE, LANE_SIZE), 2.0, 10.0, ((0, 128),), jnp.float32),
        "prior_standardize_factor": jnp.clip(1.0 + 0.18 * jax.random.normal(key_of[2], (EMBED_SIZE,), jnp.float32), 0.099609375, 1.8984375).astype(jnp.bfloat16),
        "prior_standardize_offset": gaussian(key_of[3], (EMBED_SIZE,), 0.3, 3.0, ((0, 128),)),
        "acceptor_lerp_factor": jnp.clip(1.0 * jax.random.uniform(key_of[4], (EMBED_SIZE,), jnp.float32) ** levels(key_of[4], (EMBED_SIZE,), ((0, 128),), -0.2, 0.2), 0.0, 1.0).astype(jnp.bfloat16),
        "address_lerp_factor": jnp.clip(1.0 * jax.random.uniform(key_of[5], (EMBED_SIZE,), jnp.float32) ** levels(key_of[5], (EMBED_SIZE,), ((0, 128),), -0.2, 0.2), 0.0, 1.0).astype(jnp.bfloat16),
        "content_lerp_factor": jnp.clip(1.0 * jax.random.uniform(key_of[6], (EMBED_SIZE,), jnp.float32) ** levels(key_of[6], (EMBED_SIZE,), ((0, 128),), -0.2, 0.2), 0.0, 1.0).astype(jnp.bfloat16),
        "sigmoid_lerp_factor": jnp.clip(1.0 * jax.random.uniform(key_of[7], (EMBED_SIZE,), jnp.float32) ** levels(key_of[7], (EMBED_SIZE,), ((0, 128),), -0.2, 0.2), 0.0, 1.0).astype(jnp.bfloat16),
        "acceptor_matrix": gaussian(key_of[8], (EMBED_SIZE, EMBED_SIZE), EMBED_SIZE ** -0.5, 0.21875, ((0, 128),)),
        "address_matrix": gaussian(key_of[9], (EMBED_SIZE, EMBED_SIZE), EMBED_SIZE ** -0.5, 0.21875, ((0, 128),)),
        "content_matrix": gaussian(key_of[10], (EMBED_SIZE, EMBED_SIZE), EMBED_SIZE ** -0.5, 0.21875, ((0, 128),)),
        "sigmoid_matrix": gaussian(key_of[11], (EMBED_SIZE, EMBED_SIZE), EMBED_SIZE ** -0.5, 0.21875, ((0, 128),)),
        "lane_fading_exponent": jnp.clip(-6.5 + 5.5 * jax.random.uniform(key_of[12], (EMBED_SIZE,), jnp.float32) ** levels(key_of[12], (EMBED_SIZE,), ((0, 128),), -0.2, 0.2), -6.5, -1.0).astype(jnp.bfloat16),
        "present_reward_vector": gaussian(key_of[13], (EMBED_SIZE,), 1.0, 3.0, ((0, 128),)),
        "cluster_standardize_factor": jnp.clip(1.0 + 0.18 * jax.random.normal(key_of[14], (EMBED_SIZE,), jnp.float32), 0.099609375, 1.8984375).astype(jnp.bfloat16),
        "cluster_standardize_offset": gaussian(key_of[15], (EMBED_SIZE,), 0.3, 3.0, ((0, 128),)),
        "mixer_result_matrix": gaussian(key_of[16], (EMBED_SIZE, EMBED_SIZE), EMBED_SIZE ** -0.5, 0.21875, ((0, 128),)),
        "latter_standardize_factor": jnp.clip(1.0 + 0.18 * jax.random.normal(key_of[17], (EMBED_SIZE,), jnp.float32), 0.099609375, 1.8984375).astype(jnp.bfloat16),
        "latter_standardize_offset": gaussian(key_of[18], (EMBED_SIZE,), 0.3, 3.0, ((0, 128),)),
        "feedforward_address_lerp": jnp.clip(1.0 * jax.random.uniform(key_of[19], (EMBED_SIZE,), jnp.float32) ** levels(key_of[19], (EMBED_SIZE,), ((0, 128),), -0.2, 0.2), 0.0, 1.0).astype(jnp.bfloat16),
        "feedforward_sigmoid_lerp": jnp.clip(1.0 * jax.random.uniform(key_of[20], (EMBED_SIZE,), jnp.float32) ** levels(key_of[20], (EMBED_SIZE,), ((0, 128),), -0.2, 0.2), 0.0, 1.0).astype(jnp.bfloat16),
        "feedforward_address_matrix": gaussian(key_of[21], (EMBED_SIZE, FF), EMBED_SIZE ** -0.5, 0.21875, ((0, 128),)),
        "feedforward_content_matrix": gaussian(key_of[22], (FF, EMBED_SIZE), FF ** -0.5, 0.125, ((0, 128),)),
        "feedforward_acceptor_matrix": gaussian(key_of[23], (EMBED_SIZE, EMBED_SIZE), EMBED_SIZE ** -0.5, 0.21875, ((0, 128),)),
        "upstream_derivative": gaussian(key_of[24], (TOKENS, EMBED_SIZE), 1.0, 6.0, ((0, 128),)),
    }


highest = lax.Precision.HIGHEST
norm_eps = 1e-05
group_eps = 0.00064

@jax.custom_vjp
def low(v):
    return lax.optimization_barrier(v.astype(jnp.bfloat16)).astype(jnp.float32)

@jax.custom_vjp
def low_back(v):
    return v

def low_keep(v):
    return (low(v), None)

def low_pass(kept, grad):
    return (grad,)

def back_keep(v):
    return (v, None)

def back_low(kept, grad):
    return (low(grad),)
low.defvjp(low_keep, low_pass)
low_back.defvjp(back_keep, back_low)

def layer_norm(values, scale_vec, shift_vec):
    average = lax.optimization_barrier(jnp.mean(values, axis=-1, keepdims=True))
    centred = values - average
    variance = lax.optimization_barrier(jnp.mean(centred * centred, axis=-1, keepdims=True))
    return centred * lax.rsqrt(variance + norm_eps) * scale_vec + shift_vec

def time_shift(values):
    return jnp.concatenate([jnp.zeros_like(values[..., :1, :]), values[..., :-1, :]], axis=-2)

def blend(normed, previous, weights):
    return normed * weights + previous * (1.0 - weights)

def project(inputs, matrix):
    return low_back(jnp.dot(low(inputs), matrix, precision=highest))

def memory_segment_routine(running_memory, result_fragments, fading_exponent, reward_addend):
    acceptor_vectors, address_vectors, content_vectors = result_fragments
    block_len = acceptor_vectors.shape[1]
    places = jnp.arange(block_len).astype(jnp.float32)
    fall_query = jnp.exp(places[:, None, None] * fading_exponent)
    fall_key = jnp.exp(-(places[:, None, None] + 1.0) * fading_exponent)
    tail_key = jnp.exp((block_len - 1.0 - places)[:, None, None] * fading_exponent)
    decayed = acceptor_vectors * fall_query
    scores = jnp.einsum('gthi,gshi->ghts', decayed, address_vectors * fall_key, precision=highest)
    below_diag = places[:, None] > places[None, :]
    scores = jnp.where(below_diag, scores, 0.0)
    present_position = lax.optimization_barrier(jnp.sum(acceptor_vectors * reward_addend * address_vectors, axis=-1))
    update_results = jnp.einsum('ghts,gshj->gthj', scores, content_vectors, precision=highest)
    update_results = update_results + present_position[..., None] * content_vectors
    update_results = update_results + jnp.einsum('gthi,ghij->gthj', decayed, running_memory, precision=highest)
    running_memory = jnp.exp(block_len * fading_exponent)[None, :, :, None] * running_memory + jnp.einsum('gshi,gshj->ghij', address_vectors * tail_key, content_vectors, precision=highest)
    return (running_memory, update_results)

def memory_recurrence_routine(acceptor_vectors, address_vectors, content_vectors, fading_exponent, reward_addend, opening_memory):
    groups, length = (acceptor_vectors.shape[0], acceptor_vectors.shape[1])
    blocks = length // SPAN

    def arrange(tensor):
        return jnp.moveaxis(tensor.reshape(groups, blocks, SPAN, MIXER_LANES, LANE_SIZE), 1, 0)
    recurrence_update = jax.checkpoint(lambda running_memory, result_fragments: memory_segment_routine(running_memory, result_fragments, fading_exponent, reward_addend))
    last_state, update_results = lax.scan(recurrence_update, opening_memory, (arrange(acceptor_vectors), arrange(address_vectors), arrange(content_vectors)))
    return jnp.moveaxis(update_results, 0, 1).reshape(groups, length, MIXER_LANES, LANE_SIZE)

def group_norm(update_results, scale_vec, shift_vec):
    average = lax.optimization_barrier(jnp.mean(update_results, axis=-1, keepdims=True))
    centred = update_results - average
    variance = lax.optimization_barrier(jnp.mean(centred * centred, axis=-1, keepdims=True))
    scaled = (centred * lax.rsqrt(variance + group_eps)).reshape(update_results.shape[:-2] + (MIXER_LANES * LANE_SIZE,))
    return scaled * scale_vec + shift_vec

def mixer_routine(opening_memory, acceptor_vectors, address_vectors, content_vectors, sigmoid_preactivation, lane_fading_exponent, present_reward_vector, cluster_standardize_factor, cluster_standardize_offset):
    divide_among_lanes = acceptor_vectors.shape[:-1] + (MIXER_LANES, LANE_SIZE)
    fading_exponent = -jnp.exp(lane_fading_exponent.reshape(MIXER_LANES, LANE_SIZE))
    update_results = memory_recurrence_routine(acceptor_vectors.reshape(divide_among_lanes), address_vectors.reshape(divide_among_lanes), content_vectors.reshape(divide_among_lanes), fading_exponent, present_reward_vector.reshape(MIXER_LANES, LANE_SIZE), opening_memory)
    grouped = group_norm(update_results, cluster_standardize_factor, cluster_standardize_offset)
    return grouped * jax.nn.silu(sigmoid_preactivation)

def forward(tokens, opening_memory, learnable_arrays):
    prior_standardize_factor, prior_standardize_offset, acceptor_lerp_factor, address_lerp_factor, content_lerp_factor, sigmoid_lerp_factor, acceptor_matrix, address_matrix, content_matrix, sigmoid_matrix, lane_fading_exponent, present_reward_vector, cluster_standardize_factor, cluster_standardize_offset, mixer_result_matrix, latter_standardize_factor, latter_standardize_offset, feedforward_address_lerp, feedforward_sigmoid_lerp, feedforward_address_matrix, feedforward_content_matrix, feedforward_acceptor_matrix = learnable_arrays
    normed = layer_norm(tokens, prior_standardize_factor, prior_standardize_offset)
    previous = time_shift(normed)
    acceptor_vectors = project(blend(normed, previous, acceptor_lerp_factor), acceptor_matrix)
    address_vectors = project(blend(normed, previous, address_lerp_factor), address_matrix)
    content_vectors = project(blend(normed, previous, content_lerp_factor), content_matrix)
    sigmoid_preactivation = project(blend(normed, previous, sigmoid_lerp_factor), sigmoid_matrix)
    masked_result = mixer_routine(opening_memory, acceptor_vectors, address_vectors, content_vectors, sigmoid_preactivation, lane_fading_exponent, present_reward_vector, cluster_standardize_factor, cluster_standardize_offset)
    middle = tokens + project(masked_result, mixer_result_matrix)
    normed_mid = layer_norm(middle, latter_standardize_factor, latter_standardize_offset)
    previous_mid = time_shift(normed_mid)
    pre_hidden = project(blend(normed_mid, previous_mid, feedforward_address_lerp), feedforward_address_matrix)
    hidden = jnp.square(jax.nn.relu(pre_hidden))
    value_out = project(hidden, feedforward_content_matrix)
    gating = jax.nn.sigmoid(project(blend(normed_mid, previous_mid, feedforward_sigmoid_lerp), feedforward_acceptor_matrix))
    return middle + gating * value_out

def reference(incoming_activations, sequence_opening_memory, prior_standardize_factor, prior_standardize_offset, acceptor_lerp_factor, address_lerp_factor, content_lerp_factor, sigmoid_lerp_factor, acceptor_matrix, address_matrix, content_matrix, sigmoid_matrix, lane_fading_exponent, present_reward_vector, cluster_standardize_factor, cluster_standardize_offset, mixer_result_matrix, latter_standardize_factor, latter_standardize_offset, feedforward_address_lerp, feedforward_sigmoid_lerp, feedforward_address_matrix, feedforward_content_matrix, feedforward_acceptor_matrix, upstream_derivative):
    learnable_arrays = tuple((recurrence_element.astype(jnp.float32) for recurrence_element in (prior_standardize_factor, prior_standardize_offset, acceptor_lerp_factor, address_lerp_factor, content_lerp_factor, sigmoid_lerp_factor, acceptor_matrix, address_matrix, content_matrix, sigmoid_matrix, lane_fading_exponent, present_reward_vector, cluster_standardize_factor, cluster_standardize_offset, mixer_result_matrix, latter_standardize_factor, latter_standardize_offset, feedforward_address_lerp, feedforward_sigmoid_lerp, feedforward_address_matrix, feedforward_content_matrix, feedforward_acceptor_matrix)))
    batch_seqs = math.gcd(SEQS, max(1, 4096 // TOK_DEV))
    rounds = SEQS // batch_seqs
    inputs = incoming_activations.astype(jnp.float32).reshape(rounds, batch_seqs, TOK_DEV, EMBED_SIZE)
    cotangents = upstream_derivative.astype(jnp.float32).reshape(rounds, batch_seqs, TOK_DEV, EMBED_SIZE)
    states = sequence_opening_memory.astype(jnp.float32).reshape(rounds, batch_seqs, MIXER_LANES, LANE_SIZE, LANE_SIZE)

    def one_round(totals, result_fragments):
        tokens, opening_memory, upstream = result_fragments
        update_results, pullback = jax.vjp(lambda tokens_in, weights_in: forward(tokens_in, opening_memory, weights_in), tokens, learnable_arrays)
        grad_tokens, grad_params = pullback(upstream)
        totals = tuple((left + right for left, right in zip(totals, grad_params)))
        return (totals, (update_results, grad_tokens))
    zeros = tuple((jnp.zeros_like(recurrence_element) for recurrence_element in learnable_arrays))
    totals, (update_results, grad_tokens) = lax.scan(one_round, zeros, (inputs, states, cotangents))
    return (update_results.reshape(TOKENS, EMBED_SIZE), grad_tokens.reshape(TOKENS, EMBED_SIZE), totals[0], totals[1], totals[2], totals[3], totals[4], totals[5], totals[6], totals[7], totals[8], totals[9], totals[10], totals[11], totals[12], totals[13], totals[14], totals[15], totals[16], totals[17], totals[18], totals[19], totals[20], totals[21])
```

```python
from functools import partial

import jax
import jax.numpy as jnp
import numpy as np
from jax import lax
from jax.experimental import pallas as pl
from jax.experimental.pallas import tpu as pltpu
from jax.sharding import PartitionSpec as P

MESH = pl.DeviceIdType.MESH
BF = jnp.bfloat16
F32 = jnp.float32
HIGHEST = lax.Precision.HIGHEST
VMEM = pl.BlockSpec(memory_space=pltpu.VMEM)
ANY = pl.BlockSpec(memory_space=pl.ANY)

NORM_EPS = 1e-05
GROUP_EPS = 0.00064
TOK = 128
EMB = 768
HALF = 3328
COLS = 384
W1A, W1B = 1408, 1280
FF = 2688
VEC = 3200


def _order():
    order = np.zeros(EMB, np.int64)
    for x in range(4):
        for y in range(4):
            for z in range(4):
                for c in range(2):
                    device = z * 32 + (x % 2) * 16 + y * 4 + (x // 2) * 2 + c
                    place = (x * 4 + y) * 48 + (z * 2 + c) * 6
                    order[place : place + 6] = 6 * device + np.arange(6)
    return order


def _spread():
    spread = np.zeros((EMB, EMB), np.float32)
    spread[_order(), np.arange(EMB)] = 1.0
    return spread


def _line_pick():
    pick = np.zeros((48, 64), np.float32)
    for z in range(4):
        for c in range(2):
            for r in range(6):
                pick[(z * 2 + c) * 6 + r, z * 16 + c * 8 + r] = 1.0
    return pick


def _plane_pick():
    pick = np.zeros((432, 512), np.float32)
    for chip in range(8):
        for c in range(2):
            base = chip * 64 + c * 32
            for r in range(6):
                pick[(chip * 2 + c) * 6 + r, base + r] = 1.0
            for r in range(21):
                pick[96 + (chip * 2 + c) * 21 + r, base + 6 + r] = 1.0
    return pick


def rem4(value):
    return lax.rem(value, 4)


class Place:
    def __init__(self):
        dp, fs = lax.axis_index("dp"), lax.axis_index("fsdp")
        self.z, self.xlo = lax.div(dp, 2), lax.rem(dp, 2)
        self.y, self.xhi = lax.div(fs, 4), lax.rem(lax.div(fs, 2), 2)
        self.c = lax.rem(fs, 2)
        self.x = self.xhi * 2 + self.xlo
        self.dp = dp

    def device(self, z, y, x, c):
        return (z * 2 + lax.rem(x, 2), y * 4 + lax.div(x, 2) * 2 + c)

    def sibling(self):
        return self.device(self.z, self.y, self.x, 1 - self.c)

    def up(self, k):
        return self.device(rem4(self.z + k), self.y, self.x, self.c)

    def first(self, k):
        y, x = rem4(self.y + k * (1 - self.c)), rem4(self.x + k * self.c)
        return self.device(self.z, y, x, self.c)

    def last(self, k):
        y, x = rem4(self.y + k * self.c), rem4(self.x + k * (1 - self.c))
        return self.device(self.z, y, x, self.c)

    def slot(self, m, k, core=None):
        c = self.c if core is None else core
        x = rem4(self.x + m * c + k * (1 - c))
        y = rem4(self.y + m * (1 - c) + k * c)
        return x * 4 + y

    def plane(self, k):
        index = lax.rem(self.y * 2 + self.xhi + k, 8)
        y, xhi = lax.div(index, 2), lax.rem(index, 2)
        return self.device(self.z, y, xhi * 2 + self.xlo, self.c), index

    def twin(self):
        return self.device(self.z, self.y, self.xhi * 2 + 1 - self.xlo, self.c)

    def meet(self):
        barrier = pltpu.get_barrier_semaphore()
        mates = [self.sibling(), self.twin()]
        mates += [self.up(k) for k in (1, 2, 3)]
        mates += [self.first(k) for k in (1, 2, 3)]
        mates += [self.last(k) for k in (1, 2, 3)]
        mates += [self.plane(k)[0] for k in range(1, 8)]
        for mate in mates:
            pl.semaphore_signal(barrier, inc=1, device_id=mate, device_id_type=MESH)
        pl.semaphore_wait(barrier, len(mates))


class Sender:
    def __init__(self, send_sems, recv_sems):
        self.send_sems, self.recv_sems = send_sems, recv_sems
        self.started = []

    def send(self, source, target, device):
        index = len(self.started)
        copy = pltpu.make_async_remote_copy(
            src_ref=source,
            dst_ref=target,
            send_sem=self.send_sems.at[index],
            recv_sem=self.recv_sems.at[index],
            device_id=device,
            device_id_type=MESH,
        )
        copy.start()
        self.started.append(copy)
        return copy

    def finish(self):
        for copy in self.started:
            copy.wait_send()


def rows(start, size, unit=16):
    return pl.ds(pl.multiple_of(start, unit), size)


GATHER_COPIES = 96


def gather_kernel(
    pack_n, pack_z, pick_n, pick_z, out_n, out_o, out_2,
    got_n, stage_n, block_n, half_z, stage_z, block_o, block_2,
    send_sems, recv_sems, local_sems,
):
    at = Place()
    c = at.c
    at.meet()
    net = Sender(send_sems, recv_sems)
    sib = at.sibling()

    swap_n = net.send(pack_n.at[1 - c], got_n, sib)
    swap_z = net.send(pack_z.at[1 - c], half_z.at[c], sib)
    half_z[c] = pack_z[c]
    swap_n.wait_recv()
    stage_n[at.z] = pack_n[c] + got_n[...]
    ups = [net.send(stage_n.at[at.z], stage_n.at[at.z], at.up(k)) for k in (1, 2, 3)]
    swap_z.wait_recv()
    mine = at.y * 2 + at.xhi
    planes = []
    for k in range(1, 8):
        mate, _ = at.plane(k)
        planes.append(net.send(half_z, stage_z.at[mine], mate))
    stage_z[mine] = half_z[...]

    for copy in ups:
        copy.wait_recv()
    block_n[...] = jnp.dot(
        pick_n[...], stage_n[...].reshape(64, HALF), preferred_element_type=F32
    ).astype(BF)

    def place_n(slot):
        return out_n.at[c, rows(48 * slot, 48)]

    spot = place_n(at.slot(0, 0))
    firsts = [net.send(block_n, spot, at.first(k)) for k in (1, 2, 3)]
    lasts = [[net.send(block_n, spot, at.last(k)) for k in (1, 2, 3)]]
    to_sib = [net.send(block_n, spot, sib)]
    keep_n = pltpu.make_async_copy(block_n, spot, local_sems.at[0])
    keep_n.start()

    for copy in planes:
        copy.wait_recv()
    block_z = jnp.dot(
        pick_z[...], stage_z[...].reshape(512, COLS), preferred_element_type=F32
    ).astype(BF)
    block_o[...] = block_z[:96]
    block_2[...] = block_z[96:]

    def place_o(dp):
        return out_o.at[c, rows(96 * dp, 96)]

    def place_2(dp):
        return out_2.at[c, rows(336 * dp, 336)]

    me = at.dp
    twin_o = net.send(block_o, place_o(me), at.twin())
    twin_2 = net.send(block_2, place_2(me), at.twin())
    ups_o = [[net.send(block_o, place_o(me), at.up(k)) for k in (1, 2, 3)]]
    ups_2 = [[net.send(block_2, place_2(me), at.up(k)) for k in (1, 2, 3)]]
    to_sib.append(net.send(block_o, place_o(me), sib))
    to_sib.append(net.send(block_2, place_2(me), sib))
    keep_o = pltpu.make_async_copy(block_o, place_o(me), local_sems.at[1])
    keep_2 = pltpu.make_async_copy(block_2, place_2(me), local_sems.at[2])
    keep_o.start()
    keep_2.start()

    for m in (1, 2, 3):
        firsts[m - 1].wait_recv()
        spot = place_n(at.slot(4 - m, 0))
        lasts.append([net.send(spot, spot, at.last(k)) for k in (1, 2, 3)])
        to_sib.append(net.send(spot, spot, sib))
    twin_o.wait_recv()
    twin_2.wait_recv()
    other = at.z * 2 + 1 - at.xlo
    ups_o.append([net.send(place_o(other), place_o(other), at.up(k)) for k in (1, 2, 3)])
    ups_2.append([net.send(place_2(other), place_2(other), at.up(k)) for k in (1, 2, 3)])
    to_sib.append(net.send(place_o(other), place_o(other), sib))
    to_sib.append(net.send(place_2(other), place_2(other), sib))

    for m in range(4):
        for k in (1, 2, 3):
            lasts[m][k - 1].wait_recv()
            spot = place_n(at.slot(4 - m, 4 - k))
            to_sib.append(net.send(spot, spot, sib))
    for m in range(2):
        for k in (1, 2, 3):
            z = rem4(at.z + 4 - k)
            xlo = at.xlo if m == 0 else 1 - at.xlo
            dp = z * 2 + xlo
            ups_o[m][k - 1].wait_recv()
            to_sib.append(net.send(place_o(dp), place_o(dp), sib))
            ups_2[m][k - 1].wait_recv()
            to_sib.append(net.send(place_2(dp), place_2(dp), sib))
    for copy in to_sib:
        copy.wait_recv()
    keep_n.wait()
    keep_o.wait()
    keep_2.wait()
    net.finish()


def gather(pack_n, pack_z, pick_n, pick_z):
    return pl.pallas_call(
        gather_kernel,
        out_shape=(
            jax.ShapeDtypeStruct((2, EMB, HALF), BF),
            jax.ShapeDtypeStruct((2, EMB, COLS), BF),
            jax.ShapeDtypeStruct((2, FF, COLS), BF),
        ),
        in_specs=[VMEM] * 4,
        out_specs=(ANY,) * 3,
        scratch_shapes=[
            pltpu.VMEM((16, HALF), BF),
            pltpu.VMEM((4, 16, HALF), BF),
            pltpu.VMEM((48, HALF), BF),
            pltpu.VMEM((2, 32, COLS), BF),
            pltpu.VMEM((8, 2, 32, COLS), BF),
            pltpu.VMEM((96, COLS), BF),
            pltpu.VMEM((336, COLS), BF),
            pltpu.SemaphoreType.DMA((GATHER_COPIES,)),
            pltpu.SemaphoreType.DMA((GATHER_COPIES,)),
            pltpu.SemaphoreType.DMA((3,)),
        ],
        compiler_params=pltpu.CompilerParams(
            collective_id=1, has_side_effects=True, vmem_limit_bytes=56 << 20
        ),
        name="gather_weights",
    )(pack_n, pack_z, pick_n, pick_z)


SCATTER_COPIES = 96


def scatter_kernel(
    grad_n, grad_o, grad_2, turn_n, turn_z, out_n, out_z,
    sib_n, last_n, first_n, piece_n, up_n, end_n,
    sib_o, sib_2, up_o, up_2, twin_o, twin_2, send_o, send_2, piece_z, plane_z, end_z,
    send_sems, recv_sems,
):
    at = Place()
    c = at.c
    at.meet()
    net = Sender(send_sems, recv_sems)
    sib = at.sibling()

    def band(slot):
        return rows(48 * slot, 48)

    swaps = {}
    swap_o, swap_2 = {}, {}
    for k in (1, 2, 3, 0):
        for m in range(4):
            part = band(at.slot(m, k, 1 - c))
            swaps[k, m] = net.send(grad_n.at[1 - c, part], sib_n.at[part], sib)
        z = rem4(at.z + k)
        part_o, part_2 = rows(192 * z, 192), rows(672 * z, 672)
        swap_o[k] = net.send(grad_o.at[1 - c, part_o], sib_o.at[part_o], sib)
        swap_2[k] = net.send(grad_2.at[1 - c, part_2], sib_2.at[part_2], sib)

    lasts, ups_o, ups_2 = {}, {}, {}
    for k in (1, 2, 3):
        for m in range(4):
            swaps[k, m].wait_recv()
            part = band(at.slot(m, k))
            sib_n[part] = (grad_n[c, part].astype(F32) + sib_n[part].astype(F32)).astype(BF)
            lasts[k, m] = net.send(sib_n.at[part], last_n.at[k - 1, m], at.last(k))
        z = rem4(at.z + k)
        part_o, part_2 = rows(192 * z, 192), rows(672 * z, 672)
        swap_o[k].wait_recv()
        sib_o[part_o] = (grad_o[c, part_o].astype(F32) + sib_o[part_o].astype(F32)).astype(BF)
        ups_o[k] = net.send(sib_o.at[part_o], up_o.at[k - 1], at.up(k))
        swap_2[k].wait_recv()
        sib_2[part_2] = (grad_2[c, part_2].astype(F32) + sib_2[part_2].astype(F32)).astype(BF)
        ups_2[k] = net.send(sib_2.at[part_2], up_2.at[k - 1], at.up(k))

    firsts = {}
    for m in (1, 2, 3, 0):
        swaps[0, m].wait_recv()
        part = band(at.slot(m, 0))
        total = grad_n[c, part].astype(F32) + sib_n[part].astype(F32)
        for k in (1, 2, 3):
            lasts[k, m].wait_recv()
            total += last_n[k - 1, m].astype(F32)
        if m:
            sib_n[part] = total.astype(BF)
            firsts[m] = net.send(sib_n.at[part], first_n.at[m - 1], at.first(m))
    for m in (1, 2, 3):
        firsts[m].wait_recv()
        total += first_n[m - 1].astype(F32)
    spread = jnp.dot(turn_n[...], total.astype(BF), preferred_element_type=F32)
    piece_n[...] = spread.astype(BF).reshape(4, 16, HALF)
    ups_n = {}
    for k in (1, 2, 3):
        ups_n[k] = net.send(piece_n.at[rem4(at.z + k)], up_n.at[k - 1], at.up(k))

    swap_o[0].wait_recv()
    swap_2[0].wait_recv()
    for own, away in ((False, True), (True, False)):
        xlo = at.xlo if own else 1 - at.xlo
        dp = at.z * 2 + xlo
        part_o, part_2 = rows(96 * dp, 96), rows(336 * dp, 336)
        sub_o, sub_2 = rows(96 * xlo, 96), rows(336 * xlo, 336)
        total_o = grad_o[c, part_o].astype(F32) + sib_o[part_o].astype(F32)
        total_2 = grad_2[c, part_2].astype(F32) + sib_2[part_2].astype(F32)
        for k in (1, 2, 3):
            if away:
                ups_o[k].wait_recv()
                ups_2[k].wait_recv()
            total_o += up_o[k - 1, sub_o].astype(F32)
            total_2 += up_2[k - 1, sub_2].astype(F32)
        if away:
            send_o[...] = total_o.astype(BF)
            send_2[...] = total_2.astype(BF)
            twins = [net.send(send_o, twin_o, at.twin()), net.send(send_2, twin_2, at.twin())]
    for copy in twins:
        copy.wait_recv()
    total_o += twin_o[...].astype(F32)
    total_2 += twin_2[...].astype(F32)
    spread_z = jnp.dot(turn_z[:, :96], total_o.astype(BF), preferred_element_type=F32)
    spread_z += jnp.dot(turn_z[:, 96:], total_2.astype(BF), preferred_element_type=F32)
    piece_z[...] = spread_z.astype(BF).reshape(8, 64, COLS)
    planes = []
    for k in range(1, 8):
        mate, index = at.plane(k)
        planes.append(net.send(piece_z.at[index], plane_z.at[k - 1], mate))

    total = piece_n[at.z].astype(F32)
    for k in (1, 2, 3):
        ups_n[k].wait_recv()
        total += up_n[k - 1].astype(F32)
    end_n[...] = total
    away_n, own_n = rows(8 * (1 - c), 8, 8), rows(8 * c, 8, 8)
    swap_n = net.send(end_n.at[away_n], out_n.at[c], sib)
    out_n[c] = end_n[own_n]

    total = piece_z[at.y * 2 + at.xhi].astype(F32)
    for k in range(1, 8):
        planes[k - 1].wait_recv()
        total += plane_z[k - 1].astype(F32)
    end_z[...] = total
    away_z, own_z = rows(32 * (1 - c), 32, 8), rows(32 * c, 32, 8)
    swap_z = net.send(end_z.at[away_z], out_z.at[c], sib)
    out_z[c] = end_z[own_z]
    swap_n.wait_recv()
    swap_z.wait_recv()
    net.finish()


def scatter(grad_n, grad_o, grad_2, turn_n, turn_z):
    return pl.pallas_call(
        scatter_kernel,
        out_shape=(
            jax.ShapeDtypeStruct((2, 8, HALF), F32),
            jax.ShapeDtypeStruct((2, 32, COLS), F32),
        ),
        in_specs=[VMEM] * 5,
        out_specs=(VMEM, VMEM),
        scratch_shapes=[
            pltpu.VMEM((EMB, HALF), BF),
            pltpu.VMEM((3, 4, 48, HALF), BF),
            pltpu.VMEM((3, 48, HALF), BF),
            pltpu.VMEM((4, 16, HALF), BF),
            pltpu.VMEM((3, 16, HALF), BF),
            pltpu.VMEM((16, HALF), F32),
            pltpu.VMEM((EMB, COLS), BF),
            pltpu.VMEM((FF, COLS), BF),
            pltpu.VMEM((3, 192, COLS), BF),
            pltpu.VMEM((3, 672, COLS), BF),
            pltpu.VMEM((96, COLS), BF),
            pltpu.VMEM((336, COLS), BF),
            pltpu.VMEM((96, COLS), BF),
            pltpu.VMEM((336, COLS), BF),
            pltpu.VMEM((8, 64, COLS), BF),
            pltpu.VMEM((7, 64, COLS), BF),
            pltpu.VMEM((64, COLS), F32),
            pltpu.SemaphoreType.DMA((SCATTER_COPIES,)),
            pltpu.SemaphoreType.DMA((SCATTER_COPIES,)),
        ],
        compiler_params=pltpu.CompilerParams(
            collective_id=2, has_side_effects=True, vmem_limit_bytes=56 << 20
        ),
        name="scatter_grads",
    )(grad_n, grad_o, grad_2, turn_n, turn_z)


def mm(left, right):
    return jnp.dot(left, right, preferred_element_type=F32)


def mm_t(left, right):
    return lax.dot_general(left, right, (((1,), (1,)), ((), ())), preferred_element_type=F32)


def t_mm(left, right):
    return lax.dot_general(left, right, (((0,), (0,)), ((), ())), preferred_element_type=F32)


def split(value, parts):
    found = []
    for _ in range(parts - 1):
        high = value.astype(BF)
        found.append(high)
        value = value - high.astype(F32)
    found.append(value.astype(BF))
    return found


def fine(dims, left, right):
    lh, ll = split(left, 2)
    rh, rl = split(right, 2)
    dot = partial(lax.dot_general, dimension_numbers=(dims, ((), ())), preferred_element_type=F32)
    return dot(lh, rh) + (dot(lh, rl) + dot(ll, rh))


NN, NT, TN = ((1,), (0,)), ((1,), (1,)), ((0,), (0,))


def layer_kernel(
    x_ref, up_ref, memory, spread, wn, wo, w2,
    out_ref, in_grad_ref, gn, go, g2,
    scores,
):
    lanes = lax.broadcasted_iota(jnp.int32, (1, 128), 1)
    left_head = lanes < 64
    token = lax.broadcasted_iota(jnp.int32, (TOK, 1), 0)

    def shift_down(value):
        return jnp.where(token == 0, 0.0, pltpu.roll(value, 1, 0))

    def shift_up(value):
        return jnp.where(token == TOK - 1, 0.0, pltpu.roll(value, TOK - 1, 0))

    def mean(value):
        return jnp.mean(value, axis=-1, keepdims=True)

    def tsum(value):
        return jnp.sum(value, axis=0, keepdims=True)

    def unspread(value):
        a, b, c = split(value, 3)
        return mm_t(a, spread[...]) + (mm_t(b, spread[...]) + mm_t(c, spread[...]))

    eye = (
        lax.broadcasted_iota(jnp.int32, (16, 128), 0)
        == lax.broadcasted_iota(jnp.int32, (16, 128), 1)
    ).astype(F32).astype(BF)
    vec = mm_t(eye, wn[1, :, VEC:HALF])
    gain1, bias1 = vec[0:1], vec[1:2]
    lerps = [vec[2 + i : 3 + i] for i in range(4)]
    gain2, bias2, lerp_h, lerp_g = vec[6:7], vec[7:8], vec[8:9], vec[9:10]
    heads = mm_t(vec.astype(BF), spread[...])
    rate, bonus, gain_w, bias_w = heads[10:11], heads[11:12], heads[12:13], heads[13:14]

    pair_rows = lax.broadcasted_iota(jnp.int32, (256, 128), 0)
    pair_cols = lax.broadcasted_iota(jnp.int32, (256, 128), 1)
    pair_ones = ((lax.rem(pair_rows, 128) // 64) == (pair_cols // 64)).astype(F32).astype(BF)
    below = lax.rem(pair_rows, 128) > pair_cols

    def head_sum(value):
        found = []
        for g in range(6):
            part = value[:, 128 * g : 128 * g + 128]
            found.append(mm(jnp.concatenate(split(part, 2), axis=1), pair_ones))
        return jnp.concatenate(found, axis=1)

    def stack(value):
        return jnp.concatenate(
            [jnp.where(left_head, value, 0.0), jnp.where(left_head, 0.0, value)], axis=0
        )

    def beside(value):
        return jnp.concatenate([value[:TOK], value[TOK:]], axis=1)

    tokens = mm(x_ref[...], spread[...])
    centred = tokens - mean(tokens)
    scale1 = lax.rsqrt(mean(centred * centred) + NORM_EPS)
    unit1 = centred * scale1
    normed = unit1 * gain1 + bias1
    previous = shift_down(normed)
    blended = [(normed * l + previous * (1.0 - l)).astype(BF) for l in lerps]
    recept = mm(blended[0], wn[0, :, 0:768])
    keys = mm(blended[1], wn[0, :, 768:1536])
    vals = mm(blended[2], wn[1, :, 0:768])
    gate_pre = mm(blended[3], wn[1, :, 768:1536])

    fade = -jnp.exp(rate)
    steps = token.astype(F32)
    fall_r = jnp.exp(steps * fade)
    fall_k = jnp.exp(-(steps + 1.0) * fade)
    recept_f = recept * fall_r
    keys_f = keys * fall_k
    present = head_sum(recept * bonus * keys)
    parts = []
    for g in range(6):
        cut = slice(128 * g, 128 * g + 128)
        rg, kg, vg = recept_f[:, cut], keys_f[:, cut], vals[:, cut]
        sc = jnp.where(below, fine(NT, stack(rg), kg), 0.0)
        scores[g] = sc
        parts.append(fine(NN, beside(sc), stack(vg)) + fine(NN, rg, memory[g]))
    wkv = jnp.concatenate(parts, axis=1) + present * vals

    centred_w = wkv - head_sum(wkv) * (1.0 / 64.0)
    scale_w = lax.rsqrt(head_sum(centred_w * centred_w) * (1.0 / 64.0) + GROUP_EPS)
    unit_w = centred_w * scale_w
    grouped = unit_w * gain_w + bias_w
    sig = 1.0 / (1.0 + jnp.exp(-gate_pre))
    silu = gate_pre * sig
    gated = (grouped * silu).astype(BF)
    mixed_out = jnp.concatenate([mm(gated, wo[0]), mm(gated, wo[1])], axis=1)
    middle = tokens + mixed_out

    centred = middle - mean(middle)
    scale2 = lax.rsqrt(mean(centred * centred) + NORM_EPS)
    unit2 = centred * scale2
    normed2 = unit2 * gain2 + bias2
    previous2 = shift_down(normed2)
    mixed_h = (normed2 * lerp_h + previous2 * (1.0 - lerp_h)).astype(BF)
    mixed_g = (normed2 * lerp_g + previous2 * (1.0 - lerp_g)).astype(BF)
    pre = jnp.concatenate(
        [mm(mixed_h, wn[0, :, 1536 : 1536 + W1A]), mm(mixed_h, wn[1, :, 1536 : 1536 + W1B])],
        axis=1,
    )
    pre = jnp.maximum(pre, 0.0)
    hidden = (pre * pre).astype(BF)
    value_out = jnp.concatenate([mm(hidden, w2[0]), mm(hidden, w2[1])], axis=1)
    gating = jnp.concatenate(
        [mm(mixed_g, wn[0, :, 2944:3328]), mm(mixed_g, wn[1, :, 2816:3200])], axis=1
    )
    gating = 1.0 / (1.0 + jnp.exp(-gating))
    out_ref[...] = unspread(middle + gating * value_out)

    upstream = mm(up_ref[...], spread[...])
    grad_vo = upstream * gating
    grad_gp = (grad_vo * value_out * (1.0 - gating)).astype(BF)
    grad_vo = grad_vo.astype(BF)
    for h in range(2):
        g2[h] = t_mm(hidden, grad_vo[:, COLS * h : COLS * h + COLS]).astype(BF)
    gn[0, :, 2944:3328] = t_mm(mixed_g, grad_gp[:, :COLS]).astype(BF)
    gn[1, :, 2816:3200] = t_mm(mixed_g, grad_gp[:, COLS:]).astype(BF)
    grad_hidden = mm_t(grad_vo[:, :COLS], w2[0]) + mm_t(grad_vo[:, COLS:], w2[1])
    grad_pre = (grad_hidden * 2.0 * pre).astype(BF)
    gn[0, :, 1536 : 1536 + W1A] = t_mm(mixed_h, grad_pre[:, :W1A]).astype(BF)
    gn[1, :, 1536 : 1536 + W1B] = t_mm(mixed_h, grad_pre[:, W1A:]).astype(BF)
    grad_mh = mm_t(grad_pre[:, :W1A], wn[0, :, 1536 : 1536 + W1A])
    grad_mh += mm_t(grad_pre[:, W1A:], wn[1, :, 1536 : 1536 + W1B])
    grad_mg = mm_t(grad_gp[:, :COLS], wn[0, :, 2944:3328])
    grad_mg += mm_t(grad_gp[:, COLS:], wn[1, :, 2816:3200])
    grad_n2 = grad_mh * lerp_h + grad_mg * lerp_g
    grad_n2 += shift_up(grad_mh * (1.0 - lerp_h) + grad_mg * (1.0 - lerp_g))
    delta2 = normed2 - previous2
    g_lerp_h, g_lerp_g = tsum(grad_mh * delta2), tsum(grad_mg * delta2)
    g_gain2, g_bias2 = tsum(grad_n2 * unit2), tsum(grad_n2)
    q = grad_n2 * gain2
    grad_middle = upstream + scale2 * (q - mean(q) - unit2 * mean(q * unit2))

    grad_attn = grad_middle.astype(BF)
    for h in range(2):
        go[h] = t_mm(gated, grad_attn[:, COLS * h : COLS * h + COLS]).astype(BF)
    grad_gated = mm_t(grad_attn[:, :COLS], wo[0]) + mm_t(grad_attn[:, COLS:], wo[1])
    grad_gate = (grad_gated * grouped * (sig * (1.0 + gate_pre * (1.0 - sig)))).astype(BF)
    grad_grouped = grad_gated * silu
    g_gain_w, g_bias_w = tsum(grad_grouped * unit_w), tsum(grad_grouped)
    q = grad_grouped * gain_w
    grad_wkv = scale_w * (
        q
        - head_sum(q) * (1.0 / 64.0)
        - unit_w * (head_sum(q * unit_w) * (1.0 / 64.0))
    )

    weight = head_sum(grad_wkv * vals)
    parts_r, parts_k, parts_v = [], [], []
    for g in range(6):
        cut = slice(128 * g, 128 * g + 128)
        rg, kg, vg, dg = recept_f[:, cut], keys_f[:, cut], vals[:, cut], grad_wkv[:, cut]
        ds = stack(dg)
        da = jnp.where(below, fine(NT, ds, vg), 0.0)
        parts_r.append(fine(NN, beside(da), stack(kg)) + fine(NT, dg, memory[g]))
        parts_k.append(fine(TN, da, stack(rg)))
        parts_v.append(fine(TN, scores[g], ds))
    grad_r = jnp.concatenate(parts_r, axis=1) * fall_r
    grad_k = jnp.concatenate(parts_k, axis=1) * fall_k
    grad_v = jnp.concatenate(parts_v, axis=1) + grad_wkv * present
    g_rate = fade * tsum(steps * recept * grad_r - (steps + 1.0) * keys * grad_k)
    g_bonus = tsum(recept * keys * weight)
    grad_r = (grad_r + bonus * keys * weight).astype(BF)
    grad_k = (grad_k + bonus * recept * weight).astype(BF)
    grad_v = grad_v.astype(BF)

    gn[0, :, 0:768] = t_mm(blended[0], grad_r).astype(BF)
    gn[0, :, 768:1536] = t_mm(blended[1], grad_k).astype(BF)
    gn[1, :, 0:768] = t_mm(blended[2], grad_v).astype(BF)
    gn[1, :, 768:1536] = t_mm(blended[3], grad_gate).astype(BF)
    grad_blended = [
        mm_t(grad_r, wn[0, :, 0:768]),
        mm_t(grad_k, wn[0, :, 768:1536]),
        mm_t(grad_v, wn[1, :, 0:768]),
        mm_t(grad_gate, wn[1, :, 768:1536]),
    ]
    delta = normed - previous
    g_lerps = [tsum(g * delta) for g in grad_blended]
    grad_n1 = sum(g * l for g, l in zip(grad_blended, lerps))
    grad_n1 += shift_up(sum(g * (1.0 - l) for g, l in zip(grad_blended, lerps)))
    g_gain1, g_bias1 = tsum(grad_n1 * unit1), tsum(grad_n1)
    q = grad_n1 * gain1
    grad_x = grad_middle + scale1 * (q - mean(q) - unit1 * mean(q * unit1))
    in_grad_ref[...] = unspread(grad_x)

    zero = jnp.zeros((1, EMB), F32)
    natural = jnp.concatenate([g_rate, g_bonus, g_gain_w, g_bias_w] + [zero] * 4, axis=0)
    a, b, c = split(natural, 3)
    moved = mm(a, spread[...]) + (mm(b, spread[...]) + mm(c, spread[...]))
    table = jnp.concatenate(
        [g_gain1, g_bias1] + g_lerps + [g_gain2, g_bias2, g_lerp_h, g_lerp_g]
        + [moved[0:4], jnp.zeros((114, EMB), F32)],
        axis=0,
    )
    gn[1, :, VEC:HALF] = table.T.astype(BF)


def layer(x, up, memory, spread, wn, wo, w2):
    return pl.pallas_call(
        layer_kernel,
        out_shape=(
            jax.ShapeDtypeStruct((TOK, EMB), F32),
            jax.ShapeDtypeStruct((TOK, EMB), F32),
            jax.ShapeDtypeStruct((2, EMB, HALF), BF),
            jax.ShapeDtypeStruct((2, EMB, COLS), BF),
            jax.ShapeDtypeStruct((2, FF, COLS), BF),
        ),
        in_specs=[VMEM] * 7,
        out_specs=(VMEM,) * 5,
        scratch_shapes=[pltpu.VMEM((6, 256, 128), F32)],
        compiler_params=pltpu.CompilerParams(vmem_limit_bytes=60 << 20),
        cost_estimate=pl.CostEstimate(
            flops=6 * TOK * 7667712, bytes_accessed=4 * 7667712, transcendentals=10 * TOK * EMB
        ),
        name="layer",
    )(x, up, memory, spread, wn, wo, w2)


def per_device(
    incoming_activations,
    sequence_opening_memory,
    prior_standardize_factor,
    prior_standardize_offset,
    acceptor_lerp_factor,
    address_lerp_factor,
    content_lerp_factor,
    sigmoid_lerp_factor,
    acceptor_matrix,
    address_matrix,
    content_matrix,
    sigmoid_matrix,
    lane_fading_exponent,
    present_reward_vector,
    cluster_standardize_factor,
    cluster_standardize_offset,
    mixer_result_matrix,
    latter_standardize_factor,
    latter_standardize_offset,
    feedforward_address_lerp,
    feedforward_sigmoid_lerp,
    feedforward_address_matrix,
    feedforward_content_matrix,
    feedforward_acceptor_matrix,
    upstream_derivative,
):
    spread = jnp.asarray(_spread(), BF)
    pick_n = jnp.asarray(_line_pick(), BF)
    pick_z = jnp.asarray(_plane_pick(), BF)

    columns = jnp.concatenate(
        [feedforward_acceptor_matrix, mixer_result_matrix, feedforward_content_matrix,
         jnp.zeros((31, EMB), BF)], axis=0,
    )
    columns = jnp.dot(columns, spread, preferred_element_type=F32).astype(BF)
    acceptor = columns[:6]
    pack_z = columns[6:38]
    pack_z = jnp.stack([pack_z[:, :COLS], pack_z[:, COLS:]])
    vectors = jnp.stack(
        [prior_standardize_factor, prior_standardize_offset, acceptor_lerp_factor,
         address_lerp_factor, content_lerp_factor, sigmoid_lerp_factor,
         latter_standardize_factor, latter_standardize_offset, feedforward_address_lerp,
         feedforward_sigmoid_lerp, lane_fading_exponent, present_reward_vector,
         cluster_standardize_factor, cluster_standardize_offset], axis=1,
    )
    vectors = jnp.pad(vectors, ((0, 0), (0, 114)))
    key_matrix = feedforward_address_matrix
    pack_n = jnp.stack([
        jnp.concatenate([acceptor_matrix, address_matrix, key_matrix[:, :W1A], acceptor[:, :COLS]], axis=1),
        jnp.concatenate([content_matrix, sigmoid_matrix, key_matrix[:, W1A:], acceptor[:, COLS:], vectors], axis=1),
    ])
    core = lax.rem(lax.axis_index("fsdp"), 2)
    pack_n = jnp.where(
        core == 0,
        jnp.pad(pack_n, ((0, 0), (0, 10), (0, 0))),
        jnp.pad(pack_n, ((0, 0), (8, 2), (0, 0))),
    )
    wn, wo, w2 = gather(pack_n, pack_z, pick_n, pick_z)

    memory = sequence_opening_memory.reshape(6, 2, 64, 64)
    nothing = jnp.zeros((6, 64, 64), F32)
    memory = jnp.concatenate(
        [jnp.concatenate([memory[:, 0], nothing], axis=2),
         jnp.concatenate([nothing, memory[:, 1]], axis=2)], axis=1,
    )
    out, in_grad, gn, go, g2 = layer(
        incoming_activations, upstream_derivative, memory, spread, wn, wo, w2
    )
    end_n, end_z = scatter(gn, go, g2, pick_n.T, pick_z.T)

    first, second = end_n[0, :6], end_n[1, :6]
    acceptor = jnp.concatenate([first[:, 2944:], second[:, 2816:VEC]], axis=1)
    columns = jnp.concatenate([acceptor, jnp.concatenate([end_z[0, :27], end_z[1, :27]], axis=1)], axis=0)
    columns = lax.dot_general(
        columns, spread.astype(F32), (((1,), (1,)), ((), ())),
        precision=HIGHEST, preferred_element_type=F32,
    )
    vectors = second[:, VEC : VEC + 14]
    key_matrix = jnp.concatenate([first[:, 1536:2944], second[:, 1536:2816]], axis=1)
    return (
        out,
        in_grad,
        vectors[:, 0], vectors[:, 1],
        vectors[:, 2], vectors[:, 3], vectors[:, 4], vectors[:, 5],
        first[:, 0:768], first[:, 768:1536], second[:, 0:768], second[:, 768:1536],
        vectors[:, 10], vectors[:, 11], vectors[:, 12], vectors[:, 13],
        columns[6:12],
        vectors[:, 6], vectors[:, 7], vectors[:, 8], vectors[:, 9],
        key_matrix,
        columns[12:33],
        columns[0:6],
    )


def solution(mesh):
    split_rows, split_all, split_one = P(("dp", "fsdp"), None), P(("dp", "fsdp"), None, None, None), P(("dp", "fsdp"))
    r, v = split_rows, split_one
    return jax.shard_map(
        per_device,
        mesh=mesh,
        in_specs=(r, split_all) + (v,) * 6 + (r,) * 4 + (v,) * 4 + (r,) + (v,) * 4 + (r,) * 4,
        out_specs=(r, r) + (v,) * 6 + (r,) * 4 + (v,) * 4 + (r,) + (v,) * 4 + (r,) * 3,
        check_vma=False,
    )
```

```python
from functools import partial

import jax
import jax.numpy as jnp
import numpy as np
from jax import lax
from jax.experimental import pallas as pl
from jax.experimental.pallas import tpu as pltpu
from jax.sharding import PartitionSpec as P

MESH = pl.DeviceIdType.MESH
BF = jnp.bfloat16
F32 = jnp.float32
VMEM = pl.BlockSpec(memory_space=pltpu.VMEM)

NORM_EPS = 1e-05
GROUP_EPS = 0.00064
TOK = 128
EMB = 768
FF = 2688
QUART = 1664
COLS = 384
VEC = 1536
COPIES = 256


def _order():
    order = np.zeros(EMB, np.int64)
    for x in range(4):
        for y in range(4):
            for z in range(4):
                for c in range(2):
                    device = z * 32 + (x % 2) * 16 + y * 4 + (x // 2) * 2 + c
                    place = (x * 4 + y) * 48 + (z * 2 + c) * 6
                    order[place : place + 6] = 6 * device + np.arange(6)
    return order


def _spread():
    spread = np.zeros((EMB, EMB), np.float32)
    spread[_order(), np.arange(EMB)] = 1.0
    return spread


def _line_pick():
    pick = np.zeros((96, 128), np.float32)
    for member in range(8):
        for r in range(6):
            pick[member * 6 + r, member * 16 + r] = 1.0
            pick[48 + member * 6 + r, member * 16 + 8 + r] = 1.0
    return pick


def _plane_pick():
    pick = np.zeros((432, 512), np.float32)
    for member in range(16):
        for r in range(6):
            pick[member * 6 + r, member * 32 + r] = 1.0
        for r in range(21):
            pick[96 + member * 21 + r, member * 32 + 8 + r] = 1.0
    return pick


def rem4(value):
    return lax.rem(value, 4)


class Place:
    def __init__(self):
        dp, fs = lax.axis_index("dp"), lax.axis_index("fsdp")
        self.z, self.xlo = lax.div(dp, 2), lax.rem(dp, 2)
        self.y, self.xhi = lax.div(fs, 4), lax.rem(lax.div(fs, 2), 2)
        self.c = lax.rem(fs, 2)
        self.x = self.xhi * 2 + self.xlo
        self.chip = self.y * 2 + self.xhi

    def device(self, z, y, x, c):
        return (z * 2 + lax.rem(x, 2), y * 4 + lax.div(x, 2) * 2 + c)

    def sibling(self):
        return self.device(self.z, self.y, self.x, 1 - self.c)

    def up(self, k):
        return self.device(rem4(self.z + k), self.y, self.x, self.c)

    def line(self, k):
        z = rem4(self.z + k // 2)
        core = self.c if k % 2 == 0 else 1 - self.c
        return self.device(z, self.y, self.x, core), z * 2 + core, core

    def first(self, k):
        y, x = rem4(self.y + k * (1 - self.c)), rem4(self.x + k * self.c)
        return self.device(self.z, y, x, self.c)

    def last(self, k):
        y, x = rem4(self.y + k * self.c), rem4(self.x + k * (1 - self.c))
        return self.device(self.z, y, x, self.c)

    def band(self, m, k, core=None):
        c = self.c if core is None else core
        x = rem4(self.x + m * c + k * (1 - c))
        y = rem4(self.y + m * (1 - c) + k * c)
        return rows(48 * (x * 4 + y), 48)

    def plane(self, k):
        index = lax.rem(self.chip + k, 8)
        y, xhi = lax.div(index, 2), lax.rem(index, 2)
        return self.device(self.z, y, xhi * 2 + self.xlo, self.c), index

    def twin(self):
        return self.device(self.z, self.y, self.xhi * 2 + 1 - self.xlo, self.c)

    def order(self, m, k):
        return rem4(self.z + k) * 2 + (self.xlo if m == 0 else 1 - self.xlo)

    def greet(self):
        mates = [self.twin()]
        mates += [self.line(k)[0] for k in range(1, 8)]
        mates += [self.first(k) for k in (1, 2, 3)]
        mates += [self.last(k) for k in (1, 2, 3)]
        mates += [self.plane(k)[0] for k in range(1, 8)]
        barrier = pltpu.get_barrier_semaphore()
        for mate in mates:
            pl.semaphore_signal(barrier, inc=1, device_id=mate, device_id_type=MESH)
        return lambda: pl.semaphore_wait(barrier, len(mates))


class Sender:
    def __init__(self, send_sems, recv_sems):
        self.send_sems, self.recv_sems = send_sems, recv_sems
        self.count = 0
        self.open = []

    def send(self, source, target, device):
        copy = pltpu.make_async_remote_copy(
            src_ref=source,
            dst_ref=target,
            send_sem=self.send_sems.at[self.count],
            recv_sem=self.recv_sems.at[self.count],
            device_id=device,
            device_id_type=MESH,
        )
        copy.start()
        self.count += 1
        self.open.append(copy)
        return copy

    def drain(self):
        for copy in self.open:
            copy.wait_send()
        self.open = []


def rows(start, size, unit=16):
    return pl.ds(pl.multiple_of(start, unit), size)


def mm(left, right):
    return jnp.dot(left, right, preferred_element_type=F32)


def mm_t(left, right):
    return lax.dot_general(left, right, (((1,), (1,)), ((), ())), preferred_element_type=F32)


def t_mm(left, right):
    return lax.dot_general(left, right, (((0,), (0,)), ((), ())), preferred_element_type=F32)


def split(value, parts):
    found = []
    for _ in range(parts - 1):
        high = value.astype(BF)
        found.append(high)
        value = value - high.astype(F32)
    found.append(value.astype(BF))
    return found


def fine(dims, left, right):
    lh, ll = split(left, 2)
    rh, rl = split(right, 2)
    dot = partial(lax.dot_general, dimension_numbers=(dims, ((), ())), preferred_element_type=F32)
    return dot(lh, rh) + (dot(lh, rl) + dot(ll, rh))


NN, NT, TN = ((1,), (0,)), ((1,), (1,)), ((0,), (0,))


def wide(ref):
    return ref[...].astype(F32)


def layer_kernel(
    x_ref, up_ref, memory, spread, pick_n, pick_z, turn_n, turn_z, vecs,
    acceptor, address, content, sigmoid, mixer, ff_address, ff_content, ff_acceptor,
    out_ref, in_grad_ref, end_n, end_z,
    wn, wo, w2, scores,
    pack_f, pack_n, stage_n, cols_f, pack_z, half_z, stage_z,
    sib_n, sib_o, sib_2, relay_n, last_n, first_n, acc_n, piece_n, line_n,
    relay_o, relay_2, up_o, up_2, sent_o, sent_2, twin_o, twin_2, piece_z, plane_z, swap_f,
    send_sems, recv_sems,
):
    at = Place()
    c = at.c
    sib = at.sibling()
    net = Sender(send_sems, recv_sems)
    met = at.greet()

    pack_f[...] = jnp.zeros_like(pack_f)
    cols_f[...] = jnp.zeros_like(cols_f)
    cols_f[0:6] = wide(mixer)
    cols_f[8:29] = wide(ff_content)
    cols_f[32:38] = wide(ff_acceptor)
    moved = mm(cols_f[...].astype(BF), spread[...])
    pack_f[0, 0:6, 0:768] = wide(acceptor)
    pack_f[0, 0:6, 768:1536] = wide(address)
    pack_f[1, 0:6, 0:768] = wide(content)
    pack_f[1, 0:6, 768:1536] = wide(sigmoid)
    pack_f[0, 0:6, 1536:1664] = wide(ff_address.at[:, 0:128])
    pack_f[0, 8:14, 0:1280] = wide(ff_address.at[:, 128:1408])
    pack_f[1, 8:14, 0:1280] = wide(ff_address.at[:, 1408:2688])
    eye = (
        lax.broadcasted_iota(jnp.int32, (16, 128), 0)
        == lax.broadcasted_iota(jnp.int32, (16, 128), 1)
    ).astype(F32).astype(BF)
    pack_f[1, 0:6, VEC:QUART] = mm_t(eye, vecs[...])[0:6]
    for h in range(2):
        pack_f[h, 8:16, 1280:1664] = moved[32:40, COLS * h : COLS * h + COLS]
        pack_z[h] = moved[0:32, COLS * h : COLS * h + COLS].astype(BF)
        pack_n[h] = pack_f[h].astype(BF)
    met()

    swap_z = net.send(pack_z.at[1 - c], half_z.at[c], sib)
    own = at.z * 2 + c
    lines = []
    for k in range(1, 8):
        mate, _, core = at.line(k)
        lines.append(net.send(pack_n.at[core], stage_n.at[own], mate))
    stage_n[own] = pack_n[c]
    half_z[c] = pack_z[c]
    swap_z.wait_recv()
    planes = []
    for k in range(1, 8):
        planes.append(net.send(half_z, stage_z.at[at.chip], at.plane(k)[0]))
    stage_z[at.chip] = half_z[...]

    tokens = mm(x_ref[...], spread[...])
    centred = tokens - jnp.mean(tokens, axis=-1, keepdims=True)
    scale1 = lax.rsqrt(jnp.mean(centred * centred, axis=-1, keepdims=True) + NORM_EPS)
    unit1 = centred * scale1
    upstream = mm(up_ref[...], spread[...])

    for copy in lines:
        copy.wait_recv()
    picked = mm(pick_n[...], stage_n[...].reshape(128, QUART)).astype(BF)

    def place_n(q, m, k):
        return wn.at[c, q, at.band(m, k)]

    firsts, lasts, sibs = {}, {}, {0: [], 1: [], "o": [], "2": []}

    def pass_on(q, m):
        spot = place_n(q, 4 - m, 0)
        for k in (1, 3):
            lasts[q, m, k] = net.send(spot, spot, at.last(k))
        sibs[q].append(net.send(spot, spot, sib))

    def begin(q):
        spot = place_n(q, 0, 0)
        spot[...] = picked[48 * q : 48 * q + 48]
        for k in (1, 2, 3):
            firsts[q, k] = net.send(spot, spot, at.first(k))
        pass_on(q, 0)

    def relay(q, m):
        firsts[q, m].wait_recv()
        pass_on(q, m)

    def arrive(q, m, k):
        lasts[q, m, k].wait_recv()
        spot = place_n(q, 4 - m, 4 - k)
        if k == (1 if m % 2 == 0 else 3):
            lasts[q, m, 2] = net.send(spot, spot, at.last(k))
        sibs[q].append(net.send(spot, spot, sib))

    def arrive_far(q, m):
        lasts[q, m, 2].wait_recv()
        spot = place_n(q, 4 - m, 2)
        sibs[q].append(net.send(spot, spot, sib))

    def place_z(w, m, k):
        unit = 96 if w == "o" else 336
        return (wo if w == "o" else w2).at[c, rows(unit * at.order(m, k), unit)]

    def pass_z(w, m):
        spot = place_z(w, m, 0)
        for k in (1, 3):
            lasts[w, m, k] = net.send(spot, spot, at.up(k))
        sibs[w].append(net.send(spot, spot, sib))

    def relay_z(w):
        firsts[w].wait_recv()
        pass_z(w, 1)

    def arrive_z(w, m, k):
        lasts[w, m, k].wait_recv()
        spot = place_z(w, m, 4 - k)
        if k == (1 if m == 0 else 3):
            lasts[w, m, 2] = net.send(spot, spot, at.up(k))
        sibs[w].append(net.send(spot, spot, sib))

    def arrive_z_far(w, m):
        lasts[w, m, 2].wait_recv()
        spot = place_z(w, m, 2)
        sibs[w].append(net.send(spot, spot, sib))

    begin(0)
    begin(1)
    for copy in planes:
        copy.wait_recv()
    picked_z = mm(pick_z[...], stage_z[...].reshape(512, COLS)).astype(BF)
    place_z("o", 0, 0)[...] = picked_z[:96]
    place_z("2", 0, 0)[...] = picked_z[96:]
    for w in ("o", "2"):
        spot = place_z(w, 0, 0)
        firsts[w] = net.send(spot, spot, at.twin())
        pass_z(w, 0)
    for m in (1, 2, 3):
        relay(0, m)
    for w in ("o", "2"):
        relay_z(w)
    for m in (1, 2, 3):
        relay(1, m)
    for m in range(4):
        for k in (1, 3):
            arrive(0, m, k)
    for m in range(4):
        arrive_far(0, m)
    for copy in sibs[0]:
        copy.wait_recv()

    tasks = []
    for m in range(2):
        for k in (1, 3):
            tasks.append(partial(arrive_z, "o", m, k))
    for m in range(2):
        tasks.append(partial(arrive_z_far, "o", m))
    for m in range(2):
        for k in (1, 3):
            tasks.append(partial(arrive, 1, m, k))
            tasks.append(partial(arrive_z, "2", m, k))
    for m in (2, 3):
        for k in (1, 3):
            tasks.append(partial(arrive, 1, m, k))
    for m in range(4):
        tasks.append(partial(arrive_far, 1, m))
    for m in range(2):
        tasks.append(partial(arrive_z_far, "2", m))

    def work(count):
        for _ in range(min(count, len(tasks))):
            tasks.pop(0)()

    lanes = lax.broadcasted_iota(jnp.int32, (1, 128), 1)
    left_head = lanes < 64
    token = lax.broadcasted_iota(jnp.int32, (TOK, 1), 0)

    def shift_down(value):
        return jnp.where(token == 0, 0.0, pltpu.roll(value, 1, 0))

    def shift_up(value):
        return jnp.where(token == TOK - 1, 0.0, pltpu.roll(value, TOK - 1, 0))

    def mean(value):
        return jnp.mean(value, axis=-1, keepdims=True)

    def tsum(value):
        return jnp.sum(value, axis=0, keepdims=True)

    def unspread(value):
        a, b, d = split(value, 3)
        return mm_t(a, spread[...]) + (mm_t(b, spread[...]) + mm_t(d, spread[...]))

    vec = mm_t(eye, wn[1, 0, :, VEC:QUART])
    gain1, bias1 = vec[0:1], vec[1:2]
    lerps = [vec[2 + i : 3 + i] for i in range(4)]
    gain2, bias2, lerp_h, lerp_g = vec[6:7], vec[7:8], vec[8:9], vec[9:10]
    heads = mm_t(vec.astype(BF), spread[...])
    rate, bonus, gain_w, bias_w = heads[10:11], heads[11:12], heads[12:13], heads[13:14]

    pair_rows = lax.broadcasted_iota(jnp.int32, (256, 128), 0)
    pair_cols = lax.broadcasted_iota(jnp.int32, (256, 128), 1)
    pair_ones = ((lax.rem(pair_rows, 128) // 64) == (pair_cols // 64)).astype(F32).astype(BF)
    below = lax.rem(pair_rows, 128) > pair_cols

    def head_sum(value):
        found = []
        for g in range(6):
            part = value[:, 128 * g : 128 * g + 128]
            found.append(mm(jnp.concatenate(split(part, 2), axis=1), pair_ones))
        return jnp.concatenate(found, axis=1)

    def stack(value):
        return jnp.concatenate(
            [jnp.where(left_head, value, 0.0), jnp.where(left_head, 0.0, value)], axis=0
        )

    def beside(value):
        return jnp.concatenate([value[:TOK], value[TOK:]], axis=1)

    normed = unit1 * gain1 + bias1
    previous = shift_down(normed)
    blended = [(normed * l + previous * (1.0 - l)).astype(BF) for l in lerps]
    recept = mm(blended[0], wn[0, 0, :, 0:768])
    keys = mm(blended[1], wn[0, 0, :, 768:1536])
    vals = mm(blended[2], wn[1, 0, :, 0:768])
    gate_pre = mm(blended[3], wn[1, 0, :, 768:1536])
    work(6)

    fade = -jnp.exp(rate)
    steps = token.astype(F32)
    fall_r = jnp.exp(steps * fade)
    fall_k = jnp.exp(-(steps + 1.0) * fade)
    recept_f = recept * fall_r
    keys_f = keys * fall_k
    present = head_sum(recept * bonus * keys)
    parts = []
    for g in range(6):
        cut = slice(128 * g, 128 * g + 128)
        rg, kg, vg = recept_f[:, cut], keys_f[:, cut], vals[:, cut]
        sc = jnp.where(below, fine(NT, stack(rg), kg), 0.0)
        scores[g] = sc
        parts.append(fine(NN, beside(sc), stack(vg)) + fine(NN, rg, memory[g]))
        if g % 2 == 1:
            work(4)
    wkv = jnp.concatenate(parts, axis=1) + present * vals

    centred_w = wkv - head_sum(wkv) * (1.0 / 64.0)
    scale_w = lax.rsqrt(head_sum(centred_w * centred_w) * (1.0 / 64.0) + GROUP_EPS)
    unit_w = centred_w * scale_w
    grouped = unit_w * gain_w + bias_w
    sig = 1.0 / (1.0 + jnp.exp(-gate_pre))
    silu = gate_pre * sig
    gated = (grouped * silu).astype(BF)
    for copy in sibs["o"]:
        copy.wait_recv()
    middle = tokens + jnp.concatenate([mm(gated, wo[0]), mm(gated, wo[1])], axis=1)

    centred = middle - mean(middle)
    scale2 = lax.rsqrt(mean(centred * centred) + NORM_EPS)
    unit2 = centred * scale2
    normed2 = unit2 * gain2 + bias2
    previous2 = shift_down(normed2)
    mixed_h = (normed2 * lerp_h + previous2 * (1.0 - lerp_h)).astype(BF)
    mixed_g = (normed2 * lerp_g + previous2 * (1.0 - lerp_g)).astype(BF)
    work(len(tasks))
    for copy in sibs[1]:
        copy.wait_recv()
    pre = jnp.concatenate(
        [
            mm(mixed_h, wn[0, 0, :, 1536:1664]),
            mm(mixed_h, wn[0, 1, :, 0:1280]),
            mm(mixed_h, wn[1, 1, :, 0:1280]),
        ],
        axis=1,
    )
    pre = jnp.maximum(pre, 0.0)
    hidden = (pre * pre).astype(BF)
    gating = jnp.concatenate(
        [mm(mixed_g, wn[0, 1, :, 1280:1664]), mm(mixed_g, wn[1, 1, :, 1280:1664])], axis=1
    )
    gating = 1.0 / (1.0 + jnp.exp(-gating))
    for copy in sibs["2"]:
        copy.wait_recv()
    value_out = jnp.concatenate([mm(hidden, w2[0]), mm(hidden, w2[1])], axis=1)
    layer_out = middle + gating * value_out
    net.drain()

    swaps = {}

    def fold(mine, other, *more):
        total = wide(mine) + wide(other)
        for ref in more:
            total += wide(ref)
        return total

    def swap(q):
        for k in (2, 1, 3, 0):
            for m in range(4):
                part = at.band(m, k, 1 - c)
                swaps[q, m, k] = net.send(wn.at[1 - c, q, part], sib_n.at[q, part], sib)

    def scatter_far(q, m):
        part = at.band(m, 2)
        via = 1 if m % 2 == 0 else 3
        swaps[q, m, 2].wait_recv()
        spot = sib_n.at[q, part]
        spot[...] = fold(wn.at[c, q, part], spot).astype(BF)
        lasts["g", q, m, 2] = net.send(spot, relay_n.at[q, m], at.last(via))

    def scatter_near(q, m, k):
        part = at.band(m, k)
        swaps[q, m, k].wait_recv()
        spot = sib_n.at[q, part]
        more = []
        if k == (1 if m % 2 == 0 else 3):
            lasts["g", q, m, 2].wait_recv()
            more = [relay_n.at[q, m]]
        spot[...] = fold(wn.at[c, q, part], spot, *more).astype(BF)
        lasts["g", q, m, k] = net.send(spot, last_n.at[q, k // 2, m], at.last(k))

    def scatter_own(q, m):
        part = at.band(m, 0)
        swaps[q, m, 0].wait_recv()
        spot = sib_n.at[q, part]
        lasts["g", q, m, 1].wait_recv()
        lasts["g", q, m, 3].wait_recv()
        total = fold(wn.at[c, q, part], spot, last_n.at[q, 0, m], last_n.at[q, 1, m])
        if m == 0:
            acc_n[q] = total
        else:
            spot[...] = total.astype(BF)
            firsts["g", q, m] = net.send(spot, first_n.at[q, m - 1], at.first(m))

    def scatter_end(q):
        total = acc_n[q]
        for m in (1, 2, 3):
            firsts["g", q, m].wait_recv()
            total += wide(first_n.at[q, m - 1])
        acc_n[q] = total

    def scatter_steps(q):
        steps_ = [partial(scatter_far, q, m) for m in range(4)]
        for late in (False, True):
            for m in range(4):
                for k in (1, 3):
                    if late == (k == (1 if m % 2 == 0 else 3)):
                        steps_.append(partial(scatter_near, q, m, k))
        steps_ += [partial(scatter_own, q, m) for m in (1, 2, 3, 0)]
        steps_.append(partial(scatter_end, q))
        return steps_

    z_parts = {
        "o": (96, wo, sib_o, relay_o, up_o, sent_o, twin_o),
        "2": (336, w2, sib_2, relay_2, up_2, sent_2, twin_2),
    }

    def swap_w(w):
        unit, mine, theirs = z_parts[w][:3]
        for k in (2, 1, 3, 0):
            part = rows(2 * unit * rem4(at.z + k), 2 * unit)
            swaps[w, k] = net.send(mine.at[1 - c, part], theirs.at[part], sib)

    def part_w(w, m, k):
        unit = z_parts[w][0]
        return rows(unit * at.order(m, k), unit)

    def scatter_far_w(w, m):
        unit, mine, theirs, relayed = z_parts[w][:4]
        part = part_w(w, m, 2)
        if m == 0:
            swaps[w, 2].wait_recv()
        spot = theirs.at[part]
        spot[...] = fold(mine.at[c, part], spot).astype(BF)
        lasts["g", w, m, 2] = net.send(spot, relayed.at[m], at.up(1 if m == 0 else 3))

    def scatter_near_w(w, m, k):
        unit, mine, theirs, relayed, arrived = z_parts[w][:5]
        part = part_w(w, m, k)
        if (m == 1) == (k == 1):
            swaps[w, k].wait_recv()
        more = []
        if k == (1 if m == 0 else 3):
            lasts["g", w, m, 2].wait_recv()
            more = [relayed.at[m]]
        spot = theirs.at[part]
        spot[...] = fold(mine.at[c, part], spot, *more).astype(BF)
        lasts["g", w, m, k] = net.send(spot, arrived.at[k // 2, m], at.up(k))

    def scatter_own_w(w, m):
        unit, mine, theirs, relayed, arrived, sent, twin = z_parts[w]
        part = part_w(w, m, 0)
        if m == 1:
            swaps[w, 0].wait_recv()
        lasts["g", w, m, 1].wait_recv()
        lasts["g", w, m, 3].wait_recv()
        total = fold(mine.at[c, part], theirs.at[part], arrived.at[0, m], arrived.at[1, m])
        if m == 1:
            sent[...] = total.astype(BF)
            firsts["g", w] = net.send(sent, twin, at.twin())
        else:
            firsts["g", w].wait_recv()
            sums_z[w] = (total + wide(twin)).astype(BF)

    def scatter_steps_w(w):
        steps_ = [partial(scatter_far_w, w, 0), partial(scatter_far_w, w, 1)]
        steps_ += [partial(scatter_near_w, w, 1, 1), partial(scatter_near_w, w, 0, 3)]
        steps_ += [partial(scatter_near_w, w, 0, 1), partial(scatter_near_w, w, 1, 3)]
        steps_ += [partial(scatter_own_w, w, 1), partial(scatter_own_w, w, 0)]
        return steps_

    sums_z = {}

    grad_vo = upstream * gating
    grad_gp = (grad_vo * value_out * (1.0 - gating)).astype(BF)
    grad_vo = grad_vo.astype(BF)
    grad_hidden = mm_t(grad_vo[:, :COLS], w2[0]) + mm_t(grad_vo[:, COLS:], w2[1])
    grad_pre = (grad_hidden * 2.0 * pre).astype(BF)
    for h in range(2):
        w2[h] = t_mm(hidden, grad_vo[:, COLS * h : COLS * h + COLS]).astype(BF)
    swap_w("2")
    grad_mh = mm_t(grad_pre[:, :128], wn[0, 0, :, 1536:1664])
    grad_mh += mm_t(grad_pre[:, 128:1408], wn[0, 1, :, 0:1280])
    grad_mh += mm_t(grad_pre[:, 1408:], wn[1, 1, :, 0:1280])
    grad_mg = mm_t(grad_gp[:, :COLS], wn[0, 1, :, 1280:1664])
    grad_mg += mm_t(grad_gp[:, COLS:], wn[1, 1, :, 1280:1664])
    wn[0, 1, :, 0:1280] = t_mm(mixed_h, grad_pre[:, 128:1408]).astype(BF)
    wn[1, 1, :, 0:1280] = t_mm(mixed_h, grad_pre[:, 1408:]).astype(BF)
    wn[0, 0, :, 1536:1664] = t_mm(mixed_h, grad_pre[:, :128]).astype(BF)
    wn[0, 1, :, 1280:1664] = t_mm(mixed_g, grad_gp[:, :COLS]).astype(BF)
    wn[1, 1, :, 1280:1664] = t_mm(mixed_g, grad_gp[:, COLS:]).astype(BF)
    swap(1)
    steps_2, steps_1 = scatter_steps_w("2"), scatter_steps(1)
    tasks += steps_2[:2] + steps_1[:4] + steps_2[2:4] + steps_1[4:8]
    work(len(tasks))
    tasks += steps_2[4:6] + steps_1[8:12]

    grad_n2 = grad_mh * lerp_h + grad_mg * lerp_g
    grad_n2 += shift_up(grad_mh * (1.0 - lerp_h) + grad_mg * (1.0 - lerp_g))
    delta2 = normed2 - previous2
    g_lerp_h, g_lerp_g = tsum(grad_mh * delta2), tsum(grad_mg * delta2)
    g_gain2, g_bias2 = tsum(grad_n2 * unit2), tsum(grad_n2)
    q2 = grad_n2 * gain2
    grad_middle = upstream + scale2 * (q2 - mean(q2) - unit2 * mean(q2 * unit2))

    grad_attn = grad_middle.astype(BF)
    grad_gated = mm_t(grad_attn[:, :COLS], wo[0]) + mm_t(grad_attn[:, COLS:], wo[1])
    for h in range(2):
        wo[h] = t_mm(gated, grad_attn[:, COLS * h : COLS * h + COLS]).astype(BF)
    swap_w("o")
    work(len(tasks))
    steps_o = scatter_steps_w("o")
    tasks += steps_o[:4] + steps_1[12:16] + steps_2[6:8] + steps_o[4:]
    grad_gate = (grad_gated * grouped * (sig * (1.0 + gate_pre * (1.0 - sig)))).astype(BF)
    grad_grouped = grad_gated * silu
    g_gain_w, g_bias_w = tsum(grad_grouped * unit_w), tsum(grad_grouped)
    qw = grad_grouped * gain_w
    grad_wkv = scale_w * (
        qw
        - head_sum(qw) * (1.0 / 64.0)
        - unit_w * (head_sum(qw * unit_w) * (1.0 / 64.0))
    )

    weight = head_sum(grad_wkv * vals)
    parts_r, parts_k, parts_v = [], [], []
    for g in range(6):
        cut = slice(128 * g, 128 * g + 128)
        rg, kg, vg, dg = recept_f[:, cut], keys_f[:, cut], vals[:, cut], grad_wkv[:, cut]
        ds = stack(dg)
        da = jnp.where(below, fine(NT, ds, vg), 0.0)
        parts_r.append(fine(NN, beside(da), stack(kg)) + fine(NT, dg, memory[g]))
        parts_k.append(fine(TN, da, stack(rg)))
        parts_v.append(fine(TN, scores[g], ds))
        work(2)
    grad_r = jnp.concatenate(parts_r, axis=1) * fall_r
    grad_k = jnp.concatenate(parts_k, axis=1) * fall_k
    grad_v = jnp.concatenate(parts_v, axis=1) + grad_wkv * present
    g_rate = fade * tsum(steps * recept * grad_r - (steps + 1.0) * keys * grad_k)
    g_bonus = tsum(recept * keys * weight)
    grad_r = (grad_r + bonus * keys * weight).astype(BF)
    grad_k = (grad_k + bonus * recept * weight).astype(BF)
    grad_v = grad_v.astype(BF)

    grad_blended = [
        mm_t(grad_r, wn[0, 0, :, 0:768]),
        mm_t(grad_k, wn[0, 0, :, 768:1536]),
        mm_t(grad_v, wn[1, 0, :, 0:768]),
        mm_t(grad_gate, wn[1, 0, :, 768:1536]),
    ]
    wn[0, 0, :, 0:768] = t_mm(blended[0], grad_r).astype(BF)
    wn[0, 0, :, 768:1536] = t_mm(blended[1], grad_k).astype(BF)
    wn[1, 0, :, 0:768] = t_mm(blended[2], grad_v).astype(BF)
    wn[1, 0, :, 768:1536] = t_mm(blended[3], grad_gate).astype(BF)
    delta = normed - previous
    g_lerps = [tsum(g * delta) for g in grad_blended]
    grad_n1 = sum(g * l for g, l in zip(grad_blended, lerps))
    grad_n1 += shift_up(sum(g * (1.0 - l) for g, l in zip(grad_blended, lerps)))
    g_gain1, g_bias1 = tsum(grad_n1 * unit1), tsum(grad_n1)

    zero = jnp.zeros((1, EMB), F32)
    natural = jnp.concatenate([g_rate, g_bonus, g_gain_w, g_bias_w] + [zero] * 4, axis=0)
    va, vb, vc = split(natural, 3)
    moved = mm(va, spread[...]) + (mm(vb, spread[...]) + mm(vc, spread[...]))
    table = jnp.concatenate(
        [g_gain1, g_bias1] + g_lerps + [g_gain2, g_bias2, g_lerp_h, g_lerp_g]
        + [moved[0:4], jnp.zeros((114, EMB), F32)],
        axis=0,
    )
    wn[1, 0, :, VEC:QUART] = table.T.astype(BF)
    swap(0)
    steps_0 = scatter_steps(0)
    tasks += steps_0[:8] + steps_1[16:] + steps_0[8:12]
    work(len(tasks))
    out_ref[...] = unspread(layer_out)
    q1 = grad_n1 * gain1
    grad_x = grad_middle + scale1 * (q1 - mean(q1) - unit1 * mean(q1 * unit1))
    in_grad_ref[...] = unspread(grad_x)

    spread_z = mm(turn_z[:, :96], sums_z["o"]) + mm(turn_z[:, 96:], sums_z["2"])
    piece_z[...] = spread_z.astype(BF).reshape(8, 64, COLS)
    planes = []
    for k in range(1, 8):
        mate, index = at.plane(k)
        planes.append(net.send(piece_z.at[index], plane_z.at[k - 1], mate))
    tasks += steps_0[12:]
    work(len(tasks))

    spread_n = mm(turn_n[...], jnp.concatenate([acc_n[0], acc_n[1]], axis=0).astype(BF))
    piece_n[...] = spread_n.astype(BF).reshape(8, 16, QUART)
    lines = []
    for k in range(1, 8):
        mate, index, _ = at.line(k)
        lines.append(net.send(piece_n.at[index], line_n.at[own], mate))

    total = wide(piece_z.at[at.chip])
    for k in range(1, 8):
        planes[k - 1].wait_recv()
        total += wide(plane_z.at[k - 1])
    swap_f[...] = total
    away, kept = rows(32 * (1 - c), 32, 8), rows(32 * c, 32, 8)
    last_swap = net.send(swap_f.at[away], end_z.at[c], sib)
    end_z[c] = swap_f[kept]

    line_n[own] = piece_n[own]
    for copy in lines:
        copy.wait_recv()
    for h in range(2):
        total = wide(line_n.at[h])
        for z in (1, 2, 3):
            total += wide(line_n.at[2 * z + h])
        end_n[h] = total
    last_swap.wait_recv()
    net.drain()


def layer(*operands):
    bf = lambda *shape: pltpu.VMEM(shape, BF)
    f32 = lambda *shape: pltpu.VMEM(shape, F32)
    return pl.pallas_call(
        layer_kernel,
        out_shape=(
            jax.ShapeDtypeStruct((TOK, EMB), F32),
            jax.ShapeDtypeStruct((TOK, EMB), F32),
            jax.ShapeDtypeStruct((2, 16, QUART), F32),
            jax.ShapeDtypeStruct((2, 32, COLS), F32),
        ),
        in_specs=[VMEM] * len(operands),
        out_specs=(VMEM,) * 4,
        scratch_shapes=[
            bf(2, 2, EMB, QUART), bf(2, EMB, COLS), bf(2, FF, COLS), f32(6, 256, 128),
            f32(2, 16, QUART), bf(2, 16, QUART), bf(8, 16, QUART),
            f32(48, EMB), bf(2, 32, COLS), bf(2, 32, COLS), bf(8, 2, 32, COLS),
            bf(2, EMB, QUART), bf(EMB, COLS), bf(FF, COLS),
            bf(2, 4, 48, QUART), bf(2, 2, 4, 48, QUART), bf(2, 3, 48, QUART),
            f32(2, 48, QUART), bf(8, 16, QUART), bf(8, 16, QUART),
            bf(2, 96, COLS), bf(2, 336, COLS), bf(2, 2, 96, COLS), bf(2, 2, 336, COLS),
            bf(96, COLS), bf(336, COLS), bf(96, COLS), bf(336, COLS),
            bf(8, 64, COLS), bf(7, 64, COLS), f32(64, COLS),
            pltpu.SemaphoreType.DMA((COPIES,)),
            pltpu.SemaphoreType.DMA((COPIES,)),
        ],
        compiler_params=pltpu.CompilerParams(
            collective_id=1, has_side_effects=True, vmem_limit_bytes=62 << 20
        ),
        cost_estimate=pl.CostEstimate(
            flops=6 * TOK * 7667712, bytes_accessed=4 * 7667712, transcendentals=10 * TOK * EMB
        ),
        name="layer",
    )(*operands)


def finish_kernel(end_n, end_z, spread, out_in, grad_in, out, grad, vec, *mats):
    acceptor, address, content, sigmoid, mixer, ff_address, ff_content, ff_acceptor = mats
    out[...] = out_in[...]
    grad[...] = grad_in[...]
    acceptor[...] = end_n[0, 0:6, 0:768]
    address[...] = end_n[0, 0:6, 768:1536]
    content[...] = end_n[1, 0:6, 0:768]
    sigmoid[...] = end_n[1, 0:6, 768:1536]
    ff_address[:, 0:128] = end_n[0, 0:6, 1536:1664]
    ff_address[:, 128:1408] = end_n[0, 8:14, 0:1280]
    ff_address[:, 1408:2688] = end_n[1, 8:14, 0:1280]
    vec[...] = end_n[1, 0:8, VEC:QUART]
    columns = jnp.concatenate(
        [
            jnp.concatenate([end_z[0], end_z[1]], axis=1),
            jnp.concatenate([end_n[0, 8:16, 1280:1664], end_n[1, 8:16, 1280:1664]], axis=1),
        ],
        axis=0,
    )
    a, b, d = split(columns, 3)
    moved = mm_t(a, spread[...]) + (mm_t(b, spread[...]) + mm_t(d, spread[...]))
    mixer[...] = moved[0:6]
    ff_content[...] = moved[8:29]
    ff_acceptor[...] = moved[32:38]


def finish(end_n, end_z, spread, out, grad):
    shapes = [(TOK, EMB), (TOK, EMB), (8, 128)]
    shapes += [(6, EMB)] * 5 + [(6, FF), (21, EMB), (6, EMB)]
    return pl.pallas_call(
        finish_kernel,
        out_shape=tuple(jax.ShapeDtypeStruct(shape, F32) for shape in shapes),
        in_specs=[VMEM] * 5,
        out_specs=(VMEM,) * len(shapes),
        name="finish",
    )(end_n, end_z, spread, out, grad)


def per_device(
    incoming_activations,
    sequence_opening_memory,
    prior_standardize_factor,
    prior_standardize_offset,
    acceptor_lerp_factor,
    address_lerp_factor,
    content_lerp_factor,
    sigmoid_lerp_factor,
    acceptor_matrix,
    address_matrix,
    content_matrix,
    sigmoid_matrix,
    lane_fading_exponent,
    present_reward_vector,
    cluster_standardize_factor,
    cluster_standardize_offset,
    mixer_result_matrix,
    latter_standardize_factor,
    latter_standardize_offset,
    feedforward_address_lerp,
    feedforward_sigmoid_lerp,
    feedforward_address_matrix,
    feedforward_content_matrix,
    feedforward_acceptor_matrix,
    upstream_derivative,
):
    spread = jnp.asarray(_spread(), BF)
    vectors = jnp.stack(
        [prior_standardize_factor, prior_standardize_offset, acceptor_lerp_factor,
         address_lerp_factor, content_lerp_factor, sigmoid_lerp_factor,
         latter_standardize_factor, latter_standardize_offset, feedforward_address_lerp,
         feedforward_sigmoid_lerp, lane_fading_exponent, present_reward_vector,
         cluster_standardize_factor, cluster_standardize_offset], axis=0,
    )
    vectors = jnp.pad(vectors, ((0, 114), (0, 122)))
    memory = sequence_opening_memory.reshape(6, 2, 64, 64)
    nothing = jnp.zeros((6, 64, 64), F32)
    memory = jnp.concatenate(
        [jnp.concatenate([memory[:, 0], nothing], axis=2),
         jnp.concatenate([nothing, memory[:, 1]], axis=2)], axis=1,
    )
    out, in_grad, end_n, end_z = layer(
        incoming_activations, upstream_derivative, memory, spread,
        jnp.asarray(_line_pick(), BF), jnp.asarray(_plane_pick(), BF),
        jnp.asarray(_line_pick().T, BF), jnp.asarray(_plane_pick().T, BF),
        vectors, acceptor_matrix, address_matrix, content_matrix, sigmoid_matrix,
        mixer_result_matrix, feedforward_address_matrix, feedforward_content_matrix,
        feedforward_acceptor_matrix,
    )
    (out, in_grad, vec, acceptor, address, content, sigmoid, mixer,
     ff_address, ff_content, ff_acceptor) = finish(end_n, end_z, spread, out, in_grad)
    v = [vec[:6, i] for i in range(14)]
    return (
        out, in_grad,
        v[0], v[1], v[2], v[3], v[4], v[5],
        acceptor, address, content, sigmoid,
        v[10], v[11], v[12], v[13],
        mixer,
        v[6], v[7], v[8], v[9],
        ff_address, ff_content, ff_acceptor,
    )


def solution(mesh):
    r, v = P(("dp", "fsdp"), None), P(("dp", "fsdp"))
    state = P(("dp", "fsdp"), None, None, None)
    return jax.shard_map(
        per_device,
        mesh=mesh,
        in_specs=(r, state) + (v,) * 6 + (r,) * 4 + (v,) * 4 + (r,) + (v,) * 4 + (r,) * 4,
        out_specs=(r, r) + (v,) * 6 + (r,) * 4 + (v,) * 4 + (r,) + (v,) * 4 + (r,) * 3,
        check_vma=False,
    )
```

```python
from functools import partial

import jax
import jax.numpy as jnp
import numpy as np
from jax import lax
from jax.experimental import pallas as pl
from jax.experimental.pallas import tpu as pltpu
from jax.sharding import PartitionSpec as P

MESH = pl.DeviceIdType.MESH
BF = jnp.bfloat16
F32 = jnp.float32
VMEM = pl.BlockSpec(memory_space=pltpu.VMEM)

NORM_EPS = 1e-05
GROUP_EPS = 0.00064
TOK = 128
EMB = 768
FF = 2688
COLS = 384
SENDS, ARRIVALS = 96, 160
LEFT, RIGHT = 896, 768

WIDTH = {"A": 1664, "B": 1280, "C": 384, "R": 768, "K": 896}
VEC = 1536
ORDER = (0, 1, 3, 2)


def _order():
    order = np.zeros(EMB, np.int64)
    for x in range(4):
        for y in range(4):
            for z in range(4):
                for c in range(2):
                    device = z * 32 + (x % 2) * 16 + y * 4 + (x // 2) * 2 + c
                    place = (x * 4 + y) * 48 + (z * 2 + c) * 6
                    order[place : place + 6] = 6 * device + np.arange(6)
    return order


def _spread():
    spread = np.zeros((EMB, EMB), np.float32)
    spread[_order(), np.arange(EMB)] = 1.0
    return spread


def _line_pick():
    pick = np.zeros((96, 128), np.float32)
    for member in range(8):
        for r in range(6):
            pick[member * 6 + r, member * 16 + r] = 1.0
            pick[48 + member * 6 + r, member * 16 + 8 + r] = 1.0
    return pick


def _plane_pick():
    pick = np.zeros((432, 512), np.float32)
    for member in range(16):
        for r in range(6):
            pick[member * 6 + r, member * 32 + r] = 1.0
        for r in range(21):
            pick[96 + member * 21 + r, member * 32 + 8 + r] = 1.0
    return pick


def rem4(value):
    return lax.rem(value, 4)


class Place:
    def __init__(self):
        dp, fs = lax.axis_index("dp"), lax.axis_index("fsdp")
        self.z, self.xlo = lax.div(dp, 2), lax.rem(dp, 2)
        self.y, self.xhi = lax.div(fs, 4), lax.rem(lax.div(fs, 2), 2)
        self.c = lax.rem(fs, 2)
        self.x = self.xhi * 2 + self.xlo

    def device(self, z, y, x, c):
        return (z * 2 + lax.rem(x, 2), y * 4 + lax.div(x, 2) * 2 + c)

    def sibling(self):
        return self.device(self.z, self.y, self.x, 1 - self.c)

    def up(self, k):
        return self.device(rem4(self.z + k), self.y, self.x, self.c)

    def line(self, k):
        z = rem4(self.z + k // 2)
        core = self.c if k % 2 == 0 else 1 - self.c
        return self.device(z, self.y, self.x, core), z * 2 + core, core

    def turn(self, q, sibling=False):
        return 1 if q == "C" else (1 - self.c if sibling else self.c)

    def first(self, q, k):
        t = self.turn(q)
        y, x = rem4(self.y + k * (1 - t)), rem4(self.x + k * t)
        return self.device(self.z, y, x, self.c)

    def last(self, q, k):
        t = self.turn(q)
        y, x = rem4(self.y + k * t), rem4(self.x + k * (1 - t))
        return self.device(self.z, y, x, self.c)

    def band(self, q, m, k, sibling=False):
        t = self.turn(q, sibling)
        x = rem4(self.x + m * t + k * (1 - t))
        y = rem4(self.y + m * (1 - t) + k * t)
        return rows(48 * (x * 4 + y), 48)

    def across(self, k):
        return self.device(self.z, self.y, rem4(self.x + k), self.c)

    def side(self, k):
        return self.device(self.z, rem4(self.y + k), self.x, self.c)

    def twin(self):
        return self.device(self.z, self.y, self.xhi * 2 + 1 - self.xlo, self.c)

    def pair(self):
        return self.across(2)

    def order(self, m, k):
        return rem4(self.z + k) * 2 + (self.xlo if m == 0 else 1 - self.xlo)

    def greet(self):
        mates = [self.line(k)[0] for k in range(1, 8)]
        mates += [self.across(k) for k in (1, 2, 3)]
        mates += [self.side(k) for k in (1, 2, 3)]
        barrier = pltpu.get_barrier_semaphore()
        for mate in mates:
            pl.semaphore_signal(barrier, inc=1, device_id=mate, device_id_type=MESH)
        return lambda: pl.semaphore_wait(barrier, len(mates))


class Sender:
    def __init__(self, send_sems, recv_sems):
        self.send_sems, self.recv_sems = send_sems, recv_sems
        self.sends = self.arrivals = 0
        self.open = []
        self.groups = {}

    def send(self, source, target, device, group=None):
        index = self.sends % SENDS
        if len(self.open) >= SENDS:
            self.open.pop(0).wait_send()
        self.sends += 1
        if group not in self.groups:
            self.groups[group if group is not None else self.sends] = self.arrivals
            arrival = self.arrivals
            self.arrivals += 1
        else:
            arrival = self.groups[group]
        copy = pltpu.make_async_remote_copy(
            src_ref=source,
            dst_ref=target,
            send_sem=self.send_sems.at[index],
            recv_sem=self.recv_sems.at[arrival],
            device_id=device,
            device_id_type=MESH,
        )
        copy.start()
        self.open.append(copy)
        return copy

    def wait_group(self, group, like, device):
        pltpu.make_async_remote_copy(
            src_ref=like,
            dst_ref=like,
            send_sem=self.send_sems.at[0],
            recv_sem=self.recv_sems.at[self.groups[group]],
            device_id=device,
            device_id_type=MESH,
        ).wait_recv()

    def drain(self):
        for copy in self.open:
            copy.wait_send()
        self.open = []


def rows(start, size, unit=16):
    return pl.ds(pl.multiple_of(start, unit), size)


def mm(left, right):
    return jnp.dot(left, right, preferred_element_type=F32)


def mm_t(left, right):
    return lax.dot_general(left, right, (((1,), (1,)), ((), ())), preferred_element_type=F32)


def t_mm(left, right):
    return lax.dot_general(left, right, (((0,), (0,)), ((), ())), preferred_element_type=F32)


def split(value, parts):
    found = []
    for _ in range(parts - 1):
        high = value.astype(BF)
        found.append(high)
        value = value - high.astype(F32)
    found.append(value.astype(BF))
    return found


def fine(dims, left, right):
    lh, ll = split(left, 2)
    rh, rl = split(right, 2)
    dot = partial(lax.dot_general, dimension_numbers=(dims, ((), ())), preferred_element_type=F32)
    return dot(lh, rh) + (dot(lh, rl) + dot(ll, rh))


NN, NT, TN = ((1,), (0,)), ((1,), (1,)), ((0,), (0,))


def wide(ref):
    return ref[...].astype(F32)


def layer_kernel(
    x_in, up_in, state, spread_in, pick_n_in, pick_z_in, turn_n_in, turn_z_in, *refs
):
    vecs, refs = refs[:14], refs[14:]
    (acceptor, address, content, sigmoid, mixer, ff_address, ff_content, ff_acceptor), refs = refs[:8], refs[8:]
    (
        out_ref, in_grad_ref, end_n, end_z,
        x_ref, up_ref, state_v, spread, pick_n, pick_z, turn_n, turn_z, memory,
        wa, wb, wc, wo, w2, gk, gb, gc, scores,
        vec_f, pack_f, pack_n, stage_a, stage_b, cols_f, pack_z, half_z, pair_z, stage_z,
        sib_r, sib_k, sib_b, sib_c, relay_r, relay_k, relay_b, relay_c,
        last_r, last_k, last_b, last_c, first_r, first_k, first_b, first_c,
        acc_r, acc_k, acc_b, acc_c,
        piece_a, piece_b, line_a, line_b,
        sib_o, sib_2, relay_o, relay_2, up_o, up_2, sent_o, sent_2, twin_o, twin_2,
        piece_z, side_z, half_f, sent_z, got_z, swap_f,
        send_sems, recv_sems, load_sems,
    ) = refs
    at = Place()
    c = at.c
    sib = at.sibling()
    net = Sender(send_sems, recv_sems)
    met = at.greet()

    loads = {}
    for i, (name, source, target) in enumerate([
        ("spread", spread_in, spread), ("x", x_in, x_ref), ("pick_n", pick_n_in, pick_n),
        ("up", up_in, up_ref), ("pick_z", pick_z_in, pick_z), ("state", state, state_v),
        ("turn_n", turn_n_in, turn_n), ("turn_z", turn_z_in, turn_z),
    ]):
        loads[name] = pltpu.make_async_copy(source, target, load_sems.at[i])
        loads[name].start()

    vec_f[...] = jnp.zeros_like(vec_f)
    for i, ref in enumerate(vecs):
        vec_f[i : i + 1, 0:6] = wide(ref).reshape(1, 6)
    eye = (
        lax.broadcasted_iota(jnp.int32, (16, 128), 0)
        == lax.broadcasted_iota(jnp.int32, (16, 128), 1)
    ).astype(F32).astype(BF)
    pack_f[...] = jnp.zeros_like(pack_f)
    pack_f[0, 0, 0:6, 0:768] = wide(acceptor)
    pack_f[0, 0, 0:6, 768:896] = wide(address.at[:, 0:128])
    pack_f[0, 0, 8:14, 0:640] = wide(address.at[:, 128:768])
    pack_f[0, 0, 8:14, 640:768] = wide(ff_address.at[:, 0:128])
    pack_f[1, 0, 0:6, 0:768] = wide(content)
    pack_f[1, 0, 0:6, 768:896] = wide(sigmoid.at[:, 0:128])
    pack_f[1, 0, 8:14, 0:640] = wide(sigmoid.at[:, 128:768])
    pack_f[1, 0, 8:14, 640:768] = mm_t(eye, vec_f[...].astype(BF))[0:6]
    for h in range(2):
        pack_n[0, h] = pack_f[h, 0].astype(BF)
    met()

    own = at.z * 2 + c

    def send_lines(i, stage):
        for k in range(1, 8):
            mate, _, core = at.line(k)
            net.send(pack_n.at[i, core], stage.at[own], mate, ("lines", i))
        stage[own] = pack_n[i, c]

    send_lines(0, stage_a)
    cols_f[...] = jnp.zeros_like(cols_f)
    cols_f[0:6] = wide(mixer)
    cols_f[8:29] = wide(ff_content)
    cols_f[32:38] = wide(ff_acceptor)
    loads["spread"].wait()
    moved = mm(cols_f[...].astype(BF), spread[...])
    for h in range(2):
        pack_z[h] = moved[0:32, COLS * h : COLS * h + COLS].astype(BF)
        first_col = 128 + 1280 * h
        pack_f[h, 1, 0:6, 0:896] = wide(ff_address.at[:, first_col : first_col + 896])
        pack_f[h, 1, 8:14, 0:384] = wide(ff_address.at[:, first_col + 896 : first_col + 1280])
        pack_f[h, 1, 8:16, 384:768] = moved[32:40, COLS * h : COLS * h + COLS]
        pack_n[1, h] = pack_f[h, 1].astype(BF)
    swap_z = net.send(pack_z.at[1 - c], half_z.at[c], sib)
    half_z[c] = pack_z[c]
    send_lines(1, stage_b)

    loads["x"].wait()
    tokens = mm(x_ref[...], spread[...])
    centred = tokens - jnp.mean(tokens, axis=-1, keepdims=True)
    scale1 = lax.rsqrt(jnp.mean(centred * centred, axis=-1, keepdims=True) + NORM_EPS)
    unit1 = centred * scale1
    loads["up"].wait()
    upstream = mm(up_ref[...], spread[...])
    swap_z.wait_recv()
    to_pair = net.send(half_z, pair_z.at[at.xhi], at.pair())
    pair_z[at.xhi] = half_z[...]
    loads["pick_n"].wait()
    for name in ("state", "turn_n", "turn_z", "pick_z"):
        loads[name].wait()
    blank = jnp.zeros((64, 64), F32)
    for g in range(6):
        memory[g, 0:64] = jnp.concatenate([state_v[2 * g], blank], axis=1)
        memory[g, 64:128] = jnp.concatenate([blank, state_v[2 * g + 1]], axis=1)

    def pick(i, stage):
        net.wait_group(("lines", i), stage.at[0:7], sib)
        return mm(pick_n[...], stage[...].reshape(128, LEFT)).astype(BF)

    full = {"A": wa, "B": wb, "C": wc, "o": wo, "2": w2}

    def place_n(q, m, k):
        return full[q].at[c, at.band(q, m, k)]

    firsts, lasts = {}, {}

    def pass_on(q, m):
        spot = place_n(q, 4 - m, 0)
        for k in (1, 3):
            lasts[q, m, k] = net.send(spot, spot, at.last(q, k))
        net.send(spot, spot, sib, ("sib", q))

    def begin(q, *parts):
        spot = place_n(q, 0, 0)
        spot[...] = jnp.concatenate(parts, axis=1) if len(parts) > 1 else parts[0]
        for k in (1, 3, 2):
            firsts[q, k] = net.send(spot, spot, at.first(q, k))
        pass_on(q, 0)

    def relay(q, m):
        firsts[q, m].wait_recv()
        pass_on(q, m)

    def arrive(q, m, k):
        lasts[q, m, k].wait_recv()
        spot = place_n(q, 4 - m, 4 - k)
        if k == (1 if m % 2 == 0 else 3):
            lasts[q, m, 2] = net.send(spot, spot, at.last(q, k))
        net.send(spot, spot, sib, ("sib", q))

    def arrive_far(q, m):
        lasts[q, m, 2].wait_recv()
        spot = place_n(q, 4 - m, 2)
        net.send(spot, spot, sib, ("sib", q))

    def place_z(w, m, k):
        unit = 96 if w == "o" else 336
        return full[w].at[c, rows(unit * at.order(m, k), unit)]

    def pass_z(w, m):
        spot = place_z(w, m, 0)
        for k in (1, 3):
            lasts[w, m, k] = net.send(spot, spot, at.up(k))
        net.send(spot, spot, sib, ("sib", w))

    def relay_z(w):
        firsts[w].wait_recv()
        pass_z(w, 1)

    def arrive_z(w, m, k):
        lasts[w, m, k].wait_recv()
        spot = place_z(w, m, 4 - k)
        if k == (1 if m == 0 else 3):
            lasts[w, m, 2] = net.send(spot, spot, at.up(k))
        net.send(spot, spot, sib, ("sib", w))

    def arrive_z_far(w, m):
        lasts[w, m, 2].wait_recv()
        spot = place_z(w, m, 2)
        net.send(spot, spot, sib, ("sib", w))

    picked = pick(0, stage_a)
    begin("A", picked[0:48], picked[48:96, 0:RIGHT])
    to_pair.wait_recv()
    for k in (1, 2, 3):
        net.send(pair_z, stage_z.at[at.y], at.side(k), "side")
    stage_z[at.y] = pair_z[...]
    relay("A", 1)
    relay("A", 3)
    for k in (1, 3):
        arrive("A", 0, k)
    picked = pick(1, stage_b)
    relay("A", 2)
    begin("B", picked[0:48], picked[48:96, 0:384])
    begin("C", picked[48:96, 384:768])
    net.wait_group("side", stage_z.at[0:3], sib)
    picked_z = mm(pick_z[...], stage_z[...].reshape(512, COLS)).astype(BF)
    place_z("o", 0, 0)[...] = picked_z[:96]
    place_z("2", 0, 0)[...] = picked_z[96:]
    for w in ("o", "2"):
        spot = place_z(w, 0, 0)
        firsts[w] = net.send(spot, spot, at.twin())
        pass_z(w, 0)
    for m in (1, 3):
        for k in (1, 3):
            arrive("A", m, k)
    arrive_far("A", 0)
    relay("B", 1)
    relay("B", 3)
    for k in (1, 3):
        arrive("A", 2, k)
    for w in ("o", "2"):
        relay_z(w)
    relay("B", 2)
    for m in (1, 3, 2):
        relay("C", m)
    for m in (1, 3, 2):
        arrive_far("A", m)
    tasks = []

    def plan(kind, *steps_):
        for step in steps_:
            tasks.append((kind, step))

    for m in (0, 1):
        for k in (1, 3):
            plan("B", partial(arrive, "B", m, k))
            plan("o", partial(arrive_z, "o", m, k))
            plan("2", partial(arrive_z, "2", m, k))
    for m in (0, 1):
        plan("o", partial(arrive_z_far, "o", m))
    for m in (3, 2):
        for k in (1, 3):
            plan("B", partial(arrive, "B", m, k))
    for m in ORDER:
        for k in (1, 3):
            plan("C", partial(arrive, "C", m, k))
    for m in (0, 1):
        plan("2", partial(arrive_z_far, "2", m))
    for q in ("B", "C"):
        for m in ORDER:
            plan(q, partial(arrive_far, q, m))

    def work(count=1000):
        for _ in range(min(count, len(tasks))):
            tasks.pop(0)[1]()

    def need(q):
        while any(kind == q for kind, _ in tasks):
            work(1)
        net.wait_group(("sib", q), full[q].at[1 - c], sib)

    need("A")

    lanes = lax.broadcasted_iota(jnp.int32, (1, 128), 1)
    left_head = lanes < 64
    token = lax.broadcasted_iota(jnp.int32, (TOK, 1), 0)

    def shift_down(value):
        return jnp.where(token == 0, 0.0, pltpu.roll(value, 1, 0))

    def shift_up(value):
        return jnp.where(token == TOK - 1, 0.0, pltpu.roll(value, TOK - 1, 0))

    def mean(value):
        return jnp.mean(value, axis=-1, keepdims=True)

    def tsum(value):
        return jnp.sum(value, axis=0, keepdims=True)

    def unspread(value):
        a, b, d = split(value, 3)
        return mm_t(a, spread[...]) + (mm_t(b, spread[...]) + mm_t(d, spread[...]))

    vec = mm_t(eye, wa[1, :, VEC:1664])
    gain1, bias1 = vec[0:1], vec[1:2]
    lerps = [vec[2 + i : 3 + i] for i in range(4)]
    gain2, bias2, lerp_h, lerp_g = vec[6:7], vec[7:8], vec[8:9], vec[9:10]
    heads = mm_t(vec.astype(BF), spread[...])
    rate, bonus, gain_w, bias_w = heads[10:11], heads[11:12], heads[12:13], heads[13:14]

    pair_rows = lax.broadcasted_iota(jnp.int32, (256, 128), 0)
    pair_cols = lax.broadcasted_iota(jnp.int32, (256, 128), 1)
    pair_ones = ((lax.rem(pair_rows, 128) // 64) == (pair_cols // 64)).astype(F32).astype(BF)
    below = lax.rem(pair_rows, 128) > pair_cols

    def head_sum(value):
        found = []
        for g in range(6):
            part = value[:, 128 * g : 128 * g + 128]
            found.append(mm(jnp.concatenate(split(part, 2), axis=1), pair_ones))
        return jnp.concatenate(found, axis=1)

    def stack(value):
        return jnp.concatenate(
            [jnp.where(left_head, value, 0.0), jnp.where(left_head, 0.0, value)], axis=0
        )

    def beside(value):
        return jnp.concatenate([value[:TOK], value[TOK:]], axis=1)

    normed = unit1 * gain1 + bias1
    previous = shift_down(normed)
    blended = [(normed * l + previous * (1.0 - l)).astype(BF) for l in lerps]
    recept = mm(blended[0], wa[0, :, 0:768])
    keys = mm(blended[1], wa[0, :, 768:1536])
    vals = mm(blended[2], wa[1, :, 0:768])
    gate_pre = mm(blended[3], wa[1, :, 768:1536])
    work(6)

    fade = -jnp.exp(rate)
    steps = token.astype(F32)
    fall_r = jnp.exp(steps * fade)
    fall_k = jnp.exp(-(steps + 1.0) * fade)
    recept_f = recept * fall_r
    keys_f = keys * fall_k
    present = head_sum(recept * bonus * keys)
    parts = []
    for g in range(6):
        cut = slice(128 * g, 128 * g + 128)
        rg, kg, vg = recept_f[:, cut], keys_f[:, cut], vals[:, cut]
        sc = jnp.where(below, fine(NT, stack(rg), kg), 0.0)
        scores[g] = sc
        parts.append(fine(NN, beside(sc), stack(vg)) + fine(NN, rg, memory[g]))
        if g % 2 == 1:
            work(4)
    wkv = jnp.concatenate(parts, axis=1) + present * vals

    centred_w = wkv - head_sum(wkv) * (1.0 / 64.0)
    scale_w = lax.rsqrt(head_sum(centred_w * centred_w) * (1.0 / 64.0) + GROUP_EPS)
    unit_w = centred_w * scale_w
    grouped = unit_w * gain_w + bias_w
    sig = 1.0 / (1.0 + jnp.exp(-gate_pre))
    silu = gate_pre * sig
    gated = (grouped * silu).astype(BF)
    need("o")
    middle = tokens + jnp.concatenate([mm(gated, wo[0]), mm(gated, wo[1])], axis=1)

    centred = middle - mean(middle)
    scale2 = lax.rsqrt(mean(centred * centred) + NORM_EPS)
    unit2 = centred * scale2
    normed2 = unit2 * gain2 + bias2
    previous2 = shift_down(normed2)
    mixed_h = (normed2 * lerp_h + previous2 * (1.0 - lerp_h)).astype(BF)
    mixed_g = (normed2 * lerp_g + previous2 * (1.0 - lerp_g)).astype(BF)
    need("B")
    need("C")
    pre = jnp.concatenate(
        [mm(mixed_h, wa[0, :, 1536:1664]), mm(mixed_h, wb[0]), mm(mixed_h, wb[1])], axis=1
    )
    pre = jnp.maximum(pre, 0.0)
    hidden = (pre * pre).astype(BF)
    gating = jnp.concatenate([mm(mixed_g, wc[0]), mm(mixed_g, wc[1])], axis=1)
    gating = 1.0 / (1.0 + jnp.exp(-gating))
    grad_vo = upstream * gating
    grad_vo_low = grad_vo.astype(BF)
    swaps = {}

    def fold(mine, other, *more):
        total = wide(mine) + wide(other)
        for ref in more:
            total += wide(ref)
        return total

    gr, go = wb.at[:, :, 0:768], wb.at[:, :, 768:1152]
    grads = {"R": gr, "K": gk, "B": gb, "C": gc}
    sib_of = {"R": sib_r, "K": sib_k, "B": sib_b, "C": sib_c}
    relay_of = {"R": relay_r, "K": relay_k, "B": relay_b, "C": relay_c}
    last_of = {"R": last_r, "K": last_k, "B": last_b, "C": last_c}
    first_of = {"R": first_r, "K": first_k, "B": first_b, "C": first_c}
    acc_of = {"R": acc_r, "K": acc_k, "B": acc_b, "C": acc_c}

    def swap(q):
        swaps[q] = net.send(grads[q].at[1 - c], sib_of[q], sib)

    def swapped(q):
        if q in swaps:
            swaps.pop(q).wait_recv()

    def scatter_far(q, m):
        part = at.band(q, m, 2)
        via = 1 if m % 2 == 0 else 3
        swapped(q)
        spot = sib_of[q].at[part]
        spot[...] = fold(grads[q].at[c, part], spot).astype(BF)
        lasts["g", q, m, 2] = net.send(spot, relay_of[q].at[m], at.last(q, via))

    def scatter_near(q, m, k):
        part = at.band(q, m, k)
        spot = sib_of[q].at[part]
        more = []
        if k == (1 if m % 2 == 0 else 3):
            lasts["g", q, m, 2].wait_recv()
            more = [relay_of[q].at[m]]
        spot[...] = fold(grads[q].at[c, part], spot, *more).astype(BF)
        lasts["g", q, m, k] = net.send(spot, last_of[q].at[k // 2, m], at.last(q, k))

    def scatter_own(q, m):
        part = at.band(q, m, 0)
        spot = sib_of[q].at[part]
        lasts["g", q, m, 1].wait_recv()
        lasts["g", q, m, 3].wait_recv()
        arrived = last_of[q]
        total = fold(grads[q].at[c, part], spot, arrived.at[0, m], arrived.at[1, m])
        if m == 0:
            acc_of[q][...] = total
        else:
            spot[...] = total.astype(BF)
            firsts["g", q, m] = net.send(spot, first_of[q].at[m - 1], at.first(q, m))

    def scatter_end(q):
        total = acc_of[q][...]
        for m in (1, 3, 2):
            firsts["g", q, m].wait_recv()
            total += wide(first_of[q].at[m - 1])
        acc_of[q][...] = total

    def spread_lines(i, left, right, piece, line):
        right = jnp.concatenate([right, jnp.zeros((48, LEFT - RIGHT), F32)], axis=1)
        table = jnp.concatenate([left, right], axis=0).astype(BF)
        piece[...] = mm(turn_n[...], table).astype(BF).reshape(8, 16, LEFT)
        for k in range(1, 8):
            mate, index, _ = at.line(k)
            net.send(piece.at[index], line.at[own], mate, ("grad lines", i))
        line[own] = piece[own]

    def sum_lines(i, line):
        net.wait_group(("grad lines", i), line.at[0:7], sib)
        for h in range(2):
            total = wide(line.at[h])
            for z in (1, 2, 3):
                total += wide(line.at[2 * z + h])
            end_n[h, i] = total

    def scatter_steps(q):
        steps_ = [partial(scatter_far, q, m) for m in ORDER]
        for late in (False, True):
            for m in ORDER:
                for k in (1, 3):
                    if late == (k == (1 if m % 2 == 0 else 3)):
                        steps_.append(partial(scatter_near, q, m, k))
        steps_ += [partial(scatter_own, q, m) for m in (1, 3, 2, 0)]
        steps_.append(partial(scatter_end, q))
        return steps_

    z_parts = {
        "o": (96, go, sib_o, relay_o, up_o, sent_o, twin_o),
        "2": (336, w2, sib_2, relay_2, up_2, sent_2, twin_2),
    }

    def swap_w(w):
        unit, mine, theirs = z_parts[w][:3]
        swaps[w] = net.send(mine.at[1 - c], theirs, sib)

    def part_w(w, m, k):
        unit = z_parts[w][0]
        return rows(unit * at.order(m, k), unit)

    def scatter_far_w(w, m):
        unit, mine, theirs, relayed = z_parts[w][:4]
        part = part_w(w, m, 2)
        swapped(w)
        spot = theirs.at[part]
        spot[...] = fold(mine.at[c, part], spot).astype(BF)
        lasts["g", w, m, 2] = net.send(spot, relayed.at[m], at.up(1 if m == 0 else 3))

    def scatter_near_w(w, m, k):
        unit, mine, theirs, relayed, arrived = z_parts[w][:5]
        part = part_w(w, m, k)
        more = []
        if k == (1 if m == 0 else 3):
            lasts["g", w, m, 2].wait_recv()
            more = [relayed.at[m]]
        spot = theirs.at[part]
        spot[...] = fold(mine.at[c, part], spot, *more).astype(BF)
        lasts["g", w, m, k] = net.send(spot, arrived.at[k // 2, m], at.up(k))

    def scatter_own_w(w, m):
        unit, mine, theirs, relayed, arrived, sent, twin = z_parts[w]
        part = part_w(w, m, 0)
        lasts["g", w, m, 1].wait_recv()
        lasts["g", w, m, 3].wait_recv()
        total = fold(mine.at[c, part], theirs.at[part], arrived.at[0, m], arrived.at[1, m])
        if m == 1:
            sent[...] = total.astype(BF)
            firsts["g", w] = net.send(sent, twin, at.twin())
        else:
            firsts["g", w].wait_recv()
            sums_z[w] = (total + wide(twin)).astype(BF)

    def scatter_steps_w(w):
        steps_ = [partial(scatter_far_w, w, 0), partial(scatter_far_w, w, 1)]
        steps_ += [partial(scatter_near_w, w, 1, 1), partial(scatter_near_w, w, 0, 3)]
        steps_ += [partial(scatter_near_w, w, 0, 1), partial(scatter_near_w, w, 1, 3)]
        steps_ += [partial(scatter_own_w, w, 1), partial(scatter_own_w, w, 0)]
        return steps_

    sums_z = {}

    need("2")
    steps_2, steps_o = scatter_steps_w("2"), scatter_steps_w("o")
    steps_b, steps_c = scatter_steps("B"), scatter_steps("C")
    steps_r, steps_k = scatter_steps("R"), scatter_steps("K")

    def run(*steps_):
        for step in steps_:
            step()

    grad_hidden = mm_t(grad_vo_low[:, :COLS], w2[0]) + mm_t(grad_vo_low[:, COLS:], w2[1])
    grad_pre = (grad_hidden * 2.0 * pre).astype(BF)
    gb[0] = t_mm(mixed_h, grad_pre[:, 128:1408]).astype(BF)
    gb[1] = t_mm(mixed_h, grad_pre[:, 1408:]).astype(BF)
    swap("B")
    value_out = jnp.concatenate([mm(hidden, w2[0]), mm(hidden, w2[1])], axis=1)
    layer_out = middle + gating * value_out
    net.drain()
    for h in range(2):
        w2[h] = t_mm(hidden, grad_vo_low[:, COLS * h : COLS * h + COLS]).astype(BF)
    swap_w("2")
    run(*steps_b[:8])
    grad_gp = (grad_vo * value_out * (1.0 - gating)).astype(BF)
    for h in range(2):
        gc[h] = t_mm(mixed_g, grad_gp[:, COLS * h : COLS * h + COLS]).astype(BF)
    swap("C")
    run(*steps_2[:4])
    grad_mg = mm_t(grad_gp[:, :COLS], wc[0]) + mm_t(grad_gp[:, COLS:], wc[1])
    grad_mh = mm_t(grad_pre[:, :128], wa[0, :, 1536:1664])
    grad_mh += mm_t(grad_pre[:, 128:1408], wb[0]) + mm_t(grad_pre[:, 1408:], wb[1])
    gk[0, :, 768:896] = t_mm(mixed_h, grad_pre[:, :128]).astype(BF)
    run(*steps_c[:8])

    grad_n2 = grad_mh * lerp_h + grad_mg * lerp_g
    grad_n2 += shift_up(grad_mh * (1.0 - lerp_h) + grad_mg * (1.0 - lerp_g))
    delta2 = normed2 - previous2
    g_lerp_h, g_lerp_g = tsum(grad_mh * delta2), tsum(grad_mg * delta2)
    g_gain2, g_bias2 = tsum(grad_n2 * unit2), tsum(grad_n2)
    q2 = grad_n2 * gain2
    grad_middle = upstream + scale2 * (q2 - mean(q2) - unit2 * mean(q2 * unit2))

    grad_attn = grad_middle.astype(BF)
    grad_gated = mm_t(grad_attn[:, :COLS], wo[0]) + mm_t(grad_attn[:, COLS:], wo[1])
    for h in range(2):
        go[h] = t_mm(gated, grad_attn[:, COLS * h : COLS * h + COLS]).astype(BF)
    swap_w("o")
    grad_gate = (grad_gated * grouped * (sig * (1.0 + gate_pre * (1.0 - sig)))).astype(BF)
    grad_grouped = grad_gated * silu
    g_gain_w, g_bias_w = tsum(grad_grouped * unit_w), tsum(grad_grouped)
    qw = grad_grouped * gain_w
    grad_wkv = scale_w * (
        qw
        - head_sum(qw) * (1.0 / 64.0)
        - unit_w * (head_sum(qw * unit_w) * (1.0 / 64.0))
    )

    weight = head_sum(grad_wkv * vals)
    parts_r, parts_k, parts_v = [], [], []
    for g in range(6):
        cut = slice(128 * g, 128 * g + 128)
        rg, kg, vg, dg = recept_f[:, cut], keys_f[:, cut], vals[:, cut], grad_wkv[:, cut]
        ds = stack(dg)
        da = jnp.where(below, fine(NT, ds, vg), 0.0)
        parts_r.append(fine(NN, beside(da), stack(kg)) + fine(NT, dg, memory[g]))
        parts_k.append(fine(TN, da, stack(rg)))
        parts_v.append(fine(TN, scores[g], ds))
        if g == 0:
            run(*steps_o[:4])
        if g == 3:
            run(*steps_2[4:6], *steps_b[8:12])
    grad_r = jnp.concatenate(parts_r, axis=1) * fall_r
    grad_k = jnp.concatenate(parts_k, axis=1) * fall_k
    grad_v = jnp.concatenate(parts_v, axis=1) + grad_wkv * present
    g_rate = fade * tsum(steps * recept * grad_r - (steps + 1.0) * keys * grad_k)
    g_bonus = tsum(recept * keys * weight)
    grad_r = (grad_r + bonus * keys * weight).astype(BF)
    grad_k = (grad_k + bonus * recept * weight).astype(BF)
    grad_v = grad_v.astype(BF)

    gr[0] = t_mm(blended[0], grad_r).astype(BF)
    gr[1] = t_mm(blended[2], grad_v).astype(BF)
    swap("R")
    gk[0, :, 0:768] = t_mm(blended[1], grad_k).astype(BF)
    gk[1, :, 0:768] = t_mm(blended[3], grad_gate).astype(BF)
    grad_blended = [
        mm_t(grad_r, wa[0, :, 0:768]),
        mm_t(grad_k, wa[0, :, 768:1536]),
        mm_t(grad_v, wa[1, :, 0:768]),
        mm_t(grad_gate, wa[1, :, 768:1536]),
    ]
    run(*steps_c[8:12], *steps_o[4:6], *steps_r[:8])
    delta = normed - previous
    g_lerps = [tsum(g * delta) for g in grad_blended]
    grad_n1 = sum(g * l for g, l in zip(grad_blended, lerps))
    grad_n1 += shift_up(sum(g * (1.0 - l) for g, l in zip(grad_blended, lerps)))
    g_gain1, g_bias1 = tsum(grad_n1 * unit1), tsum(grad_n1)

    zero = jnp.zeros((1, EMB), F32)
    natural = jnp.concatenate([g_rate, g_bonus, g_gain_w, g_bias_w] + [zero] * 4, axis=0)
    va, vb, vc = split(natural, 3)
    moved = mm(va, spread[...]) + (mm(vb, spread[...]) + mm(vc, spread[...]))
    table = jnp.concatenate(
        [g_gain1, g_bias1] + g_lerps + [g_gain2, g_bias2, g_lerp_h, g_lerp_g]
        + [moved[0:4], jnp.zeros((114, EMB), F32)],
        axis=0,
    )
    gk[1, :, 768:896] = table.T.astype(BF)
    swap("K")
    run(*steps_b[12:16], *steps_k[:8], *steps_2[6:8], *steps_o[6:8])
    run(*steps_r[8:12], *steps_c[12:16], *steps_k[8:12])

    spread_z = mm(turn_z[:, :96], sums_z["o"]) + mm(turn_z[:, 96:], sums_z["2"])
    piece_z[...] = spread_z.astype(BF).reshape(4, 128, COLS)
    for k in (1, 2, 3):
        net.send(piece_z.at[rem4(at.y + k)], side_z.at[k - 1], at.side(k), "grad side")
    run(steps_b[16], steps_c[16])
    spread_lines(
        1, acc_b[:, 0:LEFT], jnp.concatenate([acc_b[:, LEFT:], acc_c[...]], axis=1), piece_b, line_b
    )
    out_ref[...] = unspread(layer_out)
    run(*steps_r[12:16])
    q1 = grad_n1 * gain1
    grad_x = grad_middle + scale1 * (q1 - mean(q1) - unit1 * mean(q1 * unit1))
    in_grad_ref[...] = unspread(grad_x)
    run(*steps_k[12:16])
    net.wait_group("grad side", side_z, sib)
    total = wide(piece_z.at[at.y])
    for k in (1, 2, 3):
        total += wide(side_z.at[k - 1])
    half_f[...] = total.reshape(2, 64, COLS)
    sent_z[...] = half_f[1 - at.xhi].astype(BF)
    to_pair = net.send(sent_z, got_z, at.pair())
    run(steps_r[16], steps_k[16])
    acc_a = jnp.concatenate([acc_r[...], acc_k[...]], axis=1)
    spread_lines(0, acc_a[:, 0:LEFT], acc_a[:, LEFT:], piece_a, line_a)
    to_pair.wait_recv()
    swap_f[...] = half_f[at.xhi] + wide(got_z)
    away, kept = rows(32 * (1 - c), 32, 8), rows(32 * c, 32, 8)
    last_swap = net.send(swap_f.at[away], end_z.at[c], sib)
    end_z[c] = swap_f[kept]
    sum_lines(1, line_b)
    last_swap.wait_recv()
    sum_lines(0, line_a)
    net.drain()


def layer(*operands):
    bf = lambda *shape: pltpu.VMEM(shape, BF)
    f32 = lambda *shape: pltpu.VMEM(shape, F32)
    a, b, d, r, k = (WIDTH[q] for q in "ABCRK")
    return pl.pallas_call(
        layer_kernel,
        out_shape=(
            jax.ShapeDtypeStruct((TOK, EMB), F32),
            jax.ShapeDtypeStruct((TOK, EMB), F32),
            jax.ShapeDtypeStruct((2, 2, 16, LEFT), F32),
            jax.ShapeDtypeStruct((2, 32, COLS), F32),
        ),
        in_specs=[pl.BlockSpec(memory_space=pl.ANY)] * 8 + [VMEM] * (len(operands) - 8),
        out_specs=(VMEM,) * 4,
        scratch_shapes=[
            bf(TOK, EMB), bf(TOK, EMB), f32(12, 64, 64), bf(EMB, EMB),
            bf(96, 128), bf(432, 512), bf(128, 96), bf(512, 432), f32(6, 128, 128),
            bf(2, EMB, a), bf(2, EMB, b), bf(2, EMB, d), bf(2, EMB, COLS), bf(2, FF, COLS),
            bf(2, EMB, k), bf(2, EMB, b), bf(2, EMB, d), f32(6, 256, 128),
            f32(128, 128), f32(2, 2, 16, LEFT), bf(2, 2, 16, LEFT), bf(8, 16, LEFT), bf(8, 16, LEFT),
            f32(48, EMB), bf(2, 32, COLS), bf(2, 32, COLS), bf(2, 2, 32, COLS), bf(4, 2, 2, 32, COLS),
            *(bf(EMB, w) for w in (r, k, b, d)), *(bf(4, 48, w) for w in (r, k, b, d)),
            *(bf(2, 4, 48, w) for w in (r, k, b, d)), *(bf(3, 48, w) for w in (r, k, b, d)),
            *(f32(48, w) for w in (r, k, b, d)),
            bf(8, 16, LEFT), bf(8, 16, LEFT), bf(8, 16, LEFT), bf(8, 16, LEFT),
            bf(EMB, COLS), bf(FF, COLS),
            bf(2, 96, COLS), bf(2, 336, COLS), bf(2, 2, 96, COLS), bf(2, 2, 336, COLS),
            bf(96, COLS), bf(336, COLS), bf(96, COLS), bf(336, COLS),
            bf(4, 128, COLS), bf(3, 128, COLS), f32(2, 64, COLS), bf(64, COLS), bf(64, COLS),
            f32(64, COLS),
            pltpu.SemaphoreType.DMA((SENDS,)),
            pltpu.SemaphoreType.DMA((ARRIVALS,)),
            pltpu.SemaphoreType.DMA((8,)),
        ],
        compiler_params=pltpu.CompilerParams(
            collective_id=1, has_side_effects=True, vmem_limit_bytes=62 << 20
        ),
        cost_estimate=pl.CostEstimate(
            flops=6 * TOK * 7667712, bytes_accessed=4 * 7667712, transcendentals=10 * TOK * EMB
        ),
        name="layer",
    )(*operands)


def finish_kernel(end_n, end_z, spread, out_in, grad_in, out, grad, *refs):
    vecs, mats = refs[:14], refs[14:]
    acceptor, address, content, sigmoid, mixer, ff_address, ff_content, ff_acceptor = mats
    out[...] = out_in[...]
    grad[...] = grad_in[...]
    acceptor[...] = end_n[0, 0, 0:6, 0:768]
    address[:, 0:128] = end_n[0, 0, 0:6, 768:896]
    address[:, 128:768] = end_n[0, 0, 8:14, 0:640]
    content[...] = end_n[1, 0, 0:6, 0:768]
    sigmoid[:, 0:128] = end_n[1, 0, 0:6, 768:896]
    sigmoid[:, 128:768] = end_n[1, 0, 8:14, 0:640]
    ff_address[:, 0:128] = end_n[0, 0, 8:14, 640:768]
    for h in range(2):
        first_col = 128 + 1280 * h
        ff_address[:, first_col : first_col + 896] = end_n[h, 1, 0:6, 0:896]
        ff_address[:, first_col + 896 : first_col + 1280] = end_n[h, 1, 8:14, 0:384]
    table = jnp.concatenate([end_n[1, 0, 8:16, 640:768], jnp.zeros((120, 128), F32)], axis=0).T
    for i, ref in enumerate(vecs):
        ref[...] = table[i : i + 1, 0:6].reshape(6)
    columns = jnp.concatenate(
        [
            jnp.concatenate([end_z[0], end_z[1]], axis=1),
            jnp.concatenate([end_n[0, 1, 8:16, 384:768], end_n[1, 1, 8:16, 384:768]], axis=1),
        ],
        axis=0,
    )
    a, b, d = split(columns, 3)
    moved = mm_t(a, spread[...]) + (mm_t(b, spread[...]) + mm_t(d, spread[...]))
    mixer[...] = moved[0:6]
    ff_content[...] = moved[8:29]
    ff_acceptor[...] = moved[32:38]


def finish(end_n, end_z, spread, out, grad):
    shapes = [(TOK, EMB), (TOK, EMB)] + [(6,)] * 14
    shapes += [(6, EMB)] * 5 + [(6, FF), (21, EMB), (6, EMB)]
    return pl.pallas_call(
        finish_kernel,
        out_shape=tuple(jax.ShapeDtypeStruct(shape, F32) for shape in shapes),
        in_specs=[VMEM] * 5,
        out_specs=(VMEM,) * len(shapes),
        name="finish",
    )(end_n, end_z, spread, out, grad)


def per_device(
    incoming_activations,
    sequence_opening_memory,
    prior_standardize_factor,
    prior_standardize_offset,
    acceptor_lerp_factor,
    address_lerp_factor,
    content_lerp_factor,
    sigmoid_lerp_factor,
    acceptor_matrix,
    address_matrix,
    content_matrix,
    sigmoid_matrix,
    lane_fading_exponent,
    present_reward_vector,
    cluster_standardize_factor,
    cluster_standardize_offset,
    mixer_result_matrix,
    latter_standardize_factor,
    latter_standardize_offset,
    feedforward_address_lerp,
    feedforward_sigmoid_lerp,
    feedforward_address_matrix,
    feedforward_content_matrix,
    feedforward_acceptor_matrix,
    upstream_derivative,
):
    spread = jnp.asarray(_spread(), BF)
    out, in_grad, end_n, end_z = layer(
        incoming_activations, upstream_derivative,
        sequence_opening_memory.reshape(12, 64, 64), spread,
        jnp.asarray(_line_pick(), BF), jnp.asarray(_plane_pick(), BF),
        jnp.asarray(_line_pick().T, BF), jnp.asarray(_plane_pick().T, BF),
        prior_standardize_factor, prior_standardize_offset, acceptor_lerp_factor,
        address_lerp_factor, content_lerp_factor, sigmoid_lerp_factor,
        latter_standardize_factor, latter_standardize_offset, feedforward_address_lerp,
        feedforward_sigmoid_lerp, lane_fading_exponent, present_reward_vector,
        cluster_standardize_factor, cluster_standardize_offset,
        acceptor_matrix, address_matrix, content_matrix, sigmoid_matrix,
        mixer_result_matrix, feedforward_address_matrix, feedforward_content_matrix,
        feedforward_acceptor_matrix,
    )
    results = finish(end_n, end_z, spread, out, in_grad)
    out, in_grad, v = results[0], results[1], results[2:16]
    acceptor, address, content, sigmoid, mixer, ff_address, ff_content, ff_acceptor = results[16:]
    return (
        out, in_grad,
        v[0], v[1], v[2], v[3], v[4], v[5],
        acceptor, address, content, sigmoid,
        v[10], v[11], v[12], v[13],
        mixer,
        v[6], v[7], v[8], v[9],
        ff_address, ff_content, ff_acceptor,
    )


def solution(mesh):
    r, v = P(("dp", "fsdp"), None), P(("dp", "fsdp"))
    state = P(("dp", "fsdp"), None, None, None)
    return jax.shard_map(
        per_device,
        mesh=mesh,
        in_specs=(r, state) + (v,) * 6 + (r,) * 4 + (v,) * 4 + (r,) + (v,) * 4 + (r,) * 4,
        out_specs=(r, r) + (v,) * 6 + (r,) * 4 + (v,) * 4 + (r,) + (v,) * 4 + (r,) * 3,
        check_vma=False,
    )
```

```python
from functools import partial

import jax
import jax.numpy as jnp
import numpy as np
from jax import lax
from jax.experimental import pallas as pl
from jax.experimental.pallas import tpu as pltpu
from jax.sharding import PartitionSpec as P

MESH = pl.DeviceIdType.MESH
BF = jnp.bfloat16
F32 = jnp.float32
VMEM = pl.BlockSpec(memory_space=pltpu.VMEM)

NORM_EPS = 1e-05
GROUP_EPS = 0.00064
TOK = 128
EMB = 768
FF = 2688
COLS = 384
SENDS, ARRIVALS = 96, 160
LEFT, RIGHT = 896, 768

WIDTH = {"A": 1664, "B": 1280, "C": 384, "R": 768, "K": 896}
VEC = 1536
ORDER = (0, 1, 3, 2)


def _order():
    order = np.zeros(EMB, np.int64)
    for x in range(4):
        for y in range(4):
            for z in range(4):
                for c in range(2):
                    device = z * 32 + (x % 2) * 16 + y * 4 + (x // 2) * 2 + c
                    place = (x * 4 + y) * 48 + (z * 2 + c) * 6
                    order[place : place + 6] = 6 * device + np.arange(6)
    return order


def _spread():
    spread = np.zeros((EMB, EMB), np.float32)
    spread[_order(), np.arange(EMB)] = 1.0
    return spread


def _line_pick():
    pick = np.zeros((96, 128), np.float32)
    for member in range(8):
        for r in range(6):
            pick[member * 6 + r, member * 16 + r] = 1.0
            pick[48 + member * 6 + r, member * 16 + 8 + r] = 1.0
    return pick


def _plane_pick():
    pick = np.zeros((432, 512), np.float32)
    for member in range(16):
        for r in range(6):
            pick[member * 6 + r, member * 32 + r] = 1.0
        for r in range(21):
            pick[96 + member * 21 + r, member * 32 + 8 + r] = 1.0
    return pick


def rem4(value):
    return lax.rem(value, 4)


class Place:
    def __init__(self):
        dp, fs = lax.axis_index("dp"), lax.axis_index("fsdp")
        self.z, self.xlo = lax.div(dp, 2), lax.rem(dp, 2)
        self.y, self.xhi = lax.div(fs, 4), lax.rem(lax.div(fs, 2), 2)
        self.c = lax.rem(fs, 2)
        self.x = self.xhi * 2 + self.xlo

    def device(self, z, y, x, c):
        return (z * 2 + lax.rem(x, 2), y * 4 + lax.div(x, 2) * 2 + c)

    def sibling(self):
        return self.device(self.z, self.y, self.x, 1 - self.c)

    def up(self, k):
        return self.device(rem4(self.z + k), self.y, self.x, self.c)

    def line(self, k):
        z = rem4(self.z + k // 2)
        core = self.c if k % 2 == 0 else 1 - self.c
        return self.device(z, self.y, self.x, core), z * 2 + core, core

    def turn(self, q, sibling=False):
        return 1 if q == "C" else (1 - self.c if sibling else self.c)

    def first(self, q, k):
        t = self.turn(q)
        y, x = rem4(self.y + k * (1 - t)), rem4(self.x + k * t)
        return self.device(self.z, y, x, self.c)

    def last(self, q, k):
        t = self.turn(q)
        y, x = rem4(self.y + k * t), rem4(self.x + k * (1 - t))
        return self.device(self.z, y, x, self.c)

    def band(self, q, m, k, sibling=False):
        t = self.turn(q, sibling)
        x = rem4(self.x + m * t + k * (1 - t))
        y = rem4(self.y + m * (1 - t) + k * t)
        return rows(48 * (x * 4 + y), 48)

    def across(self, k):
        return self.device(self.z, self.y, rem4(self.x + k), self.c)

    def side(self, k):
        return self.device(self.z, rem4(self.y + k), self.x, self.c)

    def twin(self):
        return self.device(self.z, self.y, self.xhi * 2 + 1 - self.xlo, self.c)

    def pair(self):
        return self.across(2)

    def order(self, m, k):
        return rem4(self.z + k) * 2 + (self.xlo if m == 0 else 1 - self.xlo)

    def greet(self):
        mates = [self.line(k)[0] for k in range(1, 8)]
        mates += [self.across(k) for k in (1, 2, 3)]
        mates += [self.side(k) for k in (1, 2, 3)]
        barrier = pltpu.get_barrier_semaphore()
        for mate in mates:
            pl.semaphore_signal(barrier, inc=1, device_id=mate, device_id_type=MESH)
        return lambda: pl.semaphore_wait(barrier, len(mates))


class Sender:
    def __init__(self, send_sems, recv_sems):
        self.send_sems, self.recv_sems = send_sems, recv_sems
        self.sends = self.arrivals = 0
        self.open = []
        self.groups = {}

    def send(self, source, target, device, group=None):
        index = self.sends % SENDS
        if len(self.open) >= SENDS:
            self.open.pop(0).wait_send()
        self.sends += 1
        if group not in self.groups:
            self.groups[group if group is not None else self.sends] = self.arrivals
            arrival = self.arrivals
            self.arrivals += 1
        else:
            arrival = self.groups[group]
        copy = pltpu.make_async_remote_copy(
            src_ref=source,
            dst_ref=target,
            send_sem=self.send_sems.at[index],
            recv_sem=self.recv_sems.at[arrival],
            device_id=device,
            device_id_type=MESH,
        )
        copy.start()
        self.open.append(copy)
        return copy

    def wait_group(self, group, like, device):
        pltpu.make_async_remote_copy(
            src_ref=like,
            dst_ref=like,
            send_sem=self.send_sems.at[0],
            recv_sem=self.recv_sems.at[self.groups[group]],
            device_id=device,
            device_id_type=MESH,
        ).wait_recv()

    def drain(self, until=None):
        keep = 0 if until is None else self.sends - until
        while len(self.open) > keep:
            self.open.pop(0).wait_send()


def rows(start, size, unit=16):
    return pl.ds(pl.multiple_of(start, unit), size)


def mm(left, right):
    return jnp.dot(left, right, preferred_element_type=F32)


def mm_t(left, right):
    return lax.dot_general(left, right, (((1,), (1,)), ((), ())), preferred_element_type=F32)


def t_mm(left, right):
    return lax.dot_general(left, right, (((0,), (0,)), ((), ())), preferred_element_type=F32)


def split(value, parts):
    found = []
    for _ in range(parts - 1):
        high = value.astype(BF)
        found.append(high)
        value = value - high.astype(F32)
    found.append(value.astype(BF))
    return found


def fine(dims, left, right):
    lh, ll = split(left, 2)
    rh, rl = split(right, 2)
    dot = partial(lax.dot_general, dimension_numbers=(dims, ((), ())), preferred_element_type=F32)
    return dot(lh, rh) + (dot(lh, rl) + dot(ll, rh))


NN, NT, TN = ((1,), (0,)), ((1,), (1,)), ((0,), (0,))


def wide(ref):
    return ref[...].astype(F32)


def layer_kernel(
    x_in, up_in, state, spread_in, pick_n_in, pick_z_in, turn_n_in, turn_z_in, *refs
):
    vecs, refs = refs[:14], refs[14:]
    (acceptor, address, content, sigmoid, mixer, ff_address, ff_content, ff_acceptor), refs = refs[:8], refs[8:]
    (
        out_ref, in_grad_ref, end_n, end_z,
        x_ref, up_ref, state_v, spread, pick_n, pick_z, turn_n, turn_z, memory,
        wa, wb, wc, wo, w2, gk, gb, gc, scores,
        vec_f, pack_f, pack_n, stage_a, stage_b, cols_f, pack_z, half_z, pair_z, stage_z,
        sib_r, sib_k, sib_b, sib_c, relay_r, relay_k, relay_b, relay_c,
        last_r, last_k, last_b, last_c, first_r, first_k, first_b, first_c,
        acc_r, acc_k, acc_b, acc_c,
        piece_a, piece_b, line_a, line_b,
        sib_o, sib_2, relay_o, relay_2, up_o, up_2, sent_o, sent_2, twin_o, twin_2,
        piece_z, side_z, half_f, sent_z, got_z, swap_f,
        send_sems, recv_sems, load_sems,
    ) = refs
    at = Place()
    c = at.c
    sib = at.sibling()
    net = Sender(send_sems, recv_sems)
    met = at.greet()

    loads = {}
    for i, (name, source, target) in enumerate([
        ("spread", spread_in, spread), ("x", x_in, x_ref), ("pick_n", pick_n_in, pick_n),
        ("up", up_in, up_ref), ("pick_z", pick_z_in, pick_z), ("state", state, state_v),
        ("turn_n", turn_n_in, turn_n), ("turn_z", turn_z_in, turn_z),
    ]):
        loads[name] = pltpu.make_async_copy(source, target, load_sems.at[i])
        loads[name].start()

    vec_f[...] = jnp.zeros_like(vec_f)
    for i, ref in enumerate(vecs):
        vec_f[i : i + 1, 0:6] = wide(ref).reshape(1, 6)
    eye = (
        lax.broadcasted_iota(jnp.int32, (16, 128), 0)
        == lax.broadcasted_iota(jnp.int32, (16, 128), 1)
    ).astype(F32).astype(BF)
    pack_f[...] = jnp.zeros_like(pack_f)
    pack_f[0, 0, 0:6, 0:768] = wide(acceptor)
    pack_f[0, 0, 0:6, 768:896] = wide(address.at[:, 0:128])
    pack_f[0, 0, 8:14, 0:640] = wide(address.at[:, 128:768])
    pack_f[0, 0, 8:14, 640:768] = wide(ff_address.at[:, 0:128])
    pack_f[1, 0, 0:6, 0:768] = wide(content)
    pack_f[1, 0, 0:6, 768:896] = wide(sigmoid.at[:, 0:128])
    pack_f[1, 0, 8:14, 0:640] = wide(sigmoid.at[:, 128:768])
    pack_f[1, 0, 8:14, 640:768] = mm_t(eye, vec_f[...].astype(BF))[0:6]
    for h in range(2):
        pack_n[0, h] = pack_f[h, 0].astype(BF)
    met()

    own = at.z * 2 + c

    def send_lines(i, stage):
        for k in range(1, 8):
            mate, _, core = at.line(k)
            net.send(pack_n.at[i, core], stage.at[own], mate, ("lines", i))
        stage[own] = pack_n[i, c]

    send_lines(0, stage_a)
    cols_f[...] = jnp.zeros_like(cols_f)
    cols_f[0:6] = wide(mixer)
    cols_f[8:29] = wide(ff_content)
    cols_f[32:38] = wide(ff_acceptor)
    loads["spread"].wait()
    moved = mm(cols_f[...].astype(BF), spread[...])
    for h in range(2):
        pack_z[h] = moved[0:32, COLS * h : COLS * h + COLS].astype(BF)
        first_col = 128 + 1280 * h
        pack_f[h, 1, 0:6, 0:896] = wide(ff_address.at[:, first_col : first_col + 896])
        pack_f[h, 1, 8:14, 0:384] = wide(ff_address.at[:, first_col + 896 : first_col + 1280])
        pack_f[h, 1, 8:16, 384:768] = moved[32:40, COLS * h : COLS * h + COLS]
        pack_n[1, h] = pack_f[h, 1].astype(BF)
    swap_z = net.send(pack_z.at[1 - c], half_z.at[c], sib)
    half_z[c] = pack_z[c]
    send_lines(1, stage_b)

    loads["x"].wait()
    tokens = mm(x_ref[...], spread[...])
    centred = tokens - jnp.mean(tokens, axis=-1, keepdims=True)
    scale1 = lax.rsqrt(jnp.mean(centred * centred, axis=-1, keepdims=True) + NORM_EPS)
    unit1 = centred * scale1
    loads["up"].wait()
    upstream = mm(up_ref[...], spread[...])
    swap_z.wait_recv()
    to_pair = net.send(half_z, pair_z.at[at.xhi], at.pair())
    pair_z[at.xhi] = half_z[...]
    loads["pick_n"].wait()
    for name in ("state", "turn_n", "turn_z", "pick_z"):
        loads[name].wait()
    blank = jnp.zeros((64, 64), F32)
    for g in range(6):
        memory[g, 0:64] = jnp.concatenate([state_v[2 * g], blank], axis=1)
        memory[g, 64:128] = jnp.concatenate([blank, state_v[2 * g + 1]], axis=1)

    def pick(i, stage):
        net.wait_group(("lines", i), stage.at[0:7], sib)
        return mm(pick_n[...], stage[...].reshape(128, LEFT)).astype(BF)

    full = {"A": wa, "B": wb, "C": wc, "o": wo, "2": w2}

    def place_n(q, m, k):
        return full[q].at[c, at.band(q, m, k)]

    firsts, lasts = {}, {}

    def pass_on(q, m):
        spot = place_n(q, 4 - m, 0)
        for k in (1, 3):
            lasts[q, m, k] = net.send(spot, spot, at.last(q, k))
        net.send(spot, spot, sib, ("sib", q))

    def begin(q, *parts):
        spot = place_n(q, 0, 0)
        spot[...] = jnp.concatenate(parts, axis=1) if len(parts) > 1 else parts[0]
        for k in (1, 3, 2):
            firsts[q, k] = net.send(spot, spot, at.first(q, k))
        pass_on(q, 0)

    def relay(q, m):
        firsts[q, m].wait_recv()
        pass_on(q, m)

    def arrive(q, m, k):
        lasts[q, m, k].wait_recv()
        spot = place_n(q, 4 - m, 4 - k)
        if k == (1 if m % 2 == 0 else 3):
            lasts[q, m, 2] = net.send(spot, spot, at.last(q, k))
        net.send(spot, spot, sib, ("sib", q))

    def arrive_far(q, m):
        lasts[q, m, 2].wait_recv()
        spot = place_n(q, 4 - m, 2)
        net.send(spot, spot, sib, ("sib", q))

    def place_z(w, m, k):
        unit = 96 if w == "o" else 336
        return full[w].at[c, rows(unit * at.order(m, k), unit)]

    def pass_z(w, m):
        spot = place_z(w, m, 0)
        for k in (1, 3):
            lasts[w, m, k] = net.send(spot, spot, at.up(k))
        net.send(spot, spot, sib, ("sib", w))

    def relay_z(w):
        firsts[w].wait_recv()
        pass_z(w, 1)

    def arrive_z(w, m, k):
        lasts[w, m, k].wait_recv()
        spot = place_z(w, m, 4 - k)
        if k == (1 if m == 0 else 3):
            lasts[w, m, 2] = net.send(spot, spot, at.up(k))
        net.send(spot, spot, sib, ("sib", w))

    def arrive_z_far(w, m):
        lasts[w, m, 2].wait_recv()
        spot = place_z(w, m, 2)
        net.send(spot, spot, sib, ("sib", w))

    picked = pick(0, stage_a)
    begin("A", picked[0:48], picked[48:96, 0:RIGHT])
    to_pair.wait_recv()
    for k in (1, 2, 3):
        net.send(pair_z, stage_z.at[at.y], at.side(k), "side")
    stage_z[at.y] = pair_z[...]
    relay("A", 1)
    relay("A", 3)
    for k in (1, 3):
        arrive("A", 0, k)
    picked = pick(1, stage_b)
    relay("A", 2)
    begin("B", picked[0:48], picked[48:96, 0:384])
    begin("C", picked[48:96, 384:768])
    net.wait_group("side", stage_z.at[0:3], sib)
    picked_z = mm(pick_z[...], stage_z[...].reshape(512, COLS)).astype(BF)
    place_z("o", 0, 0)[...] = picked_z[:96]
    place_z("2", 0, 0)[...] = picked_z[96:]
    for w in ("o", "2"):
        spot = place_z(w, 0, 0)
        firsts[w] = net.send(spot, spot, at.twin())
        pass_z(w, 0)
    for m in (1, 3):
        for k in (1, 3):
            arrive("A", m, k)
    arrive_far("A", 0)
    relay("B", 1)
    relay("B", 3)
    for k in (1, 3):
        arrive("A", 2, k)
    for w in ("o", "2"):
        relay_z(w)
    relay("B", 2)
    for m in (1, 3, 2):
        relay("C", m)
    for m in (1, 3, 2):
        arrive_far("A", m)
    tasks = []

    def plan(kind, *steps_):
        for step in steps_:
            tasks.append((kind, step))

    for m in (0, 1):
        for k in (1, 3):
            plan("B", partial(arrive, "B", m, k))
            plan("o", partial(arrive_z, "o", m, k))
            plan("2", partial(arrive_z, "2", m, k))
    for m in (0, 1):
        plan("o", partial(arrive_z_far, "o", m))
    for m in (3, 2):
        for k in (1, 3):
            plan("B", partial(arrive, "B", m, k))
    for m in ORDER:
        for k in (1, 3):
            plan("C", partial(arrive, "C", m, k))
    for m in (0, 1):
        plan("2", partial(arrive_z_far, "2", m))
    for q in ("B", "C"):
        for m in ORDER:
            plan(q, partial(arrive_far, q, m))

    def work(count=1000):
        for _ in range(min(count, len(tasks))):
            tasks.pop(0)[1]()

    def need(q):
        while any(kind == q for kind, _ in tasks):
            work(1)
        net.wait_group(("sib", q), full[q].at[1 - c], sib)

    need("A")

    lanes = lax.broadcasted_iota(jnp.int32, (1, 128), 1)
    left_head = lanes < 64
    token = lax.broadcasted_iota(jnp.int32, (TOK, 1), 0)

    def shift_down(value):
        return jnp.where(token == 0, 0.0, pltpu.roll(value, 1, 0))

    def shift_up(value):
        return jnp.where(token == TOK - 1, 0.0, pltpu.roll(value, TOK - 1, 0))

    def mean(value):
        return jnp.mean(value, axis=-1, keepdims=True)

    def tsum(value):
        return jnp.sum(value, axis=0, keepdims=True)

    def unspread(value):
        a, b, d = split(value, 3)
        return mm_t(a, spread[...]) + (mm_t(b, spread[...]) + mm_t(d, spread[...]))

    vec = mm_t(eye, wa[1, :, VEC:1664])
    gain1, bias1 = vec[0:1], vec[1:2]
    lerps = [vec[2 + i : 3 + i] for i in range(4)]
    gain2, bias2, lerp_h, lerp_g = vec[6:7], vec[7:8], vec[8:9], vec[9:10]
    heads = mm_t(vec.astype(BF), spread[...])
    rate, bonus, gain_w, bias_w = heads[10:11], heads[11:12], heads[12:13], heads[13:14]

    pair_rows = lax.broadcasted_iota(jnp.int32, (256, 128), 0)
    pair_cols = lax.broadcasted_iota(jnp.int32, (256, 128), 1)
    pair_ones = ((lax.rem(pair_rows, 128) // 64) == (pair_cols // 64)).astype(F32).astype(BF)
    below = lax.rem(pair_rows, 128) > pair_cols

    def head_sum(value):
        found = []
        for g in range(6):
            part = value[:, 128 * g : 128 * g + 128]
            found.append(mm(jnp.concatenate(split(part, 2), axis=1), pair_ones))
        return jnp.concatenate(found, axis=1)

    def stack(value):
        return jnp.concatenate(
            [jnp.where(left_head, value, 0.0), jnp.where(left_head, 0.0, value)], axis=0
        )

    def beside(value):
        return jnp.concatenate([value[:TOK], value[TOK:]], axis=1)

    normed = unit1 * gain1 + bias1
    previous = shift_down(normed)
    blended = [(normed * l + previous * (1.0 - l)).astype(BF) for l in lerps]
    recept = mm(blended[0], wa[0, :, 0:768])
    keys = mm(blended[1], wa[0, :, 768:1536])
    vals = mm(blended[2], wa[1, :, 0:768])
    gate_pre = mm(blended[3], wa[1, :, 768:1536])
    work(6)

    fade = -jnp.exp(rate)
    steps = token.astype(F32)
    fall_r = jnp.exp(steps * fade)
    fall_k = jnp.exp(-(steps + 1.0) * fade)
    recept_f = recept * fall_r
    keys_f = keys * fall_k
    present = head_sum(recept * bonus * keys)
    parts = []
    for g in range(6):
        cut = slice(128 * g, 128 * g + 128)
        rg, kg, vg = recept_f[:, cut], keys_f[:, cut], vals[:, cut]
        sc = jnp.where(below, fine(NT, stack(rg), kg), 0.0)
        scores[g] = sc
        parts.append(fine(NN, beside(sc), stack(vg)) + fine(NN, rg, memory[g]))
        if g % 2 == 1:
            work(4)
    wkv = jnp.concatenate(parts, axis=1) + present * vals

    centred_w = wkv - head_sum(wkv) * (1.0 / 64.0)
    scale_w = lax.rsqrt(head_sum(centred_w * centred_w) * (1.0 / 64.0) + GROUP_EPS)
    unit_w = centred_w * scale_w
    grouped = unit_w * gain_w + bias_w
    sig = 1.0 / (1.0 + jnp.exp(-gate_pre))
    silu = gate_pre * sig
    gated = (grouped * silu).astype(BF)
    need("o")
    middle = tokens + jnp.concatenate([mm(gated, wo[0]), mm(gated, wo[1])], axis=1)

    centred = middle - mean(middle)
    scale2 = lax.rsqrt(mean(centred * centred) + NORM_EPS)
    unit2 = centred * scale2
    normed2 = unit2 * gain2 + bias2
    previous2 = shift_down(normed2)
    mixed_h = (normed2 * lerp_h + previous2 * (1.0 - lerp_h)).astype(BF)
    mixed_g = (normed2 * lerp_g + previous2 * (1.0 - lerp_g)).astype(BF)
    need("B")
    need("C")
    pre = jnp.concatenate(
        [mm(mixed_h, wa[0, :, 1536:1664]), mm(mixed_h, wb[0]), mm(mixed_h, wb[1])], axis=1
    )
    pre = jnp.maximum(pre, 0.0)
    hidden = (pre * pre).astype(BF)
    gating = jnp.concatenate([mm(mixed_g, wc[0]), mm(mixed_g, wc[1])], axis=1)
    gating = 1.0 / (1.0 + jnp.exp(-gating))
    grad_vo = upstream * gating
    grad_vo_low = grad_vo.astype(BF)
    swaps = {}

    def fold(mine, other, *more):
        total = wide(mine) + wide(other)
        for ref in more:
            total += wide(ref)
        return total

    gr, go = wb.at[:, :, 0:768], wb.at[:, :, 768:1152]
    grads = {"R": gr, "K": gk, "B": gb, "C": gc}
    sib_of = {"R": sib_r, "K": sib_k, "B": sib_b, "C": sib_c}
    relay_of = {"R": relay_r, "K": relay_k, "B": relay_b, "C": relay_c}
    last_of = {"R": last_r, "K": last_k, "B": last_b, "C": last_c}
    first_of = {"R": first_r, "K": first_k, "B": first_b, "C": first_c}
    acc_of = {"R": acc_r, "K": acc_k, "B": acc_b, "C": acc_c}

    def swap(q):
        swaps[q] = net.send(grads[q].at[1 - c], sib_of[q], sib)

    def swapped(q):
        if q in swaps:
            swaps.pop(q).wait_recv()

    def scatter_far(q, m):
        part = at.band(q, m, 2)
        via = 1 if m % 2 == 0 else 3
        swapped(q)
        spot = sib_of[q].at[part]
        spot[...] = fold(grads[q].at[c, part], spot).astype(BF)
        lasts["g", q, m, 2] = net.send(spot, relay_of[q].at[m], at.last(q, via))

    def scatter_near(q, m, k):
        part = at.band(q, m, k)
        spot = sib_of[q].at[part]
        more = []
        if k == (1 if m % 2 == 0 else 3):
            lasts["g", q, m, 2].wait_recv()
            more = [relay_of[q].at[m]]
        spot[...] = fold(grads[q].at[c, part], spot, *more).astype(BF)
        lasts["g", q, m, k] = net.send(spot, last_of[q].at[k // 2, m], at.last(q, k))

    def scatter_own(q, m):
        part = at.band(q, m, 0)
        spot = sib_of[q].at[part]
        lasts["g", q, m, 1].wait_recv()
        lasts["g", q, m, 3].wait_recv()
        arrived = last_of[q]
        total = fold(grads[q].at[c, part], spot, arrived.at[0, m], arrived.at[1, m])
        if m == 0:
            acc_of[q][...] = total
        else:
            spot[...] = total.astype(BF)
            firsts["g", q, m] = net.send(spot, first_of[q].at[m - 1], at.first(q, m))

    def scatter_end(q):
        total = acc_of[q][...]
        for m in (1, 3, 2):
            firsts["g", q, m].wait_recv()
            total += wide(first_of[q].at[m - 1])
        acc_of[q][...] = total

    def spread_lines(i, left, right, piece, line):
        right = jnp.concatenate([right, jnp.zeros((48, LEFT - RIGHT), F32)], axis=1)
        table = jnp.concatenate([left, right], axis=0).astype(BF)
        piece[...] = mm(turn_n[...], table).astype(BF).reshape(8, 16, LEFT)
        for k in range(1, 8):
            mate, index, _ = at.line(k)
            net.send(piece.at[index], line.at[own], mate, ("grad lines", i))
        line[own] = piece[own]

    def sum_lines(i, line):
        net.wait_group(("grad lines", i), line.at[0:7], sib)
        for h in range(2):
            total = wide(line.at[h])
            for z in (1, 2, 3):
                total += wide(line.at[2 * z + h])
            end_n[h, i] = total

    def scatter_steps(q):
        steps_ = [partial(scatter_far, q, m) for m in ORDER]
        for late in (False, True):
            for m in ORDER:
                for k in (1, 3):
                    if late == (k == (1 if m % 2 == 0 else 3)):
                        steps_.append(partial(scatter_near, q, m, k))
        steps_ += [partial(scatter_own, q, m) for m in (1, 3, 2, 0)]
        steps_.append(partial(scatter_end, q))
        return steps_

    z_parts = {
        "o": (96, go, sib_o, relay_o, up_o, sent_o, twin_o),
        "2": (336, w2, sib_2, relay_2, up_2, sent_2, twin_2),
    }

    def swap_w(w):
        unit, mine, theirs = z_parts[w][:3]
        swaps[w] = net.send(mine.at[1 - c], theirs, sib)

    def part_w(w, m, k):
        unit = z_parts[w][0]
        return rows(unit * at.order(m, k), unit)

    def scatter_far_w(w, m):
        unit, mine, theirs, relayed = z_parts[w][:4]
        part = part_w(w, m, 2)
        swapped(w)
        spot = theirs.at[part]
        spot[...] = fold(mine.at[c, part], spot).astype(BF)
        lasts["g", w, m, 2] = net.send(spot, relayed.at[m], at.up(1 if m == 0 else 3))

    def scatter_near_w(w, m, k):
        unit, mine, theirs, relayed, arrived = z_parts[w][:5]
        part = part_w(w, m, k)
        more = []
        if k == (1 if m == 0 else 3):
            lasts["g", w, m, 2].wait_recv()
            more = [relayed.at[m]]
        spot = theirs.at[part]
        spot[...] = fold(mine.at[c, part], spot, *more).astype(BF)
        lasts["g", w, m, k] = net.send(spot, arrived.at[k // 2, m], at.up(k))

    def scatter_own_w(w, m):
        unit, mine, theirs, relayed, arrived, sent, twin = z_parts[w]
        part = part_w(w, m, 0)
        lasts["g", w, m, 1].wait_recv()
        lasts["g", w, m, 3].wait_recv()
        total = fold(mine.at[c, part], theirs.at[part], arrived.at[0, m], arrived.at[1, m])
        if m == 1:
            sent[...] = total.astype(BF)
            firsts["g", w] = net.send(sent, twin, at.twin())
        else:
            firsts["g", w].wait_recv()
            sums_z[w] = (total + wide(twin)).astype(BF)

    def scatter_steps_w(w):
        steps_ = [partial(scatter_far_w, w, 0), partial(scatter_far_w, w, 1)]
        steps_ += [partial(scatter_near_w, w, 1, 1), partial(scatter_near_w, w, 0, 3)]
        steps_ += [partial(scatter_near_w, w, 0, 1), partial(scatter_near_w, w, 1, 3)]
        steps_ += [partial(scatter_own_w, w, 1), partial(scatter_own_w, w, 0)]
        return steps_

    sums_z = {}

    need("2")
    gathered = net.sends
    steps_2, steps_o = scatter_steps_w("2"), scatter_steps_w("o")
    steps_b, steps_c = scatter_steps("B"), scatter_steps("C")
    steps_r, steps_k = scatter_steps("R"), scatter_steps("K")

    def run(*steps_):
        for step in steps_:
            step()

    grad_hidden = mm_t(grad_vo_low[:, :COLS], w2[0]) + mm_t(grad_vo_low[:, COLS:], w2[1])
    grad_pre = (grad_hidden * 2.0 * pre).astype(BF)
    gb[0] = t_mm(mixed_h, grad_pre[:, 128:1408]).astype(BF)
    gb[1] = t_mm(mixed_h, grad_pre[:, 1408:]).astype(BF)
    swap("B")
    value_out = jnp.concatenate([mm(hidden, w2[0]), mm(hidden, w2[1])], axis=1)
    layer_out = middle + gating * value_out
    run(*steps_b[:8])
    net.drain(gathered)
    for h in range(2):
        w2[h] = t_mm(hidden, grad_vo_low[:, COLS * h : COLS * h + COLS]).astype(BF)
    swap_w("2")
    grad_gp = (grad_vo * value_out * (1.0 - gating)).astype(BF)
    for h in range(2):
        gc[h] = t_mm(mixed_g, grad_gp[:, COLS * h : COLS * h + COLS]).astype(BF)
    swap("C")
    grad_mg = mm_t(grad_gp[:, :COLS], wc[0]) + mm_t(grad_gp[:, COLS:], wc[1])
    grad_mh = mm_t(grad_pre[:, :128], wa[0, :, 1536:1664])
    grad_mh += mm_t(grad_pre[:, 128:1408], wb[0]) + mm_t(grad_pre[:, 1408:], wb[1])
    gk[0, :, 768:896] = t_mm(mixed_h, grad_pre[:, :128]).astype(BF)
    run(*steps_2[:4])
    run(*steps_c[:8])

    grad_n2 = grad_mh * lerp_h + grad_mg * lerp_g
    grad_n2 += shift_up(grad_mh * (1.0 - lerp_h) + grad_mg * (1.0 - lerp_g))
    delta2 = normed2 - previous2
    g_lerp_h, g_lerp_g = tsum(grad_mh * delta2), tsum(grad_mg * delta2)
    g_gain2, g_bias2 = tsum(grad_n2 * unit2), tsum(grad_n2)
    q2 = grad_n2 * gain2
    grad_middle = upstream + scale2 * (q2 - mean(q2) - unit2 * mean(q2 * unit2))

    grad_attn = grad_middle.astype(BF)
    grad_gated = mm_t(grad_attn[:, :COLS], wo[0]) + mm_t(grad_attn[:, COLS:], wo[1])
    for h in range(2):
        go[h] = t_mm(gated, grad_attn[:, COLS * h : COLS * h + COLS]).astype(BF)
    swap_w("o")
    grad_gate = (grad_gated * grouped * (sig * (1.0 + gate_pre * (1.0 - sig)))).astype(BF)
    grad_grouped = grad_gated * silu
    g_gain_w, g_bias_w = tsum(grad_grouped * unit_w), tsum(grad_grouped)
    qw = grad_grouped * gain_w
    grad_wkv = scale_w * (
        qw
        - head_sum(qw) * (1.0 / 64.0)
        - unit_w * (head_sum(qw * unit_w) * (1.0 / 64.0))
    )

    weight = head_sum(grad_wkv * vals)
    parts_r, parts_k, parts_v = [], [], []
    for g in range(6):
        cut = slice(128 * g, 128 * g + 128)
        rg, kg, vg, dg = recept_f[:, cut], keys_f[:, cut], vals[:, cut], grad_wkv[:, cut]
        ds = stack(dg)
        da = jnp.where(below, fine(NT, ds, vg), 0.0)
        parts_r.append(fine(NN, beside(da), stack(kg)) + fine(NT, dg, memory[g]))
        parts_k.append(fine(TN, da, stack(rg)))
        parts_v.append(fine(TN, scores[g], ds))
        if g == 2:
            run(*steps_o[:4])
        if g == 4:
            run(*steps_b[8:12])
    grad_r = jnp.concatenate(parts_r, axis=1) * fall_r
    grad_k = jnp.concatenate(parts_k, axis=1) * fall_k
    grad_v = jnp.concatenate(parts_v, axis=1) + grad_wkv * present
    g_rate = fade * tsum(steps * recept * grad_r - (steps + 1.0) * keys * grad_k)
    g_bonus = tsum(recept * keys * weight)
    grad_r = (grad_r + bonus * keys * weight).astype(BF)
    grad_k = (grad_k + bonus * recept * weight).astype(BF)
    grad_v = grad_v.astype(BF)

    gr[0] = t_mm(blended[0], grad_r).astype(BF)
    gr[1] = t_mm(blended[2], grad_v).astype(BF)
    swap("R")
    gk[0, :, 0:768] = t_mm(blended[1], grad_k).astype(BF)
    gk[1, :, 0:768] = t_mm(blended[3], grad_gate).astype(BF)
    grad_blended = [
        mm_t(grad_r, wa[0, :, 0:768]),
        mm_t(grad_k, wa[0, :, 768:1536]),
        mm_t(grad_v, wa[1, :, 0:768]),
        mm_t(grad_gate, wa[1, :, 768:1536]),
    ]
    run(*steps_2[4:6], *steps_r[:8])
    delta = normed - previous
    g_lerps = [tsum(g * delta) for g in grad_blended]
    grad_n1 = sum(g * l for g, l in zip(grad_blended, lerps))
    grad_n1 += shift_up(sum(g * (1.0 - l) for g, l in zip(grad_blended, lerps)))
    g_gain1, g_bias1 = tsum(grad_n1 * unit1), tsum(grad_n1)

    zero = jnp.zeros((1, EMB), F32)
    natural = jnp.concatenate([g_rate, g_bonus, g_gain_w, g_bias_w] + [zero] * 4, axis=0)
    va, vb, vc = split(natural, 3)
    moved = mm(va, spread[...]) + (mm(vb, spread[...]) + mm(vc, spread[...]))
    table = jnp.concatenate(
        [g_gain1, g_bias1] + g_lerps + [g_gain2, g_bias2, g_lerp_h, g_lerp_g]
        + [moved[0:4], jnp.zeros((114, EMB), F32)],
        axis=0,
    )
    gk[1, :, 768:896] = table.T.astype(BF)
    swap("K")
    run(*steps_c[8:12], *steps_b[12:16], *steps_k[:8], *steps_o[4:6], *steps_r[8:12])
    out_ref[...] = unspread(layer_out)
    run(steps_2[6], steps_o[6], *steps_k[8:12], steps_b[16], *steps_c[12:16])
    q1 = grad_n1 * gain1
    grad_x = grad_middle + scale1 * (q1 - mean(q1) - unit1 * mean(q1 * unit1))
    in_grad_ref[...] = unspread(grad_x)
    run(*steps_r[12:16], *steps_k[12:16])

    run(steps_2[7], steps_o[7])
    spread_z = mm(turn_z[:, :96], sums_z["o"]) + mm(turn_z[:, 96:], sums_z["2"])
    piece_z[...] = spread_z.astype(BF).reshape(4, 128, COLS)
    for k in (1, 2, 3):
        net.send(piece_z.at[rem4(at.y + k)], side_z.at[k - 1], at.side(k), "grad side")
    run(steps_c[16])
    spread_lines(
        1, acc_b[:, 0:LEFT], jnp.concatenate([acc_b[:, LEFT:], acc_c[...]], axis=1), piece_b, line_b
    )
    run(steps_r[16], steps_k[16])
    acc_a = jnp.concatenate([acc_r[...], acc_k[...]], axis=1)
    spread_lines(0, acc_a[:, 0:LEFT], acc_a[:, LEFT:], piece_a, line_a)
    net.wait_group("grad side", side_z, sib)
    total = wide(piece_z.at[at.y])
    for k in (1, 2, 3):
        total += wide(side_z.at[k - 1])
    half_f[...] = total.reshape(2, 64, COLS)
    sent_z[...] = half_f[1 - at.xhi].astype(BF)
    to_pair = net.send(sent_z, got_z, at.pair())
    sum_lines(1, line_b)
    to_pair.wait_recv()
    swap_f[...] = half_f[at.xhi] + wide(got_z)
    away, kept = rows(32 * (1 - c), 32, 8), rows(32 * c, 32, 8)
    last_swap = net.send(swap_f.at[away], end_z.at[c], sib)
    end_z[c] = swap_f[kept]
    last_swap.wait_recv()
    sum_lines(0, line_a)
    net.drain()


def layer(*operands):
    bf = lambda *shape: pltpu.VMEM(shape, BF)
    f32 = lambda *shape: pltpu.VMEM(shape, F32)
    a, b, d, r, k = (WIDTH[q] for q in "ABCRK")
    return pl.pallas_call(
        layer_kernel,
        out_shape=(
            jax.ShapeDtypeStruct((TOK, EMB), F32),
            jax.ShapeDtypeStruct((TOK, EMB), F32),
            jax.ShapeDtypeStruct((2, 2, 16, LEFT), F32),
            jax.ShapeDtypeStruct((2, 32, COLS), F32),
        ),
        in_specs=[pl.BlockSpec(memory_space=pl.ANY)] * 8 + [VMEM] * (len(operands) - 8),
        out_specs=(VMEM,) * 4,
        scratch_shapes=[
            bf(TOK, EMB), bf(TOK, EMB), f32(12, 64, 64), bf(EMB, EMB),
            bf(96, 128), bf(432, 512), bf(128, 96), bf(512, 432), f32(6, 128, 128),
            bf(2, EMB, a), bf(2, EMB, b), bf(2, EMB, d), bf(2, EMB, COLS), bf(2, FF, COLS),
            bf(2, EMB, k), bf(2, EMB, b), bf(2, EMB, d), f32(6, 256, 128),
            f32(128, 128), f32(2, 2, 16, LEFT), bf(2, 2, 16, LEFT), bf(8, 16, LEFT), bf(8, 16, LEFT),
            f32(48, EMB), bf(2, 32, COLS), bf(2, 32, COLS), bf(2, 2, 32, COLS), bf(4, 2, 2, 32, COLS),
            *(bf(EMB, w) for w in (r, k, b, d)), *(bf(4, 48, w) for w in (r, k, b, d)),
            *(bf(2, 4, 48, w) for w in (r, k, b, d)), *(bf(3, 48, w) for w in (r, k, b, d)),
            *(f32(48, w) for w in (r, k, b, d)),
            bf(8, 16, LEFT), bf(8, 16, LEFT), bf(8, 16, LEFT), bf(8, 16, LEFT),
            bf(EMB, COLS), bf(FF, COLS),
            bf(2, 96, COLS), bf(2, 336, COLS), bf(2, 2, 96, COLS), bf(2, 2, 336, COLS),
            bf(96, COLS), bf(336, COLS), bf(96, COLS), bf(336, COLS),
            bf(4, 128, COLS), bf(3, 128, COLS), f32(2, 64, COLS), bf(64, COLS), bf(64, COLS),
            f32(64, COLS),
            pltpu.SemaphoreType.DMA((SENDS,)),
            pltpu.SemaphoreType.DMA((ARRIVALS,)),
            pltpu.SemaphoreType.DMA((8,)),
        ],
        compiler_params=pltpu.CompilerParams(
            collective_id=1, has_side_effects=True, vmem_limit_bytes=62 << 20
        ),
        cost_estimate=pl.CostEstimate(
            flops=6 * TOK * 7667712, bytes_accessed=4 * 7667712, transcendentals=10 * TOK * EMB
        ),
        name="layer",
    )(*operands)


def finish_kernel(end_n, end_z, spread, out_in, grad_in, out, grad, *refs):
    vecs, mats = refs[:14], refs[14:]
    acceptor, address, content, sigmoid, mixer, ff_address, ff_content, ff_acceptor = mats
    out[...] = out_in[...]
    grad[...] = grad_in[...]
    acceptor[...] = end_n[0, 0, 0:6, 0:768]
    address[:, 0:128] = end_n[0, 0, 0:6, 768:896]
    address[:, 128:768] = end_n[0, 0, 8:14, 0:640]
    content[...] = end_n[1, 0, 0:6, 0:768]
    sigmoid[:, 0:128] = end_n[1, 0, 0:6, 768:896]
    sigmoid[:, 128:768] = end_n[1, 0, 8:14, 0:640]
    ff_address[:, 0:128] = end_n[0, 0, 8:14, 640:768]
    for h in range(2):
        first_col = 128 + 1280 * h
        ff_address[:, first_col : first_col + 896] = end_n[h, 1, 0:6, 0:896]
        ff_address[:, first_col + 896 : first_col + 1280] = end_n[h, 1, 8:14, 0:384]
    table = jnp.concatenate([end_n[1, 0, 8:16, 640:768], jnp.zeros((120, 128), F32)], axis=0).T
    for i, ref in enumerate(vecs):
        ref[...] = table[i : i + 1, 0:6].reshape(6)
    columns = jnp.concatenate(
        [
            jnp.concatenate([end_z[0], end_z[1]], axis=1),
            jnp.concatenate([end_n[0, 1, 8:16, 384:768], end_n[1, 1, 8:16, 384:768]], axis=1),
        ],
        axis=0,
    )
    a, b, d = split(columns, 3)
    moved = mm_t(a, spread[...]) + (mm_t(b, spread[...]) + mm_t(d, spread[...]))
    mixer[...] = moved[0:6]
    ff_content[...] = moved[8:29]
    ff_acceptor[...] = moved[32:38]


def finish(end_n, end_z, spread, out, grad):
    shapes = [(TOK, EMB), (TOK, EMB)] + [(6,)] * 14
    shapes += [(6, EMB)] * 5 + [(6, FF), (21, EMB), (6, EMB)]
    return pl.pallas_call(
        finish_kernel,
        out_shape=tuple(jax.ShapeDtypeStruct(shape, F32) for shape in shapes),
        in_specs=[VMEM] * 5,
        out_specs=(VMEM,) * len(shapes),
        name="finish",
    )(end_n, end_z, spread, out, grad)


def per_device(
    incoming_activations,
    sequence_opening_memory,
    prior_standardize_factor,
    prior_standardize_offset,
    acceptor_lerp_factor,
    address_lerp_factor,
    content_lerp_factor,
    sigmoid_lerp_factor,
    acceptor_matrix,
    address_matrix,
    content_matrix,
    sigmoid_matrix,
    lane_fading_exponent,
    present_reward_vector,
    cluster_standardize_factor,
    cluster_standardize_offset,
    mixer_result_matrix,
    latter_standardize_factor,
    latter_standardize_offset,
    feedforward_address_lerp,
    feedforward_sigmoid_lerp,
    feedforward_address_matrix,
    feedforward_content_matrix,
    feedforward_acceptor_matrix,
    upstream_derivative,
):
    spread = jnp.asarray(_spread(), BF)
    out, in_grad, end_n, end_z = layer(
        incoming_activations, upstream_derivative,
        sequence_opening_memory.reshape(12, 64, 64), spread,
        jnp.asarray(_line_pick(), BF), jnp.asarray(_plane_pick(), BF),
        jnp.asarray(_line_pick().T, BF), jnp.asarray(_plane_pick().T, BF),
        prior_standardize_factor, prior_standardize_offset, acceptor_lerp_factor,
        address_lerp_factor, content_lerp_factor, sigmoid_lerp_factor,
        latter_standardize_factor, latter_standardize_offset, feedforward_address_lerp,
        feedforward_sigmoid_lerp, lane_fading_exponent, present_reward_vector,
        cluster_standardize_factor, cluster_standardize_offset,
        acceptor_matrix, address_matrix, content_matrix, sigmoid_matrix,
        mixer_result_matrix, feedforward_address_matrix, feedforward_content_matrix,
        feedforward_acceptor_matrix,
    )
    results = finish(end_n, end_z, spread, out, in_grad)
    out, in_grad, v = results[0], results[1], results[2:16]
    acceptor, address, content, sigmoid, mixer, ff_address, ff_content, ff_acceptor = results[16:]
    return (
        out, in_grad,
        v[0], v[1], v[2], v[3], v[4], v[5],
        acceptor, address, content, sigmoid,
        v[10], v[11], v[12], v[13],
        mixer,
        v[6], v[7], v[8], v[9],
        ff_address, ff_content, ff_acceptor,
    )


def solution(mesh):
    r, v = P(("dp", "fsdp"), None), P(("dp", "fsdp"))
    state = P(("dp", "fsdp"), None, None, None)
    return jax.shard_map(
        per_device,
        mesh=mesh,
        in_specs=(r, state) + (v,) * 6 + (r,) * 4 + (v,) * 4 + (r,) + (v,) * 4 + (r,) * 4,
        out_specs=(r, r) + (v,) * 6 + (r,) * 4 + (v,) * 4 + (r,) + (v,) * 4 + (r,) * 3,
        check_vma=False,
    )
```

```python
from functools import partial

import jax
import jax.numpy as jnp
import numpy as np
from jax import lax
from jax.experimental import pallas as pl
from jax.experimental.pallas import tpu as pltpu
from jax.sharding import PartitionSpec as P

MESH = pl.DeviceIdType.MESH
BF = jnp.bfloat16
F32 = jnp.float32
VMEM = pl.BlockSpec(memory_space=pltpu.VMEM)

NORM_EPS = 1e-05
GROUP_EPS = 0.00064
TOK = 128
EMB = 768
FF = 2688
COLS = 384
SENDS, ARRIVALS = 96, 160
LEFT, RIGHT = 896, 768

WIDTH = {"A": 1664, "B": 1280, "C": 384, "R": 768, "K": 896}
FIXED = {"C": 1, "S": 0, "K": 1}
VEC = 1536
ORDER = (0, 1, 3, 2)


def _order():
    order = np.zeros(EMB, np.int64)
    for x in range(4):
        for y in range(4):
            for z in range(4):
                for c in range(2):
                    device = z * 32 + (x % 2) * 16 + y * 4 + (x // 2) * 2 + c
                    place = (x * 4 + y) * 48 + (z * 2 + c) * 6
                    order[place : place + 6] = 6 * device + np.arange(6)
    return order


def _spread():
    spread = np.zeros((EMB, EMB), np.float32)
    spread[_order(), np.arange(EMB)] = 1.0
    return spread


def _line_pick():
    pick = np.zeros((96, 128), np.float32)
    for member in range(8):
        for r in range(6):
            pick[member * 6 + r, member * 16 + r] = 1.0
            pick[48 + member * 6 + r, member * 16 + 8 + r] = 1.0
    return pick


def _plane_pick():
    pick = np.zeros((432, 512), np.float32)
    for member in range(16):
        for r in range(6):
            pick[member * 6 + r, member * 32 + r] = 1.0
        for r in range(21):
            pick[96 + member * 21 + r, member * 32 + 8 + r] = 1.0
    return pick


def rem4(value):
    return lax.rem(value, 4)


class Place:
    def __init__(self):
        dp, fs = lax.axis_index("dp"), lax.axis_index("fsdp")
        self.z, self.xlo = lax.div(dp, 2), lax.rem(dp, 2)
        self.y, self.xhi = lax.div(fs, 4), lax.rem(lax.div(fs, 2), 2)
        self.c = lax.rem(fs, 2)
        self.x = self.xhi * 2 + self.xlo

    def device(self, z, y, x, c):
        return (z * 2 + lax.rem(x, 2), y * 4 + lax.div(x, 2) * 2 + c)

    def sibling(self):
        return self.device(self.z, self.y, self.x, 1 - self.c)

    def up(self, k):
        return self.device(rem4(self.z + k), self.y, self.x, self.c)

    def line(self, k):
        z = rem4(self.z + k // 2)
        core = self.c if k % 2 == 0 else 1 - self.c
        return self.device(z, self.y, self.x, core), z * 2 + core, core

    def turn(self, q, sibling=False):
        if q in FIXED:
            return FIXED[q]
        return 1 - self.c if sibling else self.c

    def first(self, q, k):
        t = self.turn(q)
        y, x = rem4(self.y + k * (1 - t)), rem4(self.x + k * t)
        return self.device(self.z, y, x, self.c)

    def last(self, q, k):
        t = self.turn(q)
        y, x = rem4(self.y + k * t), rem4(self.x + k * (1 - t))
        return self.device(self.z, y, x, self.c)

    def band(self, q, m, k, sibling=False):
        t = self.turn(q, sibling)
        x = rem4(self.x + m * t + k * (1 - t))
        y = rem4(self.y + m * (1 - t) + k * t)
        return rows(48 * (x * 4 + y), 48)

    def across(self, k):
        return self.device(self.z, self.y, rem4(self.x + k), self.c)

    def side(self, k):
        return self.device(self.z, rem4(self.y + k), self.x, self.c)

    def twin(self):
        return self.device(self.z, self.y, self.xhi * 2 + 1 - self.xlo, self.c)

    def pair(self):
        return self.across(2)

    def order(self, m, k):
        return rem4(self.z + k) * 2 + (self.xlo if m == 0 else 1 - self.xlo)

    def greet(self):
        mates = [self.line(k)[0] for k in range(1, 8)]
        mates += [self.across(k) for k in (1, 2, 3)]
        mates += [self.side(k) for k in (1, 2, 3)]
        barrier = pltpu.get_barrier_semaphore()
        for mate in mates:
            pl.semaphore_signal(barrier, inc=1, device_id=mate, device_id_type=MESH)
        return lambda: pl.semaphore_wait(barrier, len(mates))


class Sender:
    def __init__(self, send_sems, recv_sems):
        self.send_sems, self.recv_sems = send_sems, recv_sems
        self.sends = self.arrivals = 0
        self.open = []
        self.groups = {}

    def send(self, source, target, device, group=None):
        index = self.sends % SENDS
        if len(self.open) >= SENDS:
            self.open.pop(0).wait_send()
        self.sends += 1
        if group not in self.groups:
            self.groups[group if group is not None else self.sends] = self.arrivals
            arrival = self.arrivals
            self.arrivals += 1
        else:
            arrival = self.groups[group]
        copy = pltpu.make_async_remote_copy(
            src_ref=source,
            dst_ref=target,
            send_sem=self.send_sems.at[index],
            recv_sem=self.recv_sems.at[arrival],
            device_id=device,
            device_id_type=MESH,
        )
        copy.start()
        self.open.append(copy)
        return copy

    def wait_group(self, group, like, device):
        pltpu.make_async_remote_copy(
            src_ref=like,
            dst_ref=like,
            send_sem=self.send_sems.at[0],
            recv_sem=self.recv_sems.at[self.groups[group]],
            device_id=device,
            device_id_type=MESH,
        ).wait_recv()

    def drain(self, until=None):
        keep = 0 if until is None else self.sends - until
        while len(self.open) > keep:
            self.open.pop(0).wait_send()


def rows(start, size, unit=16):
    return pl.ds(pl.multiple_of(start, unit), size)


def mm(left, right):
    return jnp.dot(left, right, preferred_element_type=F32)


def mm_t(left, right):
    return lax.dot_general(left, right, (((1,), (1,)), ((), ())), preferred_element_type=F32)


def t_mm(left, right):
    return lax.dot_general(left, right, (((0,), (0,)), ((), ())), preferred_element_type=F32)


def split(value, parts):
    found = []
    for _ in range(parts - 1):
        high = value.astype(BF)
        found.append(high)
        value = value - high.astype(F32)
    found.append(value.astype(BF))
    return found


def fine(dims, left, right):
    lh, ll = split(left, 2)
    rh, rl = split(right, 2)
    dot = partial(lax.dot_general, dimension_numbers=(dims, ((), ())), preferred_element_type=F32)
    return dot(lh, rh) + (dot(lh, rl) + dot(ll, rh))


NN, NT, TN = ((1,), (0,)), ((1,), (1,)), ((0,), (0,))


def wide(ref):
    return ref[...].astype(F32)


def layer_kernel(
    x_in, up_in, state, spread_in, pick_n_in, pick_z_in, turn_n_in, turn_z_in, *refs
):
    vecs, refs = refs[:14], refs[14:]
    (acceptor, address, content, sigmoid, mixer, ff_address, ff_content, ff_acceptor), refs = refs[:8], refs[8:]
    (
        out_ref, in_grad_ref, end_n, end_z,
        x_ref, up_ref, state_v, spread, pick_n, pick_z, turn_n, turn_z, memory,
        wa, wb, wc, wo, w2, gb, scores,
        vec_f, pack_f, pack_n, stage_a, stage_b, cols_f, pack_z, half_z, pair_z, stage_z,
        sib_r, sib_k, sib_b, sib_c, relay_r, relay_k, relay_b, relay_c,
        last_r, last_k, last_b, last_c, first_r, first_k, first_b, first_c,
        acc_r, acc_k, acc_b, acc_c,
        piece_a, piece_b, line_a, line_b,
        sib_o, sib_2, relay_o, relay_2, up_o, up_2, sent_o, sent_2, twin_o, twin_2,
        piece_z, side_z, half_f, sent_z, got_z, swap_f, swapped_z,
        pre_h, hid_h, gp_h, gvo_h, turned, turned_w, turned_h, turned_g,
        send_sems, recv_sems, load_sems,
    ) = refs
    at = Place()
    c = at.c
    sib = at.sibling()
    net = Sender(send_sems, recv_sems)
    met = at.greet()

    loads = {}
    for i, (name, source, target) in enumerate([
        ("spread", spread_in, spread), ("x", x_in, x_ref), ("pick_n", pick_n_in, pick_n),
        ("up", up_in, up_ref), ("pick_z", pick_z_in, pick_z), ("state", state, state_v),
        ("turn_n", turn_n_in, turn_n), ("turn_z", turn_z_in, turn_z),
    ]):
        loads[name] = pltpu.make_async_copy(source, target, load_sems.at[i])
        loads[name].start()

    vec_f[...] = jnp.zeros_like(vec_f)
    for i, ref in enumerate(vecs):
        vec_f[i : i + 1, 0:6] = wide(ref).reshape(1, 6)
    eye = (
        lax.broadcasted_iota(jnp.int32, (16, 128), 0)
        == lax.broadcasted_iota(jnp.int32, (16, 128), 1)
    ).astype(F32).astype(BF)
    pack_f[...] = jnp.zeros_like(pack_f)
    pack_f[0, 0, 0:6, 0:768] = wide(acceptor)
    pack_f[0, 0, 0:6, 768:896] = wide(address.at[:, 0:128])
    pack_f[0, 0, 8:14, 0:640] = wide(address.at[:, 128:768])
    pack_f[0, 0, 8:14, 640:768] = wide(ff_address.at[:, 0:128])
    pack_f[1, 0, 0:6, 0:768] = wide(content)
    pack_f[1, 0, 0:6, 768:896] = wide(sigmoid.at[:, 0:128])
    pack_f[1, 0, 8:14, 0:640] = wide(sigmoid.at[:, 128:768])
    pack_f[1, 0, 8:14, 640:768] = mm_t(eye, vec_f[...].astype(BF))[0:6]
    for h in range(2):
        pack_n[0, h] = pack_f[h, 0].astype(BF)
    met()

    own = at.z * 2 + c

    def send_lines(i, stage):
        for k in range(1, 8):
            mate, _, core = at.line(k)
            net.send(pack_n.at[i, core], stage.at[own], mate, ("lines", i))
        stage[own] = pack_n[i, c]

    send_lines(0, stage_a)
    cols_f[...] = jnp.zeros_like(cols_f)
    cols_f[0:6] = wide(mixer)
    cols_f[8:29] = wide(ff_content)
    cols_f[32:38] = wide(ff_acceptor)
    loads["spread"].wait()
    moved = mm(cols_f[...].astype(BF), spread[...])
    for h in range(2):
        pack_z[h] = moved[0:32, COLS * h : COLS * h + COLS].astype(BF)
        first_col = 128 + 1280 * h
        pack_f[h, 1, 0:6, 0:896] = wide(ff_address.at[:, first_col : first_col + 896])
        pack_f[h, 1, 8:14, 0:384] = wide(ff_address.at[:, first_col + 896 : first_col + 1280])
        pack_f[h, 1, 8:16, 384:768] = moved[32:40, COLS * h : COLS * h + COLS]
        pack_n[1, h] = pack_f[h, 1].astype(BF)
    swap_z = net.send(pack_z.at[1 - c], half_z.at[c], sib)
    half_z[c] = pack_z[c]
    send_lines(1, stage_b)

    loads["x"].wait()
    tokens = mm(x_ref[...], spread[...])
    centred = tokens - jnp.mean(tokens, axis=-1, keepdims=True)
    scale1 = lax.rsqrt(jnp.mean(centred * centred, axis=-1, keepdims=True) + NORM_EPS)
    unit1 = centred * scale1
    loads["up"].wait()
    upstream = mm(up_ref[...], spread[...])
    swap_z.wait_recv()
    to_pair = net.send(half_z, pair_z.at[at.xhi], at.pair())
    pair_z[at.xhi] = half_z[...]
    loads["pick_n"].wait()
    for name in ("state", "turn_n", "turn_z", "pick_z"):
        loads[name].wait()
    blank = jnp.zeros((64, 64), F32)
    for g in range(6):
        memory[g, 0:64] = jnp.concatenate([state_v[2 * g], blank], axis=1)
        memory[g, 64:128] = jnp.concatenate([blank, state_v[2 * g + 1]], axis=1)

    def pick(i, stage):
        net.wait_group(("lines", i), stage.at[0:7], sib)
        return mm(pick_n[...], stage[...].reshape(128, LEFT)).astype(BF)

    full = {"A": wa, "B": wb, "C": wc, "o": wo, "2": w2}

    def place_n(q, m, k):
        return full[q].at[c, at.band(q, m, k)]

    firsts, lasts = {}, {}

    def pass_on(q, m):
        spot = place_n(q, 4 - m, 0)
        for k in (1, 3):
            lasts[q, m, k] = net.send(spot, spot, at.last(q, k))
        net.send(spot, spot, sib, ("sib", q))

    def begin(q, *parts):
        spot = place_n(q, 0, 0)
        spot[...] = jnp.concatenate(parts, axis=1) if len(parts) > 1 else parts[0]
        for k in (1, 3, 2):
            firsts[q, k] = net.send(spot, spot, at.first(q, k))
        pass_on(q, 0)

    def relay(q, m):
        firsts[q, m].wait_recv()
        pass_on(q, m)

    def arrive(q, m, k):
        lasts[q, m, k].wait_recv()
        spot = place_n(q, 4 - m, 4 - k)
        if k == (1 if m % 2 == 0 else 3):
            lasts[q, m, 2] = net.send(spot, spot, at.last(q, k))
        net.send(spot, spot, sib, ("sib", q))

    def arrive_far(q, m):
        lasts[q, m, 2].wait_recv()
        spot = place_n(q, 4 - m, 2)
        net.send(spot, spot, sib, ("sib", q))

    def place_z(w, m, k):
        unit = 96 if w == "o" else 336
        return full[w].at[c, rows(unit * at.order(m, k), unit)]

    def pass_z(w, m):
        spot = place_z(w, m, 0)
        for k in (1, 3):
            lasts[w, m, k] = net.send(spot, spot, at.up(k))
        net.send(spot, spot, sib, ("sib", w))

    def relay_z(w):
        firsts[w].wait_recv()
        pass_z(w, 1)

    def arrive_z(w, m, k):
        lasts[w, m, k].wait_recv()
        spot = place_z(w, m, 4 - k)
        if k == (1 if m == 0 else 3):
            lasts[w, m, 2] = net.send(spot, spot, at.up(k))
        net.send(spot, spot, sib, ("sib", w))

    def arrive_z_far(w, m):
        lasts[w, m, 2].wait_recv()
        spot = place_z(w, m, 2)
        net.send(spot, spot, sib, ("sib", w))

    picked = pick(0, stage_a)
    begin("A", picked[0:48], picked[48:96, 0:RIGHT])
    to_pair.wait_recv()
    for k in (1, 2, 3):
        net.send(pair_z, stage_z.at[at.y], at.side(k), "side")
    stage_z[at.y] = pair_z[...]
    relay("A", 1)
    relay("A", 3)
    for k in (1, 3):
        arrive("A", 0, k)
    picked = pick(1, stage_b)
    relay("A", 2)
    begin("B", picked[0:48], picked[48:96, 0:384])
    begin("C", picked[48:96, 384:768])
    net.wait_group("side", stage_z.at[0:3], sib)
    picked_z = mm(pick_z[...], stage_z[...].reshape(512, COLS)).astype(BF)
    place_z("o", 0, 0)[...] = picked_z[:96]
    place_z("2", 0, 0)[...] = picked_z[96:]
    for w in ("o", "2"):
        spot = place_z(w, 0, 0)
        firsts[w] = net.send(spot, spot, at.twin())
        pass_z(w, 0)
    for m in (1, 3):
        for k in (1, 3):
            arrive("A", m, k)
    arrive_far("A", 0)
    relay("B", 1)
    relay("B", 3)
    for k in (1, 3):
        arrive("A", 2, k)
    for w in ("o", "2"):
        relay_z(w)
    relay("B", 2)
    for m in (1, 3, 2):
        relay("C", m)
    for m in (1, 3, 2):
        arrive_far("A", m)
    tasks = []

    def plan(kind, *steps_):
        for step in steps_:
            tasks.append((kind, step))

    for m in (0, 1):
        for k in (1, 3):
            plan("B", partial(arrive, "B", m, k))
            plan("o", partial(arrive_z, "o", m, k))
            plan("2", partial(arrive_z, "2", m, k))
    for m in (0, 1):
        plan("o", partial(arrive_z_far, "o", m))
    for m in (3, 2):
        for k in (1, 3):
            plan("B", partial(arrive, "B", m, k))
    for m in ORDER:
        for k in (1, 3):
            plan("C", partial(arrive, "C", m, k))
    for m in (0, 1):
        plan("2", partial(arrive_z_far, "2", m))
    for q in ("B", "C"):
        for m in ORDER:
            plan(q, partial(arrive_far, q, m))

    def work(count=1000):
        for _ in range(min(count, len(tasks))):
            tasks.pop(0)[1]()

    def need(q):
        while any(kind == q for kind, _ in tasks):
            work(1)
        net.wait_group(("sib", q), full[q].at[1 - c], sib)

    need("A")

    lanes = lax.broadcasted_iota(jnp.int32, (1, 128), 1)
    left_head = lanes < 64
    token = lax.broadcasted_iota(jnp.int32, (TOK, 1), 0)

    def shift_down(value):
        return jnp.where(token == 0, 0.0, pltpu.roll(value, 1, 0))

    def shift_up(value):
        return jnp.where(token == TOK - 1, 0.0, pltpu.roll(value, TOK - 1, 0))

    def mean(value):
        return jnp.mean(value, axis=-1, keepdims=True)

    def tsum(value):
        return jnp.sum(value, axis=0, keepdims=True)

    def unspread(value):
        a, b, d = split(value, 3)
        return mm_t(a, spread[...]) + (mm_t(b, spread[...]) + mm_t(d, spread[...]))

    vec = mm_t(eye, wa[1, :, VEC:1664])
    gain1, bias1 = vec[0:1], vec[1:2]
    lerps = [vec[2 + i : 3 + i] for i in range(4)]
    gain2, bias2, lerp_h, lerp_g = vec[6:7], vec[7:8], vec[8:9], vec[9:10]
    heads = mm_t(vec.astype(BF), spread[...])
    rate, bonus, gain_w, bias_w = heads[10:11], heads[11:12], heads[12:13], heads[13:14]

    pair_rows = lax.broadcasted_iota(jnp.int32, (256, 128), 0)
    pair_cols = lax.broadcasted_iota(jnp.int32, (256, 128), 1)
    pair_ones = ((lax.rem(pair_rows, 128) // 64) == (pair_cols // 64)).astype(F32).astype(BF)
    below = lax.rem(pair_rows, 128) > pair_cols

    def head_sum(value):
        found = []
        for g in range(6):
            part = value[:, 128 * g : 128 * g + 128]
            found.append(mm(jnp.concatenate(split(part, 2), axis=1), pair_ones))
        return jnp.concatenate(found, axis=1)

    def stack(value):
        return jnp.concatenate(
            [jnp.where(left_head, value, 0.0), jnp.where(left_head, 0.0, value)], axis=0
        )

    def beside(value):
        return jnp.concatenate([value[:TOK], value[TOK:]], axis=1)

    normed = unit1 * gain1 + bias1
    previous = shift_down(normed)
    blended = [(normed * l + previous * (1.0 - l)).astype(BF) for l in lerps]
    for i in range(4):
        turned[i] = blended[i].astype(F32).T.astype(BF)
    recept = mm(blended[0], wa[0, :, 0:768])
    keys = mm(blended[1], wa[0, :, 768:1536])
    vals = mm(blended[2], wa[1, :, 0:768])
    gate_pre = mm(blended[3], wa[1, :, 768:1536])
    work(6)

    fade = -jnp.exp(rate)
    steps = token.astype(F32)
    fall_r = jnp.exp(steps * fade)
    fall_k = jnp.exp(-(steps + 1.0) * fade)
    recept_f = recept * fall_r
    keys_f = keys * fall_k
    present = head_sum(recept * bonus * keys)
    parts = []
    for g in range(6):
        cut = slice(128 * g, 128 * g + 128)
        rg, kg, vg = recept_f[:, cut], keys_f[:, cut], vals[:, cut]
        sc = jnp.where(below, fine(NT, stack(rg), kg), 0.0)
        scores[g] = sc
        parts.append(fine(NN, beside(sc), stack(vg)) + fine(NN, rg, memory[g]))
        if g % 2 == 1:
            work(4)
    wkv = jnp.concatenate(parts, axis=1) + present * vals

    centred_w = wkv - head_sum(wkv) * (1.0 / 64.0)
    scale_w = lax.rsqrt(head_sum(centred_w * centred_w) * (1.0 / 64.0) + GROUP_EPS)
    unit_w = centred_w * scale_w
    grouped = unit_w * gain_w + bias_w
    sig = 1.0 / (1.0 + jnp.exp(-gate_pre))
    silu = gate_pre * sig
    gated = (grouped * silu).astype(BF)
    turned_w[...] = gated.astype(F32).T.astype(BF)
    need("o")
    middle = tokens + jnp.concatenate([mm(gated, wo[0]), mm(gated, wo[1])], axis=1)

    centred = middle - mean(middle)
    scale2 = lax.rsqrt(mean(centred * centred) + NORM_EPS)
    unit2 = centred * scale2
    normed2 = unit2 * gain2 + bias2
    previous2 = shift_down(normed2)
    mixed_h = (normed2 * lerp_h + previous2 * (1.0 - lerp_h)).astype(BF)
    mixed_g = (normed2 * lerp_g + previous2 * (1.0 - lerp_g)).astype(BF)
    turned_h[...] = mixed_h.astype(F32).T.astype(BF)
    turned_g[...] = mixed_g.astype(F32).T.astype(BF)
    need("B")
    halves = (1 - c, c)
    pre_s = jnp.maximum(mm(mixed_h, wa[0, :, 1536:1664]), 0.0)
    hidden_s = (pre_s * pre_s).astype(BF)
    for h in halves:
        pre = jnp.maximum(mm(mixed_h, wb[h]), 0.0)
        pre_h[h] = pre
        hid_h[h] = (pre * pre).astype(BF)
    need("C")
    gating = jnp.concatenate([mm(mixed_g, wc[0]), mm(mixed_g, wc[1])], axis=1)
    gating = 1.0 / (1.0 + jnp.exp(-gating))
    grad_vo = upstream * gating
    for h in range(2):
        gvo_h[h] = grad_vo[:, COLS * h : COLS * h + COLS].astype(BF)

    swaps = {}

    def fold(mine, other, *more):
        total = wide(mine) + wide(other)
        for ref in more:
            total += wide(ref)
        return total

    gr, go = wb.at[:, :, 0:768], wb.at[:, :, 768:1152]
    gk, gc = wa.at[:, :, 768:1664], wc
    grads = {"R": gr, "K": gk, "B": gb, "S": gc}
    sib_of = {"R": sib_r, "K": sib_k, "B": sib_b, "S": sib_c}
    relay_of = {"R": relay_r, "K": relay_k, "B": relay_b, "S": relay_c}
    last_of = {"R": last_r, "K": last_k, "B": last_b, "S": last_c}
    first_of = {"R": first_r, "K": first_k, "B": first_b, "S": first_c}
    acc_of = {"R": acc_r, "K": acc_k, "B": acc_b, "S": acc_c}

    def swap(q):
        swaps[q] = net.send(grads[q].at[1 - c], sib_of[q], sib)

    def swapped(q):
        if q in swaps:
            swaps.pop(q).wait_recv()

    def scatter_far(q, m):
        part = at.band(q, m, 2)
        via = 1 if m % 2 == 0 else 3
        swapped(q)
        spot = sib_of[q].at[part]
        spot[...] = fold(grads[q].at[c, part], spot).astype(BF)
        lasts["g", q, m, 2] = net.send(spot, relay_of[q].at[m], at.last(q, via))

    def scatter_near(q, m, k):
        part = at.band(q, m, k)
        spot = sib_of[q].at[part]
        more = []
        if k == (1 if m % 2 == 0 else 3):
            lasts["g", q, m, 2].wait_recv()
            more = [relay_of[q].at[m]]
        spot[...] = fold(grads[q].at[c, part], spot, *more).astype(BF)
        lasts["g", q, m, k] = net.send(spot, last_of[q].at[k // 2, m], at.last(q, k))

    def scatter_own(q, m):
        part = at.band(q, m, 0)
        spot = sib_of[q].at[part]
        lasts["g", q, m, 1].wait_recv()
        lasts["g", q, m, 3].wait_recv()
        arrived = last_of[q]
        total = fold(grads[q].at[c, part], spot, arrived.at[0, m], arrived.at[1, m])
        if m == 0:
            acc_of[q][...] = total
        else:
            spot[...] = total.astype(BF)
            firsts["g", q, m] = net.send(spot, first_of[q].at[m - 1], at.first(q, m))

    def scatter_end(q):
        total = acc_of[q][...]
        for m in (1, 3, 2):
            firsts["g", q, m].wait_recv()
            total += wide(first_of[q].at[m - 1])
        acc_of[q][...] = total

    def spread_lines(i, left, right, piece, line):
        right = jnp.concatenate([right, jnp.zeros((48, LEFT - RIGHT), F32)], axis=1)
        table = jnp.concatenate([left, right], axis=0).astype(BF)
        piece[...] = mm(turn_n[...], table).astype(BF).reshape(8, 16, LEFT)
        for k in range(1, 8):
            mate, index, _ = at.line(k)
            net.send(piece.at[index], line.at[own], mate, ("grad lines", i))
        line[own] = piece[own]

    def sum_lines(i, line):
        net.wait_group(("grad lines", i), line.at[0:7], sib)
        for h in range(2):
            total = wide(line.at[h])
            for z in (1, 2, 3):
                total += wide(line.at[2 * z + h])
            end_n[h, i] = total

    def scatter_steps(q):
        steps_ = [partial(scatter_far, q, m) for m in ORDER]
        for late in (False, True):
            for m in ORDER:
                for k in (1, 3):
                    if late == (k == (1 if m % 2 == 0 else 3)):
                        steps_.append(partial(scatter_near, q, m, k))
        steps_ += [partial(scatter_own, q, m) for m in (1, 3, 2, 0)]
        steps_.append(partial(scatter_end, q))
        return steps_

    z_parts = {
        "o": (96, go, sib_o, relay_o, up_o, sent_o, twin_o),
        "2": (336, w2, sib_2, relay_2, up_2, sent_2, twin_2),
    }

    def swap_w(w):
        unit, mine, theirs = z_parts[w][:3]
        swaps[w] = net.send(mine.at[1 - c], theirs, sib)

    def part_w(w, m, k):
        unit = z_parts[w][0]
        return rows(unit * at.order(m, k), unit)

    def scatter_far_w(w, m):
        unit, mine, theirs, relayed = z_parts[w][:4]
        part = part_w(w, m, 2)
        swapped(w)
        spot = theirs.at[part]
        spot[...] = fold(mine.at[c, part], spot).astype(BF)
        lasts["g", w, m, 2] = net.send(spot, relayed.at[m], at.up(1 if m == 0 else 3))

    def scatter_near_w(w, m, k):
        unit, mine, theirs, relayed, arrived = z_parts[w][:5]
        part = part_w(w, m, k)
        more = []
        if k == (1 if m == 0 else 3):
            lasts["g", w, m, 2].wait_recv()
            more = [relayed.at[m]]
        spot = theirs.at[part]
        spot[...] = fold(mine.at[c, part], spot, *more).astype(BF)
        lasts["g", w, m, k] = net.send(spot, arrived.at[k // 2, m], at.up(k))

    def scatter_own_w(w, m):
        unit, mine, theirs, relayed, arrived, sent, twin = z_parts[w]
        part = part_w(w, m, 0)
        lasts["g", w, m, 1].wait_recv()
        lasts["g", w, m, 3].wait_recv()
        total = fold(mine.at[c, part], theirs.at[part], arrived.at[0, m], arrived.at[1, m])
        if m == 1:
            sent[...] = total.astype(BF)
            firsts["g", w] = net.send(sent, twin, at.twin())
        else:
            firsts["g", w].wait_recv()
            sums_z[w] = (total + wide(twin)).astype(BF)

    def scatter_steps_w(w):
        steps_ = [partial(scatter_far_w, w, 0), partial(scatter_far_w, w, 1)]
        steps_ += [partial(scatter_near_w, w, 1, 1), partial(scatter_near_w, w, 0, 3)]
        steps_ += [partial(scatter_near_w, w, 0, 1), partial(scatter_near_w, w, 1, 3)]
        steps_ += [partial(scatter_own_w, w, 1), partial(scatter_own_w, w, 0)]
        return steps_

    sums_z = {}

    need("2")
    gathered = net.sends
    steps_2, steps_o = scatter_steps_w("2"), scatter_steps_w("o")
    steps_b, steps_c = scatter_steps("B"), scatter_steps("S")
    steps_r, steps_k = scatter_steps("R"), scatter_steps("K")

    def run(*steps_):
        for step in steps_:
            step()

    for h in halves:
        part = rows(128 + 1280 * h, 1280)
        grad_hidden = mm_t(gvo_h[0], w2[0, part]) + mm_t(gvo_h[1], w2[1, part])
        gp_h[h] = (grad_hidden * 2.0 * pre_h[h]).astype(BF)
        gb[h] = mm(turned_h[...], gp_h[h]).astype(BF)
        if h is halves[0]:
            swap("B")
    grad_hidden = mm_t(gvo_h[0], w2[0, 0:128]) + mm_t(gvo_h[1], w2[1, 0:128])
    grad_pre_s = (grad_hidden * 2.0 * pre_s).astype(BF)
    value_out = jnp.concatenate(
        [
            mm(hidden_s, w2[n, 0:128]) + mm(hid_h[0], w2[n, 128:1408]) + mm(hid_h[1], w2[n, 1408:2688])
            for n in range(2)
        ],
        axis=1,
    )
    layer_out = middle + gating * value_out
    run(*steps_b[:8])
    net.drain(gathered)
    for n in halves:
        w2[n, 0:128] = t_mm(hidden_s, gvo_h[n]).astype(BF)
        w2[n, 128:1408] = t_mm(hid_h[0], gvo_h[n]).astype(BF)
        w2[n, 1408:2688] = t_mm(hid_h[1], gvo_h[n]).astype(BF)
        if n is halves[0]:
            swap_w("2")
    grad_gp = (grad_vo * value_out * (1.0 - gating)).astype(BF)
    grad_mg = mm_t(grad_gp[:, :COLS], wc[0]) + mm_t(grad_gp[:, COLS:], wc[1])
    for h in range(2):
        gc[h] = mm(turned_g[...], grad_gp[:, COLS * h : COLS * h + COLS]).astype(BF)
    swap("S")
    grad_mh = mm_t(grad_pre_s, wa[0, :, 1536:1664])
    grad_mh += mm_t(gp_h[0], wb[0]) + mm_t(gp_h[1], wb[1])
    gk[0, :, 768:896] = mm(turned_h[...], grad_pre_s).astype(BF)
    run(*steps_2[:4])
    run(*steps_c[:8])

    grad_n2 = grad_mh * lerp_h + grad_mg * lerp_g
    grad_n2 += shift_up(grad_mh * (1.0 - lerp_h) + grad_mg * (1.0 - lerp_g))
    delta2 = normed2 - previous2
    g_lerp_h, g_lerp_g = tsum(grad_mh * delta2), tsum(grad_mg * delta2)
    g_gain2, g_bias2 = tsum(grad_n2 * unit2), tsum(grad_n2)
    q2 = grad_n2 * gain2
    grad_middle = upstream + scale2 * (q2 - mean(q2) - unit2 * mean(q2 * unit2))

    grad_attn = grad_middle.astype(BF)
    grad_gated = mm_t(grad_attn[:, :COLS], wo[0]) + mm_t(grad_attn[:, COLS:], wo[1])
    for h in range(2):
        go[h] = mm(turned_w[...], grad_attn[:, COLS * h : COLS * h + COLS]).astype(BF)
    swap_w("o")
    grad_gate = (grad_gated * grouped * (sig * (1.0 + gate_pre * (1.0 - sig)))).astype(BF)
    grad_grouped = grad_gated * silu
    g_gain_w, g_bias_w = tsum(grad_grouped * unit_w), tsum(grad_grouped)
    qw = grad_grouped * gain_w
    grad_wkv = scale_w * (
        qw
        - head_sum(qw) * (1.0 / 64.0)
        - unit_w * (head_sum(qw * unit_w) * (1.0 / 64.0))
    )

    weight = head_sum(grad_wkv * vals)
    parts_r, parts_k, parts_v = [], [], []
    for g in range(6):
        cut = slice(128 * g, 128 * g + 128)
        rg, kg, vg, dg = recept_f[:, cut], keys_f[:, cut], vals[:, cut], grad_wkv[:, cut]
        ds = stack(dg)
        da = jnp.where(below, fine(NT, ds, vg), 0.0)
        parts_r.append(fine(NN, beside(da), stack(kg)) + fine(NT, dg, memory[g]))
        parts_k.append(fine(TN, da, stack(rg)))
        parts_v.append(fine(TN, scores[g], ds))
        if g == 2:
            run(*steps_o[:4])
        if g == 4:
            run(*steps_b[8:12])
    grad_r = jnp.concatenate(parts_r, axis=1) * fall_r
    grad_k = jnp.concatenate(parts_k, axis=1) * fall_k
    grad_v = jnp.concatenate(parts_v, axis=1) + grad_wkv * present
    g_rate = fade * tsum(steps * recept * grad_r - (steps + 1.0) * keys * grad_k)
    g_bonus = tsum(recept * keys * weight)
    grad_r = (grad_r + bonus * keys * weight).astype(BF)
    grad_k = (grad_k + bonus * recept * weight).astype(BF)
    grad_v = grad_v.astype(BF)

    gr[0] = mm(turned[0], grad_r).astype(BF)
    gr[1] = mm(turned[2], grad_v).astype(BF)
    swap("R")
    grad_blended = [
        mm_t(grad_r, wa[0, :, 0:768]),
        mm_t(grad_k, wa[0, :, 768:1536]),
        mm_t(grad_v, wa[1, :, 0:768]),
        mm_t(grad_gate, wa[1, :, 768:1536]),
    ]
    gk[0, :, 0:768] = mm(turned[1], grad_k).astype(BF)
    gk[1, :, 0:768] = mm(turned[3], grad_gate).astype(BF)
    run(*steps_2[4:6], *steps_r[:8])
    delta = normed - previous
    g_lerps = [tsum(g * delta) for g in grad_blended]
    grad_n1 = sum(g * l for g, l in zip(grad_blended, lerps))
    grad_n1 += shift_up(sum(g * (1.0 - l) for g, l in zip(grad_blended, lerps)))
    g_gain1, g_bias1 = tsum(grad_n1 * unit1), tsum(grad_n1)

    zero = jnp.zeros((1, EMB), F32)
    natural = jnp.concatenate([g_rate, g_bonus, g_gain_w, g_bias_w] + [zero] * 4, axis=0)
    va, vb, vc = split(natural, 3)
    moved = mm(va, spread[...]) + (mm(vb, spread[...]) + mm(vc, spread[...]))
    table = jnp.concatenate(
        [g_gain1, g_bias1] + g_lerps + [g_gain2, g_bias2, g_lerp_h, g_lerp_g]
        + [moved[0:4], jnp.zeros((114, EMB), F32)],
        axis=0,
    )
    gk[1, :, 768:896] = table.T.astype(BF)
    swap("K")
    run(*steps_c[8:12], *steps_b[12:16], *steps_k[:8], *steps_o[4:6], *steps_r[8:12])
    out_v, grad_v_ = pre_h.at[0, :, 0:768], pre_h.at[1, :, 0:768]
    out_v[...] = unspread(layer_out)
    out_copy = pltpu.make_async_copy(out_v, out_ref, load_sems.at[8])
    out_copy.start()
    run(*steps_k[8:12], steps_2[6], steps_o[6], steps_b[16], *steps_c[12:16])
    q1 = grad_n1 * gain1
    grad_x = grad_middle + scale1 * (q1 - mean(q1) - unit1 * mean(q1 * unit1))
    grad_v_[...] = unspread(grad_x)
    grad_copy = pltpu.make_async_copy(grad_v_, in_grad_ref, load_sems.at[9])
    grad_copy.start()
    run(*steps_r[12:16])

    run(steps_2[7], steps_o[7])
    spread_z = mm(turn_z[:, :96], sums_z["o"]) + mm(turn_z[:, 96:], sums_z["2"])
    piece_z[...] = spread_z.astype(BF).reshape(4, 128, COLS)
    for k in (1, 2, 3):
        net.send(piece_z.at[rem4(at.y + k)], side_z.at[k - 1], at.side(k), "grad side")
    run(steps_c[16])
    spread_lines(
        1, acc_b[:, 0:LEFT], jnp.concatenate([acc_b[:, LEFT:], acc_c[...]], axis=1), piece_b, line_b
    )
    run(*steps_k[12:16])
    net.wait_group("grad side", side_z, sib)
    total = wide(piece_z.at[at.y])
    for k in (1, 2, 3):
        total += wide(side_z.at[k - 1])
    half_f[...] = total.reshape(2, 64, COLS)
    sent_z[...] = half_f[1 - at.xhi].astype(BF)
    to_pair = net.send(sent_z, got_z, at.pair())
    run(steps_r[16], steps_k[16])
    acc_a = jnp.concatenate([acc_r[...], acc_k[...]], axis=1)
    spread_lines(0, acc_a[:, 0:LEFT], acc_a[:, LEFT:], piece_a, line_a)
    sum_lines(1, line_b)
    to_pair.wait_recv()
    swap_f[...] = half_f[at.xhi] + wide(got_z)
    away, kept = rows(32 * (1 - c), 32, 8), rows(32 * c, 32, 8)
    last_swap = net.send(swap_f.at[away], swapped_z.at[c], sib)
    swapped_z[c] = swap_f[kept]
    last_swap.wait_recv()
    columns = jnp.concatenate(
        [
            jnp.concatenate([swapped_z[0], swapped_z[1]], axis=1),
            jnp.concatenate([end_n[0, 1, 8:16, 384:768], end_n[1, 1, 8:16, 384:768]], axis=1),
        ],
        axis=0,
    )
    end_z[...] = unspread(columns)
    out_copy.wait()
    grad_copy.wait()
    sum_lines(0, line_a)
    net.drain()


def layer(*operands):
    bf = lambda *shape: pltpu.VMEM(shape, BF)
    f32 = lambda *shape: pltpu.VMEM(shape, F32)
    a, b, d, r, k = (WIDTH[q] for q in "ABCRK")
    return pl.pallas_call(
        layer_kernel,
        out_shape=(
            jax.ShapeDtypeStruct((TOK, EMB), F32),
            jax.ShapeDtypeStruct((TOK, EMB), F32),
            jax.ShapeDtypeStruct((2, 2, 16, LEFT), F32),
            jax.ShapeDtypeStruct((40, EMB), F32),
        ),
        in_specs=[pl.BlockSpec(memory_space=pl.ANY)] * 8 + [VMEM] * (len(operands) - 8),
        out_specs=(pl.BlockSpec(memory_space=pl.ANY),) * 2 + (VMEM,) * 2,
        scratch_shapes=[
            bf(TOK, EMB), bf(TOK, EMB), f32(12, 64, 64), bf(EMB, EMB),
            bf(96, 128), bf(432, 512), bf(128, 96), bf(512, 432), f32(6, 128, 128),
            bf(2, EMB, a), bf(2, EMB, b), bf(2, EMB, d), bf(2, EMB, COLS), bf(2, FF, COLS),
            bf(2, EMB, b), f32(6, 256, 128),
            f32(128, 128), f32(2, 2, 16, LEFT), bf(2, 2, 16, LEFT), bf(8, 16, LEFT), bf(8, 16, LEFT),
            f32(48, EMB), bf(2, 32, COLS), bf(2, 32, COLS), bf(2, 2, 32, COLS), bf(4, 2, 2, 32, COLS),
            *(bf(EMB, w) for w in (r, k, b, d)), *(bf(4, 48, w) for w in (r, k, b, d)),
            *(bf(2, 4, 48, w) for w in (r, k, b, d)), *(bf(3, 48, w) for w in (r, k, b, d)),
            *(f32(48, w) for w in (r, k, b, d)),
            bf(8, 16, LEFT), bf(8, 16, LEFT), bf(8, 16, LEFT), bf(8, 16, LEFT),
            bf(EMB, COLS), bf(FF, COLS),
            bf(2, 96, COLS), bf(2, 336, COLS), bf(2, 2, 96, COLS), bf(2, 2, 336, COLS),
            bf(96, COLS), bf(336, COLS), bf(96, COLS), bf(336, COLS),
            bf(4, 128, COLS), bf(3, 128, COLS), f32(2, 64, COLS), bf(64, COLS), bf(64, COLS),
            f32(64, COLS), f32(2, 32, COLS),
            f32(2, TOK, b), bf(2, TOK, b), bf(2, TOK, b), bf(2, TOK, COLS),
            bf(4, EMB, TOK), bf(EMB, TOK), bf(EMB, TOK), bf(EMB, TOK),
            pltpu.SemaphoreType.DMA((SENDS,)),
            pltpu.SemaphoreType.DMA((ARRIVALS,)),
            pltpu.SemaphoreType.DMA((10,)),
        ],
        compiler_params=pltpu.CompilerParams(
            collective_id=1, has_side_effects=True, vmem_limit_bytes=62 << 20
        ),
        cost_estimate=pl.CostEstimate(
            flops=6 * TOK * 7667712, bytes_accessed=4 * 7667712, transcendentals=10 * TOK * EMB
        ),
        name="layer",
    )(*operands)


def finish_kernel(end_n, end_z, out_in, grad_in, out, grad, *refs):
    vecs, mats = refs[:14], refs[14:]
    acceptor, address, content, sigmoid, mixer, ff_address, ff_content, ff_acceptor = mats
    out[...] = out_in[...]
    grad[...] = grad_in[...]
    acceptor[...] = end_n[0, 0, 0:6, 0:768]
    address[:, 0:128] = end_n[0, 0, 0:6, 768:896]
    address[:, 128:768] = end_n[0, 0, 8:14, 0:640]
    content[...] = end_n[1, 0, 0:6, 0:768]
    sigmoid[:, 0:128] = end_n[1, 0, 0:6, 768:896]
    sigmoid[:, 128:768] = end_n[1, 0, 8:14, 0:640]
    ff_address[:, 0:128] = end_n[0, 0, 8:14, 640:768]
    for h in range(2):
        first_col = 128 + 1280 * h
        ff_address[:, first_col : first_col + 896] = end_n[h, 1, 0:6, 0:896]
        ff_address[:, first_col + 896 : first_col + 1280] = end_n[h, 1, 8:14, 0:384]
    table = jnp.concatenate([end_n[1, 0, 8:16, 640:768], jnp.zeros((120, 128), F32)], axis=0).T
    for i, ref in enumerate(vecs):
        ref[...] = table[i : i + 1, 0:6].reshape(6)
    mixer[...] = end_z[0:6]
    ff_content[...] = end_z[8:29]
    ff_acceptor[...] = end_z[32:38]


def finish(end_n, end_z, out, grad):
    shapes = [(TOK, EMB), (TOK, EMB)] + [(6,)] * 14
    shapes += [(6, EMB)] * 5 + [(6, FF), (21, EMB), (6, EMB)]
    return pl.pallas_call(
        finish_kernel,
        out_shape=tuple(jax.ShapeDtypeStruct(shape, F32) for shape in shapes),
        in_specs=[VMEM] * 4,
        out_specs=(VMEM,) * len(shapes),
        name="finish",
    )(end_n, end_z, out, grad)


def per_device(
    incoming_activations,
    sequence_opening_memory,
    prior_standardize_factor,
    prior_standardize_offset,
    acceptor_lerp_factor,
    address_lerp_factor,
    content_lerp_factor,
    sigmoid_lerp_factor,
    acceptor_matrix,
    address_matrix,
    content_matrix,
    sigmoid_matrix,
    lane_fading_exponent,
    present_reward_vector,
    cluster_standardize_factor,
    cluster_standardize_offset,
    mixer_result_matrix,
    latter_standardize_factor,
    latter_standardize_offset,
    feedforward_address_lerp,
    feedforward_sigmoid_lerp,
    feedforward_address_matrix,
    feedforward_content_matrix,
    feedforward_acceptor_matrix,
    upstream_derivative,
):
    spread = jnp.asarray(_spread(), BF)
    out, in_grad, end_n, end_z = layer(
        incoming_activations, upstream_derivative,
        sequence_opening_memory.reshape(12, 64, 64), spread,
        jnp.asarray(_line_pick(), BF), jnp.asarray(_plane_pick(), BF),
        jnp.asarray(_line_pick().T, BF), jnp.asarray(_plane_pick().T, BF),
        prior_standardize_factor, prior_standardize_offset, acceptor_lerp_factor,
        address_lerp_factor, content_lerp_factor, sigmoid_lerp_factor,
        latter_standardize_factor, latter_standardize_offset, feedforward_address_lerp,
        feedforward_sigmoid_lerp, lane_fading_exponent, present_reward_vector,
        cluster_standardize_factor, cluster_standardize_offset,
        acceptor_matrix, address_matrix, content_matrix, sigmoid_matrix,
        mixer_result_matrix, feedforward_address_matrix, feedforward_content_matrix,
        feedforward_acceptor_matrix,
    )
    results = finish(end_n, end_z, out, in_grad)
    out, in_grad, v = results[0], results[1], results[2:16]
    acceptor, address, content, sigmoid, mixer, ff_address, ff_content, ff_acceptor = results[16:]
    return (
        out, in_grad,
        v[0], v[1], v[2], v[3], v[4], v[5],
        acceptor, address, content, sigmoid,
        v[10], v[11], v[12], v[13],
        mixer,
        v[6], v[7], v[8], v[9],
        ff_address, ff_content, ff_acceptor,
    )


def solution(mesh):
    r, v = P(("dp", "fsdp"), None), P(("dp", "fsdp"))
    state = P(("dp", "fsdp"), None, None, None)
    return jax.shard_map(
        per_device,
        mesh=mesh,
        in_specs=(r, state) + (v,) * 6 + (r,) * 4 + (v,) * 4 + (r,) + (v,) * 4 + (r,) * 4,
        out_specs=(r, r) + (v,) * 6 + (r,) * 4 + (v,) * 4 + (r,) + (v,) * 4 + (r,) * 3,
        check_vma=False,
    )
```

```python
from functools import partial

import jax
import jax.numpy as jnp
import numpy as np
from jax import lax
from jax.experimental import pallas as pl
from jax.experimental.pallas import tpu as pltpu
from jax.sharding import PartitionSpec as P

MESH = pl.DeviceIdType.MESH
BF = jnp.bfloat16
F32 = jnp.float32
VMEM = pl.BlockSpec(memory_space=pltpu.VMEM)

NORM_EPS = 1e-05
GROUP_EPS = 0.00064
TOK = 128
EMB = 768
FF = 2688
COLS = 384
SENDS, ARRIVALS = 96, 160
LEFT, RIGHT = 896, 768

WIDTH = {"A": 1664, "B": 1280, "C": 384, "R": 768, "K": 896}
FIXED = {"S": 0}
VEC = 1536
ORDER = (0, 1, 3, 2)


def _order():
    order = np.zeros(EMB, np.int64)
    for x in range(4):
        for y in range(4):
            for z in range(4):
                for c in range(2):
                    device = z * 32 + (x % 2) * 16 + y * 4 + (x // 2) * 2 + c
                    place = (x * 4 + y) * 48 + (z * 2 + c) * 6
                    order[place : place + 6] = 6 * device + np.arange(6)
    return order


def _spread():
    spread = np.zeros((EMB, EMB), np.float32)
    spread[_order(), np.arange(EMB)] = 1.0
    return spread


def _line_pick():
    pick = np.zeros((96, 128), np.float32)
    for member in range(8):
        for r in range(6):
            pick[member * 6 + r, member * 16 + r] = 1.0
            pick[48 + member * 6 + r, member * 16 + 8 + r] = 1.0
    return pick


def _plane_pick():
    pick = np.zeros((432, 512), np.float32)
    for member in range(16):
        y, xhi, core = member // 4, member // 2 % 2, member % 2
        staged = (xhi * 8 + y * 2 + core) * 32
        for r in range(6):
            pick[member * 6 + r, staged + r] = 1.0
        for r in range(21):
            pick[96 + member * 21 + r, staged + 8 + r] = 1.0
    return pick


def rem4(value):
    return lax.rem(value, 4)


class Place:
    def __init__(self):
        dp, fs = lax.axis_index("dp"), lax.axis_index("fsdp")
        self.z, self.xlo = lax.div(dp, 2), lax.rem(dp, 2)
        self.y, self.xhi = lax.div(fs, 4), lax.rem(lax.div(fs, 2), 2)
        self.c = lax.rem(fs, 2)
        self.x = self.xhi * 2 + self.xlo
        self.one, self.two = self.by_core(self.y, self.x), self.by_core(self.x, self.y)

    def by_core(self, zero, one):
        return zero * (1 - self.c) + one * self.c

    def device(self, z, y, x, c):
        return (z * 2 + lax.rem(x, 2), y * 4 + lax.div(x, 2) * 2 + c)

    def sibling(self):
        return self.device(self.z, self.y, self.x, 1 - self.c)

    def up(self, k):
        return self.device(rem4(self.z + k), self.y, self.x, self.c)

    def line(self, k):
        z = rem4(self.z + k // 2)
        core = self.c if k % 2 == 0 else 1 - self.c
        return self.device(z, self.y, self.x, core), z * 2 + core, core

    def turn(self, q, sibling=False):
        if q in FIXED:
            return FIXED[q]
        return 1 - self.c if sibling else self.c

    def first(self, q, k):
        t = self.turn(q)
        y, x = rem4(self.y + k * (1 - t)), rem4(self.x + k * t)
        return self.device(self.z, y, x, self.c)

    def last(self, q, k):
        t = self.turn(q)
        y, x = rem4(self.y + k * t), rem4(self.x + k * (1 - t))
        return self.device(self.z, y, x, self.c)

    def band(self, q, m, k, sibling=False):
        t = self.turn(q, sibling)
        x = rem4(self.x + m * t + k * (1 - t))
        y = rem4(self.y + m * (1 - t) + k * t)
        return rows(48 * (x * 4 + y), 48)

    def across(self, k):
        return self.device(self.z, self.y, rem4(self.x + k), self.c)

    def side(self, k):
        return self.device(self.z, rem4(self.y + k), self.x, self.c)

    def order(self, m, k):
        return rem4(self.z + k) * 2 + m

    def greet(self):
        mates = [self.line(k)[0] for k in range(1, 8)]
        mates += [self.across(k) for k in (1, 2, 3)]
        mates += [self.side(k) for k in (1, 2, 3)]
        barrier = pltpu.get_barrier_semaphore()
        for mate in mates:
            pl.semaphore_signal(barrier, inc=1, device_id=mate, device_id_type=MESH)
        return lambda: pl.semaphore_wait(barrier, len(mates))


class Sender:
    def __init__(self, send_sems, recv_sems):
        self.send_sems, self.recv_sems = send_sems, recv_sems
        self.sends = self.arrivals = 0
        self.open = []
        self.groups = {}

    def send(self, source, target, device, group=None):
        index = self.sends % SENDS
        if len(self.open) >= SENDS:
            self.open.pop(0).wait_send()
        self.sends += 1
        if group not in self.groups:
            self.groups[group if group is not None else self.sends] = self.arrivals
            arrival = self.arrivals
            self.arrivals += 1
        else:
            arrival = self.groups[group]
        copy = pltpu.make_async_remote_copy(
            src_ref=source,
            dst_ref=target,
            send_sem=self.send_sems.at[index],
            recv_sem=self.recv_sems.at[arrival],
            device_id=device,
            device_id_type=MESH,
        )
        copy.start()
        self.open.append(copy)
        return copy

    def wait_group(self, group, like, device):
        pltpu.make_async_remote_copy(
            src_ref=like,
            dst_ref=like,
            send_sem=self.send_sems.at[0],
            recv_sem=self.recv_sems.at[self.groups[group]],
            device_id=device,
            device_id_type=MESH,
        ).wait_recv()

    def drain(self, until=None):
        keep = 0 if until is None else self.sends - until
        while len(self.open) > keep:
            self.open.pop(0).wait_send()


def rows(start, size, unit=16):
    return pl.ds(pl.multiple_of(start, unit), size)


def mm(left, right):
    return jnp.dot(left, right, preferred_element_type=F32)


def mm_t(left, right):
    return lax.dot_general(left, right, (((1,), (1,)), ((), ())), preferred_element_type=F32)


def t_mm(left, right):
    return lax.dot_general(left, right, (((0,), (0,)), ((), ())), preferred_element_type=F32)


def split(value, parts):
    found = []
    for _ in range(parts - 1):
        high = value.astype(BF)
        found.append(high)
        value = value - high.astype(F32)
    found.append(value.astype(BF))
    return found


def fine(dims, left, right):
    lh, ll = split(left, 2)
    rh, rl = split(right, 2)
    dot = partial(lax.dot_general, dimension_numbers=(dims, ((), ())), preferred_element_type=F32)
    return dot(lh, rh) + (dot(lh, rl) + dot(ll, rh))


NN, NT, TN = ((1,), (0,)), ((1,), (1,)), ((0,), (0,))


def wide(ref):
    return ref[...].astype(F32)


def layer_kernel(
    x_in, up_in, state, spread_in, pick_n_in, pick_z_in, turn_n_in, turn_z_in, *refs
):
    vecs, refs = refs[:14], refs[14:]
    (acceptor, address, content, sigmoid, mixer, ff_address, ff_content, ff_acceptor), refs = refs[:8], refs[8:]
    (
        out_ref, in_grad_ref, end_n, end_z,
        x_ref, up_ref, state_v, spread, pick_n, pick_z, turn_n, turn_z, memory,
        wa, wb, wc, wo, w2, gb, scores,
        vec_f, pack_f, pack_n, stage_a, stage_b, cols_f, pack_z, half_z, row_z, stage_z,
        sib_r, sib_k, sib_b, sib_c, relay_r, relay_k, relay_b, relay_c,
        last_r, last_k, last_b, last_c, first_r, first_k, first_b, first_c,
        acc_r, acc_k, acc_b, acc_c,
        piece_a, piece_b, line_a, line_b,
        sib_o, sib_2, relay_o, relay_2, up_o, up_2, sum_z,
        piece_z, across_z, row_f, row_b, side_z, swap_f, swapped_z,
        pre_h, hid_h, gp_h, gvo_h, turned, turned_w, turned_h, turned_g,
        send_sems, recv_sems, load_sems,
    ) = refs
    at = Place()
    c = at.c
    sib = at.sibling()
    net = Sender(send_sems, recv_sems)
    met = at.greet()

    loads = {}
    for i, (name, source, target) in enumerate([
        ("spread", spread_in, spread), ("x", x_in, x_ref), ("pick_n", pick_n_in, pick_n),
        ("up", up_in, up_ref), ("pick_z", pick_z_in, pick_z), ("state", state, state_v),
        ("turn_n", turn_n_in, turn_n), ("turn_z", turn_z_in, turn_z),
    ]):
        loads[name] = pltpu.make_async_copy(source, target, load_sems.at[i])
        loads[name].start()

    vec_f[...] = jnp.zeros_like(vec_f)
    for i, ref in enumerate(vecs):
        vec_f[i : i + 1, 0:6] = wide(ref).reshape(1, 6)
    eye = (
        lax.broadcasted_iota(jnp.int32, (16, 128), 0)
        == lax.broadcasted_iota(jnp.int32, (16, 128), 1)
    ).astype(F32).astype(BF)
    pack_f[...] = jnp.zeros_like(pack_f)
    pack_f[0, 0, 0:6, 0:768] = wide(acceptor)
    pack_f[0, 0, 0:6, 768:896] = wide(address.at[:, 0:128])
    pack_f[0, 0, 8:14, 0:640] = wide(address.at[:, 128:768])
    pack_f[0, 0, 8:14, 640:768] = wide(ff_address.at[:, 0:128])
    pack_f[1, 0, 0:6, 0:768] = wide(content)
    pack_f[1, 0, 0:6, 768:896] = wide(sigmoid.at[:, 0:128])
    pack_f[1, 0, 8:14, 0:640] = wide(sigmoid.at[:, 128:768])
    pack_f[1, 0, 8:14, 640:768] = mm_t(eye, vec_f[...].astype(BF))[0:6]
    for h in range(2):
        pack_n[0, h] = pack_f[h, 0].astype(BF)
    met()

    own = at.z * 2 + c

    def send_lines(i, stage):
        for k in range(1, 8):
            mate, _, core = at.line(k)
            net.send(pack_n.at[i, core], stage.at[own], mate, ("lines", i))
        stage[own] = pack_n[i, c]

    send_lines(0, stage_a)
    cols_f[...] = jnp.zeros_like(cols_f)
    cols_f[0:6] = wide(mixer)
    cols_f[8:29] = wide(ff_content)
    cols_f[32:38] = wide(ff_acceptor)
    loads["spread"].wait()
    moved = mm(cols_f[...].astype(BF), spread[...])
    for h in range(2):
        pack_z[h] = moved[0:32, COLS * h : COLS * h + COLS].astype(BF)
        first_col = 128 + 1280 * h
        pack_f[h, 1, 0:6, 0:896] = wide(ff_address.at[:, first_col : first_col + 896])
        pack_f[h, 1, 8:14, 0:384] = wide(ff_address.at[:, first_col + 896 : first_col + 1280])
        pack_f[h, 1, 8:16, 384:768] = moved[32:40, COLS * h : COLS * h + COLS]
        pack_n[1, h] = pack_f[h, 1].astype(BF)
    swap_z = net.send(pack_z.at[1 - c], half_z.at[c], sib)
    half_z[c] = pack_z[c]
    send_lines(1, stage_b)

    loads["x"].wait()
    tokens = mm(x_ref[...], spread[...])
    centred = tokens - jnp.mean(tokens, axis=-1, keepdims=True)
    scale1 = lax.rsqrt(jnp.mean(centred * centred, axis=-1, keepdims=True) + NORM_EPS)
    unit1 = centred * scale1
    loads["up"].wait()
    upstream = mm(up_ref[...], spread[...])
    swap_z.wait_recv()
    for k in (1, 2, 3):
        net.send(half_z, row_z.at[at.one], at.first("B", k), "one")
    row_z[at.one] = half_z[...]
    loads["pick_n"].wait()
    for name in ("state", "turn_n", "turn_z", "pick_z"):
        loads[name].wait()
    blank = jnp.zeros((64, 64), F32)
    for g in range(6):
        memory[g, 0:64] = jnp.concatenate([state_v[2 * g], blank], axis=1)
        memory[g, 64:128] = jnp.concatenate([blank, state_v[2 * g + 1]], axis=1)

    def pick(i, stage):
        net.wait_group(("lines", i), stage.at[0:7], sib)
        return mm(pick_n[...], stage[...].reshape(128, LEFT)).astype(BF)

    full = {"A": wa, "B": wb, "C": wc, "o": wo, "2": w2}

    def place_n(q, m, k):
        return full[q].at[c, at.band(q, m, k)]

    firsts, lasts = {}, {}

    def pass_on(q, m):
        spot = place_n(q, 4 - m, 0)
        for k in (1, 3):
            lasts[q, m, k] = net.send(spot, spot, at.last(q, k))
        net.send(spot, spot, sib, ("sib", q))

    def begin(q, *parts):
        spot = place_n(q, 0, 0)
        spot[...] = jnp.concatenate(parts, axis=1) if len(parts) > 1 else parts[0]
        for k in (1, 3, 2):
            firsts[q, k] = net.send(spot, spot, at.first(q, k))
        pass_on(q, 0)

    def relay(q, m):
        firsts[q, m].wait_recv()
        pass_on(q, m)

    def arrive(q, m, k):
        lasts[q, m, k].wait_recv()
        spot = place_n(q, 4 - m, 4 - k)
        if k == (1 if m % 2 == 0 else 3):
            lasts[q, m, 2] = net.send(spot, spot, at.last(q, k))
        net.send(spot, spot, sib, ("sib", q))

    def arrive_far(q, m):
        lasts[q, m, 2].wait_recv()
        spot = place_n(q, 4 - m, 2)
        net.send(spot, spot, sib, ("sib", q))

    def place_z(w, m, k):
        unit = 96 if w == "o" else 336
        return full[w].at[c, rows(unit * at.order(m, k), unit)]

    def pass_z(w, m):
        spot = place_z(w, m, 0)
        for k in (1, 3):
            lasts[w, m, k] = net.send(spot, spot, at.up(k))
        net.send(spot, spot, sib, ("sib", w))

    def arrive_z(w, m, k):
        lasts[w, m, k].wait_recv()
        spot = place_z(w, m, 4 - k)
        if k == (1 if m == 0 else 3):
            lasts[w, m, 2] = net.send(spot, spot, at.up(k))
        net.send(spot, spot, sib, ("sib", w))

    def arrive_z_far(w, m):
        lasts[w, m, 2].wait_recv()
        spot = place_z(w, m, 2)
        net.send(spot, spot, sib, ("sib", w))

    picked = pick(0, stage_a)
    begin("A", picked[0:48], picked[48:96, 0:RIGHT])
    net.wait_group("one", row_z.at[0:3], sib)
    for k in (1, 3, 2):
        net.send(row_z, stage_z.at[at.two], at.last("B", k), "two")
    stage_z[at.two] = row_z[...]
    relay("A", 1)
    relay("A", 3)
    for k in (1, 3):
        arrive("A", 0, k)
    picked = pick(1, stage_b)
    relay("A", 2)
    begin("B", picked[0:48], picked[48:96, 0:384])
    begin("C", picked[48:96, 384:768])
    net.wait_group("two", stage_z.at[0:3], sib)
    for m in range(2):
        staged = []
        for x in (m, 2 + m):
            block = jnp.where(c == 0, stage_z[x].astype(F32), stage_z[:, x].astype(F32))
            staged.append(block.reshape(256, COLS).astype(BF))
        picked_z = mm(pick_z[...], jnp.concatenate(staged, axis=0)).astype(BF)
        place_z("o", m, 0)[...] = picked_z[:96]
        place_z("2", m, 0)[...] = picked_z[96:]
        pass_z("o", m)
        pass_z("2", m)
    for m in (1, 3):
        for k in (1, 3):
            arrive("A", m, k)
    arrive_far("A", 0)
    relay("B", 1)
    relay("B", 3)
    for k in (1, 3):
        arrive("A", 2, k)
    relay("B", 2)
    for m in (1, 3, 2):
        relay("C", m)
    for k in (1, 3):
        arrive("B", 0, k)
    for w in ("o", "2"):
        for k in (1, 3):
            arrive_z(w, 0, k)
    arrive_far("A", 1)
    for k in (1, 3):
        arrive_z("o", 1, k)
    arrive_far("A", 3)
    for k in (1, 3):
        arrive("B", 1, k)
    arrive_far("A", 2)
    for k in (1, 3):
        arrive("B", 3, k)

    tasks = []

    def plan(kind, *steps_):
        for step in steps_:
            tasks.append((kind, step))

    for k in (1, 3):
        plan("B", partial(arrive, "B", 2, k))
    for k in (1, 3):
        plan("2", partial(arrive_z, "2", 1, k))
    for m in ORDER:
        for k in (1, 3):
            plan("C", partial(arrive, "C", m, k))
    for m in (0, 1):
        plan("o", partial(arrive_z_far, "o", m))
    for q in ("B", "C"):
        for m in ORDER:
            plan(q, partial(arrive_far, q, m))
    for m in (0, 1):
        plan("2", partial(arrive_z_far, "2", m))

    def work(count=1000):
        for _ in range(min(count, len(tasks))):
            tasks.pop(0)[1]()

    def need(q):
        while any(kind == q for kind, _ in tasks):
            work(1)
        net.wait_group(("sib", q), full[q].at[1 - c], sib)

    need("A")

    lanes = lax.broadcasted_iota(jnp.int32, (1, 128), 1)
    left_head = lanes < 64
    token = lax.broadcasted_iota(jnp.int32, (TOK, 1), 0)

    def shift_down(value):
        return jnp.where(token == 0, 0.0, pltpu.roll(value, 1, 0))

    def shift_up(value):
        return jnp.where(token == TOK - 1, 0.0, pltpu.roll(value, TOK - 1, 0))

    def mean(value):
        return jnp.mean(value, axis=-1, keepdims=True)

    def tsum(value):
        return jnp.sum(value, axis=0, keepdims=True)

    def unspread(value):
        a, b, d = split(value, 3)
        return mm_t(a, spread[...]) + (mm_t(b, spread[...]) + mm_t(d, spread[...]))

    vec = mm_t(eye, wa[1, :, VEC:1664])
    gain1, bias1 = vec[0:1], vec[1:2]
    lerps = [vec[2 + i : 3 + i] for i in range(4)]
    gain2, bias2, lerp_h, lerp_g = vec[6:7], vec[7:8], vec[8:9], vec[9:10]
    heads = mm_t(vec.astype(BF), spread[...])
    rate, bonus, gain_w, bias_w = heads[10:11], heads[11:12], heads[12:13], heads[13:14]

    pair_rows = lax.broadcasted_iota(jnp.int32, (256, 128), 0)
    pair_cols = lax.broadcasted_iota(jnp.int32, (256, 128), 1)
    pair_ones = ((lax.rem(pair_rows, 128) // 64) == (pair_cols // 64)).astype(F32).astype(BF)
    below = lax.rem(pair_rows, 128) > pair_cols

    def head_sum(value):
        found = []
        for g in range(6):
            part = value[:, 128 * g : 128 * g + 128]
            found.append(mm(jnp.concatenate(split(part, 2), axis=1), pair_ones))
        return jnp.concatenate(found, axis=1)

    def stack(value):
        return jnp.concatenate(
            [jnp.where(left_head, value, 0.0), jnp.where(left_head, 0.0, value)], axis=0
        )

    def beside(value):
        return jnp.concatenate([value[:TOK], value[TOK:]], axis=1)

    work(2)
    normed = unit1 * gain1 + bias1
    previous = shift_down(normed)
    blended = [(normed * l + previous * (1.0 - l)).astype(BF) for l in lerps]
    for i in range(4):
        turned[i] = blended[i].astype(F32).T.astype(BF)
    recept = mm(blended[0], wa[0, :, 0:768])
    keys = mm(blended[1], wa[0, :, 768:1536])
    vals = mm(blended[2], wa[1, :, 0:768])
    gate_pre = mm(blended[3], wa[1, :, 768:1536])
    work(12)

    fade = -jnp.exp(rate)
    steps = token.astype(F32)
    fall_r = jnp.exp(steps * fade)
    fall_k = jnp.exp(-(steps + 1.0) * fade)
    recept_f = recept * fall_r
    keys_f = keys * fall_k
    present = head_sum(recept * bonus * keys)
    parts = []
    for g in range(6):
        cut = slice(128 * g, 128 * g + 128)
        rg, kg, vg = recept_f[:, cut], keys_f[:, cut], vals[:, cut]
        sc = jnp.where(below, fine(NT, stack(rg), kg), 0.0)
        scores[g] = sc
        parts.append(fine(NN, beside(sc), stack(vg)) + fine(NN, rg, memory[g]))
        if g in (3, 5):
            work(4)
    wkv = jnp.concatenate(parts, axis=1) + present * vals

    centred_w = wkv - head_sum(wkv) * (1.0 / 64.0)
    scale_w = lax.rsqrt(head_sum(centred_w * centred_w) * (1.0 / 64.0) + GROUP_EPS)
    unit_w = centred_w * scale_w
    grouped = unit_w * gain_w + bias_w
    sig = 1.0 / (1.0 + jnp.exp(-gate_pre))
    silu = gate_pre * sig
    gated = (grouped * silu).astype(BF)
    turned_w[...] = gated.astype(F32).T.astype(BF)
    need("o")
    middle = tokens + jnp.concatenate([mm(gated, wo[0]), mm(gated, wo[1])], axis=1)

    work()

    centred = middle - mean(middle)
    scale2 = lax.rsqrt(mean(centred * centred) + NORM_EPS)
    unit2 = centred * scale2
    normed2 = unit2 * gain2 + bias2
    previous2 = shift_down(normed2)
    mixed_h = (normed2 * lerp_h + previous2 * (1.0 - lerp_h)).astype(BF)
    mixed_g = (normed2 * lerp_g + previous2 * (1.0 - lerp_g)).astype(BF)
    turned_h[...] = mixed_h.astype(F32).T.astype(BF)
    turned_g[...] = mixed_g.astype(F32).T.astype(BF)
    need("B")
    halves = (1 - c, c)
    pre_s = jnp.maximum(mm(mixed_h, wa[0, :, 1536:1664]), 0.0)
    hidden_s = (pre_s * pre_s).astype(BF)
    for h in halves:
        pre = jnp.maximum(mm(mixed_h, wb[h]), 0.0)
        pre_h[h] = pre
        hid_h[h] = (pre * pre).astype(BF)
    need("C")
    gating = jnp.concatenate([mm(mixed_g, wc[0]), mm(mixed_g, wc[1])], axis=1)
    gating = 1.0 / (1.0 + jnp.exp(-gating))
    grad_vo = upstream * gating
    for h in range(2):
        gvo_h[h] = grad_vo[:, COLS * h : COLS * h + COLS].astype(BF)

    swaps = {}

    def fold(mine, other, *more):
        total = wide(mine) + wide(other)
        for ref in more:
            total += wide(ref)
        return total

    gr, go = wb.at[:, :, 0:768], wb.at[:, :, 768:1152]
    gk, gc = wa.at[:, :, 768:1664], wc
    grads = {"R": gr, "K": gk, "B": gb, "S": gc}
    sib_of = {"R": sib_r, "K": sib_k, "B": sib_b, "S": sib_c}
    relay_of = {"R": relay_r, "K": relay_k, "B": relay_b, "S": relay_c}
    last_of = {"R": last_r, "K": last_k, "B": last_b, "S": last_c}
    first_of = {"R": first_r, "K": first_k, "B": first_b, "S": first_c}
    acc_of = {"R": acc_r, "K": acc_k, "B": acc_b, "S": acc_c}

    def swap(q):
        swaps[q] = net.send(grads[q].at[1 - c], sib_of[q], sib)

    def swapped(q):
        if q in swaps:
            swaps.pop(q).wait_recv()

    def scatter_far(q, m):
        part = at.band(q, m, 2)
        via = 1 if m % 2 == 0 else 3
        swapped(q)
        spot = sib_of[q].at[part]
        spot[...] = fold(grads[q].at[c, part], spot).astype(BF)
        lasts["g", q, m, 2] = net.send(spot, relay_of[q].at[m], at.last(q, via))

    def scatter_near(q, m, k):
        part = at.band(q, m, k)
        spot = sib_of[q].at[part]
        more = []
        if k == (1 if m % 2 == 0 else 3):
            lasts["g", q, m, 2].wait_recv()
            more = [relay_of[q].at[m]]
        spot[...] = fold(grads[q].at[c, part], spot, *more).astype(BF)
        lasts["g", q, m, k] = net.send(spot, last_of[q].at[k // 2, m], at.last(q, k))

    def scatter_own(q, m):
        part = at.band(q, m, 0)
        spot = sib_of[q].at[part]
        lasts["g", q, m, 1].wait_recv()
        lasts["g", q, m, 3].wait_recv()
        arrived = last_of[q]
        total = fold(grads[q].at[c, part], spot, arrived.at[0, m], arrived.at[1, m])
        if m == 0:
            acc_of[q][...] = total
        else:
            spot[...] = total.astype(BF)
            firsts["g", q, m] = net.send(spot, first_of[q].at[m - 1], at.first(q, m))

    def scatter_end(q):
        total = acc_of[q][...]
        for m in (1, 3, 2):
            firsts["g", q, m].wait_recv()
            total += wide(first_of[q].at[m - 1])
        acc_of[q][...] = total

    def spread_lines(i, left, right, piece, line):
        right = jnp.concatenate([right, jnp.zeros((48, LEFT - RIGHT), F32)], axis=1)
        table = jnp.concatenate([left, right], axis=0).astype(BF)
        piece[...] = mm(turn_n[...], table).astype(BF).reshape(8, 16, LEFT)
        for k in range(1, 8):
            mate, index, _ = at.line(k)
            net.send(piece.at[index], line.at[own], mate, ("grad lines", i))
        line[own] = piece[own]

    def sum_lines(i, line):
        net.wait_group(("grad lines", i), line.at[0:7], sib)
        for h in range(2):
            total = wide(line.at[h])
            for z in (1, 2, 3):
                total += wide(line.at[2 * z + h])
            end_n[h, i] = total

    def scatter_steps(q):
        steps_ = [partial(scatter_far, q, m) for m in ORDER]
        for late in (False, True):
            for m in ORDER:
                for k in (1, 3):
                    if late == (k == (1 if m % 2 == 0 else 3)):
                        steps_.append(partial(scatter_near, q, m, k))
        steps_ += [partial(scatter_own, q, m) for m in (1, 3, 2, 0)]
        steps_.append(partial(scatter_end, q))
        return steps_

    z_parts = {
        "o": (96, go, sib_o, relay_o, up_o, sum_z.at[:, 0:96]),
        "2": (336, w2, sib_2, relay_2, up_2, sum_z.at[:, 96:432]),
    }

    def swap_w(w):
        unit, mine, theirs = z_parts[w][:3]
        swaps[w] = net.send(mine.at[1 - c], theirs, sib)

    def part_w(w, m, k):
        unit = z_parts[w][0]
        return rows(unit * at.order(m, k), unit)

    def scatter_far_w(w, m):
        unit, mine, theirs, relayed = z_parts[w][:4]
        part = part_w(w, m, 2)
        swapped(w)
        spot = theirs.at[part]
        spot[...] = fold(mine.at[c, part], spot).astype(BF)
        lasts["g", w, m, 2] = net.send(spot, relayed.at[m], at.up(1 if m == 0 else 3))

    def scatter_near_w(w, m, k):
        unit, mine, theirs, relayed, arrived = z_parts[w][:5]
        part = part_w(w, m, k)
        more = []
        if k == (1 if m == 0 else 3):
            lasts["g", w, m, 2].wait_recv()
            more = [relayed.at[m]]
        spot = theirs.at[part]
        spot[...] = fold(mine.at[c, part], spot, *more).astype(BF)
        lasts["g", w, m, k] = net.send(spot, arrived.at[k // 2, m], at.up(k))

    def scatter_own_w(w, m):
        unit, mine, theirs, relayed, arrived, sums = z_parts[w]
        part = part_w(w, m, 0)
        lasts["g", w, m, 1].wait_recv()
        lasts["g", w, m, 3].wait_recv()
        total = fold(mine.at[c, part], theirs.at[part], arrived.at[0, m], arrived.at[1, m])
        sums[m] = total.astype(BF)

    def scatter_steps_w(w):
        steps_ = [partial(scatter_far_w, w, 0), partial(scatter_far_w, w, 1)]
        steps_ += [partial(scatter_near_w, w, 1, 1), partial(scatter_near_w, w, 0, 3)]
        steps_ += [partial(scatter_near_w, w, 0, 1), partial(scatter_near_w, w, 1, 3)]
        steps_ += [partial(scatter_own_w, w, 0), partial(scatter_own_w, w, 1)]
        return steps_

    need("2")
    gathered = net.sends
    steps_2, steps_o = scatter_steps_w("2"), scatter_steps_w("o")
    steps_b, steps_c = scatter_steps("B"), scatter_steps("S")
    steps_r, steps_k = scatter_steps("R"), scatter_steps("K")

    def run(*steps_):
        for step in steps_:
            step()

    for h in halves:
        part = rows(128 + 1280 * h, 1280)
        grad_hidden = mm_t(gvo_h[0], w2[0, part]) + mm_t(gvo_h[1], w2[1, part])
        gp_h[h] = (grad_hidden * 2.0 * pre_h[h]).astype(BF)
    grad_hidden = mm_t(gvo_h[0], w2[0, 0:128]) + mm_t(gvo_h[1], w2[1, 0:128])
    grad_pre_s = (grad_hidden * 2.0 * pre_s).astype(BF)
    value_out = jnp.concatenate(
        [
            mm(hidden_s, w2[n, 0:128]) + mm(hid_h[0], w2[n, 128:1408]) + mm(hid_h[1], w2[n, 1408:2688])
            for n in range(2)
        ],
        axis=1,
    )
    layer_out = middle + gating * value_out
    net.drain(gathered)
    for n in halves:
        w2[n, 0:128] = t_mm(hidden_s, gvo_h[n]).astype(BF)
        w2[n, 128:1408] = t_mm(hid_h[0], gvo_h[n]).astype(BF)
        w2[n, 1408:2688] = t_mm(hid_h[1], gvo_h[n]).astype(BF)
        if n is halves[0]:
            swap_w("2")
    for h in halves:
        gb[h] = mm(turned_h[...], gp_h[h]).astype(BF)
        if h is halves[0]:
            swap("B")
    run(*steps_2[:4])
    grad_gp = (grad_vo * value_out * (1.0 - gating)).astype(BF)
    grad_mg = mm_t(grad_gp[:, :COLS], wc[0]) + mm_t(grad_gp[:, COLS:], wc[1])
    for h in range(2):
        gc[h] = mm(turned_g[...], grad_gp[:, COLS * h : COLS * h + COLS]).astype(BF)
    swap("S")
    run(*steps_b[:8])
    grad_mh = mm_t(grad_pre_s, wa[0, :, 1536:1664])
    grad_mh += mm_t(gp_h[0], wb[0]) + mm_t(gp_h[1], wb[1])
    gk[0, :, 768:896] = mm(turned_h[...], grad_pre_s).astype(BF)
    run(*steps_c[:8])

    grad_n2 = grad_mh * lerp_h + grad_mg * lerp_g
    grad_n2 += shift_up(grad_mh * (1.0 - lerp_h) + grad_mg * (1.0 - lerp_g))
    delta2 = normed2 - previous2
    g_lerp_h, g_lerp_g = tsum(grad_mh * delta2), tsum(grad_mg * delta2)
    g_gain2, g_bias2 = tsum(grad_n2 * unit2), tsum(grad_n2)
    q2 = grad_n2 * gain2
    grad_middle = upstream + scale2 * (q2 - mean(q2) - unit2 * mean(q2 * unit2))

    grad_attn = grad_middle.astype(BF)
    grad_gated = mm_t(grad_attn[:, :COLS], wo[0]) + mm_t(grad_attn[:, COLS:], wo[1])
    for h in range(2):
        go[h] = mm(turned_w[...], grad_attn[:, COLS * h : COLS * h + COLS]).astype(BF)
    swap_w("o")
    grad_gate = (grad_gated * grouped * (sig * (1.0 + gate_pre * (1.0 - sig)))).astype(BF)
    grad_grouped = grad_gated * silu
    g_gain_w, g_bias_w = tsum(grad_grouped * unit_w), tsum(grad_grouped)
    qw = grad_grouped * gain_w
    grad_wkv = scale_w * (
        qw
        - head_sum(qw) * (1.0 / 64.0)
        - unit_w * (head_sum(qw * unit_w) * (1.0 / 64.0))
    )

    weight = head_sum(grad_wkv * vals)
    parts_r, parts_k, parts_v = [], [], []
    for g in range(6):
        cut = slice(128 * g, 128 * g + 128)
        rg, kg, vg, dg = recept_f[:, cut], keys_f[:, cut], vals[:, cut], grad_wkv[:, cut]
        ds = stack(dg)
        da = jnp.where(below, fine(NT, ds, vg), 0.0)
        parts_r.append(fine(NN, beside(da), stack(kg)) + fine(NT, dg, memory[g]))
        parts_k.append(fine(TN, da, stack(rg)))
        parts_v.append(fine(TN, scores[g], ds))
        if g == 2:
            run(*steps_o[:4])
        if g == 4:
            run(*steps_b[8:12])
    grad_r = jnp.concatenate(parts_r, axis=1) * fall_r
    grad_k = jnp.concatenate(parts_k, axis=1) * fall_k
    grad_v = jnp.concatenate(parts_v, axis=1) + grad_wkv * present
    g_rate = fade * tsum(steps * recept * grad_r - (steps + 1.0) * keys * grad_k)
    g_bonus = tsum(recept * keys * weight)
    grad_r = (grad_r + bonus * keys * weight).astype(BF)
    grad_k = (grad_k + bonus * recept * weight).astype(BF)
    grad_v = grad_v.astype(BF)

    gr[0] = mm(turned[0], grad_r).astype(BF)
    gr[1] = mm(turned[2], grad_v).astype(BF)
    swap("R")
    grad_blended = [
        mm_t(grad_r, wa[0, :, 0:768]),
        mm_t(grad_k, wa[0, :, 768:1536]),
        mm_t(grad_v, wa[1, :, 0:768]),
        mm_t(grad_gate, wa[1, :, 768:1536]),
    ]
    gk[0, :, 0:768] = mm(turned[1], grad_k).astype(BF)
    gk[1, :, 0:768] = mm(turned[3], grad_gate).astype(BF)
    run(*steps_2[4:6], *steps_r[:8])
    delta = normed - previous
    g_lerps = [tsum(g * delta) for g in grad_blended]
    grad_n1 = sum(g * l for g, l in zip(grad_blended, lerps))
    grad_n1 += shift_up(sum(g * (1.0 - l) for g, l in zip(grad_blended, lerps)))
    g_gain1, g_bias1 = tsum(grad_n1 * unit1), tsum(grad_n1)

    zero = jnp.zeros((1, EMB), F32)
    natural = jnp.concatenate([g_rate, g_bonus, g_gain_w, g_bias_w] + [zero] * 4, axis=0)
    va, vb, vc = split(natural, 3)
    moved = mm(va, spread[...]) + (mm(vb, spread[...]) + mm(vc, spread[...]))
    table = jnp.concatenate(
        [g_gain1, g_bias1] + g_lerps + [g_gain2, g_bias2, g_lerp_h, g_lerp_g]
        + [moved[0:4], jnp.zeros((114, EMB), F32)],
        axis=0,
    )
    gk[1, :, 768:896] = table.T.astype(BF)
    swap("K")
    run(*steps_c[8:12], *steps_b[12:16], *steps_k[:8], *steps_o[4:6], *steps_r[8:12])
    out_v, grad_v_ = pre_h.at[0, :, 0:768], pre_h.at[1, :, 0:768]
    out_v[...] = unspread(layer_out)
    out_copy = pltpu.make_async_copy(out_v, out_ref, load_sems.at[8])
    out_copy.start()
    run(*steps_c[12:16], *steps_k[8:12], *steps_2[6:8])

    def spread_z(m):
        table = mm(turn_z[...], sum_z[m])
        for xhi in range(2):
            for y in range(4):
                x = xhi * 2 + m
                at_ = (xhi * 4 + y) * 64
                piece_z[at.by_core(x, y), at.by_core(y, x)] = table[at_ : at_ + 64].astype(BF)

    run(*steps_o[6:8])
    spread_z(0)
    spread_z(1)
    for k in (1, 3, 2):
        net.send(piece_z.at[rem4(at.two + k)], across_z.at[k - 1], at.last("B", k), "grad two")
    run(steps_b[16])
    q1 = grad_n1 * gain1
    grad_x = grad_middle + scale1 * (q1 - mean(q1) - unit1 * mean(q1 * unit1))
    grad_v_[...] = unspread(grad_x)
    grad_copy = pltpu.make_async_copy(grad_v_, in_grad_ref, load_sems.at[9])
    grad_copy.start()
    run(*steps_r[12:16], *steps_k[12:16], steps_c[16])
    spread_lines(
        1, acc_b[:, 0:LEFT], jnp.concatenate([acc_b[:, LEFT:], acc_c[...]], axis=1), piece_b, line_b
    )
    net.wait_group("grad two", across_z, sib)
    total = wide(piece_z.at[at.two])
    for k in (1, 2, 3):
        total += wide(across_z.at[k - 1])
    row_f[...] = total
    row_b[...] = row_f[...].astype(BF)
    for k in (1, 2, 3):
        net.send(row_b.at[rem4(at.one + k)], side_z.at[k - 1], at.first("B", k), "grad one")
    run(steps_r[16], steps_k[16])
    acc_a = jnp.concatenate([acc_r[...], acc_k[...]], axis=1)
    spread_lines(0, acc_a[:, 0:LEFT], acc_a[:, LEFT:], piece_a, line_a)
    sum_lines(1, line_b)
    net.wait_group("grad one", side_z, sib)
    total = row_f[at.one]
    for k in (1, 2, 3):
        total += wide(side_z.at[k - 1])
    swap_f[...] = total
    away, kept = rows(32 * (1 - c), 32, 8), rows(32 * c, 32, 8)
    last_swap = net.send(swap_f.at[away], swapped_z.at[c], sib)
    swapped_z[c] = swap_f[kept]
    last_swap.wait_recv()
    columns = jnp.concatenate(
        [
            jnp.concatenate([swapped_z[0], swapped_z[1]], axis=1),
            jnp.concatenate([end_n[0, 1, 8:16, 384:768], end_n[1, 1, 8:16, 384:768]], axis=1),
        ],
        axis=0,
    )
    end_z[...] = unspread(columns)
    out_copy.wait()
    grad_copy.wait()
    sum_lines(0, line_a)
    net.drain()


def layer(*operands):
    bf = lambda *shape: pltpu.VMEM(shape, BF)
    f32 = lambda *shape: pltpu.VMEM(shape, F32)
    a, b, d, r, k = (WIDTH[q] for q in "ABCRK")
    return pl.pallas_call(
        layer_kernel,
        out_shape=(
            jax.ShapeDtypeStruct((TOK, EMB), F32),
            jax.ShapeDtypeStruct((TOK, EMB), F32),
            jax.ShapeDtypeStruct((2, 2, 16, LEFT), F32),
            jax.ShapeDtypeStruct((40, EMB), F32),
        ),
        in_specs=[pl.BlockSpec(memory_space=pl.ANY)] * 8 + [VMEM] * (len(operands) - 8),
        out_specs=(pl.BlockSpec(memory_space=pl.ANY),) * 2 + (VMEM,) * 2,
        scratch_shapes=[
            bf(TOK, EMB), bf(TOK, EMB), f32(12, 64, 64), bf(EMB, EMB),
            bf(96, 128), bf(432, 512), bf(128, 96), bf(512, 432), f32(6, 128, 128),
            bf(2, EMB, a), bf(2, EMB, b), bf(2, EMB, d), bf(2, EMB, COLS), bf(2, FF, COLS),
            bf(2, EMB, b), f32(6, 256, 128),
            f32(128, 128), f32(2, 2, 16, LEFT), bf(2, 2, 16, LEFT), bf(8, 16, LEFT), bf(8, 16, LEFT),
            f32(48, EMB), bf(2, 32, COLS), bf(2, 32, COLS), bf(4, 2, 32, COLS), bf(4, 4, 2, 32, COLS),
            *(bf(EMB, w) for w in (r, k, b, d)), *(bf(4, 48, w) for w in (r, k, b, d)),
            *(bf(2, 4, 48, w) for w in (r, k, b, d)), *(bf(3, 48, w) for w in (r, k, b, d)),
            *(f32(48, w) for w in (r, k, b, d)),
            bf(8, 16, LEFT), bf(8, 16, LEFT), bf(8, 16, LEFT), bf(8, 16, LEFT),
            bf(EMB, COLS), bf(FF, COLS),
            bf(2, 96, COLS), bf(2, 336, COLS), bf(2, 2, 96, COLS), bf(2, 2, 336, COLS),
            bf(2, 432, COLS),
            bf(4, 4, 64, COLS), bf(3, 4, 64, COLS), f32(4, 64, COLS), bf(4, 64, COLS), bf(3, 64, COLS),
            f32(64, COLS), f32(2, 32, COLS),
            f32(2, TOK, b), bf(2, TOK, b), bf(2, TOK, b), bf(2, TOK, COLS),
            bf(4, EMB, TOK), bf(EMB, TOK), bf(EMB, TOK), bf(EMB, TOK),
            pltpu.SemaphoreType.DMA((SENDS,)),
            pltpu.SemaphoreType.DMA((ARRIVALS,)),
            pltpu.SemaphoreType.DMA((10,)),
        ],
        compiler_params=pltpu.CompilerParams(
            collective_id=1, has_side_effects=True, vmem_limit_bytes=62 << 20
        ),
        cost_estimate=pl.CostEstimate(
            flops=6 * TOK * 7667712, bytes_accessed=4 * 7667712, transcendentals=10 * TOK * EMB
        ),
        name="layer",
    )(*operands)


def finish_kernel(end_n, end_z, out_in, grad_in, out, grad, *refs):
    vecs, mats = refs[:14], refs[14:]
    acceptor, address, content, sigmoid, mixer, ff_address, ff_content, ff_acceptor = mats
    out[...] = out_in[...]
    grad[...] = grad_in[...]
    acceptor[...] = end_n[0, 0, 0:6, 0:768]
    address[:, 0:128] = end_n[0, 0, 0:6, 768:896]
    address[:, 128:768] = end_n[0, 0, 8:14, 0:640]
    content[...] = end_n[1, 0, 0:6, 0:768]
    sigmoid[:, 0:128] = end_n[1, 0, 0:6, 768:896]
    sigmoid[:, 128:768] = end_n[1, 0, 8:14, 0:640]
    ff_address[:, 0:128] = end_n[0, 0, 8:14, 640:768]
    for h in range(2):
        first_col = 128 + 1280 * h
        ff_address[:, first_col : first_col + 896] = end_n[h, 1, 0:6, 0:896]
        ff_address[:, first_col + 896 : first_col + 1280] = end_n[h, 1, 8:14, 0:384]
    table = jnp.concatenate([end_n[1, 0, 8:16, 640:768], jnp.zeros((120, 128), F32)], axis=0).T
    for i, ref in enumerate(vecs):
        ref[...] = table[i : i + 1, 0:6].reshape(6)
    mixer[...] = end_z[0:6]
    ff_content[...] = end_z[8:29]
    ff_acceptor[...] = end_z[32:38]


def finish(end_n, end_z, out, grad):
    shapes = [(TOK, EMB), (TOK, EMB)] + [(6,)] * 14
    shapes += [(6, EMB)] * 5 + [(6, FF), (21, EMB), (6, EMB)]
    return pl.pallas_call(
        finish_kernel,
        out_shape=tuple(jax.ShapeDtypeStruct(shape, F32) for shape in shapes),
        in_specs=[VMEM] * 4,
        out_specs=(VMEM,) * len(shapes),
        name="finish",
    )(end_n, end_z, out, grad)


def per_device(
    incoming_activations,
    sequence_opening_memory,
    prior_standardize_factor,
    prior_standardize_offset,
    acceptor_lerp_factor,
    address_lerp_factor,
    content_lerp_factor,
    sigmoid_lerp_factor,
    acceptor_matrix,
    address_matrix,
    content_matrix,
    sigmoid_matrix,
    lane_fading_exponent,
    present_reward_vector,
    cluster_standardize_factor,
    cluster_standardize_offset,
    mixer_result_matrix,
    latter_standardize_factor,
    latter_standardize_offset,
    feedforward_address_lerp,
    feedforward_sigmoid_lerp,
    feedforward_address_matrix,
    feedforward_content_matrix,
    feedforward_acceptor_matrix,
    upstream_derivative,
):
    spread = jnp.asarray(_spread(), BF)
    out, in_grad, end_n, end_z = layer(
        incoming_activations, upstream_derivative,
        sequence_opening_memory.reshape(12, 64, 64), spread,
        jnp.asarray(_line_pick(), BF), jnp.asarray(_plane_pick(), BF),
        jnp.asarray(_line_pick().T, BF), jnp.asarray(_plane_pick().T, BF),
        prior_standardize_factor, prior_standardize_offset, acceptor_lerp_factor,
        address_lerp_factor, content_lerp_factor, sigmoid_lerp_factor,
        latter_standardize_factor, latter_standardize_offset, feedforward_address_lerp,
        feedforward_sigmoid_lerp, lane_fading_exponent, present_reward_vector,
        cluster_standardize_factor, cluster_standardize_offset,
        acceptor_matrix, address_matrix, content_matrix, sigmoid_matrix,
        mixer_result_matrix, feedforward_address_matrix, feedforward_content_matrix,
        feedforward_acceptor_matrix,
    )
    results = finish(end_n, end_z, out, in_grad)
    out, in_grad, v = results[0], results[1], results[2:16]
    acceptor, address, content, sigmoid, mixer, ff_address, ff_content, ff_acceptor = results[16:]
    return (
        out, in_grad,
        v[0], v[1], v[2], v[3], v[4], v[5],
        acceptor, address, content, sigmoid,
        v[10], v[11], v[12], v[13],
        mixer,
        v[6], v[7], v[8], v[9],
        ff_address, ff_content, ff_acceptor,
    )


def solution(mesh):
    r, v = P(("dp", "fsdp"), None), P(("dp", "fsdp"))
    state = P(("dp", "fsdp"), None, None, None)
    return jax.shard_map(
        per_device,
        mesh=mesh,
        in_specs=(r, state) + (v,) * 6 + (r,) * 4 + (v,) * 4 + (r,) + (v,) * 4 + (r,) * 4,
        out_specs=(r, r) + (v,) * 6 + (r,) * 4 + (v,) * 4 + (r,) + (v,) * 4 + (r,) * 3,
        check_vma=False,
    )
```

```python
from functools import partial

import jax
import jax.numpy as jnp
import numpy as np
from jax import lax
from jax.experimental import pallas as pl
from jax.experimental.pallas import tpu as pltpu
from jax.sharding import PartitionSpec as P

MESH = pl.DeviceIdType.MESH
BF = jnp.bfloat16
F32 = jnp.float32
VMEM = pl.BlockSpec(memory_space=pltpu.VMEM)

NORM_EPS = 1e-05
GROUP_EPS = 0.00064
TOK = 128
EMB = 768
FF = 2688
COLS = 384
SENDS, ARRIVALS = 96, 160
LEFT, RIGHT = 896, 768

WIDTH = {"A": 1664, "B": 1280, "C": 384, "R": 768, "K": 896}
FIXED = {"S": 0}
VEC = 1536
ORDER = (0, 1, 3, 2)


def _order():
    order = np.zeros(EMB, np.int64)
    for x in range(4):
        for y in range(4):
            for z in range(4):
                for c in range(2):
                    device = z * 32 + (x % 2) * 16 + y * 4 + (x // 2) * 2 + c
                    place = (x * 4 + y) * 48 + (z * 2 + c) * 6
                    order[place : place + 6] = 6 * device + np.arange(6)
    return order


def _spread():
    spread = np.zeros((EMB, EMB), np.float32)
    spread[_order(), np.arange(EMB)] = 1.0
    return spread


def _line_pick():
    pick = np.zeros((96, 128), np.float32)
    for member in range(8):
        for r in range(6):
            pick[member * 6 + r, member * 16 + r] = 1.0
            pick[48 + member * 6 + r, member * 16 + 8 + r] = 1.0
    return pick


def _plane_pick():
    pick = np.zeros((432, 512), np.float32)
    for member in range(16):
        y, xhi, core = member // 4, member // 2 % 2, member % 2
        staged = (xhi * 8 + y * 2 + core) * 32
        for r in range(6):
            pick[member * 6 + r, staged + r] = 1.0
        for r in range(21):
            pick[96 + member * 21 + r, staged + 8 + r] = 1.0
    return pick


def rem4(value):
    return lax.rem(value, 4)


class Place:
    def __init__(self):
        dp, fs = lax.axis_index("dp"), lax.axis_index("fsdp")
        self.z, self.xlo = lax.div(dp, 2), lax.rem(dp, 2)
        self.y, self.xhi = lax.div(fs, 4), lax.rem(lax.div(fs, 2), 2)
        self.c = lax.rem(fs, 2)
        self.x = self.xhi * 2 + self.xlo
        self.one, self.two = self.by_core(self.y, self.x), self.by_core(self.x, self.y)

    def by_core(self, zero, one):
        return zero * (1 - self.c) + one * self.c

    def device(self, z, y, x, c):
        return (z * 2 + lax.rem(x, 2), y * 4 + lax.div(x, 2) * 2 + c)

    def sibling(self):
        return self.device(self.z, self.y, self.x, 1 - self.c)

    def up(self, k):
        return self.device(rem4(self.z + k), self.y, self.x, self.c)

    def line(self, k):
        z = rem4(self.z + k // 2)
        core = self.c if k % 2 == 0 else 1 - self.c
        return self.device(z, self.y, self.x, core), z * 2 + core, core

    def turn(self, q, sibling=False):
        if q in FIXED:
            return FIXED[q]
        return 1 - self.c if sibling else self.c

    def first(self, q, k):
        t = self.turn(q)
        y, x = rem4(self.y + k * (1 - t)), rem4(self.x + k * t)
        return self.device(self.z, y, x, self.c)

    def last(self, q, k):
        t = self.turn(q)
        y, x = rem4(self.y + k * t), rem4(self.x + k * (1 - t))
        return self.device(self.z, y, x, self.c)

    def band(self, q, m, k, sibling=False):
        t = self.turn(q, sibling)
        x = rem4(self.x + m * t + k * (1 - t))
        y = rem4(self.y + m * (1 - t) + k * t)
        return rows(48 * (x * 4 + y), 48)

    def across(self, k):
        return self.device(self.z, self.y, rem4(self.x + k), self.c)

    def side(self, k):
        return self.device(self.z, rem4(self.y + k), self.x, self.c)

    def order(self, m, k):
        return rem4(self.z + k) * 2 + m

    def greet(self):
        mates = [self.line(k)[0] for k in range(1, 8)]
        mates += [self.across(k) for k in (1, 2, 3)]
        mates += [self.side(k) for k in (1, 2, 3)]
        barrier = pltpu.get_barrier_semaphore()
        for mate in mates:
            pl.semaphore_signal(barrier, inc=1, device_id=mate, device_id_type=MESH)
        return lambda: pl.semaphore_wait(barrier, len(mates))


class Sender:
    def __init__(self, send_sems, recv_sems):
        self.send_sems, self.recv_sems = send_sems, recv_sems
        self.sends = self.arrivals = 0
        self.open = []
        self.groups = {}

    def send(self, source, target, device, group=None):
        index = self.sends % SENDS
        if len(self.open) >= SENDS:
            self.open.pop(0).wait_send()
        self.sends += 1
        if group not in self.groups:
            self.groups[group if group is not None else self.sends] = self.arrivals
            arrival = self.arrivals
            self.arrivals += 1
        else:
            arrival = self.groups[group]
        copy = pltpu.make_async_remote_copy(
            src_ref=source,
            dst_ref=target,
            send_sem=self.send_sems.at[index],
            recv_sem=self.recv_sems.at[arrival],
            device_id=device,
            device_id_type=MESH,
        )
        copy.start()
        self.open.append(copy)
        return copy

    def wait_group(self, group, like, device):
        pltpu.make_async_remote_copy(
            src_ref=like,
            dst_ref=like,
            send_sem=self.send_sems.at[0],
            recv_sem=self.recv_sems.at[self.groups[group]],
            device_id=device,
            device_id_type=MESH,
        ).wait_recv()

    def drain(self):
        for copy in self.open:
            copy.wait_send()
        self.open = []


def rows(start, size, unit=16):
    return pl.ds(pl.multiple_of(start, unit), size)


def mm(left, right):
    return jnp.dot(left, right, preferred_element_type=F32)


def mm_t(left, right):
    return lax.dot_general(left, right, (((1,), (1,)), ((), ())), preferred_element_type=F32)


def t_mm(left, right):
    return lax.dot_general(left, right, (((0,), (0,)), ((), ())), preferred_element_type=F32)


def split(value, parts):
    found = []
    for _ in range(parts - 1):
        high = value.astype(BF)
        found.append(high)
        value = value - high.astype(F32)
    found.append(value.astype(BF))
    return found


def fine(dims, left, right):
    lh, ll = split(left, 2)
    rh, rl = split(right, 2)
    dot = partial(lax.dot_general, dimension_numbers=(dims, ((), ())), preferred_element_type=F32)
    return dot(lh, rh) + (dot(lh, rl) + dot(ll, rh))


NN, NT, TN = ((1,), (0,)), ((1,), (1,)), ((0,), (0,))


def wide(ref):
    return ref[...].astype(F32)


def layer_kernel(
    x_in, up_in, state, spread_in, pick_n_in, pick_z_in, turn_n_in, turn_z_in, *refs
):
    vecs, refs = refs[:14], refs[14:]
    (acceptor, address, content, sigmoid, mixer, ff_address, ff_content, ff_acceptor), refs = refs[:8], refs[8:]
    (
        out_ref, in_grad_ref, end_n, end_z,
        x_ref, up_ref, state_v, spread, pick_n, pick_z, turn_n, turn_z, memory,
        wa, wb, wc, wo, w2, gb, scores,
        vec_f, pack_f, pack_n, stage_a, stage_b, cols_f, pack_z, half_z, row_z, stage_z,
        sib_r, sib_k, sib_b, sib_c, relay_r, relay_k, relay_b, relay_c,
        last_r, last_k, last_b, last_c, first_r, first_k, first_b, first_c,
        acc_r, acc_k, acc_b, acc_c,
        piece_a, piece_b, line_a, line_b,
        sib_o, sib_2, relay_o, relay_2, up_o, up_2, sum_z,
        across_z, row_f, row_b, side_z, swap_f, swapped_z,
        pre_h, hid_h, gp_h, gvo_h, turned, turned_w, turned_h, turned_g,
        send_sems, recv_sems, load_sems,
    ) = refs
    at = Place()
    c = at.c
    sib = at.sibling()
    net = Sender(send_sems, recv_sems)
    met = at.greet()

    loads = {}
    for i, (name, source, target) in enumerate([
        ("spread", spread_in, spread), ("x", x_in, x_ref), ("pick_n", pick_n_in, pick_n),
        ("up", up_in, up_ref), ("pick_z", pick_z_in, pick_z), ("state", state, state_v),
        ("turn_n", turn_n_in, turn_n), ("turn_z", turn_z_in, turn_z),
    ]):
        loads[name] = pltpu.make_async_copy(source, target, load_sems.at[i])
        loads[name].start()

    vec_f[...] = jnp.zeros_like(vec_f)
    for i, ref in enumerate(vecs):
        vec_f[i : i + 1, 0:6] = wide(ref).reshape(1, 6)
    eye = (
        lax.broadcasted_iota(jnp.int32, (16, 128), 0)
        == lax.broadcasted_iota(jnp.int32, (16, 128), 1)
    ).astype(F32).astype(BF)
    pack_f[...] = jnp.zeros_like(pack_f)
    pack_f[0, 0, 0:6, 0:768] = wide(acceptor)
    pack_f[0, 0, 0:6, 768:896] = wide(address.at[:, 0:128])
    pack_f[0, 0, 8:14, 0:640] = wide(address.at[:, 128:768])
    pack_f[0, 0, 8:14, 640:768] = wide(ff_address.at[:, 0:128])
    pack_f[1, 0, 0:6, 0:768] = wide(content)
    pack_f[1, 0, 0:6, 768:896] = wide(sigmoid.at[:, 0:128])
    pack_f[1, 0, 8:14, 0:640] = wide(sigmoid.at[:, 128:768])
    pack_f[1, 0, 8:14, 640:768] = mm_t(eye, vec_f[...].astype(BF))[0:6]
    for h in range(2):
        pack_n[0, h] = pack_f[h, 0].astype(BF)
    met()

    own = at.z * 2 + c

    def send_lines(i, stage):
        for k in range(1, 8):
            mate, _, core = at.line(k)
            net.send(pack_n.at[i, core], stage.at[own], mate, ("lines", i))
        stage[own] = pack_n[i, c]

    send_lines(0, stage_a)
    cols_f[...] = jnp.zeros_like(cols_f)
    cols_f[0:6] = wide(mixer)
    cols_f[8:29] = wide(ff_content)
    cols_f[32:38] = wide(ff_acceptor)
    loads["spread"].wait()
    moved = mm(cols_f[...].astype(BF), spread[...])
    for h in range(2):
        pack_z[h] = moved[0:32, COLS * h : COLS * h + COLS].astype(BF)
        first_col = 128 + 1280 * h
        pack_f[h, 1, 0:6, 0:896] = wide(ff_address.at[:, first_col : first_col + 896])
        pack_f[h, 1, 8:14, 0:384] = wide(ff_address.at[:, first_col + 896 : first_col + 1280])
        pack_f[h, 1, 8:16, 384:768] = moved[32:40, COLS * h : COLS * h + COLS]
        pack_n[1, h] = pack_f[h, 1].astype(BF)
    mine_z = rows(32 * c, 32)
    swap_z = net.send(pack_z.at[1 - c], half_z.at[mine_z], sib)
    half_z[mine_z] = pack_z[c]
    send_lines(1, stage_b)

    loads["x"].wait()
    tokens = mm(x_ref[...], spread[...])
    centred = tokens - jnp.mean(tokens, axis=-1, keepdims=True)
    scale1 = lax.rsqrt(jnp.mean(centred * centred, axis=-1, keepdims=True) + NORM_EPS)
    unit1 = centred * scale1
    loads["up"].wait()
    upstream = mm(up_ref[...], spread[...])
    swap_z.wait_recv()
    for k in (1, 2, 3):
        net.send(half_z, row_z.at[at.one], at.first("B", k), "one")
    row_z[at.one] = half_z[...]
    loads["pick_n"].wait()
    for name in ("state", "turn_n", "turn_z", "pick_z"):
        loads[name].wait()
    blank = jnp.zeros((64, 64), F32)
    for g in range(6):
        memory[g, 0:64] = jnp.concatenate([state_v[2 * g], blank], axis=1)
        memory[g, 64:128] = jnp.concatenate([blank, state_v[2 * g + 1]], axis=1)

    def pick(i, stage):
        net.wait_group(("lines", i), stage.at[0:7], sib)
        return mm(pick_n[...], stage[...].reshape(128, LEFT)).astype(BF)

    full = {"A": wa, "B": wb, "C": wc, "o": wo, "2": w2}

    def place_n(q, m, k):
        return full[q].at[c, at.band(q, m, k)]

    firsts, lasts = {}, {}

    def pass_on(q, m):
        spot = place_n(q, 4 - m, 0)
        for k in (1, 3):
            lasts[q, m, k] = net.send(spot, spot, at.last(q, k))
        net.send(spot, spot, sib, ("sib", q))

    def begin(q, *parts):
        spot = place_n(q, 0, 0)
        spot[...] = jnp.concatenate(parts, axis=1) if len(parts) > 1 else parts[0]
        for k in (1, 3, 2):
            firsts[q, k] = net.send(spot, spot, at.first(q, k))
        pass_on(q, 0)

    def relay(q, m):
        firsts[q, m].wait_recv()
        pass_on(q, m)

    def arrive(q, m, k):
        lasts[q, m, k].wait_recv()
        spot = place_n(q, 4 - m, 4 - k)
        if k == (1 if m % 2 == 0 else 3):
            lasts[q, m, 2] = net.send(spot, spot, at.last(q, k))
        net.send(spot, spot, sib, ("sib", q))

    def arrive_far(q, m):
        lasts[q, m, 2].wait_recv()
        spot = place_n(q, 4 - m, 2)
        net.send(spot, spot, sib, ("sib", q))

    def place_z(w, m, k):
        unit = 96 if w == "o" else 336
        return full[w].at[c, rows(unit * at.order(m, k), unit)]

    def pass_z(w, m):
        spot = place_z(w, m, 0)
        for k in (1, 3):
            lasts[w, m, k] = net.send(spot, spot, at.up(k))
        net.send(spot, spot, sib, ("sib", w))

    def arrive_z(w, m, k):
        lasts[w, m, k].wait_recv()
        spot = place_z(w, m, 4 - k)
        if k == (1 if m == 0 else 3):
            lasts[w, m, 2] = net.send(spot, spot, at.up(k))
        net.send(spot, spot, sib, ("sib", w))

    def arrive_z_far(w, m):
        lasts[w, m, 2].wait_recv()
        spot = place_z(w, m, 2)
        net.send(spot, spot, sib, ("sib", w))

    picked = pick(0, stage_a)
    begin("A", picked[0:48], picked[48:96, 0:RIGHT])
    net.wait_group("one", row_z.at[0:3], sib)
    for k in (1, 3, 2):
        net.send(row_z, stage_z.at[at.two], at.last("B", k), "two")
    stage_z[at.two] = row_z[...]
    relay("A", 1)
    relay("A", 3)
    for k in (1, 3):
        arrive("A", 0, k)
    picked = pick(1, stage_b)
    relay("A", 2)
    begin("B", picked[0:48], picked[48:96, 0:384])
    begin("C", picked[48:96, 384:768])
    net.wait_group("two", stage_z.at[0:3], sib)
    for m in range(2):
        staged = []
        for x in (m, 2 + m):
            block = jnp.where(c == 0, stage_z[x].astype(F32), stage_z[:, x].astype(F32))
            staged.append(block.reshape(256, COLS).astype(BF))
        picked_z = mm(pick_z[...], jnp.concatenate(staged, axis=0)).astype(BF)
        place_z("o", m, 0)[...] = picked_z[:96]
        place_z("2", m, 0)[...] = picked_z[96:]
        pass_z("o", m)
        pass_z("2", m)
    for m in (1, 3):
        for k in (1, 3):
            arrive("A", m, k)
    arrive_far("A", 0)
    relay("B", 1)
    relay("B", 3)
    for k in (1, 3):
        arrive("A", 2, k)
    relay("B", 2)
    for m in (1, 3, 2):
        relay("C", m)
    for k in (1, 3):
        arrive("B", 0, k)
    for w in ("o", "2"):
        for k in (1, 3):
            arrive_z(w, 0, k)
    arrive_far("A", 1)
    for k in (1, 3):
        arrive_z("o", 1, k)
    arrive_far("A", 3)
    for k in (1, 3):
        arrive("B", 1, k)
    arrive_far("A", 2)
    for k in (1, 3):
        arrive("B", 3, k)

    tasks = []

    def plan(kind, *steps_):
        for step in steps_:
            tasks.append((kind, step))

    for k in (1, 3):
        plan("B", partial(arrive, "B", 2, k))
    for k in (1, 3):
        plan("2", partial(arrive_z, "2", 1, k))
    for m in ORDER:
        for k in (1, 3):
            plan("C", partial(arrive, "C", m, k))
    for m in (0, 1):
        plan("o", partial(arrive_z_far, "o", m))
    for q in ("B", "C"):
        for m in ORDER:
            plan(q, partial(arrive_far, q, m))
    for m in (0, 1):
        plan("2", partial(arrive_z_far, "2", m))

    def work(count=1000):
        for _ in range(min(count, len(tasks))):
            tasks.pop(0)[1]()

    def need(q):
        while any(kind == q for kind, _ in tasks):
            work(1)
        net.wait_group(("sib", q), full[q].at[1 - c], sib)

    need("A")

    lanes = lax.broadcasted_iota(jnp.int32, (1, 128), 1)
    left_head = lanes < 64
    token = lax.broadcasted_iota(jnp.int32, (TOK, 1), 0)

    def shift_down(value):
        return jnp.where(token == 0, 0.0, pltpu.roll(value, 1, 0))

    def shift_up(value):
        return jnp.where(token == TOK - 1, 0.0, pltpu.roll(value, TOK - 1, 0))

    def mean(value):
        return jnp.mean(value, axis=-1, keepdims=True)

    def tsum(value):
        return jnp.sum(value, axis=0, keepdims=True)

    def unspread(value):
        a, b, d = split(value, 3)
        return mm_t(a, spread[...]) + (mm_t(b, spread[...]) + mm_t(d, spread[...]))

    vec = mm_t(eye, wa[1, :, VEC:1664])
    gain1, bias1 = vec[0:1], vec[1:2]
    lerps = [vec[2 + i : 3 + i] for i in range(4)]
    gain2, bias2, lerp_h, lerp_g = vec[6:7], vec[7:8], vec[8:9], vec[9:10]
    heads = mm_t(vec.astype(BF), spread[...])
    rate, bonus, gain_w, bias_w = heads[10:11], heads[11:12], heads[12:13], heads[13:14]

    pair_rows = lax.broadcasted_iota(jnp.int32, (256, 128), 0)
    pair_cols = lax.broadcasted_iota(jnp.int32, (256, 128), 1)
    pair_ones = ((lax.rem(pair_rows, 128) // 64) == (pair_cols // 64)).astype(F32).astype(BF)
    below = lax.rem(pair_rows, 128) > pair_cols

    def head_sum(value):
        found = []
        for g in range(6):
            part = value[:, 128 * g : 128 * g + 128]
            found.append(mm(jnp.concatenate(split(part, 2), axis=1), pair_ones))
        return jnp.concatenate(found, axis=1)

    def stack(value):
        return jnp.concatenate(
            [jnp.where(left_head, value, 0.0), jnp.where(left_head, 0.0, value)], axis=0
        )

    def beside(value):
        return jnp.concatenate([value[:TOK], value[TOK:]], axis=1)

    work(2)
    normed = unit1 * gain1 + bias1
    previous = shift_down(normed)
    blended = [(normed * l + previous * (1.0 - l)).astype(BF) for l in lerps]
    for i in range(4):
        turned[i] = blended[i].astype(F32).T.astype(BF)
    recept = mm(blended[0], wa[0, :, 0:768])
    keys = mm(blended[1], wa[0, :, 768:1536])
    vals = mm(blended[2], wa[1, :, 0:768])
    gate_pre = mm(blended[3], wa[1, :, 768:1536])
    work(12)

    fade = -jnp.exp(rate)
    steps = token.astype(F32)
    fall_r = jnp.exp(steps * fade)
    fall_k = jnp.exp(-(steps + 1.0) * fade)
    recept_f = recept * fall_r
    keys_f = keys * fall_k
    present = head_sum(recept * bonus * keys)
    parts = []
    for g in range(6):
        cut = slice(128 * g, 128 * g + 128)
        rg, kg, vg = recept_f[:, cut], keys_f[:, cut], vals[:, cut]
        sc = jnp.where(below, fine(NT, stack(rg), kg), 0.0)
        scores[g] = sc
        parts.append(fine(NN, beside(sc), stack(vg)) + fine(NN, rg, memory[g]))
        if g in (3, 5):
            work(4)
    wkv = jnp.concatenate(parts, axis=1) + present * vals

    centred_w = wkv - head_sum(wkv) * (1.0 / 64.0)
    scale_w = lax.rsqrt(head_sum(centred_w * centred_w) * (1.0 / 64.0) + GROUP_EPS)
    unit_w = centred_w * scale_w
    grouped = unit_w * gain_w + bias_w
    sig = 1.0 / (1.0 + jnp.exp(-gate_pre))
    silu = gate_pre * sig
    gated = (grouped * silu).astype(BF)
    turned_w[...] = gated.astype(F32).T.astype(BF)
    need("o")
    middle = tokens + jnp.concatenate([mm(gated, wo[0]), mm(gated, wo[1])], axis=1)

    work()

    centred = middle - mean(middle)
    scale2 = lax.rsqrt(mean(centred * centred) + NORM_EPS)
    unit2 = centred * scale2
    normed2 = unit2 * gain2 + bias2
    previous2 = shift_down(normed2)
    mixed_h = (normed2 * lerp_h + previous2 * (1.0 - lerp_h)).astype(BF)
    mixed_g = (normed2 * lerp_g + previous2 * (1.0 - lerp_g)).astype(BF)
    turned_h[...] = mixed_h.astype(F32).T.astype(BF)
    turned_g[...] = mixed_g.astype(F32).T.astype(BF)
    need("B")
    halves = (1 - c, c)
    pre_s = jnp.maximum(mm(mixed_h, wa[0, :, 1536:1664]), 0.0)
    hidden_s = (pre_s * pre_s).astype(BF)
    for h in halves:
        pre = jnp.maximum(mm(mixed_h, wb[h]), 0.0)
        pre_h[h] = pre
        hid_h[h] = (pre * pre).astype(BF)
    need("C")
    gating = jnp.concatenate([mm(mixed_g, wc[0]), mm(mixed_g, wc[1])], axis=1)
    gating = 1.0 / (1.0 + jnp.exp(-gating))
    grad_vo = upstream * gating
    for h in range(2):
        gvo_h[h] = grad_vo[:, COLS * h : COLS * h + COLS].astype(BF)

    def grad_w2(target, low, high, h):
        for start, width, part in ((0, 128, None), (128, 1280, 0), (1408, 1280, 1)):
            a, b = max(low, start), min(high, start + width)
            if a < b:
                cut_ = slice(a - start, b - start)
                left = hidden_s[:, cut_] if part is None else hid_h[part, :, cut_]
                target[a - low : b - low] = t_mm(left, gvo_h[h]).astype(BF)

    for spot, low, high in (
        (gb.at[1, :, 0:384], 0, 768),
        (gb.at[1, :, 384:768], 768, 1536),
        (gb.at[1, :, 768:1152], 1536, 2304),
        (gb.at[0, 0:384, 0:384], 2304, 2688),
    ):
        grad_w2(spot, low, high, 1 - c)
        net.send(spot, sib_2.at[low:high], sib, "swap 2")

    swaps = {"2": partial(net.wait_group, "swap 2", sib_2, sib)}

    def fold(mine, other, *more):
        total = wide(mine) + wide(other)
        for ref in more:
            total += wide(ref)
        return total

    gr, go = wb.at[:, :, 0:768], wb.at[:, :, 768:1152]
    gk, gc = wa.at[:, :, 768:1664], wc
    grads = {"R": gr, "K": gk, "B": gb, "S": gc}
    sib_of = {"R": sib_r, "K": sib_k, "B": sib_b, "S": sib_c}
    relay_of = {"R": relay_r, "K": relay_k, "B": relay_b, "S": relay_c}
    last_of = {"R": last_r, "K": last_k, "B": last_b, "S": last_c}
    first_of = {"R": first_r, "K": first_k, "B": first_b, "S": first_c}
    acc_of = {"R": acc_r, "K": acc_k, "B": acc_b, "S": acc_c}

    def swap(q):
        swaps[q] = net.send(grads[q].at[1 - c], sib_of[q], sib).wait_recv

    def swapped(q):
        if q in swaps:
            swaps.pop(q)()

    def scatter_far(q, m):
        part = at.band(q, m, 2)
        via = 1 if m % 2 == 0 else 3
        swapped(q)
        spot = sib_of[q].at[part]
        spot[...] = fold(grads[q].at[c, part], spot).astype(BF)
        lasts["g", q, m, 2] = net.send(spot, relay_of[q].at[m], at.last(q, via))

    def scatter_near(q, m, k):
        part = at.band(q, m, k)
        spot = sib_of[q].at[part]
        more = []
        if k == (1 if m % 2 == 0 else 3):
            lasts["g", q, m, 2].wait_recv()
            more = [relay_of[q].at[m]]
        spot[...] = fold(grads[q].at[c, part], spot, *more).astype(BF)
        lasts["g", q, m, k] = net.send(spot, last_of[q].at[k // 2, m], at.last(q, k))

    def scatter_own(q, m):
        part = at.band(q, m, 0)
        spot = sib_of[q].at[part]
        lasts["g", q, m, 1].wait_recv()
        lasts["g", q, m, 3].wait_recv()
        arrived = last_of[q]
        total = fold(grads[q].at[c, part], spot, arrived.at[0, m], arrived.at[1, m])
        if m == 0:
            acc_of[q][...] = total
        else:
            spot[...] = total.astype(BF)
            firsts["g", q, m] = net.send(spot, first_of[q].at[m - 1], at.first(q, m))

    def scatter_end(q):
        total = acc_of[q][...]
        for m in (1, 3, 2):
            firsts["g", q, m].wait_recv()
            total += wide(first_of[q].at[m - 1])
        acc_of[q][...] = total

    def spread_lines(i, left, right, piece, line):
        right = jnp.concatenate([right, jnp.zeros((48, LEFT - RIGHT), F32)], axis=1)
        table = jnp.concatenate([left, right], axis=0).astype(BF)
        piece[...] = mm(turn_n[...], table).astype(BF).reshape(8, 16, LEFT)
        for k in range(1, 8):
            mate, index, _ = at.line(k)
            net.send(piece.at[index], line.at[own], mate, ("grad lines", i))
        line[own] = piece[own]

    def sum_lines(i, line):
        net.wait_group(("grad lines", i), line.at[0:7], sib)
        for h in range(2):
            total = wide(line.at[h])
            for z in (1, 2, 3):
                total += wide(line.at[2 * z + h])
            end_n[h, i] = total

    def scatter_steps(q):
        steps_ = [partial(scatter_far, q, m) for m in ORDER]
        for late in (False, True):
            for m in ORDER:
                for k in (1, 3):
                    if late == (k == (1 if m % 2 == 0 else 3)):
                        steps_.append(partial(scatter_near, q, m, k))
        steps_ += [partial(scatter_own, q, m) for m in (1, 3, 2, 0)]
        steps_.append(partial(scatter_end, q))
        return steps_

    z_parts = {
        "o": (96, go, sib_o, relay_o, up_o, sum_z.at[:, 0:96]),
        "2": (336, w2, sib_2, relay_2, up_2, sum_z.at[:, 96:432]),
    }

    def swap_w(w):
        unit, mine, theirs = z_parts[w][:3]
        swaps[w] = net.send(mine.at[1 - c], theirs, sib).wait_recv

    def part_w(w, m, k):
        unit = z_parts[w][0]
        return rows(unit * at.order(m, k), unit)

    def scatter_far_w(w, m):
        unit, mine, theirs, relayed = z_parts[w][:4]
        part = part_w(w, m, 2)
        swapped(w)
        spot = theirs.at[part]
        spot[...] = fold(mine.at[c, part], spot).astype(BF)
        lasts["g", w, m, 2] = net.send(spot, relayed.at[m], at.up(1 if m == 0 else 3))

    def scatter_near_w(w, m, k):
        unit, mine, theirs, relayed, arrived = z_parts[w][:5]
        part = part_w(w, m, k)
        more = []
        if k == (1 if m == 0 else 3):
            lasts["g", w, m, 2].wait_recv()
            more = [relayed.at[m]]
        spot = theirs.at[part]
        spot[...] = fold(mine.at[c, part], spot, *more).astype(BF)
        lasts["g", w, m, k] = net.send(spot, arrived.at[k // 2, m], at.up(k))

    def scatter_own_w(w, m):
        unit, mine, theirs, relayed, arrived, sums = z_parts[w]
        part = part_w(w, m, 0)
        lasts["g", w, m, 1].wait_recv()
        lasts["g", w, m, 3].wait_recv()
        total = fold(mine.at[c, part], theirs.at[part], arrived.at[0, m], arrived.at[1, m])
        sums[m] = total.astype(BF)

    def scatter_steps_w(w):
        steps_ = [partial(scatter_far_w, w, 0), partial(scatter_far_w, w, 1)]
        steps_ += [partial(scatter_near_w, w, 1, 1), partial(scatter_near_w, w, 0, 3)]
        steps_ += [partial(scatter_near_w, w, 0, 1), partial(scatter_near_w, w, 1, 3)]
        steps_ += [partial(scatter_own_w, w, 0), partial(scatter_own_w, w, 1)]
        return steps_

    need("2")
    steps_2, steps_o = scatter_steps_w("2"), scatter_steps_w("o")
    steps_b, steps_c = scatter_steps("B"), scatter_steps("S")
    steps_r, steps_k = scatter_steps("R"), scatter_steps("K")

    def run(*steps_):
        for step in steps_:
            step()

    for h in halves:
        part = rows(128 + 1280 * h, 1280)
        grad_hidden = mm_t(gvo_h[0], w2[0, part]) + mm_t(gvo_h[1], w2[1, part])
        gp_h[h] = (grad_hidden * 2.0 * pre_h[h]).astype(BF)
    net.drain()
    for h in halves:
        gb[h] = mm(turned_h[...], gp_h[h]).astype(BF)
        if h is halves[0]:
            swap("B")
    grad_hidden = mm_t(gvo_h[0], w2[0, 0:128]) + mm_t(gvo_h[1], w2[1, 0:128])
    grad_pre_s = (grad_hidden * 2.0 * pre_s).astype(BF)
    value_out = jnp.concatenate(
        [
            mm(hidden_s, w2[n, 0:128]) + mm(hid_h[0], w2[n, 128:1408]) + mm(hid_h[1], w2[n, 1408:2688])
            for n in range(2)
        ],
        axis=1,
    )
    layer_out = middle + gating * value_out
    grad_w2(w2.at[c], 0, FF, c)
    run(*steps_2[:4], *steps_b[:8])
    grad_gp = (grad_vo * value_out * (1.0 - gating)).astype(BF)
    grad_mg = mm_t(grad_gp[:, :COLS], wc[0]) + mm_t(grad_gp[:, COLS:], wc[1])
    for h in range(2):
        gc[h] = mm(turned_g[...], grad_gp[:, COLS * h : COLS * h + COLS]).astype(BF)
    swap("S")
    grad_mh = mm_t(grad_pre_s, wa[0, :, 1536:1664])
    grad_mh += mm_t(gp_h[0], wb[0]) + mm_t(gp_h[1], wb[1])
    gk[0, :, 768:896] = mm(turned_h[...], grad_pre_s).astype(BF)
    run(*steps_c[:8])

    grad_n2 = grad_mh * lerp_h + grad_mg * lerp_g
    grad_n2 += shift_up(grad_mh * (1.0 - lerp_h) + grad_mg * (1.0 - lerp_g))
    delta2 = normed2 - previous2
    g_lerp_h, g_lerp_g = tsum(grad_mh * delta2), tsum(grad_mg * delta2)
    g_gain2, g_bias2 = tsum(grad_n2 * unit2), tsum(grad_n2)
    q2 = grad_n2 * gain2
    grad_middle = upstream + scale2 * (q2 - mean(q2) - unit2 * mean(q2 * unit2))

    grad_attn = grad_middle.astype(BF)
    grad_gated = mm_t(grad_attn[:, :COLS], wo[0]) + mm_t(grad_attn[:, COLS:], wo[1])
    for h in range(2):
        go[h] = mm(turned_w[...], grad_attn[:, COLS * h : COLS * h + COLS]).astype(BF)
    swap_w("o")
    grad_gate = (grad_gated * grouped * (sig * (1.0 + gate_pre * (1.0 - sig)))).astype(BF)
    grad_grouped = grad_gated * silu
    g_gain_w, g_bias_w = tsum(grad_grouped * unit_w), tsum(grad_grouped)
    qw = grad_grouped * gain_w
    grad_wkv = scale_w * (
        qw
        - head_sum(qw) * (1.0 / 64.0)
        - unit_w * (head_sum(qw * unit_w) * (1.0 / 64.0))
    )

    weight = head_sum(grad_wkv * vals)
    parts_r, parts_k, parts_v = [], [], []
    for g in range(6):
        cut = slice(128 * g, 128 * g + 128)
        rg, kg, vg, dg = recept_f[:, cut], keys_f[:, cut], vals[:, cut], grad_wkv[:, cut]
        ds = stack(dg)
        da = jnp.where(below, fine(NT, ds, vg), 0.0)
        parts_r.append(fine(NN, beside(da), stack(kg)) + fine(NT, dg, memory[g]))
        parts_k.append(fine(TN, da, stack(rg)))
        parts_v.append(fine(TN, scores[g], ds))
        if g == 3:
            run(*steps_b[8:12])
        if g == 5:
            run(*steps_o[:4])
    grad_r = jnp.concatenate(parts_r, axis=1) * fall_r
    grad_k = jnp.concatenate(parts_k, axis=1) * fall_k
    grad_v = jnp.concatenate(parts_v, axis=1) + grad_wkv * present
    g_rate = fade * tsum(steps * recept * grad_r - (steps + 1.0) * keys * grad_k)
    g_bonus = tsum(recept * keys * weight)
    grad_r = (grad_r + bonus * keys * weight).astype(BF)
    grad_k = (grad_k + bonus * recept * weight).astype(BF)
    grad_v = grad_v.astype(BF)

    gr[0] = mm(turned[0], grad_r).astype(BF)
    gr[1] = mm(turned[2], grad_v).astype(BF)
    swap("R")
    grad_blended = [
        mm_t(grad_r, wa[0, :, 0:768]),
        mm_t(grad_k, wa[0, :, 768:1536]),
        mm_t(grad_v, wa[1, :, 0:768]),
        mm_t(grad_gate, wa[1, :, 768:1536]),
    ]
    gk[0, :, 0:768] = mm(turned[1], grad_k).astype(BF)
    gk[1, :, 0:768] = mm(turned[3], grad_gate).astype(BF)
    run(*steps_r[:8], *steps_2[4:6])
    delta = normed - previous
    g_lerps = [tsum(g * delta) for g in grad_blended]
    grad_n1 = sum(g * l for g, l in zip(grad_blended, lerps))
    grad_n1 += shift_up(sum(g * (1.0 - l) for g, l in zip(grad_blended, lerps)))
    g_gain1, g_bias1 = tsum(grad_n1 * unit1), tsum(grad_n1)

    zero = jnp.zeros((1, EMB), F32)
    natural = jnp.concatenate([g_rate, g_bonus, g_gain_w, g_bias_w] + [zero] * 4, axis=0)
    va, vb, vc = split(natural, 3)
    moved = mm(va, spread[...]) + (mm(vb, spread[...]) + mm(vc, spread[...]))
    table = jnp.concatenate(
        [g_gain1, g_bias1] + g_lerps + [g_gain2, g_bias2, g_lerp_h, g_lerp_g]
        + [moved[0:4], jnp.zeros((114, EMB), F32)],
        axis=0,
    )
    gk[1, :, 768:896] = table.T.astype(BF)
    swap("K")
    run(*steps_c[8:12], *steps_b[12:16], *steps_k[:8], *steps_r[8:12])
    out_v, grad_v_ = pre_h.at[0, :, 0:768], pre_h.at[1, :, 0:768]
    out_v[...] = unspread(layer_out)
    out_copy = pltpu.make_async_copy(out_v, out_ref, load_sems.at[8])
    out_copy.start()
    run(*steps_o[4:6], *steps_c[12:16], *steps_k[8:12], *steps_2[6:8])

    piece_z = stage_z

    def spread_z(m):
        table = mm(turn_z[...], sum_z[m])
        for xhi in range(2):
            for y in range(4):
                x = xhi * 2 + m
                at_ = (xhi * 4 + y) * 64
                piece_z[at.by_core(x, y), at.by_core(y, x)] = table[at_ : at_ + 64].astype(BF)

    run(*steps_o[6:8])
    spread_z(0)
    spread_z(1)
    for k in (1, 3, 2):
        net.send(piece_z.at[rem4(at.two + k)], across_z.at[k - 1], at.last("B", k), "grad two")
    run(steps_b[16])
    q1 = grad_n1 * gain1
    grad_x = grad_middle + scale1 * (q1 - mean(q1) - unit1 * mean(q1 * unit1))
    grad_v_[...] = unspread(grad_x)
    grad_copy = pltpu.make_async_copy(grad_v_, in_grad_ref, load_sems.at[9])
    grad_copy.start()
    run(*steps_r[12:16], *steps_k[12:16], steps_c[16])
    spread_lines(
        1, acc_b[:, 0:LEFT], jnp.concatenate([acc_b[:, LEFT:], acc_c[...]], axis=1), piece_b, line_b
    )
    net.wait_group("grad two", across_z, sib)
    total = wide(piece_z.at[at.two])
    for k in (1, 2, 3):
        total += wide(across_z.at[k - 1])
    row_f[...] = total
    row_b[...] = row_f[...].astype(BF)
    for k in (1, 2, 3):
        net.send(row_b.at[rem4(at.one + k)], side_z.at[k - 1], at.first("B", k), "grad one")
    run(steps_r[16], steps_k[16])
    acc_a = jnp.concatenate([acc_r[...], acc_k[...]], axis=1)
    spread_lines(0, acc_a[:, 0:LEFT], acc_a[:, LEFT:], piece_a, line_a)
    sum_lines(1, line_b)
    net.wait_group("grad one", side_z, sib)
    total = row_f[at.one]
    for k in (1, 2, 3):
        total += wide(side_z.at[k - 1])
    swap_f[...] = total
    away, kept = rows(32 * (1 - c), 32, 8), rows(32 * c, 32, 8)
    last_swap = net.send(swap_f.at[away], swapped_z.at[c], sib)
    swapped_z[c] = swap_f[kept]
    last_swap.wait_recv()
    columns = jnp.concatenate(
        [
            jnp.concatenate([swapped_z[0], swapped_z[1]], axis=1),
            jnp.concatenate([end_n[0, 1, 8:16, 384:768], end_n[1, 1, 8:16, 384:768]], axis=1),
        ],
        axis=0,
    )
    end_z[...] = unspread(columns)
    out_copy.wait()
    grad_copy.wait()
    sum_lines(0, line_a)
    net.drain()


def layer(*operands):
    bf = lambda *shape: pltpu.VMEM(shape, BF)
    f32 = lambda *shape: pltpu.VMEM(shape, F32)
    a, b, d, r, k = (WIDTH[q] for q in "ABCRK")
    return pl.pallas_call(
        layer_kernel,
        out_shape=(
            jax.ShapeDtypeStruct((TOK, EMB), F32),
            jax.ShapeDtypeStruct((TOK, EMB), F32),
            jax.ShapeDtypeStruct((2, 2, 16, LEFT), F32),
            jax.ShapeDtypeStruct((40, EMB), F32),
        ),
        in_specs=[pl.BlockSpec(memory_space=pl.ANY)] * 8 + [VMEM] * (len(operands) - 8),
        out_specs=(pl.BlockSpec(memory_space=pl.ANY),) * 2 + (VMEM,) * 2,
        scratch_shapes=[
            bf(TOK, EMB), bf(TOK, EMB), f32(12, 64, 64), bf(EMB, EMB),
            bf(96, 128), bf(432, 512), bf(128, 96), bf(512, 432), f32(6, 128, 128),
            bf(2, EMB, a), bf(2, EMB, b), bf(2, EMB, d), bf(2, EMB, COLS), bf(2, FF, COLS),
            bf(2, EMB, b), f32(6, 256, 128),
            f32(128, 128), f32(2, 2, 16, LEFT), bf(2, 2, 16, LEFT), bf(8, 16, LEFT), bf(8, 16, LEFT),
            f32(48, EMB), bf(2, 32, COLS), bf(64, COLS), bf(4, 64, COLS), bf(4, 4, 64, COLS),
            *(bf(EMB, w) for w in (r, k, b, d)), *(bf(4, 48, w) for w in (r, k, b, d)),
            *(bf(2, 4, 48, w) for w in (r, k, b, d)), *(bf(3, 48, w) for w in (r, k, b, d)),
            *(f32(48, w) for w in (r, k, b, d)),
            bf(8, 16, LEFT), bf(8, 16, LEFT), bf(8, 16, LEFT), bf(8, 16, LEFT),
            bf(EMB, COLS), bf(FF, COLS),
            bf(2, 96, COLS), bf(2, 336, COLS), bf(2, 2, 96, COLS), bf(2, 2, 336, COLS),
            bf(2, 432, COLS),
            bf(3, 4, 64, COLS), f32(4, 64, COLS), bf(4, 64, COLS), bf(3, 64, COLS),
            f32(64, COLS), f32(2, 32, COLS),
            f32(2, TOK, b), bf(2, TOK, b), bf(2, TOK, b), bf(2, TOK, COLS),
            bf(4, EMB, TOK), bf(EMB, TOK), bf(EMB, TOK), bf(EMB, TOK),
            pltpu.SemaphoreType.DMA((SENDS,)),
            pltpu.SemaphoreType.DMA((ARRIVALS,)),
            pltpu.SemaphoreType.DMA((10,)),
        ],
        compiler_params=pltpu.CompilerParams(
            collective_id=1, has_side_effects=True, vmem_limit_bytes=62 << 20
        ),
        cost_estimate=pl.CostEstimate(
            flops=6 * TOK * 7667712, bytes_accessed=4 * 7667712, transcendentals=10 * TOK * EMB
        ),
        name="layer",
    )(*operands)


def finish_kernel(end_n, end_z, out_in, grad_in, out, grad, *refs):
    vecs, mats = refs[:14], refs[14:]
    acceptor, address, content, sigmoid, mixer, ff_address, ff_content, ff_acceptor = mats
    out[...] = out_in[...]
    grad[...] = grad_in[...]
    acceptor[...] = end_n[0, 0, 0:6, 0:768]
    address[:, 0:128] = end_n[0, 0, 0:6, 768:896]
    address[:, 128:768] = end_n[0, 0, 8:14, 0:640]
    content[...] = end_n[1, 0, 0:6, 0:768]
    sigmoid[:, 0:128] = end_n[1, 0, 0:6, 768:896]
    sigmoid[:, 128:768] = end_n[1, 0, 8:14, 0:640]
    ff_address[:, 0:128] = end_n[0, 0, 8:14, 640:768]
    for h in range(2):
        first_col = 128 + 1280 * h
        ff_address[:, first_col : first_col + 896] = end_n[h, 1, 0:6, 0:896]
        ff_address[:, first_col + 896 : first_col + 1280] = end_n[h, 1, 8:14, 0:384]
    table = jnp.concatenate([end_n[1, 0, 8:16, 640:768], jnp.zeros((120, 128), F32)], axis=0).T
    for i, ref in enumerate(vecs):
        ref[...] = table[i : i + 1, 0:6].reshape(6)
    mixer[...] = end_z[0:6]
    ff_content[...] = end_z[8:29]
    ff_acceptor[...] = end_z[32:38]


def finish(end_n, end_z, out, grad):
    shapes = [(TOK, EMB), (TOK, EMB)] + [(6,)] * 14
    shapes += [(6, EMB)] * 5 + [(6, FF), (21, EMB), (6, EMB)]
    return pl.pallas_call(
        finish_kernel,
        out_shape=tuple(jax.ShapeDtypeStruct(shape, F32) for shape in shapes),
        in_specs=[VMEM] * 4,
        out_specs=(VMEM,) * len(shapes),
        name="finish",
    )(end_n, end_z, out, grad)


def per_device(
    incoming_activations,
    sequence_opening_memory,
    prior_standardize_factor,
    prior_standardize_offset,
    acceptor_lerp_factor,
    address_lerp_factor,
    content_lerp_factor,
    sigmoid_lerp_factor,
    acceptor_matrix,
    address_matrix,
    content_matrix,
    sigmoid_matrix,
    lane_fading_exponent,
    present_reward_vector,
    cluster_standardize_factor,
    cluster_standardize_offset,
    mixer_result_matrix,
    latter_standardize_factor,
    latter_standardize_offset,
    feedforward_address_lerp,
    feedforward_sigmoid_lerp,
    feedforward_address_matrix,
    feedforward_content_matrix,
    feedforward_acceptor_matrix,
    upstream_derivative,
):
    spread = jnp.asarray(_spread(), BF)
    out, in_grad, end_n, end_z = layer(
        incoming_activations, upstream_derivative,
        sequence_opening_memory.reshape(12, 64, 64), spread,
        jnp.asarray(_line_pick(), BF), jnp.asarray(_plane_pick(), BF),
        jnp.asarray(_line_pick().T, BF), jnp.asarray(_plane_pick().T, BF),
        prior_standardize_factor, prior_standardize_offset, acceptor_lerp_factor,
        address_lerp_factor, content_lerp_factor, sigmoid_lerp_factor,
        latter_standardize_factor, latter_standardize_offset, feedforward_address_lerp,
        feedforward_sigmoid_lerp, lane_fading_exponent, present_reward_vector,
        cluster_standardize_factor, cluster_standardize_offset,
        acceptor_matrix, address_matrix, content_matrix, sigmoid_matrix,
        mixer_result_matrix, feedforward_address_matrix, feedforward_content_matrix,
        feedforward_acceptor_matrix,
    )
    results = finish(end_n, end_z, out, in_grad)
    out, in_grad, v = results[0], results[1], results[2:16]
    acceptor, address, content, sigmoid, mixer, ff_address, ff_content, ff_acceptor = results[16:]
    return (
        out, in_grad,
        v[0], v[1], v[2], v[3], v[4], v[5],
        acceptor, address, content, sigmoid,
        v[10], v[11], v[12], v[13],
        mixer,
        v[6], v[7], v[8], v[9],
        ff_address, ff_content, ff_acceptor,
    )


def solution(mesh):
    r, v = P(("dp", "fsdp"), None), P(("dp", "fsdp"))
    state = P(("dp", "fsdp"), None, None, None)
    return jax.shard_map(
        per_device,
        mesh=mesh,
        in_specs=(r, state) + (v,) * 6 + (r,) * 4 + (v,) * 4 + (r,) + (v,) * 4 + (r,) * 4,
        out_specs=(r, r) + (v,) * 6 + (r,) * 4 + (v,) * 4 + (r,) + (v,) * 4 + (r,) * 3,
        check_vma=False,
    )
```

```python
from functools import partial

import jax
import jax.numpy as jnp
import numpy as np
from jax import lax
from jax.experimental import pallas as pl
from jax.experimental.pallas import tpu as pltpu
from jax.sharding import PartitionSpec as P

MESH = pl.DeviceIdType.MESH
BF = jnp.bfloat16
F32 = jnp.float32
VMEM = pl.BlockSpec(memory_space=pltpu.VMEM)

NORM_EPS = 1e-05
GROUP_EPS = 0.00064
TOK = 128
EMB = 768
FF = 2688
COLS = 384
SENDS, ARRIVALS = 64, 150
LEFT, RIGHT = 896, 768

WIDTH = {"A": 1664, "B": 1280, "C": 384, "R": 768, "K": 896}
FIXED = {"S": 0}
VEC = 1536
ORDER = (0, 1, 3, 2)


def _order():
    order = np.zeros(EMB, np.int64)
    for x in range(4):
        for y in range(4):
            for z in range(4):
                for c in range(2):
                    device = z * 32 + (x % 2) * 16 + y * 4 + (x // 2) * 2 + c
                    place = (x * 4 + y) * 48 + (z * 2 + c) * 6
                    order[place : place + 6] = 6 * device + np.arange(6)
    return order


def _spread():
    spread = np.zeros((EMB, EMB), np.float32)
    spread[_order(), np.arange(EMB)] = 1.0
    return spread


def _line_pick():
    pick = np.zeros((96, 128), np.float32)
    for member in range(8):
        for r in range(6):
            pick[member * 6 + r, member * 16 + r] = 1.0
            pick[48 + member * 6 + r, member * 16 + 8 + r] = 1.0
    return pick


def _plane_pick():
    pick = np.zeros((432, 512), np.float32)
    for member in range(16):
        y, xhi, core = member // 4, member // 2 % 2, member % 2
        staged = (xhi * 8 + y * 2 + core) * 32
        for r in range(6):
            pick[member * 6 + r, staged + r] = 1.0
        for r in range(21):
            pick[96 + member * 21 + r, staged + 8 + r] = 1.0
    return pick


def rem4(value):
    return lax.rem(value, 4)


class Place:
    def __init__(self):
        dp, fs = lax.axis_index("dp"), lax.axis_index("fsdp")
        self.z, self.xlo = lax.div(dp, 2), lax.rem(dp, 2)
        self.y, self.xhi = lax.div(fs, 4), lax.rem(lax.div(fs, 2), 2)
        self.c = lax.rem(fs, 2)
        self.x = self.xhi * 2 + self.xlo
        self.one, self.two = self.by_core(self.y, self.x), self.by_core(self.x, self.y)

    def by_core(self, zero, one):
        return zero * (1 - self.c) + one * self.c

    def device(self, z, y, x, c):
        return (z * 2 + lax.rem(x, 2), y * 4 + lax.div(x, 2) * 2 + c)

    def sibling(self):
        return self.device(self.z, self.y, self.x, 1 - self.c)

    def up(self, k):
        return self.device(rem4(self.z + k), self.y, self.x, self.c)

    def line(self, k):
        z = rem4(self.z + k // 2)
        core = self.c if k % 2 == 0 else 1 - self.c
        return self.device(z, self.y, self.x, core), z * 2 + core, core

    def turn(self, q, sibling=False):
        if q in FIXED:
            return FIXED[q]
        return 1 - self.c if sibling else self.c

    def first(self, q, k):
        t = self.turn(q)
        y, x = rem4(self.y + k * (1 - t)), rem4(self.x + k * t)
        return self.device(self.z, y, x, self.c)

    def last(self, q, k):
        t = self.turn(q)
        y, x = rem4(self.y + k * t), rem4(self.x + k * (1 - t))
        return self.device(self.z, y, x, self.c)

    def band(self, q, m, k, sibling=False):
        t = self.turn(q, sibling)
        x = rem4(self.x + m * t + k * (1 - t))
        y = rem4(self.y + m * (1 - t) + k * t)
        return rows(48 * (x * 4 + y), 48)

    def across(self, k):
        return self.device(self.z, self.y, rem4(self.x + k), self.c)

    def side(self, k):
        return self.device(self.z, rem4(self.y + k), self.x, self.c)

    def order(self, m, k):
        return rem4(self.z + k) * 2 + m

    def greet(self):
        mates = [self.line(k)[0] for k in range(1, 8)]
        mates += [self.across(k) for k in (1, 2, 3)]
        mates += [self.side(k) for k in (1, 2, 3)]
        barrier = pltpu.get_barrier_semaphore()
        for mate in mates:
            pl.semaphore_signal(barrier, inc=1, device_id=mate, device_id_type=MESH)
        return lambda: pl.semaphore_wait(barrier, len(mates))


class Sender:
    def __init__(self, send_sems, recv_sems):
        self.send_sems, self.recv_sems = send_sems, recv_sems
        self.sends = self.arrivals = 0
        self.open = []
        self.groups = {}

    def send(self, source, target, device, group=None):
        index = self.sends % SENDS
        if len(self.open) >= SENDS:
            self.open.pop(0).wait_send()
        self.sends += 1
        if group not in self.groups:
            self.groups[group if group is not None else self.sends] = self.arrivals
            arrival = self.arrivals
            self.arrivals += 1
        else:
            arrival = self.groups[group]
        copy = pltpu.make_async_remote_copy(
            src_ref=source,
            dst_ref=target,
            send_sem=self.send_sems.at[index],
            recv_sem=self.recv_sems.at[arrival],
            device_id=device,
            device_id_type=MESH,
        )
        copy.start()
        self.open.append(copy)
        return copy

    def wait_group(self, group, like, device):
        pltpu.make_async_remote_copy(
            src_ref=like,
            dst_ref=like,
            send_sem=self.send_sems.at[0],
            recv_sem=self.recv_sems.at[self.groups[group]],
            device_id=device,
            device_id_type=MESH,
        ).wait_recv()

    def drain(self, until=None):
        keep = 0 if until is None else self.sends - until
        while len(self.open) > keep:
            self.open.pop(0).wait_send()


def rows(start, size, unit=16):
    return pl.ds(pl.multiple_of(start, unit), size)


def mm(left, right):
    return jnp.dot(left, right, preferred_element_type=F32)


def mm_t(left, right):
    return lax.dot_general(left, right, (((1,), (1,)), ((), ())), preferred_element_type=F32)


def t_mm(left, right):
    return lax.dot_general(left, right, (((0,), (0,)), ((), ())), preferred_element_type=F32)


def split(value, parts):
    found = []
    for _ in range(parts - 1):
        high = value.astype(BF)
        found.append(high)
        value = value - high.astype(F32)
    found.append(value.astype(BF))
    return found


def fine(dims, left, right):
    lh, ll = split(left, 2)
    rh, rl = split(right, 2)
    dot = partial(lax.dot_general, dimension_numbers=(dims, ((), ())), preferred_element_type=F32)
    return dot(lh, rh) + (dot(lh, rl) + dot(ll, rh))


NN, NT, TN = ((1,), (0,)), ((1,), (1,)), ((0,), (0,))


def wide(ref):
    return ref[...].astype(F32)


def layer_kernel(
    x_in, up_in, state, spread_in, pick_n_in, pick_z_in, turn_n_in, turn_z_in, *refs
):
    vecs, refs = refs[:14], refs[14:]
    (acceptor, address, content, sigmoid, mixer, ff_address, ff_content, ff_acceptor), refs = refs[:8], refs[8:]
    (
        out_ref, in_grad_ref, end_n, end_z,
        x_ref, up_ref, state_v, spread, pick_n, pick_z, turn_n, turn_z, memory,
        wa, wb, wc, wo, w2, gb, scores,
        vec_f, pack_f, pack_n, stage_a, stage_b, cols_f, pack_z, half_z, row_z, stage_z,
        sib_r, sib_k, sib_b, sib_c, relay_r, relay_k, relay_b, relay_c,
        last_r, last_k, last_b, last_c, first_r, first_k, first_b, first_c,
        acc_r, acc_k, acc_b, acc_c,
        piece_a, piece_b, line_a, line_b,
        sib_o, sib_2, relay_o, relay_2, up_o, up_2, sum_z,
        across_z, row_f, row_b, side_z, swap_f, swapped_z,
        pre_h, hid_h, gp_h, gvo_h, turned, turned_w, turned_h, turned_g,
        send_sems, recv_sems, load_sems,
    ) = refs
    at = Place()
    c = at.c
    sib = at.sibling()
    net = Sender(send_sems, recv_sems)
    met = at.greet()

    loads = {}
    for i, (name, source, target) in enumerate([
        ("spread", spread_in, spread), ("x", x_in, x_ref), ("pick_n", pick_n_in, pick_n),
        ("up", up_in, up_ref), ("pick_z", pick_z_in, pick_z), ("state", state, state_v),
        ("turn_n", turn_n_in, turn_n), ("turn_z", turn_z_in, turn_z),
    ]):
        loads[name] = pltpu.make_async_copy(source, target, load_sems.at[i])
        loads[name].start()

    vec_f[...] = jnp.zeros_like(vec_f)
    for i, ref in enumerate(vecs):
        vec_f[i : i + 1, 0:6] = wide(ref).reshape(1, 6)
    eye = (
        lax.broadcasted_iota(jnp.int32, (16, 128), 0)
        == lax.broadcasted_iota(jnp.int32, (16, 128), 1)
    ).astype(F32).astype(BF)
    pack_f[...] = jnp.zeros_like(pack_f)
    pack_f[0, 0, 0:6, 0:768] = wide(acceptor)
    pack_f[0, 0, 0:6, 768:896] = wide(address.at[:, 0:128])
    pack_f[0, 0, 8:14, 0:640] = wide(address.at[:, 128:768])
    pack_f[0, 0, 8:14, 640:768] = wide(ff_address.at[:, 0:128])
    pack_f[1, 0, 0:6, 0:768] = wide(content)
    pack_f[1, 0, 0:6, 768:896] = wide(sigmoid.at[:, 0:128])
    pack_f[1, 0, 8:14, 0:640] = wide(sigmoid.at[:, 128:768])
    pack_f[1, 0, 8:14, 640:768] = mm_t(eye, vec_f[...].astype(BF))[0:6]
    for h in range(2):
        pack_n[0, h] = pack_f[h, 0].astype(BF)
    met()

    own = at.z * 2 + c

    def send_lines(i, stage):
        for k in range(1, 8):
            mate, _, core = at.line(k)
            net.send(pack_n.at[i, core], stage.at[own], mate, ("lines", i))
        stage[own] = pack_n[i, c]

    send_lines(0, stage_a)
    cols_f[...] = jnp.zeros_like(cols_f)
    cols_f[0:6] = wide(mixer)
    cols_f[8:29] = wide(ff_content)
    cols_f[32:38] = wide(ff_acceptor)
    loads["spread"].wait()
    moved = mm(cols_f[...].astype(BF), spread[...])
    for h in range(2):
        pack_z[h] = moved[0:32, COLS * h : COLS * h + COLS].astype(BF)
        first_col = 128 + 1280 * h
        pack_f[h, 1, 0:6, 0:896] = wide(ff_address.at[:, first_col : first_col + 896])
        pack_f[h, 1, 8:14, 0:384] = wide(ff_address.at[:, first_col + 896 : first_col + 1280])
        pack_f[h, 1, 8:16, 384:768] = moved[32:40, COLS * h : COLS * h + COLS]
        pack_n[1, h] = pack_f[h, 1].astype(BF)
    mine_z = rows(32 * c, 32)
    swap_z = net.send(pack_z.at[1 - c], half_z.at[mine_z], sib)
    half_z[mine_z] = pack_z[c]

    loads["x"].wait()
    tokens = mm(x_ref[...], spread[...])
    centred = tokens - jnp.mean(tokens, axis=-1, keepdims=True)
    scale1 = lax.rsqrt(jnp.mean(centred * centred, axis=-1, keepdims=True) + NORM_EPS)
    unit1 = centred * scale1
    loads["up"].wait()
    upstream = mm(up_ref[...], spread[...])
    swap_z.wait_recv()
    for k in (1, 2, 3):
        net.send(half_z, row_z.at[rows(64 * at.one, 64)], at.first("B", k), "one")
    row_z[rows(64 * at.one, 64)] = half_z[...]
    loads["pick_n"].wait()
    for name in ("state", "turn_n", "turn_z", "pick_z"):
        loads[name].wait()
    blank = jnp.zeros((64, 64), F32)
    for g in range(6):
        memory[g, 0:64] = jnp.concatenate([state_v[2 * g], blank], axis=1)
        memory[g, 64:128] = jnp.concatenate([blank, state_v[2 * g + 1]], axis=1)

    def pick(i, stage):
        net.wait_group(("lines", i), stage.at[0:7], sib)
        return mm(pick_n[...], stage[...].reshape(128, LEFT)).astype(BF)

    full = {"A": wa, "B": wb, "C": wc, "o": wo, "2": w2}

    def place_n(q, m, k):
        return full[q].at[c, at.band(q, m, k)]

    firsts, lasts = {}, {}

    def pass_on(q, m):
        spot = place_n(q, 4 - m, 0)
        for k in (1, 3):
            lasts[q, m, k] = net.send(spot, spot, at.last(q, k))
        net.send(spot, spot, sib, ("sib", q))

    def begin(q, *parts):
        spot = place_n(q, 0, 0)
        spot[...] = jnp.concatenate(parts, axis=1) if len(parts) > 1 else parts[0]
        for k in (1, 3, 2):
            firsts[q, k] = net.send(spot, spot, at.first(q, k))
        pass_on(q, 0)

    def relay(q, m):
        firsts[q, m].wait_recv()
        pass_on(q, m)

    def arrive(q, m, k):
        lasts[q, m, k].wait_recv()
        spot = place_n(q, 4 - m, 4 - k)
        if k == (1 if m % 2 == 0 else 3):
            lasts[q, m, 2] = net.send(spot, spot, at.last(q, k))
        net.send(spot, spot, sib, ("sib", q))

    def arrive_far(q, m):
        lasts[q, m, 2].wait_recv()
        spot = place_n(q, 4 - m, 2)
        net.send(spot, spot, sib, ("sib", q))

    def place_z(w, m, k):
        unit = 96 if w == "o" else 336
        return full[w].at[c, rows(unit * at.order(m, k), unit)]

    def pass_z(w, m):
        spot = place_z(w, m, 0)
        for k in (1, 3):
            lasts[w, m, k] = net.send(spot, spot, at.up(k))
        net.send(spot, spot, sib, ("sib", w))

    def arrive_z(w, m, k):
        lasts[w, m, k].wait_recv()
        spot = place_z(w, m, 4 - k)
        if k == (1 if m == 0 else 3):
            lasts[w, m, 2] = net.send(spot, spot, at.up(k))
        net.send(spot, spot, sib, ("sib", w))

    def arrive_z_far(w, m):
        lasts[w, m, 2].wait_recv()
        spot = place_z(w, m, 2)
        net.send(spot, spot, sib, ("sib", w))

    picked = pick(0, stage_a)
    begin("A", picked[0:48], picked[48:96, 0:RIGHT])
    send_lines(1, stage_b)
    net.wait_group("one", row_z.at[0:192], sib)
    for k in (1, 3, 2):
        net.send(row_z, stage_z.at[at.two], at.last("B", k), "two")
    stage_z[at.two] = row_z[...]
    relay("A", 1)
    relay("A", 3)
    for k in (1, 3):
        arrive("A", 0, k)
    picked = pick(1, stage_b)
    relay("A", 2)
    begin("B", picked[0:48], picked[48:96, 0:384])
    begin("C", picked[48:96, 384:768])
    net.wait_group("two", stage_z.at[0:3], sib)
    for m in range(2):
        staged = []
        for x in (m, 2 + m):
            other = stage_z[:, 64 * x : 64 * x + 64].reshape(256, COLS)
            block = jnp.where(c == 0, stage_z[x].astype(F32), other.astype(F32))
            staged.append(block.astype(BF))
        picked_z = mm(pick_z[...], jnp.concatenate(staged, axis=0)).astype(BF)
        place_z("o", m, 0)[...] = picked_z[:96]
        place_z("2", m, 0)[...] = picked_z[96:]
        pass_z("o", m)
        pass_z("2", m)
    for m in (1, 3):
        for k in (1, 3):
            arrive("A", m, k)
    arrive_far("A", 0)
    relay("B", 1)
    relay("B", 3)
    for k in (1, 3):
        arrive("A", 2, k)
    relay("B", 2)
    for m in (1, 3, 2):
        relay("C", m)
    for k in (1, 3):
        arrive("B", 0, k)
    for w in ("o", "2"):
        for k in (1, 3):
            arrive_z(w, 0, k)
    arrive_far("A", 1)
    for k in (1, 3):
        arrive_z("o", 1, k)
    arrive_far("A", 3)
    for k in (1, 3):
        arrive("B", 1, k)
    arrive_far("A", 2)
    for k in (1, 3):
        arrive("B", 3, k)

    tasks = []

    def plan(kind, *steps_):
        for step in steps_:
            tasks.append((kind, step))

    for k in (1, 3):
        plan("B", partial(arrive, "B", 2, k))
    for k in (1, 3):
        plan("2", partial(arrive_z, "2", 1, k))
    for m in ORDER:
        for k in (1, 3):
            plan("C", partial(arrive, "C", m, k))
    for m in (0, 1):
        plan("o", partial(arrive_z_far, "o", m))
    for q in ("B", "C"):
        for m in ORDER:
            plan(q, partial(arrive_far, q, m))
    for m in (0, 1):
        plan("2", partial(arrive_z_far, "2", m))

    def work(count=1000):
        for _ in range(min(count, len(tasks))):
            tasks.pop(0)[1]()

    def need(q):
        while any(kind == q for kind, _ in tasks):
            work(1)
        net.wait_group(("sib", q), full[q].at[1 - c], sib)

    need("A")

    lanes = lax.broadcasted_iota(jnp.int32, (1, 128), 1)
    left_head = lanes < 64
    token = lax.broadcasted_iota(jnp.int32, (TOK, 1), 0)

    def shift_down(value):
        return jnp.where(token == 0, 0.0, pltpu.roll(value, 1, 0))

    def shift_up(value):
        return jnp.where(token == TOK - 1, 0.0, pltpu.roll(value, TOK - 1, 0))

    def mean(value):
        return jnp.mean(value, axis=-1, keepdims=True)

    def tsum(value):
        return jnp.sum(value, axis=0, keepdims=True)

    def unspread(value):
        high, low = split(value, 2)
        return mm_t(high, spread[...]) + mm_t(low, spread[...])

    vec = mm_t(eye, wa[1, :, VEC:1664])
    gain1, bias1 = vec[0:1], vec[1:2]
    lerps = [vec[2 + i : 3 + i] for i in range(4)]
    gain2, bias2, lerp_h, lerp_g = vec[6:7], vec[7:8], vec[8:9], vec[9:10]
    heads = mm_t(vec.astype(BF), spread[...])
    rate, bonus, gain_w, bias_w = heads[10:11], heads[11:12], heads[12:13], heads[13:14]

    pair_rows = lax.broadcasted_iota(jnp.int32, (256, 128), 0)
    pair_cols = lax.broadcasted_iota(jnp.int32, (256, 128), 1)
    pair_ones = ((lax.rem(pair_rows, 128) // 64) == (pair_cols // 64)).astype(F32).astype(BF)
    below = lax.rem(pair_rows, 128) > pair_cols

    def head_sum(value):
        found = []
        for g in range(6):
            part = value[:, 128 * g : 128 * g + 128]
            found.append(mm(jnp.concatenate(split(part, 2), axis=1), pair_ones))
        return jnp.concatenate(found, axis=1)

    def stack(value):
        return jnp.concatenate(
            [jnp.where(left_head, value, 0.0), jnp.where(left_head, 0.0, value)], axis=0
        )

    def beside(value):
        return jnp.concatenate([value[:TOK], value[TOK:]], axis=1)

    work(2)
    normed = unit1 * gain1 + bias1
    previous = shift_down(normed)
    blended = [(normed * l + previous * (1.0 - l)).astype(BF) for l in lerps]
    for i in range(4):
        turned[i] = blended[i].astype(F32).T.astype(BF)
    recept = mm(blended[0], wa[0, :, 0:768])
    keys = mm(blended[1], wa[0, :, 768:1536])
    vals = mm(blended[2], wa[1, :, 0:768])
    gate_pre = mm(blended[3], wa[1, :, 768:1536])
    work(12)

    fade = -jnp.exp(rate)
    steps = token.astype(F32)
    fall_r = jnp.exp(steps * fade)
    fall_k = jnp.exp(-(steps + 1.0) * fade)
    recept_f = recept * fall_r
    keys_f = keys * fall_k
    present = head_sum(recept * bonus * keys)
    parts = []
    for g in range(6):
        cut = slice(128 * g, 128 * g + 128)
        rg, kg, vg = recept_f[:, cut], keys_f[:, cut], vals[:, cut]
        sc = jnp.where(below, fine(NT, stack(rg), kg), 0.0)
        scores[g] = sc
        parts.append(fine(NN, beside(sc), stack(vg)) + fine(NN, rg, memory[g]))
        if g in (3, 5):
            work(4)
    wkv = jnp.concatenate(parts, axis=1) + present * vals

    centred_w = wkv - head_sum(wkv) * (1.0 / 64.0)
    scale_w = lax.rsqrt(head_sum(centred_w * centred_w) * (1.0 / 64.0) + GROUP_EPS)
    unit_w = centred_w * scale_w
    grouped = unit_w * gain_w + bias_w
    sig = 1.0 / (1.0 + jnp.exp(-gate_pre))
    silu = gate_pre * sig
    gated = (grouped * silu).astype(BF)
    turned_w[...] = gated.astype(F32).T.astype(BF)
    need("o")
    middle = tokens + jnp.concatenate([mm(gated, wo[0]), mm(gated, wo[1])], axis=1)

    work()

    centred = middle - mean(middle)
    scale2 = lax.rsqrt(mean(centred * centred) + NORM_EPS)
    unit2 = centred * scale2
    normed2 = unit2 * gain2 + bias2
    previous2 = shift_down(normed2)
    mixed_h = (normed2 * lerp_h + previous2 * (1.0 - lerp_h)).astype(BF)
    mixed_g = (normed2 * lerp_g + previous2 * (1.0 - lerp_g)).astype(BF)
    turned_h[...] = mixed_h.astype(F32).T.astype(BF)
    turned_g[...] = mixed_g.astype(F32).T.astype(BF)
    need("B")
    halves = (1 - c, c)
    pre_s = jnp.maximum(mm(mixed_h, wa[0, :, 1536:1664]), 0.0)
    hidden_s = (pre_s * pre_s).astype(BF)
    for h in halves:
        pre = jnp.maximum(mm(mixed_h, wb[h]), 0.0)
        pre_h[h] = pre
        hid_h[h] = (pre * pre).astype(BF)
    need("C")
    gating = jnp.concatenate([mm(mixed_g, wc[0]), mm(mixed_g, wc[1])], axis=1)
    gating = 1.0 / (1.0 + jnp.exp(-gating))
    grad_vo = upstream * gating
    for h in range(2):
        gvo_h[h] = grad_vo[:, COLS * h : COLS * h + COLS].astype(BF)

    def grad_w2(target, low, high, h):
        for start, width, part in ((0, 128, None), (128, 1280, 0), (1408, 1280, 1)):
            a, b = max(low, start), min(high, start + width)
            if a < b:
                cut_ = slice(a - start, b - start)
                left = hidden_s[:, cut_] if part is None else hid_h[part, :, cut_]
                target[a - low : b - low] = t_mm(left, gvo_h[h]).astype(BF)

    for spot, low, high in (
        (gb.at[c, :, 0:384], 0, 768),
        (gb.at[c, :, 384:768], 768, 1536),
        (gb.at[c, :, 768:1152], 1536, 2304),
        (stage_z.at[0], 2304, 2560),
        (stage_z.at[1, 0:128], 2560, 2688),
    ):
        grad_w2(spot, low, high, 1 - c)
        net.send(spot, sib_2.at[low:high], sib, "swap 2")

    swaps = {"2": partial(net.wait_group, "swap 2", sib_2, sib)}

    def fold(mine, other, *more):
        total = wide(mine) + wide(other)
        for ref in more:
            total += wide(ref)
        return total

    gr, go = wb.at[:, :, 0:768], wb.at[:, :, 768:1152]
    gk, gc = wa.at[:, :, 768:1664], wc
    grads = {"R": gr, "K": gk, "B": gb, "S": gc}
    sib_of = {"R": sib_r, "K": sib_k, "B": sib_b, "S": sib_c}
    relay_of = {"R": relay_r, "K": relay_k, "B": relay_b, "S": relay_c}
    last_of = {"R": last_r, "K": last_k, "B": last_b, "S": last_c}
    first_of = {"R": first_r, "K": first_k, "B": first_b, "S": first_c}
    acc_of = {"R": acc_r, "K": acc_k, "B": acc_b, "S": acc_c}

    def swap(q):
        swaps[q] = net.send(grads[q].at[1 - c], sib_of[q], sib).wait_recv

    def swapped(q):
        if q in swaps:
            swaps.pop(q)()

    def scatter_far(q, m):
        part = at.band(q, m, 2)
        via = 1 if m % 2 == 0 else 3
        swapped(q)
        spot = sib_of[q].at[part]
        spot[...] = fold(grads[q].at[c, part], spot).astype(BF)
        lasts["g", q, m, 2] = net.send(spot, relay_of[q].at[m], at.last(q, via))

    def scatter_near(q, m, k):
        part = at.band(q, m, k)
        spot = sib_of[q].at[part]
        more = []
        if k == (1 if m % 2 == 0 else 3):
            lasts["g", q, m, 2].wait_recv()
            more = [relay_of[q].at[m]]
        spot[...] = fold(grads[q].at[c, part], spot, *more).astype(BF)
        lasts["g", q, m, k] = net.send(spot, last_of[q].at[k // 2, m], at.last(q, k))

    def scatter_own(q, m):
        part = at.band(q, m, 0)
        spot = sib_of[q].at[part]
        lasts["g", q, m, 1].wait_recv()
        lasts["g", q, m, 3].wait_recv()
        arrived = last_of[q]
        total = fold(grads[q].at[c, part], spot, arrived.at[0, m], arrived.at[1, m])
        if m == 0:
            acc_of[q][...] = total
        else:
            spot[...] = total.astype(BF)
            firsts["g", q, m] = net.send(spot, first_of[q].at[m - 1], at.first(q, m))

    def scatter_end(q):
        total = acc_of[q][...]
        for m in (1, 3, 2):
            firsts["g", q, m].wait_recv()
            total += wide(first_of[q].at[m - 1])
        acc_of[q][...] = total

    def spread_lines(i, left, right, piece, line):
        right = jnp.concatenate([right, jnp.zeros((48, LEFT - RIGHT), F32)], axis=1)
        table = jnp.concatenate([left, right], axis=0).astype(BF)
        piece[...] = mm(turn_n[...], table).astype(BF).reshape(8, 16, LEFT)
        for k in range(1, 8):
            mate, index, _ = at.line(k)
            net.send(piece.at[index], line.at[own], mate, ("grad lines", i))
        line[own] = piece[own]

    def sum_lines(i, line):
        net.wait_group(("grad lines", i), line.at[0:7], sib)
        for h in range(2):
            total = wide(line.at[h])
            for z in (1, 2, 3):
                total += wide(line.at[2 * z + h])
            end_n[h, i] = total

    def scatter_steps(q):
        steps_ = [partial(scatter_far, q, m) for m in ORDER]
        for late in (False, True):
            for m in ORDER:
                for k in (1, 3):
                    if late == (k == (1 if m % 2 == 0 else 3)):
                        steps_.append(partial(scatter_near, q, m, k))
        steps_ += [partial(scatter_own, q, m) for m in (1, 3, 2, 0)]
        steps_.append(partial(scatter_end, q))
        return steps_

    z_parts = {
        "o": (96, go, sib_o, relay_o, up_o, sum_z.at[:, 0:96]),
        "2": (336, w2, sib_2, relay_2, up_2, sum_z.at[:, 96:432]),
    }

    def swap_w(w):
        unit, mine, theirs = z_parts[w][:3]
        swaps[w] = net.send(mine.at[1 - c], theirs, sib).wait_recv

    def part_w(w, m, k):
        unit = z_parts[w][0]
        return rows(unit * at.order(m, k), unit)

    def scatter_far_w(w, m):
        unit, mine, theirs, relayed = z_parts[w][:4]
        part = part_w(w, m, 2)
        swapped(w)
        spot = theirs.at[part]
        spot[...] = fold(mine.at[c, part], spot).astype(BF)
        lasts["g", w, m, 2] = net.send(spot, relayed.at[m], at.up(1 if m == 0 else 3))

    def scatter_near_w(w, m, k):
        unit, mine, theirs, relayed, arrived = z_parts[w][:5]
        part = part_w(w, m, k)
        more = []
        if k == (1 if m == 0 else 3):
            lasts["g", w, m, 2].wait_recv()
            more = [relayed.at[m]]
        spot = theirs.at[part]
        spot[...] = fold(mine.at[c, part], spot, *more).astype(BF)
        lasts["g", w, m, k] = net.send(spot, arrived.at[k // 2, m], at.up(k))

    def scatter_own_w(w, m):
        unit, mine, theirs, relayed, arrived, sums = z_parts[w]
        part = part_w(w, m, 0)
        lasts["g", w, m, 1].wait_recv()
        lasts["g", w, m, 3].wait_recv()
        total = fold(mine.at[c, part], theirs.at[part], arrived.at[0, m], arrived.at[1, m])
        sums[m] = total.astype(BF)

    def scatter_steps_w(w):
        steps_ = [partial(scatter_far_w, w, 0), partial(scatter_far_w, w, 1)]
        steps_ += [partial(scatter_near_w, w, 1, 1), partial(scatter_near_w, w, 0, 3)]
        steps_ += [partial(scatter_near_w, w, 0, 1), partial(scatter_near_w, w, 1, 3)]
        steps_ += [partial(scatter_own_w, w, 0), partial(scatter_own_w, w, 1)]
        return steps_

    need("2")
    steps_2, steps_o = scatter_steps_w("2"), scatter_steps_w("o")
    steps_b, steps_c = scatter_steps("B"), scatter_steps("S")
    steps_r, steps_k = scatter_steps("R"), scatter_steps("K")

    def run(*steps_):
        for step in steps_:
            step()

    for h in halves:
        part = rows(128 + 1280 * h, 1280)
        grad_hidden = mm_t(gvo_h[0], w2[0, part]) + mm_t(gvo_h[1], w2[1, part])
        gp_h[h] = (grad_hidden * 2.0 * pre_h[h]).astype(BF)
    sent = net.sends
    for h in halves:
        gb[h] = mm(turned_h[...], gp_h[h]).astype(BF)
        if h is halves[0]:
            swap("B")
            net.drain(sent)
    grad_hidden = mm_t(gvo_h[0], w2[0, 0:128]) + mm_t(gvo_h[1], w2[1, 0:128])
    grad_pre_s = (grad_hidden * 2.0 * pre_s).astype(BF)
    value_out = jnp.concatenate(
        [
            mm(hidden_s, w2[n, 0:128]) + mm(hid_h[0], w2[n, 128:1408]) + mm(hid_h[1], w2[n, 1408:2688])
            for n in range(2)
        ],
        axis=1,
    )
    layer_out = middle + gating * value_out
    grad_w2(w2.at[c], 0, FF, c)
    run(*steps_2[:4], *steps_b[:8])
    grad_gp = (grad_vo * value_out * (1.0 - gating)).astype(BF)
    grad_mg = mm_t(grad_gp[:, :COLS], wc[0]) + mm_t(grad_gp[:, COLS:], wc[1])
    for h in range(2):
        gc[h] = mm(turned_g[...], grad_gp[:, COLS * h : COLS * h + COLS]).astype(BF)
    swap("S")
    grad_mh = mm_t(grad_pre_s, wa[0, :, 1536:1664])
    grad_mh += mm_t(gp_h[0], wb[0]) + mm_t(gp_h[1], wb[1])
    gk[0, :, 768:896] = mm(turned_h[...], grad_pre_s).astype(BF)
    run(*steps_c[:8])

    grad_n2 = grad_mh * lerp_h + grad_mg * lerp_g
    grad_n2 += shift_up(grad_mh * (1.0 - lerp_h) + grad_mg * (1.0 - lerp_g))
    delta2 = normed2 - previous2
    g_lerp_h, g_lerp_g = tsum(grad_mh * delta2), tsum(grad_mg * delta2)
    g_gain2, g_bias2 = tsum(grad_n2 * unit2), tsum(grad_n2)
    q2 = grad_n2 * gain2
    grad_middle = upstream + scale2 * (q2 - mean(q2) - unit2 * mean(q2 * unit2))

    grad_attn = grad_middle.astype(BF)
    grad_gated = mm_t(grad_attn[:, :COLS], wo[0]) + mm_t(grad_attn[:, COLS:], wo[1])
    for h in range(2):
        go[h] = mm(turned_w[...], grad_attn[:, COLS * h : COLS * h + COLS]).astype(BF)
    swap_w("o")
    grad_gate = (grad_gated * grouped * (sig * (1.0 + gate_pre * (1.0 - sig)))).astype(BF)
    grad_grouped = grad_gated * silu
    g_gain_w, g_bias_w = tsum(grad_grouped * unit_w), tsum(grad_grouped)
    qw = grad_grouped * gain_w
    grad_wkv = scale_w * (
        qw
        - head_sum(qw) * (1.0 / 64.0)
        - unit_w * (head_sum(qw * unit_w) * (1.0 / 64.0))
    )

    weight = head_sum(grad_wkv * vals)
    parts_r, parts_k, parts_v = [], [], []
    for g in range(6):
        cut = slice(128 * g, 128 * g + 128)
        rg, kg, vg, dg = recept_f[:, cut], keys_f[:, cut], vals[:, cut], grad_wkv[:, cut]
        ds = stack(dg)
        da = jnp.where(below, fine(NT, ds, vg), 0.0)
        parts_r.append(fine(NN, beside(da), stack(kg)) + fine(NT, dg, memory[g]))
        parts_k.append(fine(TN, da, stack(rg)))
        parts_v.append(fine(TN, scores[g], ds))
        if g == 3:
            run(*steps_b[8:12])
        if g == 5:
            run(*steps_o[:4])
    grad_r = jnp.concatenate(parts_r, axis=1) * fall_r
    grad_k = jnp.concatenate(parts_k, axis=1) * fall_k
    grad_v = jnp.concatenate(parts_v, axis=1) + grad_wkv * present
    g_rate = fade * tsum(steps * recept * grad_r - (steps + 1.0) * keys * grad_k)
    g_bonus = tsum(recept * keys * weight)
    grad_r = (grad_r + bonus * keys * weight).astype(BF)
    grad_k = (grad_k + bonus * recept * weight).astype(BF)
    grad_v = grad_v.astype(BF)

    gr[0] = mm(turned[0], grad_r).astype(BF)
    gr[1] = mm(turned[2], grad_v).astype(BF)
    swap("R")
    grad_blended = [
        mm_t(grad_r, wa[0, :, 0:768]),
        mm_t(grad_k, wa[0, :, 768:1536]),
        mm_t(grad_v, wa[1, :, 0:768]),
        mm_t(grad_gate, wa[1, :, 768:1536]),
    ]
    gk[0, :, 0:768] = mm(turned[1], grad_k).astype(BF)
    gk[1, :, 0:768] = mm(turned[3], grad_gate).astype(BF)
    run(*steps_r[:8], *steps_2[4:6])
    delta = normed - previous
    g_lerps = [tsum(g * delta) for g in grad_blended]
    grad_n1 = sum(g * l for g, l in zip(grad_blended, lerps))
    grad_n1 += shift_up(sum(g * (1.0 - l) for g, l in zip(grad_blended, lerps)))
    g_gain1, g_bias1 = tsum(grad_n1 * unit1), tsum(grad_n1)

    zero = jnp.zeros((1, EMB), F32)
    natural = jnp.concatenate([g_rate, g_bonus, g_gain_w, g_bias_w] + [zero] * 4, axis=0)
    high, low = split(natural, 2)
    moved = mm(high, spread[...]) + mm(low, spread[...])
    table = jnp.concatenate(
        [g_gain1, g_bias1] + g_lerps + [g_gain2, g_bias2, g_lerp_h, g_lerp_g]
        + [moved[0:4], jnp.zeros((114, EMB), F32)],
        axis=0,
    )
    gk[1, :, 768:896] = table.T.astype(BF)
    swap("K")
    run(*steps_c[8:12], *steps_b[12:16], *steps_k[:8], *steps_r[8:12])
    out_v, grad_v_ = pre_h.at[0, :, 0:768], pre_h.at[1, :, 0:768]
    out_v[...] = unspread(layer_out)
    out_copy = pltpu.make_async_copy(out_v, out_ref, load_sems.at[8])
    out_copy.start()
    run(*steps_o[4:6], *steps_c[12:16], *steps_k[8:12], *steps_2[6:8])

    piece_z = stage_z

    def spread_z(m):
        table = mm(turn_z[...], sum_z[m])
        for xhi in range(2):
            for y in range(4):
                x = xhi * 2 + m
                at_ = (xhi * 4 + y) * 64
                spot = piece_z.at[at.by_core(x, y), rows(64 * at.by_core(y, x), 64)]
                spot[...] = table[at_ : at_ + 64].astype(BF)

    run(*steps_o[6:8])
    spread_z(0)
    spread_z(1)
    for k in (1, 3, 2):
        net.send(piece_z.at[rem4(at.two + k)], across_z.at[k - 1], at.last("B", k), "grad two")
    run(steps_b[16])
    q1 = grad_n1 * gain1
    grad_x = grad_middle + scale1 * (q1 - mean(q1) - unit1 * mean(q1 * unit1))
    grad_v_[...] = unspread(grad_x)
    grad_copy = pltpu.make_async_copy(grad_v_, in_grad_ref, load_sems.at[9])
    grad_copy.start()
    run(*steps_r[12:16], *steps_k[12:16], steps_c[16])
    spread_lines(
        1, acc_b[:, 0:LEFT], jnp.concatenate([acc_b[:, LEFT:], acc_c[...]], axis=1), piece_b, line_b
    )
    net.wait_group("grad two", across_z, sib)
    total = wide(piece_z.at[at.two])
    for k in (1, 2, 3):
        total += wide(across_z.at[k - 1])
    row_f[...] = total.reshape(4, 64, COLS)
    row_b[...] = row_f[...].astype(BF)
    for k in (1, 2, 3):
        net.send(row_b.at[rem4(at.one + k)], side_z.at[k - 1], at.first("B", k), "grad one")
    run(steps_r[16], steps_k[16])
    acc_a = jnp.concatenate([acc_r[...], acc_k[...]], axis=1)
    spread_lines(0, acc_a[:, 0:LEFT], acc_a[:, LEFT:], piece_a, line_a)
    sum_lines(1, line_b)
    net.wait_group("grad one", side_z, sib)
    total = row_f[at.one]
    for k in (1, 2, 3):
        total += wide(side_z.at[k - 1])
    swap_f[...] = total
    away, kept = rows(32 * (1 - c), 32, 8), rows(32 * c, 32, 8)
    last_swap = net.send(swap_f.at[away], swapped_z.at[c], sib)
    swapped_z[c] = swap_f[kept]
    last_swap.wait_recv()
    columns = jnp.concatenate(
        [
            jnp.concatenate([swapped_z[0], swapped_z[1]], axis=1),
            jnp.concatenate([end_n[0, 1, 8:16, 384:768], end_n[1, 1, 8:16, 384:768]], axis=1),
        ],
        axis=0,
    )
    end_z[...] = unspread(columns)
    out_copy.wait()
    grad_copy.wait()
    sum_lines(0, line_a)
    net.drain()


def layer(*operands):
    bf = lambda *shape: pltpu.VMEM(shape, BF)
    f32 = lambda *shape: pltpu.VMEM(shape, F32)
    a, b, d, r, k = (WIDTH[q] for q in "ABCRK")
    return pl.pallas_call(
        layer_kernel,
        out_shape=(
            jax.ShapeDtypeStruct((TOK, EMB), F32),
            jax.ShapeDtypeStruct((TOK, EMB), F32),
            jax.ShapeDtypeStruct((2, 2, 16, LEFT), F32),
            jax.ShapeDtypeStruct((40, EMB), F32),
        ),
        in_specs=[pl.BlockSpec(memory_space=pl.ANY)] * 8 + [VMEM] * (len(operands) - 8),
        out_specs=(pl.BlockSpec(memory_space=pl.ANY),) * 2 + (VMEM,) * 2,
        scratch_shapes=[
            bf(TOK, EMB), bf(TOK, EMB), f32(12, 64, 64), bf(EMB, EMB),
            bf(96, 128), bf(432, 512), bf(128, 96), bf(512, 432), f32(6, 128, 128),
            bf(2, EMB, a), bf(2, EMB, b), bf(2, EMB, d), bf(2, EMB, COLS), bf(2, FF, COLS),
            bf(2, EMB, b), f32(6, 256, 128),
            f32(128, 128), f32(2, 2, 16, LEFT), bf(2, 2, 16, LEFT), bf(8, 16, LEFT), bf(8, 16, LEFT),
            f32(48, EMB), bf(2, 32, COLS), bf(64, COLS), bf(256, COLS), bf(4, 256, COLS),
            *(bf(EMB, w) for w in (r, k, b, d)), *(bf(4, 48, w) for w in (r, k, b, d)),
            *(bf(2, 4, 48, w) for w in (r, k, b, d)), *(bf(3, 48, w) for w in (r, k, b, d)),
            *(f32(48, w) for w in (r, k, b, d)),
            bf(8, 16, LEFT), bf(8, 16, LEFT), bf(8, 16, LEFT), bf(8, 16, LEFT),
            bf(EMB, COLS), bf(FF, COLS),
            bf(2, 96, COLS), bf(2, 336, COLS), bf(2, 2, 96, COLS), bf(2, 2, 336, COLS),
            bf(2, 432, COLS),
            bf(3, 256, COLS), f32(4, 64, COLS), bf(4, 64, COLS), bf(3, 64, COLS),
            f32(64, COLS), f32(2, 32, COLS),
            f32(2, TOK, b), bf(2, TOK, b), bf(2, TOK, b), bf(2, TOK, COLS),
            bf(4, EMB, TOK), bf(EMB, TOK), bf(EMB, TOK), bf(EMB, TOK),
            pltpu.SemaphoreType.DMA((SENDS,)),
            pltpu.SemaphoreType.DMA((ARRIVALS,)),
            pltpu.SemaphoreType.DMA((10,)),
        ],
        compiler_params=pltpu.CompilerParams(
            collective_id=1, has_side_effects=True, vmem_limit_bytes=62 << 20
        ),
        cost_estimate=pl.CostEstimate(
            flops=6 * TOK * 7667712, bytes_accessed=4 * 7667712, transcendentals=10 * TOK * EMB
        ),
        name="layer",
    )(*operands)


def finish_kernel(end_n, end_z, out_in, grad_in, out, grad, *refs):
    vecs, mats = refs[:14], refs[14:]
    acceptor, address, content, sigmoid, mixer, ff_address, ff_content, ff_acceptor = mats
    out[...] = out_in[...]
    grad[...] = grad_in[...]
    acceptor[...] = end_n[0, 0, 0:6, 0:768]
    address[:, 0:128] = end_n[0, 0, 0:6, 768:896]
    address[:, 128:768] = end_n[0, 0, 8:14, 0:640]
    content[...] = end_n[1, 0, 0:6, 0:768]
    sigmoid[:, 0:128] = end_n[1, 0, 0:6, 768:896]
    sigmoid[:, 128:768] = end_n[1, 0, 8:14, 0:640]
    ff_address[:, 0:128] = end_n[0, 0, 8:14, 640:768]
    for h in range(2):
        first_col = 128 + 1280 * h
        ff_address[:, first_col : first_col + 896] = end_n[h, 1, 0:6, 0:896]
        ff_address[:, first_col + 896 : first_col + 1280] = end_n[h, 1, 8:14, 0:384]
    table = jnp.concatenate([end_n[1, 0, 8:16, 640:768], jnp.zeros((120, 128), F32)], axis=0).T
    for i, ref in enumerate(vecs):
        ref[...] = table[i : i + 1, 0:6].reshape(6)
    mixer[...] = end_z[0:6]
    ff_content[...] = end_z[8:29]
    ff_acceptor[...] = end_z[32:38]


def finish(end_n, end_z, out, grad):
    shapes = [(TOK, EMB), (TOK, EMB)] + [(6,)] * 14
    shapes += [(6, EMB)] * 5 + [(6, FF), (21, EMB), (6, EMB)]
    return pl.pallas_call(
        finish_kernel,
        out_shape=tuple(jax.ShapeDtypeStruct(shape, F32) for shape in shapes),
        in_specs=[VMEM] * 4,
        out_specs=(VMEM,) * len(shapes),
        name="finish",
    )(end_n, end_z, out, grad)


def per_device(
    incoming_activations,
    sequence_opening_memory,
    prior_standardize_factor,
    prior_standardize_offset,
    acceptor_lerp_factor,
    address_lerp_factor,
    content_lerp_factor,
    sigmoid_lerp_factor,
    acceptor_matrix,
    address_matrix,
    content_matrix,
    sigmoid_matrix,
    lane_fading_exponent,
    present_reward_vector,
    cluster_standardize_factor,
    cluster_standardize_offset,
    mixer_result_matrix,
    latter_standardize_factor,
    latter_standardize_offset,
    feedforward_address_lerp,
    feedforward_sigmoid_lerp,
    feedforward_address_matrix,
    feedforward_content_matrix,
    feedforward_acceptor_matrix,
    upstream_derivative,
):
    spread = jnp.asarray(_spread(), BF)
    out, in_grad, end_n, end_z = layer(
        incoming_activations, upstream_derivative,
        sequence_opening_memory.reshape(12, 64, 64), spread,
        jnp.asarray(_line_pick(), BF), jnp.asarray(_plane_pick(), BF),
        jnp.asarray(_line_pick().T, BF), jnp.asarray(_plane_pick().T, BF),
        prior_standardize_factor, prior_standardize_offset, acceptor_lerp_factor,
        address_lerp_factor, content_lerp_factor, sigmoid_lerp_factor,
        latter_standardize_factor, latter_standardize_offset, feedforward_address_lerp,
        feedforward_sigmoid_lerp, lane_fading_exponent, present_reward_vector,
        cluster_standardize_factor, cluster_standardize_offset,
        acceptor_matrix, address_matrix, content_matrix, sigmoid_matrix,
        mixer_result_matrix, feedforward_address_matrix, feedforward_content_matrix,
        feedforward_acceptor_matrix,
    )
    results = finish(end_n, end_z, out, in_grad)
    out, in_grad, v = results[0], results[1], results[2:16]
    acceptor, address, content, sigmoid, mixer, ff_address, ff_content, ff_acceptor = results[16:]
    return (
        out, in_grad,
        v[0], v[1], v[2], v[3], v[4], v[5],
        acceptor, address, content, sigmoid,
        v[10], v[11], v[12], v[13],
        mixer,
        v[6], v[7], v[8], v[9],
        ff_address, ff_content, ff_acceptor,
    )


def solution(mesh):
    r, v = P(("dp", "fsdp"), None), P(("dp", "fsdp"))
    state = P(("dp", "fsdp"), None, None, None)
    return jax.shard_map(
        per_device,
        mesh=mesh,
        in_specs=(r, state) + (v,) * 6 + (r,) * 4 + (v,) * 4 + (r,) + (v,) * 4 + (r,) * 4,
        out_specs=(r, r) + (v,) * 6 + (r,) * 4 + (v,) * 4 + (r,) + (v,) * 4 + (r,) * 3,
        check_vma=False,
    )
```

```python
from functools import partial

import jax
import jax.numpy as jnp
import numpy as np
from jax import lax
from jax.experimental import pallas as pl
from jax.experimental.pallas import tpu as pltpu
from jax.sharding import PartitionSpec as P

MESH = pl.DeviceIdType.MESH
BF = jnp.bfloat16
F32 = jnp.float32
VMEM = pl.BlockSpec(memory_space=pltpu.VMEM)

NORM_EPS = 1e-05
GROUP_EPS = 0.00064
TOK = 128
EMB = 768
FF = 2688
COLS = 384
SENDS, ARRIVALS = 64, 150
LEFT, RIGHT = 896, 768

WIDTH = {"A": 1664, "B": 1280, "C": 384, "R": 768, "K": 896}
FIXED = {"S": 0}
VEC = 1536
ORDER = (0, 1, 3, 2)


def _order():
    order = np.zeros(EMB, np.int64)
    for x in range(4):
        for y in range(4):
            for z in range(4):
                for c in range(2):
                    device = z * 32 + (x % 2) * 16 + y * 4 + (x // 2) * 2 + c
                    place = (x * 4 + y) * 48 + (z * 2 + c) * 6
                    order[place : place + 6] = 6 * device + np.arange(6)
    return order


def _spread():
    spread = np.zeros((EMB, EMB), np.float32)
    spread[_order(), np.arange(EMB)] = 1.0
    return spread


def _line_pick():
    pick = np.zeros((96, 128), np.float32)
    for member in range(8):
        for r in range(6):
            pick[member * 6 + r, member * 16 + r] = 1.0
            pick[48 + member * 6 + r, member * 16 + 8 + r] = 1.0
    return pick


def _plane_pick():
    pick = np.zeros((432, 512), np.float32)
    for member in range(16):
        y, xhi, core = member // 4, member // 2 % 2, member % 2
        staged = (xhi * 8 + y * 2 + core) * 32
        for r in range(6):
            pick[member * 6 + r, staged + r] = 1.0
        for r in range(21):
            pick[96 + member * 21 + r, staged + 8 + r] = 1.0
    return pick


def rem4(value):
    return lax.rem(value, 4)


class Place:
    def __init__(self):
        dp, fs = lax.axis_index("dp"), lax.axis_index("fsdp")
        self.z, self.xlo = lax.div(dp, 2), lax.rem(dp, 2)
        self.y, self.xhi = lax.div(fs, 4), lax.rem(lax.div(fs, 2), 2)
        self.c = lax.rem(fs, 2)
        self.x = self.xhi * 2 + self.xlo
        self.one, self.two = self.by_core(self.y, self.x), self.by_core(self.x, self.y)

    def by_core(self, zero, one):
        return zero * (1 - self.c) + one * self.c

    def device(self, z, y, x, c):
        return (z * 2 + lax.rem(x, 2), y * 4 + lax.div(x, 2) * 2 + c)

    def sibling(self):
        return self.device(self.z, self.y, self.x, 1 - self.c)

    def up(self, k):
        return self.device(rem4(self.z + k), self.y, self.x, self.c)

    def line(self, k):
        z = rem4(self.z + k // 2)
        core = self.c if k % 2 == 0 else 1 - self.c
        return self.device(z, self.y, self.x, core), z * 2 + core, core

    def turn(self, q, sibling=False):
        if q in FIXED:
            return FIXED[q]
        return 1 - self.c if sibling else self.c

    def first(self, q, k):
        t = self.turn(q)
        y, x = rem4(self.y + k * (1 - t)), rem4(self.x + k * t)
        return self.device(self.z, y, x, self.c)

    def last(self, q, k):
        t = self.turn(q)
        y, x = rem4(self.y + k * t), rem4(self.x + k * (1 - t))
        return self.device(self.z, y, x, self.c)

    def band(self, q, m, k, sibling=False):
        t = self.turn(q, sibling)
        x = rem4(self.x + m * t + k * (1 - t))
        y = rem4(self.y + m * (1 - t) + k * t)
        return rows(48 * (x * 4 + y), 48)

    def across(self, k):
        return self.device(self.z, self.y, rem4(self.x + k), self.c)

    def side(self, k):
        return self.device(self.z, rem4(self.y + k), self.x, self.c)

    def order(self, m, k):
        return rem4(self.z + k) * 2 + m

    def greet(self):
        mates = [self.line(k)[0] for k in range(1, 8)]
        mates += [self.across(k) for k in (1, 2, 3)]
        mates += [self.side(k) for k in (1, 2, 3)]
        barrier = pltpu.get_barrier_semaphore()
        for mate in mates:
            pl.semaphore_signal(barrier, inc=1, device_id=mate, device_id_type=MESH)
        return lambda: pl.semaphore_wait(barrier, len(mates))


class Sender:
    def __init__(self, send_sems, recv_sems):
        self.send_sems, self.recv_sems = send_sems, recv_sems
        self.sends = self.arrivals = 0
        self.open = []
        self.groups = {}

    def send(self, source, target, device, group=None):
        index = self.sends % SENDS
        if len(self.open) >= SENDS:
            self.open.pop(0).wait_send()
        self.sends += 1
        if group not in self.groups:
            self.groups[group if group is not None else self.sends] = self.arrivals
            arrival = self.arrivals
            self.arrivals += 1
        else:
            arrival = self.groups[group]
        copy = pltpu.make_async_remote_copy(
            src_ref=source,
            dst_ref=target,
            send_sem=self.send_sems.at[index],
            recv_sem=self.recv_sems.at[arrival],
            device_id=device,
            device_id_type=MESH,
        )
        copy.start()
        self.open.append(copy)
        return copy

    def wait_group(self, group, like, device):
        pltpu.make_async_remote_copy(
            src_ref=like,
            dst_ref=like,
            send_sem=self.send_sems.at[0],
            recv_sem=self.recv_sems.at[self.groups[group]],
            device_id=device,
            device_id_type=MESH,
        ).wait_recv()

    def drain(self, until=None):
        keep = 0 if until is None else self.sends - until
        while len(self.open) > keep:
            self.open.pop(0).wait_send()


def rows(start, size, unit=16):
    return pl.ds(pl.multiple_of(start, unit), size)


def mm(left, right):
    return jnp.dot(left, right, preferred_element_type=F32)


def mm_t(left, right):
    return lax.dot_general(left, right, (((1,), (1,)), ((), ())), preferred_element_type=F32)


def t_mm(left, right):
    return lax.dot_general(left, right, (((0,), (0,)), ((), ())), preferred_element_type=F32)


def split(value, parts):
    found = []
    for _ in range(parts - 1):
        high = value.astype(BF)
        found.append(high)
        value = value - high.astype(F32)
    found.append(value.astype(BF))
    return found


def fine(dims, left, right):
    lh, ll = split(left, 2)
    rh, rl = split(right, 2)
    dot = partial(lax.dot_general, dimension_numbers=(dims, ((), ())), preferred_element_type=F32)
    return dot(lh, rh) + (dot(lh, rl) + dot(ll, rh))


NN, NT, TN = ((1,), (0,)), ((1,), (1,)), ((0,), (0,))


def wide(ref):
    return ref[...].astype(F32)


def layer_kernel(
    x_in, up_in, state, spread_in, pick_n_in, pick_z_in, turn_n_in, turn_z_in, *refs
):
    vecs, refs = refs[:14], refs[14:]
    (acceptor, address, content, sigmoid, mixer, ff_address, ff_content, ff_acceptor), refs = refs[:8], refs[8:]
    (
        out_ref, in_grad_ref, end_n, end_z,
        x_ref, up_ref, state_v, spread, pick_n, pick_z, turn_n, turn_z, memory,
        wa, wb, wc, wo, w2, gb, scores,
        vec_f, pack_f, pack_n, stage_a, stage_b, cols_f, pack_z, half_z, row_z, stage_z,
        sib_r, sib_k, sib_b, sib_c, relay_r, relay_k, relay_b, relay_c,
        last_r, last_k, last_b, last_c, first_r, first_k, first_b, first_c,
        acc_r, acc_k, acc_b, acc_c,
        piece_a, piece_b, line_a, line_b,
        sib_o, sib_2, relay_o, relay_2, up_o, up_2, sum_z,
        across_z, row_f, row_b, side_z, swap_f, swapped_z,
        pre_h, hid_h, gp_h, gvo_h, turned, turned_w, turned_h, turned_g,
        send_sems, recv_sems, load_sems,
    ) = refs
    at = Place()
    c = at.c
    sib = at.sibling()
    net = Sender(send_sems, recv_sems)
    met = at.greet()

    loads = {}
    for i, (name, source, target) in enumerate([
        ("spread", spread_in, spread), ("x", x_in, x_ref), ("pick_n", pick_n_in, pick_n),
        ("up", up_in, up_ref), ("pick_z", pick_z_in, pick_z), ("state", state, state_v),
        ("turn_n", turn_n_in, turn_n), ("turn_z", turn_z_in, turn_z),
    ]):
        loads[name] = pltpu.make_async_copy(source, target, load_sems.at[i])
        loads[name].start()

    vec_f[...] = jnp.zeros_like(vec_f)
    for i, ref in enumerate(vecs):
        vec_f[i : i + 1, 0:6] = wide(ref).reshape(1, 6)
    eye = (
        lax.broadcasted_iota(jnp.int32, (16, 128), 0)
        == lax.broadcasted_iota(jnp.int32, (16, 128), 1)
    ).astype(F32).astype(BF)
    pack_f[...] = jnp.zeros_like(pack_f)
    pack_f[0, 0, 0:6, 0:768] = wide(acceptor)
    pack_f[0, 0, 0:6, 768:896] = wide(address.at[:, 0:128])
    pack_f[0, 0, 8:14, 0:640] = wide(address.at[:, 128:768])
    pack_f[0, 0, 8:14, 640:768] = wide(ff_address.at[:, 0:128])
    pack_f[1, 0, 0:6, 0:768] = wide(content)
    pack_f[1, 0, 0:6, 768:896] = wide(sigmoid.at[:, 0:128])
    pack_f[1, 0, 8:14, 0:640] = wide(sigmoid.at[:, 128:768])
    pack_f[1, 0, 8:14, 640:768] = mm_t(eye, vec_f[...].astype(BF))[0:6]
    for h in range(2):
        pack_n[0, h] = pack_f[h, 0].astype(BF)
    met()

    own = at.z * 2 + c

    def send_lines(i, stage):
        for k in range(1, 8):
            mate, _, core = at.line(k)
            net.send(pack_n.at[i, core], stage.at[own], mate, ("lines", i))
        stage[own] = pack_n[i, c]

    send_lines(0, stage_a)
    cols_f[...] = jnp.zeros_like(cols_f)
    cols_f[0:6] = wide(mixer)
    cols_f[8:29] = wide(ff_content)
    cols_f[32:38] = wide(ff_acceptor)
    loads["spread"].wait()
    moved = mm(cols_f[...].astype(BF), spread[...])
    for h in range(2):
        pack_z[h] = moved[0:32, COLS * h : COLS * h + COLS].astype(BF)
        first_col = 128 + 1280 * h
        pack_f[h, 1, 0:6, 0:896] = wide(ff_address.at[:, first_col : first_col + 896])
        pack_f[h, 1, 8:14, 0:384] = wide(ff_address.at[:, first_col + 896 : first_col + 1280])
        pack_f[h, 1, 8:16, 384:768] = moved[32:40, COLS * h : COLS * h + COLS]
        pack_n[1, h] = pack_f[h, 1].astype(BF)
    mine_z = rows(32 * c, 32)
    swap_z = net.send(pack_z.at[1 - c], half_z.at[mine_z], sib)
    half_z[mine_z] = pack_z[c]

    loads["x"].wait()
    tokens = mm(x_ref[...], spread[...])
    centred = tokens - jnp.mean(tokens, axis=-1, keepdims=True)
    scale1 = lax.rsqrt(jnp.mean(centred * centred, axis=-1, keepdims=True) + NORM_EPS)
    unit1 = centred * scale1
    loads["up"].wait()
    upstream = mm(up_ref[...], spread[...])
    swap_z.wait_recv()
    for k in (1, 2, 3):
        net.send(half_z, row_z.at[rows(64 * at.one, 64)], at.first("B", k), "one")
    row_z[rows(64 * at.one, 64)] = half_z[...]
    loads["pick_n"].wait()
    for name in ("state", "turn_n", "turn_z", "pick_z"):
        loads[name].wait()
    blank = jnp.zeros((64, 64), F32)
    for g in range(6):
        memory[g, 0:64] = jnp.concatenate([state_v[2 * g], blank], axis=1)
        memory[g, 64:128] = jnp.concatenate([blank, state_v[2 * g + 1]], axis=1)

    def pick(i, stage):
        net.wait_group(("lines", i), stage.at[0:7], sib)
        return mm(pick_n[...], stage[...].reshape(128, LEFT)).astype(BF)

    full = {"A": wa, "B": wb, "C": wc, "o": wo, "2": w2}

    def place_n(q, m, k):
        return full[q].at[c, at.band(q, m, k)]

    firsts, lasts = {}, {}

    def pass_on(q, m):
        spot = place_n(q, 4 - m, 0)
        for k in (1, 3):
            lasts[q, m, k] = net.send(spot, spot, at.last(q, k))
        net.send(spot, spot, sib, ("sib", q))

    def begin(q, *parts):
        spot = place_n(q, 0, 0)
        spot[...] = jnp.concatenate(parts, axis=1) if len(parts) > 1 else parts[0]
        for k in (1, 3, 2):
            firsts[q, k] = net.send(spot, spot, at.first(q, k))
        pass_on(q, 0)

    def relay(q, m):
        firsts[q, m].wait_recv()
        pass_on(q, m)

    def arrive(q, m, k):
        lasts[q, m, k].wait_recv()
        spot = place_n(q, 4 - m, 4 - k)
        if k == (1 if m % 2 == 0 else 3):
            lasts[q, m, 2] = net.send(spot, spot, at.last(q, k))
        net.send(spot, spot, sib, ("sib", q))

    def arrive_far(q, m):
        lasts[q, m, 2].wait_recv()
        spot = place_n(q, 4 - m, 2)
        net.send(spot, spot, sib, ("sib", q))

    def place_z(w, m, k):
        unit = 96 if w == "o" else 336
        return full[w].at[c, rows(unit * at.order(m, k), unit)]

    def pass_z(w, m):
        spot = place_z(w, m, 0)
        for k in (1, 3):
            lasts[w, m, k] = net.send(spot, spot, at.up(k))
        net.send(spot, spot, sib, ("sib", w))

    def arrive_z(w, m, k):
        lasts[w, m, k].wait_recv()
        spot = place_z(w, m, 4 - k)
        if k == (1 if m == 0 else 3):
            lasts[w, m, 2] = net.send(spot, spot, at.up(k))
        net.send(spot, spot, sib, ("sib", w))

    def arrive_z_far(w, m):
        lasts[w, m, 2].wait_recv()
        spot = place_z(w, m, 2)
        net.send(spot, spot, sib, ("sib", w))

    picked = pick(0, stage_a)
    begin("A", picked[0:48], picked[48:96, 0:RIGHT])
    send_lines(1, stage_b)
    net.wait_group("one", row_z.at[0:192], sib)
    for k in (1, 3, 2):
        net.send(row_z, stage_z.at[at.two], at.last("B", k), "two")
    stage_z[at.two] = row_z[...]
    relay("A", 1)
    relay("A", 3)
    for k in (1, 3):
        arrive("A", 0, k)
    picked = pick(1, stage_b)
    relay("A", 2)
    begin("B", picked[0:48], picked[48:96, 0:384])
    begin("C", picked[48:96, 384:768])
    net.wait_group("two", stage_z.at[0:3], sib)
    for m in range(2):
        staged = []
        for x in (m, 2 + m):
            other = stage_z[:, 64 * x : 64 * x + 64].reshape(256, COLS)
            block = jnp.where(c == 0, stage_z[x].astype(F32), other.astype(F32))
            staged.append(block.astype(BF))
        picked_z = mm(pick_z[...], jnp.concatenate(staged, axis=0)).astype(BF)
        place_z("o", m, 0)[...] = picked_z[:96]
        place_z("2", m, 0)[...] = picked_z[96:]
        pass_z("o", m)
        pass_z("2", m)
    for m in (1, 3):
        for k in (1, 3):
            arrive("A", m, k)
    arrive_far("A", 0)
    relay("B", 1)
    relay("B", 3)
    for k in (1, 3):
        arrive("A", 2, k)
    relay("B", 2)
    for m in (1, 3, 2):
        relay("C", m)
    for k in (1, 3):
        arrive("B", 0, k)
    for w in ("o", "2"):
        for k in (1, 3):
            arrive_z(w, 0, k)
    arrive_far("A", 1)
    for k in (1, 3):
        arrive_z("o", 1, k)
    arrive_far("A", 3)
    for k in (1, 3):
        arrive("B", 1, k)
    arrive_far("A", 2)
    for k in (1, 3):
        arrive("B", 3, k)

    tasks = []

    def plan(kind, *steps_):
        for step in steps_:
            tasks.append((kind, step))

    for k in (1, 3):
        plan("B", partial(arrive, "B", 2, k))
    for k in (1, 3):
        plan("2", partial(arrive_z, "2", 1, k))
    for m in ORDER:
        for k in (1, 3):
            plan("C", partial(arrive, "C", m, k))
    for m in (0, 1):
        plan("o", partial(arrive_z_far, "o", m))
    for q in ("B", "C"):
        for m in ORDER:
            plan(q, partial(arrive_far, q, m))
    for m in (0, 1):
        plan("2", partial(arrive_z_far, "2", m))

    def work(count=1000):
        for _ in range(min(count, len(tasks))):
            tasks.pop(0)[1]()

    def need(q):
        while any(kind == q for kind, _ in tasks):
            work(1)
        net.wait_group(("sib", q), full[q].at[1 - c], sib)

    need("A")

    lanes = lax.broadcasted_iota(jnp.int32, (1, 128), 1)
    left_head = lanes < 64
    token = lax.broadcasted_iota(jnp.int32, (TOK, 1), 0)

    def shift_down(value):
        return jnp.where(token == 0, 0.0, pltpu.roll(value, 1, 0))

    def shift_up(value):
        return jnp.where(token == TOK - 1, 0.0, pltpu.roll(value, TOK - 1, 0))

    def mean(value):
        return jnp.mean(value, axis=-1, keepdims=True)

    def tsum(value):
        return jnp.sum(value, axis=0, keepdims=True)

    def unspread(value):
        high, low = split(value, 2)
        return mm_t(high, spread[...]) + mm_t(low, spread[...])

    vec = mm_t(eye, wa[1, :, VEC:1664])
    gain1, bias1 = vec[0:1], vec[1:2]
    lerps = [vec[2 + i : 3 + i] for i in range(4)]
    gain2, bias2, lerp_h, lerp_g = vec[6:7], vec[7:8], vec[8:9], vec[9:10]
    heads = mm_t(vec.astype(BF), spread[...])
    rate, bonus, gain_w, bias_w = heads[10:11], heads[11:12], heads[12:13], heads[13:14]

    pair_rows = lax.broadcasted_iota(jnp.int32, (256, 128), 0)
    pair_cols = lax.broadcasted_iota(jnp.int32, (256, 128), 1)
    pair_ones = ((lax.rem(pair_rows, 128) // 64) == (pair_cols // 64)).astype(F32).astype(BF)
    below = lax.rem(pair_rows, 128) > pair_cols

    def head_sum(value):
        found = []
        for g in range(6):
            part = value[:, 128 * g : 128 * g + 128]
            found.append(mm(jnp.concatenate(split(part, 2), axis=1), pair_ones))
        return jnp.concatenate(found, axis=1)

    def stack(value):
        return jnp.concatenate(
            [jnp.where(left_head, value, 0.0), jnp.where(left_head, 0.0, value)], axis=0
        )

    def beside(value):
        return jnp.concatenate([value[:TOK], value[TOK:]], axis=1)

    work(2)
    normed = unit1 * gain1 + bias1
    previous = shift_down(normed)
    blended = [(normed * l + previous * (1.0 - l)).astype(BF) for l in lerps]
    for i in range(4):
        turned[i] = blended[i].astype(F32).T.astype(BF)
    recept = mm(blended[0], wa[0, :, 0:768])
    keys = mm(blended[1], wa[0, :, 768:1536])
    vals = mm(blended[2], wa[1, :, 0:768])
    gate_pre = mm(blended[3], wa[1, :, 768:1536])
    work(12)

    fade = -jnp.exp(rate)
    steps = token.astype(F32)
    fall_r = jnp.exp(steps * fade)
    fall_k = jnp.exp(-(steps + 1.0) * fade)
    recept_f = recept * fall_r
    keys_f = keys * fall_k
    present = head_sum(recept * bonus * keys)
    parts = []
    for g in range(6):
        cut = slice(128 * g, 128 * g + 128)
        rg, kg, vg = recept_f[:, cut], keys_f[:, cut], vals[:, cut]
        sc = jnp.where(below, fine(NT, stack(rg), kg), 0.0)
        scores[g] = sc
        parts.append(fine(NN, beside(sc), stack(vg)) + fine(NN, rg, memory[g]))
        if g in (3, 5):
            work(4)
    wkv = jnp.concatenate(parts, axis=1) + present * vals

    centred_w = wkv - head_sum(wkv) * (1.0 / 64.0)
    scale_w = lax.rsqrt(head_sum(centred_w * centred_w) * (1.0 / 64.0) + GROUP_EPS)
    unit_w = centred_w * scale_w
    grouped = unit_w * gain_w + bias_w
    sig = 1.0 / (1.0 + jnp.exp(-gate_pre))
    silu = gate_pre * sig
    gated = (grouped * silu).astype(BF)
    turned_w[...] = gated.astype(F32).T.astype(BF)
    need("o")
    middle = tokens + jnp.concatenate([mm(gated, wo[0]), mm(gated, wo[1])], axis=1)

    work()

    centred = middle - mean(middle)
    scale2 = lax.rsqrt(mean(centred * centred) + NORM_EPS)
    unit2 = centred * scale2
    normed2 = unit2 * gain2 + bias2
    previous2 = shift_down(normed2)
    mixed_h = (normed2 * lerp_h + previous2 * (1.0 - lerp_h)).astype(BF)
    mixed_g = (normed2 * lerp_g + previous2 * (1.0 - lerp_g)).astype(BF)
    turned_h[...] = mixed_h.astype(F32).T.astype(BF)
    turned_g[...] = mixed_g.astype(F32).T.astype(BF)
    need("B")
    halves = (1 - c, c)
    pre_s = jnp.maximum(mm(mixed_h, wa[0, :, 1536:1664]), 0.0)
    hidden_s = (pre_s * pre_s).astype(BF)
    for h in halves:
        pre = jnp.maximum(mm(mixed_h, wb[h]), 0.0)
        pre_h[h] = pre
        hid_h[h] = (pre * pre).astype(BF)
    need("C")
    gating = jnp.concatenate([mm(mixed_g, wc[0]), mm(mixed_g, wc[1])], axis=1)
    gating = 1.0 / (1.0 + jnp.exp(-gating))
    grad_vo = upstream * gating
    for h in range(2):
        gvo_h[h] = grad_vo[:, COLS * h : COLS * h + COLS].astype(BF)

    def grad_w2(target, low, high, h):
        for start, width, part in ((0, 128, None), (128, 1280, 0), (1408, 1280, 1)):
            a, b = max(low, start), min(high, start + width)
            if a < b:
                cut_ = slice(a - start, b - start)
                left = hidden_s[:, cut_] if part is None else hid_h[part, :, cut_]
                target[a - low : b - low] = t_mm(left, gvo_h[h]).astype(BF)

    for spot, low, high in (
        (gb.at[c, :, 0:384], 0, 768),
        (gb.at[c, :, 384:768], 768, 1536),
        (gb.at[c, :, 768:1152], 1536, 2304),
        (stage_z.at[0], 2304, 2560),
        (stage_z.at[1, 0:128], 2560, 2688),
    ):
        grad_w2(spot, low, high, 1 - c)
        net.send(spot, sib_2.at[low:high], sib, "swap 2")

    swaps = {"2": partial(net.wait_group, "swap 2", sib_2, sib)}

    def fold(mine, other, *more):
        total = wide(mine) + wide(other)
        for ref in more:
            total += wide(ref)
        return total

    gr, go = wb.at[:, :, 0:768], wb.at[:, :, 768:1152]
    gk, gc = wa.at[:, :, 768:1664], wc
    grads = {"R": gr, "K": gk, "B": gb, "S": gc}
    sib_of = {"R": sib_r, "K": sib_k, "B": sib_b, "S": sib_c}
    relay_of = {"R": relay_r, "K": relay_k, "B": relay_b, "S": relay_c}
    last_of = {"R": last_r, "K": last_k, "B": last_b, "S": last_c}
    first_of = {"R": first_r, "K": first_k, "B": first_b, "S": first_c}
    acc_of = {"R": acc_r, "K": acc_k, "B": acc_b, "S": acc_c}

    def swap(q):
        swaps[q] = net.send(grads[q].at[1 - c], sib_of[q], sib).wait_recv

    def swapped(q):
        if q in swaps:
            swaps.pop(q)()

    def scatter_far(q, m):
        part = at.band(q, m, 2)
        via = 1 if m % 2 == 0 else 3
        swapped(q)
        spot = sib_of[q].at[part]
        spot[...] = fold(grads[q].at[c, part], spot).astype(BF)
        lasts["g", q, m, 2] = net.send(spot, relay_of[q].at[m], at.last(q, via))

    def scatter_near(q, m, k):
        part = at.band(q, m, k)
        spot = sib_of[q].at[part]
        more = []
        if k == (1 if m % 2 == 0 else 3):
            lasts["g", q, m, 2].wait_recv()
            more = [relay_of[q].at[m]]
        spot[...] = fold(grads[q].at[c, part], spot, *more).astype(BF)
        lasts["g", q, m, k] = net.send(spot, last_of[q].at[k // 2, m], at.last(q, k))

    def scatter_own(q, m):
        part = at.band(q, m, 0)
        spot = sib_of[q].at[part]
        lasts["g", q, m, 1].wait_recv()
        lasts["g", q, m, 3].wait_recv()
        arrived = last_of[q]
        total = fold(grads[q].at[c, part], spot, arrived.at[0, m], arrived.at[1, m])
        if m == 0:
            acc_of[q][...] = total
        else:
            spot[...] = total.astype(BF)
            firsts["g", q, m] = net.send(spot, first_of[q].at[m - 1], at.first(q, m))

    def scatter_end(q):
        total = acc_of[q][...]
        for m in (1, 3, 2):
            firsts["g", q, m].wait_recv()
            total += wide(first_of[q].at[m - 1])
        acc_of[q][...] = total

    def spread_lines(i, left, right, piece, line):
        right = jnp.concatenate([right, jnp.zeros((48, LEFT - RIGHT), F32)], axis=1)
        table = jnp.concatenate([left, right], axis=0).astype(BF)
        piece[...] = mm(turn_n[...], table).astype(BF).reshape(8, 16, LEFT)
        for k in range(1, 8):
            mate, index, _ = at.line(k)
            net.send(piece.at[index], line.at[own], mate, ("grad lines", i))
        line[own] = piece[own]

    def sum_lines(i, line):
        net.wait_group(("grad lines", i), line.at[0:7], sib)
        for h in range(2):
            total = wide(line.at[h])
            for z in (1, 2, 3):
                total += wide(line.at[2 * z + h])
            end_n[h, i] = total

    def scatter_steps(q):
        steps_ = [partial(scatter_far, q, m) for m in ORDER]
        for late in (False, True):
            for m in ORDER:
                for k in (1, 3):
                    if late == (k == (1 if m % 2 == 0 else 3)):
                        steps_.append(partial(scatter_near, q, m, k))
        steps_ += [partial(scatter_own, q, m) for m in (1, 3, 2, 0)]
        steps_.append(partial(scatter_end, q))
        return steps_

    z_parts = {
        "o": (96, go, sib_o, relay_o, up_o, sum_z.at[:, 0:96]),
        "2": (336, w2, sib_2, relay_2, up_2, sum_z.at[:, 96:432]),
    }

    def swap_w(w):
        unit, mine, theirs = z_parts[w][:3]
        swaps[w] = net.send(mine.at[1 - c], theirs, sib).wait_recv

    def part_w(w, m, k):
        unit = z_parts[w][0]
        return rows(unit * at.order(m, k), unit)

    def scatter_far_w(w, m):
        unit, mine, theirs, relayed = z_parts[w][:4]
        part = part_w(w, m, 2)
        swapped(w)
        spot = theirs.at[part]
        spot[...] = fold(mine.at[c, part], spot).astype(BF)
        lasts["g", w, m, 2] = net.send(spot, relayed.at[m], at.up(1 if m == 0 else 3))

    def scatter_near_w(w, m, k):
        unit, mine, theirs, relayed, arrived = z_parts[w][:5]
        part = part_w(w, m, k)
        more = []
        if k == (1 if m == 0 else 3):
            lasts["g", w, m, 2].wait_recv()
            more = [relayed.at[m]]
        spot = theirs.at[part]
        spot[...] = fold(mine.at[c, part], spot, *more).astype(BF)
        lasts["g", w, m, k] = net.send(spot, arrived.at[k // 2, m], at.up(k))

    def scatter_own_w(w, m):
        unit, mine, theirs, relayed, arrived, sums = z_parts[w]
        part = part_w(w, m, 0)
        lasts["g", w, m, 1].wait_recv()
        lasts["g", w, m, 3].wait_recv()
        total = fold(mine.at[c, part], theirs.at[part], arrived.at[0, m], arrived.at[1, m])
        sums[m] = total.astype(BF)

    def scatter_steps_w(w):
        steps_ = [partial(scatter_far_w, w, 0), partial(scatter_far_w, w, 1)]
        steps_ += [partial(scatter_near_w, w, 1, 1), partial(scatter_near_w, w, 0, 3)]
        steps_ += [partial(scatter_near_w, w, 0, 1), partial(scatter_near_w, w, 1, 3)]
        steps_ += [partial(scatter_own_w, w, 0), partial(scatter_own_w, w, 1)]
        return steps_

    need("2")
    steps_2, steps_o = scatter_steps_w("2"), scatter_steps_w("o")
    steps_b, steps_c = scatter_steps("B"), scatter_steps("S")
    steps_r, steps_k = scatter_steps("R"), scatter_steps("K")

    def run(*steps_):
        for step in steps_:
            step()

    for h in halves:
        part = rows(128 + 1280 * h, 1280)
        grad_hidden = mm_t(gvo_h[0], w2[0, part]) + mm_t(gvo_h[1], w2[1, part])
        gp_h[h] = (grad_hidden * 2.0 * pre_h[h]).astype(BF)
    sent = net.sends
    for h in halves:
        gb[h] = mm(turned_h[...], gp_h[h]).astype(BF)
        if h is halves[0]:
            swap("B")
            net.drain(sent)
    grad_hidden = mm_t(gvo_h[0], w2[0, 0:128]) + mm_t(gvo_h[1], w2[1, 0:128])
    grad_pre_s = (grad_hidden * 2.0 * pre_s).astype(BF)
    value_out = jnp.concatenate(
        [
            mm(hidden_s, w2[n, 0:128]) + mm(hid_h[0], w2[n, 128:1408]) + mm(hid_h[1], w2[n, 1408:2688])
            for n in range(2)
        ],
        axis=1,
    )
    layer_out = middle + gating * value_out
    grad_w2(w2.at[c], 0, FF, c)
    run(*steps_2[:4], *steps_b[:8])
    grad_gp = (grad_vo * value_out * (1.0 - gating)).astype(BF)
    grad_mg = mm_t(grad_gp[:, :COLS], wc[0]) + mm_t(grad_gp[:, COLS:], wc[1])
    for h in range(2):
        gc[h] = mm(turned_g[...], grad_gp[:, COLS * h : COLS * h + COLS]).astype(BF)
    swap("S")
    grad_mh = mm_t(grad_pre_s, wa[0, :, 1536:1664])
    grad_mh += mm_t(gp_h[0], wb[0]) + mm_t(gp_h[1], wb[1])
    gk[0, :, 768:896] = mm(turned_h[...], grad_pre_s).astype(BF)
    run(*steps_c[:8])

    grad_n2 = grad_mh * lerp_h + grad_mg * lerp_g
    grad_n2 += shift_up(grad_mh * (1.0 - lerp_h) + grad_mg * (1.0 - lerp_g))
    delta2 = normed2 - previous2
    g_lerp_h, g_lerp_g = tsum(grad_mh * delta2), tsum(grad_mg * delta2)
    g_gain2, g_bias2 = tsum(grad_n2 * unit2), tsum(grad_n2)
    q2 = grad_n2 * gain2
    grad_middle = upstream + scale2 * (q2 - mean(q2) - unit2 * mean(q2 * unit2))

    grad_attn = grad_middle.astype(BF)
    grad_gated = mm_t(grad_attn[:, :COLS], wo[0]) + mm_t(grad_attn[:, COLS:], wo[1])
    for h in range(2):
        go[h] = mm(turned_w[...], grad_attn[:, COLS * h : COLS * h + COLS]).astype(BF)
    swap_w("o")
    grad_gate = (grad_gated * grouped * (sig * (1.0 + gate_pre * (1.0 - sig)))).astype(BF)
    grad_grouped = grad_gated * silu
    g_gain_w, g_bias_w = tsum(grad_grouped * unit_w), tsum(grad_grouped)
    qw = grad_grouped * gain_w
    grad_wkv = scale_w * (
        qw
        - head_sum(qw) * (1.0 / 64.0)
        - unit_w * (head_sum(qw * unit_w) * (1.0 / 64.0))
    )

    weight = head_sum(grad_wkv * vals)
    parts_r, parts_k, parts_v = [], [], []
    for g in range(6):
        cut = slice(128 * g, 128 * g + 128)
        rg, kg, vg, dg = recept_f[:, cut], keys_f[:, cut], vals[:, cut], grad_wkv[:, cut]
        ds = stack(dg)
        da = jnp.where(below, fine(NT, ds, vg), 0.0)
        parts_r.append(fine(NN, beside(da), stack(kg)) + fine(NT, dg, memory[g]))
        parts_k.append(fine(TN, da, stack(rg)))
        parts_v.append(fine(TN, scores[g], ds))
        if g == 3:
            run(*steps_b[8:12])
        if g == 5:
            run(*steps_o[:4])
    grad_r = jnp.concatenate(parts_r, axis=1) * fall_r
    grad_k = jnp.concatenate(parts_k, axis=1) * fall_k
    grad_v = jnp.concatenate(parts_v, axis=1) + grad_wkv * present
    g_rate = fade * tsum(steps * recept * grad_r - (steps + 1.0) * keys * grad_k)
    g_bonus = tsum(recept * keys * weight)
    grad_r = (grad_r + bonus * keys * weight).astype(BF)
    grad_k = (grad_k + bonus * recept * weight).astype(BF)
    grad_v = grad_v.astype(BF)

    gr[0] = mm(turned[0], grad_r).astype(BF)
    gr[1] = mm(turned[2], grad_v).astype(BF)
    swap("R")
    grad_blended = [
        mm_t(grad_r, wa[0, :, 0:768]),
        mm_t(grad_k, wa[0, :, 768:1536]),
        mm_t(grad_v, wa[1, :, 0:768]),
        mm_t(grad_gate, wa[1, :, 768:1536]),
    ]
    gk[0, :, 0:768] = mm(turned[1], grad_k).astype(BF)
    gk[1, :, 0:768] = mm(turned[3], grad_gate).astype(BF)
    net.send(gk.at[1 - c, :, 0:768], sib_k.at[:, 0:768], sib, "swap K")
    run(*steps_r[:8], *steps_2[4:6])
    delta = normed - previous
    g_lerps = [tsum(g * delta) for g in grad_blended]
    grad_n1 = sum(g * l for g, l in zip(grad_blended, lerps))
    grad_n1 += shift_up(sum(g * (1.0 - l) for g, l in zip(grad_blended, lerps)))
    g_gain1, g_bias1 = tsum(grad_n1 * unit1), tsum(grad_n1)

    zero = jnp.zeros((1, EMB), F32)
    natural = jnp.concatenate([g_rate, g_bonus, g_gain_w, g_bias_w] + [zero] * 4, axis=0)
    high, low = split(natural, 2)
    moved = mm(high, spread[...]) + mm(low, spread[...])
    table = jnp.concatenate(
        [g_gain1, g_bias1] + g_lerps + [g_gain2, g_bias2, g_lerp_h, g_lerp_g]
        + [moved[0:4], jnp.zeros((114, EMB), F32)],
        axis=0,
    )
    gk[1, :, 768:896] = table.T.astype(BF)
    net.send(gk.at[1 - c, :, 768:896], sib_k.at[:, 768:896], sib, "swap K")
    swaps["K"] = partial(net.wait_group, "swap K", sib_k, sib)
    run(*steps_c[8:12], *steps_b[12:16], *steps_k[:8], *steps_r[8:12])
    out_v, grad_v_ = pre_h.at[0, :, 0:768], pre_h.at[1, :, 0:768]
    out_v[...] = unspread(layer_out)
    out_copy = pltpu.make_async_copy(out_v, out_ref, load_sems.at[8])
    out_copy.start()
    run(*steps_o[4:6], *steps_c[12:16], *steps_k[8:12], *steps_2[6:8])

    piece_z = stage_z

    def spread_z(m):
        table = mm(turn_z[...], sum_z[m])
        for xhi in range(2):
            for y in range(4):
                x = xhi * 2 + m
                at_ = (xhi * 4 + y) * 64
                spot = piece_z.at[at.by_core(x, y), rows(64 * at.by_core(y, x), 64)]
                spot[...] = table[at_ : at_ + 64].astype(BF)

    run(*steps_o[6:8])
    spread_z(0)
    spread_z(1)
    for k in (1, 3, 2):
        net.send(piece_z.at[rem4(at.two + k)], across_z.at[k - 1], at.last("B", k), "grad two")
    run(steps_b[16])
    q1 = grad_n1 * gain1
    grad_x = grad_middle + scale1 * (q1 - mean(q1) - unit1 * mean(q1 * unit1))
    grad_v_[...] = unspread(grad_x)
    grad_copy = pltpu.make_async_copy(grad_v_, in_grad_ref, load_sems.at[9])
    grad_copy.start()
    run(*steps_r[12:16], *steps_k[12:16], steps_c[16])
    spread_lines(
        1, acc_b[:, 0:LEFT], jnp.concatenate([acc_b[:, LEFT:], acc_c[...]], axis=1), piece_b, line_b
    )
    net.wait_group("grad two", across_z, sib)
    total = wide(piece_z.at[at.two])
    for k in (1, 2, 3):
        total += wide(across_z.at[k - 1])
    row_f[...] = total.reshape(4, 64, COLS)
    row_b[...] = row_f[...].astype(BF)
    for k in (1, 2, 3):
        net.send(row_b.at[rem4(at.one + k)], side_z.at[k - 1], at.first("B", k), "grad one")
    run(steps_r[16], steps_k[16])
    acc_a = jnp.concatenate([acc_r[...], acc_k[...]], axis=1)
    spread_lines(0, acc_a[:, 0:LEFT], acc_a[:, LEFT:], piece_a, line_a)
    sum_lines(1, line_b)
    net.wait_group("grad one", side_z, sib)
    total = row_f[at.one]
    for k in (1, 2, 3):
        total += wide(side_z.at[k - 1])
    swap_f[...] = total
    away, kept = rows(32 * (1 - c), 32, 8), rows(32 * c, 32, 8)
    last_swap = net.send(swap_f.at[away], swapped_z.at[c], sib)
    swapped_z[c] = swap_f[kept]
    last_swap.wait_recv()
    columns = jnp.concatenate(
        [
            jnp.concatenate([swapped_z[0], swapped_z[1]], axis=1),
            jnp.concatenate([end_n[0, 1, 8:16, 384:768], end_n[1, 1, 8:16, 384:768]], axis=1),
        ],
        axis=0,
    )
    end_z[...] = unspread(columns)
    out_copy.wait()
    grad_copy.wait()
    sum_lines(0, line_a)
    net.drain()


def layer(*operands):
    bf = lambda *shape: pltpu.VMEM(shape, BF)
    f32 = lambda *shape: pltpu.VMEM(shape, F32)
    a, b, d, r, k = (WIDTH[q] for q in "ABCRK")
    return pl.pallas_call(
        layer_kernel,
        out_shape=(
            jax.ShapeDtypeStruct((TOK, EMB), F32),
            jax.ShapeDtypeStruct((TOK, EMB), F32),
            jax.ShapeDtypeStruct((2, 2, 16, LEFT), F32),
            jax.ShapeDtypeStruct((40, EMB), F32),
        ),
        in_specs=[pl.BlockSpec(memory_space=pl.ANY)] * 8 + [VMEM] * (len(operands) - 8),
        out_specs=(pl.BlockSpec(memory_space=pl.ANY),) * 2 + (VMEM,) * 2,
        scratch_shapes=[
            bf(TOK, EMB), bf(TOK, EMB), f32(12, 64, 64), bf(EMB, EMB),
            bf(96, 128), bf(432, 512), bf(128, 96), bf(512, 432), f32(6, 128, 128),
            bf(2, EMB, a), bf(2, EMB, b), bf(2, EMB, d), bf(2, EMB, COLS), bf(2, FF, COLS),
            bf(2, EMB, b), f32(6, 256, 128),
            f32(128, 128), f32(2, 2, 16, LEFT), bf(2, 2, 16, LEFT), bf(8, 16, LEFT), bf(8, 16, LEFT),
            f32(48, EMB), bf(2, 32, COLS), bf(64, COLS), bf(256, COLS), bf(4, 256, COLS),
            *(bf(EMB, w) for w in (r, k, b, d)), *(bf(4, 48, w) for w in (r, k, b, d)),
            *(bf(2, 4, 48, w) for w in (r, k, b, d)), *(bf(3, 48, w) for w in (r, k, b, d)),
            *(f32(48, w) for w in (r, k, b, d)),
            bf(8, 16, LEFT), bf(8, 16, LEFT), bf(8, 16, LEFT), bf(8, 16, LEFT),
            bf(EMB, COLS), bf(FF, COLS),
            bf(2, 96, COLS), bf(2, 336, COLS), bf(2, 2, 96, COLS), bf(2, 2, 336, COLS),
            bf(2, 432, COLS),
            bf(3, 256, COLS), f32(4, 64, COLS), bf(4, 64, COLS), bf(3, 64, COLS),
            f32(64, COLS), f32(2, 32, COLS),
            f32(2, TOK, b), bf(2, TOK, b), bf(2, TOK, b), bf(2, TOK, COLS),
            bf(4, EMB, TOK), bf(EMB, TOK), bf(EMB, TOK), bf(EMB, TOK),
            pltpu.SemaphoreType.DMA((SENDS,)),
            pltpu.SemaphoreType.DMA((ARRIVALS,)),
            pltpu.SemaphoreType.DMA((10,)),
        ],
        compiler_params=pltpu.CompilerParams(
            collective_id=1, has_side_effects=True, vmem_limit_bytes=62 << 20
        ),
        cost_estimate=pl.CostEstimate(
            flops=6 * TOK * 7667712, bytes_accessed=4 * 7667712, transcendentals=10 * TOK * EMB
        ),
        name="layer",
    )(*operands)


def finish_kernel(end_n, end_z, out_in, grad_in, out, grad, *refs):
    vecs, mats = refs[:14], refs[14:]
    acceptor, address, content, sigmoid, mixer, ff_address, ff_content, ff_acceptor = mats
    out[...] = out_in[...]
    grad[...] = grad_in[...]
    acceptor[...] = end_n[0, 0, 0:6, 0:768]
    address[:, 0:128] = end_n[0, 0, 0:6, 768:896]
    address[:, 128:768] = end_n[0, 0, 8:14, 0:640]
    content[...] = end_n[1, 0, 0:6, 0:768]
    sigmoid[:, 0:128] = end_n[1, 0, 0:6, 768:896]
    sigmoid[:, 128:768] = end_n[1, 0, 8:14, 0:640]
    ff_address[:, 0:128] = end_n[0, 0, 8:14, 640:768]
    for h in range(2):
        first_col = 128 + 1280 * h
        ff_address[:, first_col : first_col + 896] = end_n[h, 1, 0:6, 0:896]
        ff_address[:, first_col + 896 : first_col + 1280] = end_n[h, 1, 8:14, 0:384]
    table = jnp.concatenate([end_n[1, 0, 8:16, 640:768], jnp.zeros((120, 128), F32)], axis=0).T
    for i, ref in enumerate(vecs):
        ref[...] = table[i : i + 1, 0:6].reshape(6)
    mixer[...] = end_z[0:6]
    ff_content[...] = end_z[8:29]
    ff_acceptor[...] = end_z[32:38]


def finish(end_n, end_z, out, grad):
    shapes = [(TOK, EMB), (TOK, EMB)] + [(6,)] * 14
    shapes += [(6, EMB)] * 5 + [(6, FF), (21, EMB), (6, EMB)]
    return pl.pallas_call(
        finish_kernel,
        out_shape=tuple(jax.ShapeDtypeStruct(shape, F32) for shape in shapes),
        in_specs=[VMEM] * 4,
        out_specs=(VMEM,) * len(shapes),
        name="finish",
    )(end_n, end_z, out, grad)


def per_device(
    incoming_activations,
    sequence_opening_memory,
    prior_standardize_factor,
    prior_standardize_offset,
    acceptor_lerp_factor,
    address_lerp_factor,
    content_lerp_factor,
    sigmoid_lerp_factor,
    acceptor_matrix,
    address_matrix,
    content_matrix,
    sigmoid_matrix,
    lane_fading_exponent,
    present_reward_vector,
    cluster_standardize_factor,
    cluster_standardize_offset,
    mixer_result_matrix,
    latter_standardize_factor,
    latter_standardize_offset,
    feedforward_address_lerp,
    feedforward_sigmoid_lerp,
    feedforward_address_matrix,
    feedforward_content_matrix,
    feedforward_acceptor_matrix,
    upstream_derivative,
):
    spread = jnp.asarray(_spread(), BF)
    out, in_grad, end_n, end_z = layer(
        incoming_activations, upstream_derivative,
        sequence_opening_memory.reshape(12, 64, 64), spread,
        jnp.asarray(_line_pick(), BF), jnp.asarray(_plane_pick(), BF),
        jnp.asarray(_line_pick().T, BF), jnp.asarray(_plane_pick().T, BF),
        prior_standardize_factor, prior_standardize_offset, acceptor_lerp_factor,
        address_lerp_factor, content_lerp_factor, sigmoid_lerp_factor,
        latter_standardize_factor, latter_standardize_offset, feedforward_address_lerp,
        feedforward_sigmoid_lerp, lane_fading_exponent, present_reward_vector,
        cluster_standardize_factor, cluster_standardize_offset,
        acceptor_matrix, address_matrix, content_matrix, sigmoid_matrix,
        mixer_result_matrix, feedforward_address_matrix, feedforward_content_matrix,
        feedforward_acceptor_matrix,
    )
    results = finish(end_n, end_z, out, in_grad)
    out, in_grad, v = results[0], results[1], results[2:16]
    acceptor, address, content, sigmoid, mixer, ff_address, ff_content, ff_acceptor = results[16:]
    return (
        out, in_grad,
        v[0], v[1], v[2], v[3], v[4], v[5],
        acceptor, address, content, sigmoid,
        v[10], v[11], v[12], v[13],
        mixer,
        v[6], v[7], v[8], v[9],
        ff_address, ff_content, ff_acceptor,
    )


def solution(mesh):
    r, v = P(("dp", "fsdp"), None), P(("dp", "fsdp"))
    state = P(("dp", "fsdp"), None, None, None)
    return jax.shard_map(
        per_device,
        mesh=mesh,
        in_specs=(r, state) + (v,) * 6 + (r,) * 4 + (v,) * 4 + (r,) + (v,) * 4 + (r,) * 4,
        out_specs=(r, r) + (v,) * 6 + (r,) * 4 + (v,) * 4 + (r,) + (v,) * 4 + (r,) * 3,
        check_vma=False,
    )
```
